32 devices in a mesh: grp: 2 (over y), dp: 4 (over x, core), slab: 4 (over z).
Axes of the slice: x: 2, y: 2, z: 4, core: 2. Of those that a mesh axis runs over, the one named last changes fastest.
Arguments:
- feats: bfloat16 [8, 32, 32, 128, 128], P(('grp', 'dp'), None, 'slab'), parts along dimension 0, may hold values from -6 to 6
- grains: int32 [8, 32, 128, 128], P(('grp', 'dp'), 'slab'), parts along dimension 0, may hold values from 0 to 4095
- spec_weight: bfloat16 [256, 16, 2048], P('slab'), may hold values from -0.75 to 0.75
- taps: float32 [27, 32], replicated, may hold values from -1.25 to 1.25
- point_weight: bfloat16 [32, 32], replicated, may hold values from -1 to 1
- bias: float32 [32], replicated, may hold values from -4 to 4
- cotangent: bfloat16 [8, 32, 32, 128, 128], P(('grp', 'dp'), None, 'slab'), parts along dimension 0, may hold values from -3 to 3
Outputs:
- grad_feats: bfloat16 [8, 32, 32, 128, 128], P(('grp', 'dp'), None, 'slab'), parts along dimension 0
- grad_spec: float32 [256, 32, 2048], P('slab', 'grp', 'dp'), parts along dimension 1
The draws below stay inside these ranges and needn't reach their ends.
There are 2 independent parts, one for each index of `grp`. The reference program is written for one: setup_inputs(seed, part) draws one part's arguments, and reference() takes and returns one part's arrays. A program takes and returns all parts, laid end to end along the dimension named above; an argument that names none is the same for every part. Nothing has to cross between parts.
All inputs are finite; a program needn't handle non-finite values.
Results may differ from the reference program's by a relative error of at most 0.017.
Values may be sent and summed in bfloat16 or wider, within the bound.
No kernel may reach another device: no remote copies, remote signals or barrier semaphores. Data moves between devices by JAX's collectives and lax.ppermute only.
A program may use at most 192 MiB of HBM per device.

```python
import math
import jax
import jax.numpy as jnp
from jax import lax

C = 32
NX = 128
NY = 128
NZ = 32
KX = 16
KY = 16
KZ = 16
GRAINS = 4096
SAMPLES = 4


def draw_grains(key, part):
    key_table, key_shift_x, key_shift_y = jax.random.split(jax.random.fold_in(key, 11), 3)
    blocks_x = NX // 8 + 1
    blocks_y = NY // 8 + 1
    table = jax.random.randint(key_table, (SAMPLES, NZ, blocks_x, blocks_y), 0, GRAINS, dtype=jnp.int32)
    table = table.at[0, 0, 0, 0].set(GRAINS - 1)
    shift_x = jax.random.randint(key_shift_x, (SAMPLES, NZ, 1, NY), 0, 8, dtype=jnp.int32)
    shift_y = jax.random.randint(key_shift_y, (SAMPLES, NZ, NX, 1), 0, 8, dtype=jnp.int32)
    block_x = (jnp.arange(NX, dtype=jnp.int32)[None, None, :, None] + shift_x) // 8
    block_y = (jnp.arange(NY, dtype=jnp.int32)[None, None, None, :] + shift_y) // 8
    sample_index = jnp.arange(SAMPLES, dtype=jnp.int32)[:, None, None, None]
    plane_index = jnp.arange(NZ, dtype=jnp.int32)[None, :, None, None]
    return table[sample_index, plane_index, block_x, block_y]


def level_of(stream_key, extent, cuts, smallest, top_value):
    gain, own = 1.0, jax.random.fold_in(stream_key, 6)
    for dim, shards_of in cuts:
        draws = jnp.exp(jax.random.uniform(jax.random.fold_in(own, dim), (shards_of,), jnp.float32, smallest / len(cuts), top_value / len(cuts)))
        gain = gain * jnp.repeat(draws, extent[dim] // shards_of).reshape([-1 if axis == dim else 1 for axis in range(len(extent))])
    return gain


def centred(stream_key, dims, scale, most, cuts=(), kind=jnp.bfloat16):
    array = jax.random.normal(stream_key, dims, jnp.float32) * scale
    if len(cuts) > 0:
        array = level_of(stream_key, dims, cuts, -0.22, 0.18) * array
    return jnp.clip(array, min=-most, max=most).astype(kind)


def setup_inputs(seed: int = 0, part: int = 0) -> dict:
    seeds = jax.random.split(jax.random.key(seed), 8)
    part_splits = jax.random.split(jax.random.fold_in(seeds[7], part), 8)
    feats = centred(part_splits[0], (SAMPLES, C, NZ, NX, NY), 1.0, 6.0, ((0, 4), (2, 4)))
    grains = draw_grains(jax.random.fold_in(jax.random.fold_in(seeds[7], part), 71), part)
    spec_weight = centred(seeds[2], (KX * KY, KZ, 2 * C * C), (2 * C) ** -0.5, 0.75, ((0, 4),))
    taps = centred(seeds[3], (27, C), 27 ** -0.5, 1.25, (), jnp.float32)
    point_weight = centred(seeds[4], (C, C), C ** -0.5, 1.0)
    bias = centred(seeds[5], (C,), 1.0, 4.0, (), jnp.float32)
    cotangent = centred(part_splits[6], (SAMPLES, C, NZ, NX, NY), 0.5, 3.0, ((0, 4), (2, 4)))
    return {"feats": feats, "grains": grains, "spec_weight": spec_weight, "taps": taps, "point_weight": point_weight, "bias": bias, "cotangent": cotangent}


HIGHEST = lax.Precision.HIGHEST

def tables(count, length, start, span):
    indices = jnp.arange(count, dtype=jnp.int32)
    frequency = jnp.where(indices < count // 2, indices, length - count + indices)
    position = start + jnp.arange(span, dtype=jnp.int32)
    phases = frequency[:, None] * position[None, :] % length
    angles = phases.astype(jnp.float32) * (2.0 * math.pi / length)
    return (jnp.cos(angles), jnp.sin(angles))

def mobility(grains):
    leading = [(0, 0)] * (grains.ndim - 2)
    along_x = (grains[..., 1:, :] != grains[..., :-1, :]).astype(jnp.float32)
    along_y = (grains[..., :, 1:] != grains[..., :, :-1]).astype(jnp.float32)
    differ = jnp.pad(along_x, leading + [(1, 0), (0, 0)]) + jnp.pad(along_x, leading + [(0, 1), (0, 0)])
    differ = differ + jnp.pad(along_y, leading + [(0, 0), (1, 0)]) + jnp.pad(along_y, leading + [(0, 0), (0, 1)])
    return 0.25 * (1.0 + differ)

def stencil(padded, taps, adjoint):
    planes = padded.shape[-3] - 2
    rows_x = padded.shape[-2] - 2
    rows_y = padded.shape[-1] - 2
    total = jnp.zeros(padded.shape[:-3] + (planes, rows_x, rows_y), jnp.float32)
    for offset in range(27):
        shift_z, shift_x, shift_y = (offset // 9, offset // 3 % 3, offset % 3)
        if adjoint:
            shift_z, shift_x, shift_y = (2 - shift_z, 2 - shift_x, 2 - shift_y)
        window = padded[..., shift_z:shift_z + planes, shift_x:shift_x + rows_x, shift_y:shift_y + rows_y]
        total = total + taps[offset][:, None, None, None] * window.astype(jnp.float32)
    return total

def plane_forward(field, cos_x, sin_x, cos_y, sin_y):
    real_y = jnp.einsum('...xy,ky->...xk', field, cos_y, precision=HIGHEST)
    imag_y = -jnp.einsum('...xy,ky->...xk', field, sin_y, precision=HIGHEST)
    real_part = jnp.einsum('...xk,jx->...jk', real_y, cos_x, precision=HIGHEST) + jnp.einsum('...xk,jx->...jk', imag_y, sin_x, precision=HIGHEST)
    imag_part = jnp.einsum('...xk,jx->...jk', imag_y, cos_x, precision=HIGHEST) - jnp.einsum('...xk,jx->...jk', real_y, sin_x, precision=HIGHEST)
    return (real_part, imag_part)

def plane_inverse(real_part, imag_part, cos_x, sin_x, cos_y, sin_y):
    real_x = jnp.einsum('...jk,jx->...xk', real_part, cos_x, precision=HIGHEST) - jnp.einsum('...jk,jx->...xk', imag_part, sin_x, precision=HIGHEST)
    imag_x = jnp.einsum('...jk,jx->...xk', imag_part, cos_x, precision=HIGHEST) + jnp.einsum('...jk,jx->...xk', real_part, sin_x, precision=HIGHEST)
    return jnp.einsum('...xk,ky->...xy', real_x, cos_y, precision=HIGHEST) - jnp.einsum('...xk,ky->...xy', imag_x, sin_y, precision=HIGHEST)

def reference(feats, grains, spec_weight, taps, point_weight, bias, cotangent):
    cos_x, sin_x = tables(KX, NX, 0, NX)
    cos_y, sin_y = tables(KY, NY, 0, NY)
    cos_z, sin_z = tables(KZ, NZ, 0, NZ)
    cell_scale = math.sqrt(NX * NY * NZ)
    mode_scale = math.sqrt(KX * KY * KZ)
    weights = spec_weight.astype(jnp.float32).reshape(KX * KY, KZ, 2, C, C)
    w_real = weights[:, :, 0]
    w_imag = weights[:, :, 1]
    point_wide = point_weight.astype(jnp.float32)

    def forward_modes(field):
        real_plane, imag_plane = plane_forward(field, cos_x, sin_x, cos_y, sin_y)
        real_modes = jnp.einsum('czjk,lz->cljk', real_plane, cos_z, precision=HIGHEST) + jnp.einsum('czjk,lz->cljk', imag_plane, sin_z, precision=HIGHEST)
        imag_modes = jnp.einsum('czjk,lz->cljk', imag_plane, cos_z, precision=HIGHEST) - jnp.einsum('czjk,lz->cljk', real_plane, sin_z, precision=HIGHEST)
        real_modes = real_modes.transpose(2, 3, 1, 0).reshape(KX * KY, KZ, C)
        imag_modes = imag_modes.transpose(2, 3, 1, 0).reshape(KX * KY, KZ, C)
        return (real_modes, imag_modes)

    def inverse_modes(real_modes, imag_modes):
        real_in = real_modes.reshape(KX, KY, KZ, C).transpose(3, 2, 0, 1)
        imag_in = imag_modes.reshape(KX, KY, KZ, C).transpose(3, 2, 0, 1)
        real_plane = jnp.einsum('cljk,lz->czjk', real_in, cos_z, precision=HIGHEST) - jnp.einsum('cljk,lz->czjk', imag_in, sin_z, precision=HIGHEST)
        imag_plane = jnp.einsum('cljk,lz->czjk', imag_in, cos_z, precision=HIGHEST) + jnp.einsum('cljk,lz->czjk', real_in, sin_z, precision=HIGHEST)
        return plane_inverse(real_plane, imag_plane, cos_x, sin_x, cos_y, sin_y)

    def one_sample(carry, inputs):
        field, sample_grains, sample_cotangent = inputs
        moving = mobility(sample_grains)[None]
        padded = jnp.pad(field, ((0, 0), (1, 1), (1, 1), (1, 1)))
        smooth = stencil(padded, taps, False).astype(jnp.bfloat16)
        local_part = moving * jnp.einsum('czxy,co->ozxy', smooth.astype(jnp.float32), point_wide, precision=HIGHEST)
        spec_real, spec_imag = forward_modes(field.astype(jnp.float32))
        spec_real = spec_real / cell_scale
        spec_imag = spec_imag / cell_scale
        mixed_real = jnp.einsum('pkc,pkco->pko', spec_real, w_real, precision=HIGHEST) - jnp.einsum('pkc,pkco->pko', spec_imag, w_imag, precision=HIGHEST)
        mixed_imag = jnp.einsum('pkc,pkco->pko', spec_real, w_imag, precision=HIGHEST) + jnp.einsum('pkc,pkco->pko', spec_imag, w_real, precision=HIGHEST)
        spectral = inverse_modes(mixed_real, mixed_imag) / mode_scale
        pre = spectral + local_part + bias[:, None, None, None]
        gate = jax.nn.sigmoid(pre)
        delta = (sample_cotangent.astype(jnp.float32) * gate * (1.0 + pre * (1.0 - gate))).astype(jnp.bfloat16)
        dual_real, dual_imag = forward_modes(delta.astype(jnp.float32))
        dual_real = dual_real / mode_scale
        dual_imag = dual_imag / mode_scale
        grad_real = jnp.einsum('pkc,pko->pkco', spec_real, dual_real, precision=HIGHEST) + jnp.einsum('pkc,pko->pkco', spec_imag, dual_imag, precision=HIGHEST)
        grad_imag = jnp.einsum('pkc,pko->pkco', spec_real, dual_imag, precision=HIGHEST) - jnp.einsum('pkc,pko->pkco', spec_imag, dual_real, precision=HIGHEST)
        back_real = jnp.einsum('pko,pkco->pkc', dual_real, w_real, precision=HIGHEST) + jnp.einsum('pko,pkco->pkc', dual_imag, w_imag, precision=HIGHEST)
        back_imag = jnp.einsum('pko,pkco->pkc', dual_imag, w_real, precision=HIGHEST) - jnp.einsum('pko,pkco->pkc', dual_real, w_imag, precision=HIGHEST)
        spectral_back = inverse_modes(back_real, back_imag) / cell_scale
        spread = (moving * jnp.einsum('ozxy,co->czxy', delta.astype(jnp.float32), point_wide, precision=HIGHEST)).astype(jnp.bfloat16)
        local_back = stencil(jnp.pad(spread, ((0, 0), (1, 1), (1, 1), (1, 1))), taps, True)
        grad_field = (spectral_back + local_back).astype(jnp.bfloat16)
        carry = carry + jnp.stack([grad_real, grad_imag], axis=2)
        return (carry, grad_field)
    start = jnp.zeros((KX * KY, KZ, 2, C, C), jnp.float32)
    summed, grad_feats = lax.scan(one_sample, start, (feats, grains, cotangent))
    grad_spec = (summed / SAMPLES).reshape(KX * KY, KZ, 2 * C * C)
    return (grad_feats, grad_spec)
```

```python
import functools
import math

import jax
import jax.numpy as jnp
import ml_dtypes
import numpy as np
from jax import lax
from jax.experimental import pallas as pl
from jax.experimental.pallas import tpu as pltpu
from jax.sharding import PartitionSpec as P

NX = 128
NY = 128
NZ = 32
KX = 16
KY = 16
KZ = 16


HIGHEST = lax.Precision.HIGHEST


def extended(shard, sides, width):
    for axis, dim in sides:
        size, length = (lax.axis_size(axis), shard.shape[dim])
        up = [(i, (i + 1) % size) for i in range(size - 1)]
        down = [(j, i) for i, j in up]
        last = lax.slice_in_dim(shard, length - width, length, axis=dim)
        first = lax.slice_in_dim(shard, 0, width, axis=dim)
        before = lax.ppermute(last, axis, up)
        after = lax.ppermute(first, axis, down)
        shard = jnp.concatenate([before, shard, after], axis=dim)
    return shard


def tables(count, length, span):
    indices = jnp.arange(count, dtype=jnp.int32)
    frequency = jnp.where(indices < count // 2, indices, length - count + indices)
    position = jnp.arange(span, dtype=jnp.int32)
    phases = frequency[:, None] * position[None, :] % length
    angles = phases.astype(jnp.float32) * (2.0 * math.pi / length)
    return (jnp.cos(angles), jnp.sin(angles))


def mobility(grains):
    leading = [(0, 0)] * (grains.ndim - 2)
    along_x = (grains[..., 1:, :] != grains[..., :-1, :]).astype(jnp.float32)
    along_y = (grains[..., :, 1:] != grains[..., :, :-1]).astype(jnp.float32)
    differ = jnp.pad(along_x, leading + [(1, 0), (0, 0)]) + jnp.pad(
        along_x, leading + [(0, 1), (0, 0)]
    )
    differ = (
        differ
        + jnp.pad(along_y, leading + [(0, 0), (1, 0)])
        + jnp.pad(along_y, leading + [(0, 0), (0, 1)])
    )
    return 0.25 * (1.0 + differ)


def stencil(padded, taps, adjoint):
    planes = padded.shape[-3] - 2
    rows_x = padded.shape[-2] - 2
    rows_y = padded.shape[-1] - 2
    total = jnp.zeros(padded.shape[:-3] + (planes, rows_x, rows_y), jnp.float32)
    for offset in range(27):
        shift_z, shift_x, shift_y = (offset // 9, offset // 3 % 3, offset % 3)
        if adjoint:
            shift_z, shift_x, shift_y = (2 - shift_z, 2 - shift_x, 2 - shift_y)
        window = padded[
            ..., shift_z : shift_z + planes, shift_x : shift_x + rows_x, shift_y : shift_y + rows_y
        ]
        total = total + taps[offset][:, None, None, None] * window.astype(jnp.float32)
    return total


def plane_forward(field, cos_x, sin_x, cos_y, sin_y):
    real_y = jnp.einsum("...xy,ky->...xk", field, cos_y, precision=HIGHEST)
    imag_y = -jnp.einsum("...xy,ky->...xk", field, sin_y, precision=HIGHEST)
    real_part = jnp.einsum("...xk,jx->...jk", real_y, cos_x, precision=HIGHEST) + jnp.einsum(
        "...xk,jx->...jk", imag_y, sin_x, precision=HIGHEST
    )
    imag_part = jnp.einsum("...xk,jx->...jk", imag_y, cos_x, precision=HIGHEST) - jnp.einsum(
        "...xk,jx->...jk", real_y, sin_x, precision=HIGHEST
    )
    return (real_part, imag_part)


def plane_inverse(real_part, imag_part, cos_x, sin_x, cos_y, sin_y):
    real_x = jnp.einsum("...jk,jx->...xk", real_part, cos_x, precision=HIGHEST) - jnp.einsum(
        "...jk,jx->...xk", imag_part, sin_x, precision=HIGHEST
    )
    imag_x = jnp.einsum("...jk,jx->...xk", imag_part, cos_x, precision=HIGHEST) + jnp.einsum(
        "...jk,jx->...xk", real_part, sin_x, precision=HIGHEST
    )
    return jnp.einsum("...xk,ky->...xy", real_x, cos_y, precision=HIGHEST) - jnp.einsum(
        "...xk,ky->...xy", imag_x, sin_y, precision=HIGHEST
    )


def depth_forward(packed, cos_table, sin_table):
    width = packed.shape[-1] // 2
    real_in = packed[..., :width]
    imag_in = packed[..., width:]
    real_out = jnp.einsum("pszc,kz->pskc", real_in, cos_table, precision=HIGHEST) + jnp.einsum(
        "pszc,kz->pskc", imag_in, sin_table, precision=HIGHEST
    )
    imag_out = jnp.einsum("pszc,kz->pskc", imag_in, cos_table, precision=HIGHEST) - jnp.einsum(
        "pszc,kz->pskc", real_in, sin_table, precision=HIGHEST
    )
    return jnp.concatenate([real_out, imag_out], axis=-1)


def depth_inverse(real_modes, imag_modes, cos_table, sin_table):
    real_out = jnp.einsum("pskc,kz->pszc", real_modes, cos_table, precision=HIGHEST) - jnp.einsum(
        "pskc,kz->pszc", imag_modes, sin_table, precision=HIGHEST
    )
    imag_out = jnp.einsum("pskc,kz->pszc", imag_modes, cos_table, precision=HIGHEST) + jnp.einsum(
        "pskc,kz->pszc", real_modes, sin_table, precision=HIGHEST
    )
    return jnp.concatenate([real_out, imag_out], axis=-1)


def rim_planes(field):
    return extended(field, (("slab", 2),), 1)


def local_any(feats, grains, spec_weight, taps, point_weight, bias, cotangent):
    samples_here = feats.shape[0]
    channels = feats.shape[1]
    planes = feats.shape[2]
    cos_x, sin_x = tables(KX, NX, NX)
    cos_y, sin_y = tables(KY, NY, NY)
    cos_full, sin_full = tables(KZ, NZ, NZ)
    cell_scale = math.sqrt(NX * NY * NZ)
    mode_scale = math.sqrt(KX * KY * KZ)
    mode_rows = spec_weight.shape[0]
    weights = spec_weight.astype(jnp.float32).reshape(mode_rows, KZ, 2, channels, channels)
    w_real = weights[:, :, 0]
    w_imag = weights[:, :, 1]
    moving = mobility(grains)[:, None]

    def to_modes(field):
        real_plane, imag_plane = plane_forward(field, cos_x, sin_x, cos_y, sin_y)
        packed = jnp.stack([real_plane, imag_plane], axis=1)
        packed = packed.transpose(4, 5, 0, 3, 1, 2).reshape(
            KX * KY, samples_here, planes, 2 * channels
        )
        moved = lax.all_to_all(packed, "slab", split_axis=0, concat_axis=2, tiled=True)
        summed = depth_forward(moved, cos_full, sin_full)
        return (summed[..., :channels], summed[..., channels:])

    def from_modes(real_modes, imag_modes):
        planar = depth_inverse(real_modes, imag_modes, cos_full, sin_full)
        packed = lax.all_to_all(planar, "slab", split_axis=2, concat_axis=0, tiled=True)
        grouped = packed.reshape(KX, KY, samples_here, planes, 2, channels).transpose(
            2, 4, 5, 3, 0, 1
        )
        return plane_inverse(grouped[:, 0], grouped[:, 1], cos_x, sin_x, cos_y, sin_y)

    zero_rim = ((0, 0), (0, 0), (0, 0), (1, 1), (1, 1))
    padded = jnp.pad(rim_planes(feats), zero_rim)
    smooth = stencil(padded, taps, False).astype(jnp.bfloat16)
    local_part = moving * jnp.einsum(
        "sczxy,co->sozxy", smooth, point_weight, preferred_element_type=jnp.float32
    )
    spec_real, spec_imag = to_modes(feats.astype(jnp.float32))
    spec_real = spec_real / cell_scale
    spec_imag = spec_imag / cell_scale
    mixed_real = jnp.einsum("pskc,pkco->psko", spec_real, w_real, precision=HIGHEST) - jnp.einsum(
        "pskc,pkco->psko", spec_imag, w_imag, precision=HIGHEST
    )
    mixed_imag = jnp.einsum("pskc,pkco->psko", spec_real, w_imag, precision=HIGHEST) + jnp.einsum(
        "pskc,pkco->psko", spec_imag, w_real, precision=HIGHEST
    )
    spectral = from_modes(mixed_real, mixed_imag) / mode_scale
    pre = spectral + local_part + bias[None, :, None, None, None]
    gate = jax.nn.sigmoid(pre)
    delta = (cotangent.astype(jnp.float32) * gate * (1.0 + pre * (1.0 - gate))).astype(jnp.bfloat16)
    dual_real, dual_imag = to_modes(delta.astype(jnp.float32))
    dual_real = dual_real / mode_scale
    dual_imag = dual_imag / mode_scale
    batch_total = samples_here * lax.axis_size("dp")
    grad_real = jnp.einsum("pskc,psko->pkco", spec_real, dual_real, precision=HIGHEST) + jnp.einsum(
        "pskc,psko->pkco", spec_imag, dual_imag, precision=HIGHEST
    )
    grad_imag = jnp.einsum("pskc,psko->pkco", spec_real, dual_imag, precision=HIGHEST) - jnp.einsum(
        "pskc,psko->pkco", spec_imag, dual_real, precision=HIGHEST
    )
    grad_terms = (jnp.stack([grad_real, grad_imag], axis=2) / batch_total).reshape(
        mode_rows, KZ, 2 * channels * channels
    )
    grad_spec = lax.psum_scatter(
        grad_terms.astype(jnp.bfloat16), "dp", scatter_dimension=2, tiled=True
    ).astype(jnp.float32)
    back_real = jnp.einsum("psko,pkco->pskc", dual_real, w_real, precision=HIGHEST) + jnp.einsum(
        "psko,pkco->pskc", dual_imag, w_imag, precision=HIGHEST
    )
    back_imag = jnp.einsum("psko,pkco->pskc", dual_imag, w_real, precision=HIGHEST) - jnp.einsum(
        "psko,pkco->pskc", dual_real, w_imag, precision=HIGHEST
    )
    spectral_back = from_modes(back_real, back_imag) / cell_scale
    spread = (
        moving
        * jnp.einsum("sozxy,co->sczxy", delta, point_weight, preferred_element_type=jnp.float32)
    ).astype(jnp.bfloat16)
    spread_padded = jnp.pad(rim_planes(spread), zero_rim)
    local_back = stencil(spread_padded, taps, True)
    grad_feats = (spectral_back + local_back).astype(jnp.bfloat16)
    return (grad_feats, grad_spec)


def frequencies(count, length):
    index = np.arange(count)
    return np.where(index < count // 2, index, length - count + index)


def angles(count, length):
    phases = np.outer(frequencies(count, length), np.arange(length)) % length
    return phases * (2.0 * np.pi / length)


def constant(array):
    return jnp.asarray(np.asarray(array, np.float32).astype(ml_dtypes.bfloat16))


def forward_x_table(slabs):
    a = angles(KX, NX).reshape(slabs, KX // slabs, NX)
    trig = np.stack([np.cos(a), np.sin(a)])
    table = np.einsum("tsjx,cd->tscjdx", trig, np.eye(2))
    return table.reshape(2 * slabs * 2 * (KX // slabs), 2 * NX)


def forward_y_table(planes):
    a = angles(KY, NY)
    cos, sin = np.cos(a).T, np.sin(a).T
    block = np.stack([np.stack([cos, -sin], 1), np.stack([-sin, -cos], 1)])
    pick = np.eye(planes).reshape(planes // 2, 2, planes)
    table = np.einsum("pqz,tyrk->pqtyzrk", pick, block)
    return table.reshape(planes // 2, 4 * NY, planes * 2 * KY)


def forward_z_table():
    a = angles(KZ, NZ)
    cos, sin = np.cos(a).T, np.sin(a).T
    block = np.stack([np.stack([cos, -sin], 1), np.stack([sin, cos], 1)], 1)
    table = np.einsum("zrqm,kl->zrkqlm", block, np.eye(KY))
    return table.reshape(NZ * 2 * KY, 2 * KY * KZ)


def inverse_z_table():
    a = angles(KZ, NZ)
    cos, sin = np.cos(a), np.sin(a)
    block = np.stack([np.stack([cos, sin], 2), np.stack([-sin, cos], 2)])
    table = np.einsum("rmzq,kl->rkmzql", block, np.eye(KY))
    return table.reshape(2 * KY * KZ, NZ * 2 * KY)


def inverse_y_table(planes):
    a = angles(KY, NY)
    cos, sin = np.cos(a), np.sin(a)
    block = np.stack([np.stack([cos, -sin], 1), np.stack([-sin, -cos], 1)])
    pick = np.eye(planes).reshape(planes // 2, 2, planes)
    table = np.einsum("pqz,rkty->pzrktqy", pick, block)
    return table.reshape(planes // 2, planes * 2 * KY, 4 * NY)


def inverse_x_table(slabs):
    a = angles(KX, NX).reshape(slabs, KX // slabs, NX)
    trig = np.stack([np.cos(a), np.sin(a)])
    table = np.einsum("tsjx,cd->cxstdj", trig, np.eye(8))
    return table.reshape(8 * NX, 2 * KX * 8)


def first_table(channels, depth):
    table = np.einsum("ac,j,b->ajcb", np.eye(channels), np.ones(depth), np.ones(channels))
    return table.reshape(channels * depth, channels * channels)


def second_table(channels, depth):
    table = np.einsum("ac,j,b->ajbc", np.eye(channels), np.ones(depth), np.ones(channels))
    return table.reshape(channels * depth, channels * channels)


def dot(a, b):
    return jnp.dot(a, b, preferred_element_type=jnp.float32)


def whole(shape):
    return pl.BlockSpec(shape, lambda *_: (0,) * len(shape))


def params(**kw):
    return pltpu.CompilerParams(vmem_limit_bytes=48 * 2**20, **kw)


def modes_step(load, x_table, y_table, rows, total, pair):
    slabs = total.shape[0]
    for i in range(rows.shape[3] // 8):
        part = dot(x_table[...], load(i))
        for t in range(2):
            for s in range(slabs):
                at = 8 * (t * slabs + s)
                for q in range(2):
                    rows[q, t, s, 8 * i : 8 * i + 8, :] = part[at : at + 8, q * NY : q * NY + NY]
    for s in range(slabs):
        left = [rows[q, t, s].astype(jnp.bfloat16) for q in range(2) for t in range(2)]
        step = dot(jnp.concatenate(left, axis=1), y_table[0])
        before = jnp.where(pair == 0, 0.0, total[s])
        total[s] = before + step


def forward_kernel(field, x_table, y_table, out, rows, total):
    pair = pl.program_id(0)

    def load(i):
        halves = [field[2 * i : 2 * i + 2, q].reshape(2 * NX, NY) for q in range(2)]
        return jnp.concatenate(halves, axis=1)

    modes_step(load, x_table, y_table, rows, total, pair)

    @pl.when(pair == pl.num_programs(0) - 1)
    def _():
        out[...] = total[...].astype(jnp.bfloat16)


def forward_modes(field, slabs):
    channels, planes = field.shape[:2]
    lines = channels * (KX // slabs)
    x_table = constant(forward_x_table(slabs))
    y_table = constant(forward_y_table(planes))
    shape = (slabs, lines, planes * 2 * KY)
    return pl.pallas_call(
        forward_kernel,
        grid=(planes // 2,),
        in_specs=[
            pl.BlockSpec((channels, 2, NX, NY), lambda p: (0, p, 0, 0)),
            whole(x_table.shape),
            pl.BlockSpec((1,) + y_table.shape[1:], lambda p: (p, 0, 0)),
        ],
        out_specs=whole(shape),
        out_shape=jax.ShapeDtypeStruct(shape, jnp.bfloat16),
        scratch_shapes=[
            pltpu.VMEM((2, 2, slabs, lines, NY), jnp.float32),
            pltpu.VMEM(shape, jnp.float32),
        ],
        compiler_params=params(),
        cost_estimate=pl.CostEstimate(flops=10**10, bytes_accessed=10**7, transcendentals=0),
        name="forward_modes",
    )(field, x_table, y_table)


def mixing_kernel(scale_in, scale_out, adjoint, planar, weight, z_in, z_out, spread_table,
                  sum_table, spectrum, out, total):
    step = pl.program_id(0)
    steps = pl.num_programs(0)
    slabs = planar.shape[0]
    width = planar.shape[2]
    half = spectrum.shape[0] // 2
    lanes = weight.shape[1] // 2

    @pl.when(step == 0)
    def _():
        modes = dot(planar[0], z_in[0:width, :])
        for s in range(1, slabs):
            modes = modes + dot(planar[s], z_in[s * width : (s + 1) * width, :])
        spectrum[...] = (modes.T * scale_in).astype(jnp.bfloat16)
        total[...] = jnp.zeros_like(total)

    block = 64
    lane = lax.broadcasted_iota(jnp.int32, (1, spectrum.shape[1]), 1)
    mine = lane % steps == step
    for at in range(0, half, block):
        real_in = jnp.where(mine, spectrum[at : at + block, :], 0)
        imag_in = jnp.where(mine, spectrum[half + at : half + at + block, :], 0)
        real_wide = dot(real_in, spread_table[...])
        imag_wide = dot(imag_in, spread_table[...])
        w_real = weight[at : at + block, :lanes].astype(jnp.float32)
        w_imag = weight[at : at + block, lanes:].astype(jnp.float32)
        if adjoint:
            real = real_wide * w_real + imag_wide * w_imag
            imag = imag_wide * w_real - real_wide * w_imag
        else:
            real = real_wide * w_real - imag_wide * w_imag
            imag = real_wide * w_imag + imag_wide * w_real
        real_sum = dot(real.astype(jnp.bfloat16), sum_table[...])
        imag_sum = dot(imag.astype(jnp.bfloat16), sum_table[...])
        total[at : at + block, :] += jnp.where(mine, real_sum, 0.0)
        total[half + at : half + at + block, :] += jnp.where(mine, imag_sum, 0.0)

    @pl.when(step == steps - 1)
    def _():
        modes = (total[...] * scale_out).T.astype(jnp.bfloat16)
        for s in range(slabs):
            out[s] = dot(modes, z_out[:, s * width : (s + 1) * width]).astype(jnp.bfloat16)


def mix(planar, weight, scale_in, scale_out, adjoint):
    slabs, lines, width = planar.shape
    depth = KX // slabs
    channels = lines // depth
    rows = KY * KZ
    z_in = constant(forward_z_table())
    z_out = constant(inverse_z_table())
    first = first_table(channels, depth)
    second = second_table(channels, depth)
    spread_table = constant(second if adjoint else first)
    sum_table = constant((first if adjoint else second).T)
    shape = (2 * rows, lines)
    return pl.pallas_call(
        functools.partial(mixing_kernel, scale_in, scale_out, adjoint),
        grid=(depth,),
        in_specs=[
            whole(planar.shape),
            pl.BlockSpec((rows, weight.shape[1]), lambda j: (j, 0)),
            whole(z_in.shape),
            whole(z_out.shape),
            whole(spread_table.shape),
            whole(sum_table.shape),
        ],
        out_specs=[whole(shape), whole(planar.shape)],
        out_shape=[
            jax.ShapeDtypeStruct(shape, jnp.bfloat16),
            jax.ShapeDtypeStruct(planar.shape, jnp.bfloat16),
        ],
        scratch_shapes=[pltpu.VMEM(shape, jnp.float32)],
        compiler_params=params(),
        cost_estimate=pl.CostEstimate(flops=4 * 10**9, bytes_accessed=10**7, transcendentals=0),
        name="mix_back" if adjoint else "mix",
    )(planar, weight, z_in, z_out, spread_table, sum_table)


def inverse_step(planar, x_table, y_table, waves, store):
    slabs = planar.shape[0]
    for s in range(slabs):
        step = dot(planar[s], y_table[0]).astype(jnp.bfloat16)
        for t in range(2):
            waves[s, t] = step[:, 2 * NY * t : 2 * NY * (t + 1)]
    group = 8 * (KX // slabs)
    for g in range(planar.shape[1] // group):
        right = [waves[s, t, g * group : (g + 1) * group, :] for s in range(slabs) for t in range(2)]
        step = dot(x_table[...], jnp.concatenate(right, axis=0))
        store(g, step.reshape(8, NX, 2 * NY))


def plane_mobility(grains):
    same = [
        jnp.concatenate([grains[:1], grains[:-1]], axis=0),
        jnp.concatenate([grains[1:], grains[-1:]], axis=0),
        jnp.concatenate([grains[:, :1], grains[:, :-1]], axis=1),
        jnp.concatenate([grains[:, 1:], grains[:, -1:]], axis=1),
    ]
    total = jnp.full(grains.shape, 0.25, jnp.float32)
    for other in same:
        total = total + jnp.where(grains != other, 0.25, 0.0)
    return total


def layer_kernel(planar, smooth, cotangent, grains, bias, mix_out, mix_in, ix_table, iy_table,
                 x_table, y_table, spread, out, waves, spectral, moving, delta, rows, total):
    pair = pl.program_id(0)
    channels = smooth.shape[0]

    def store(g, value):
        spectral[8 * g : 8 * g + 8] = value

    inverse_step(planar, ix_table, iy_table, waves, store)
    for q in range(2):
        moving[:, q * NY : (q + 1) * NY] = plane_mobility(grains[q])

    def wide(ref, x):
        halves = [ref[:, q, pl.ds(x, 16), :] for q in range(2)]
        return jnp.concatenate(halves, axis=2).astype(jnp.float32)

    def body(i, _):
        x = pl.multiple_of(16 * i, 16)
        smooth_here = wide(smooth, x)
        cotangent_here = wide(cotangent, x)
        deltas = []
        spreads = []
        for h in range(2):
            at = pl.ds(pl.multiple_of(x + 8 * h, 8), 8)
            mobile = moving[at, :][None]
            right = smooth_here[:, 8 * h : 8 * h + 8, :].reshape(8 * channels, 2 * NY)
            local = dot(mix_out[...], right.astype(jnp.bfloat16)).reshape(channels, 8, 2 * NY)
            pre = spectral[:, at, :] + mobile * local + bias[...]
            gate = 0.5 * jnp.tanh(0.5 * pre) + 0.5
            slope = gate * (1.0 + pre * (1.0 - gate))
            change = cotangent_here[:, 8 * h : 8 * h + 8, :] * slope
            deltas.append(change)
            right = change.reshape(8 * channels, 2 * NY).astype(jnp.bfloat16)
            back = dot(mix_in[...], right).reshape(channels, 8, 2 * NY)
            spreads.append(mobile * back)
        delta[:, pl.ds(x, 16), :] = jnp.concatenate(deltas, axis=1).astype(jnp.bfloat16)
        both = jnp.concatenate(spreads, axis=1).astype(jnp.bfloat16)
        for q in range(2):
            spread[:, q, pl.ds(x, 16), :] = both[:, :, q * NY : (q + 1) * NY]
        return 0

    lax.fori_loop(0, NX // 16, body, 0)

    def load(i):
        return delta[2 * i : 2 * i + 2].reshape(2 * NX, 2 * NY)

    modes_step(load, x_table, y_table, rows, total, pair)

    @pl.when(pair == pl.num_programs(0) - 1)
    def _():
        out[...] = total[...].astype(jnp.bfloat16)


def layer(planar, smooth, cotangent, grains, bias, point_weight):
    slabs, lines, width = planar.shape
    channels, planes = smooth.shape[:2]
    eye = jnp.eye(8, dtype=jnp.bfloat16)
    mix_in = jnp.kron(point_weight, eye)
    mix_out = jnp.kron(point_weight.T, eye)
    bias_wide = jnp.broadcast_to(bias[:, None, None], (channels, 8, 2 * NY))
    tables = [
        constant(inverse_x_table(slabs)),
        constant(inverse_y_table(planes)),
        constant(forward_x_table(slabs)),
        constant(forward_y_table(planes)),
    ]

    def paired(shape):
        return pl.BlockSpec((1,) + shape[1:], lambda p: (p, 0, 0))

    field = pl.BlockSpec((channels, 2, NX, NY), lambda p: (0, p, 0, 0))
    return pl.pallas_call(
        layer_kernel,
        grid=(planes // 2,),
        in_specs=[
            whole(planar.shape),
            field,
            field,
            pl.BlockSpec((2, NX, NY), lambda p: (p, 0, 0)),
            whole(bias_wide.shape),
            whole(mix_out.shape),
            whole(mix_in.shape),
            whole(tables[0].shape),
            paired(tables[1].shape),
            whole(tables[2].shape),
            paired(tables[3].shape),
        ],
        out_specs=[field, whole(planar.shape)],
        out_shape=[
            jax.ShapeDtypeStruct(smooth.shape, jnp.bfloat16),
            jax.ShapeDtypeStruct(planar.shape, jnp.bfloat16),
        ],
        scratch_shapes=[
            pltpu.VMEM((slabs, 2, lines, 2 * NY), jnp.bfloat16),
            pltpu.VMEM((channels, NX, 2 * NY), jnp.float32),
            pltpu.VMEM((NX, 2 * NY), jnp.float32),
            pltpu.VMEM((channels, NX, 2 * NY), jnp.bfloat16),
            pltpu.VMEM((2, 2, slabs, lines, NY), jnp.float32),
            pltpu.VMEM(planar.shape, jnp.float32),
        ],
        compiler_params=params(),
        cost_estimate=pl.CostEstimate(flops=3 * 10**10, bytes_accessed=3 * 10**7, transcendentals=4 * 10**6),
        name="layer",
    )(planar, smooth, cotangent, grains, bias_wide, mix_out, mix_in, *tables)


def finish_kernel(planar, near, ix_table, iy_table, out, waves):
    def store(g, value):
        for q in range(2):
            here = slice(8 * g, 8 * g + 8)
            total = value[:, :, q * NY : (q + 1) * NY] + near[here, q].astype(jnp.float32)
            out[here, q] = total.astype(jnp.bfloat16)

    inverse_step(planar, ix_table, iy_table, waves, store)


def finish(planar, near):
    slabs, lines, width = planar.shape
    channels, planes = near.shape[:2]
    ix_table = constant(inverse_x_table(slabs))
    iy_table = constant(inverse_y_table(planes))
    field = pl.BlockSpec((channels, 2, NX, NY), lambda p: (0, p, 0, 0))
    return pl.pallas_call(
        finish_kernel,
        grid=(planes // 2,),
        in_specs=[
            whole(planar.shape),
            field,
            whole(ix_table.shape),
            pl.BlockSpec((1,) + iy_table.shape[1:], lambda p: (p, 0, 0)),
        ],
        out_specs=field,
        out_shape=jax.ShapeDtypeStruct(near.shape, jnp.bfloat16),
        scratch_shapes=[pltpu.VMEM((slabs, 2, lines, 2 * NY), jnp.bfloat16)],
        compiler_params=params(),
        cost_estimate=pl.CostEstimate(flops=10**10, bytes_accessed=2 * 10**7, transcendentals=0),
        name="finish",
    )(planar, near, ix_table, iy_table)


def stencil_kernel(taps, before, field, after, out, band):
    channel = pl.program_id(0)
    planes = field.shape[1]
    row = lax.broadcasted_iota(jnp.int32, (NY, NY), 0)
    column = lax.broadcasted_iota(jnp.int32, (NY, NY), 1)
    offset = row - column

    @pl.when(channel == 0)
    def _():
        band[...] = jnp.zeros_like(band)

    for dz in range(3):
        for dx in range(3):
            first = 9 * dz + 3 * dx
            block = jnp.where(offset == -1, taps[first, channel], 0.0)
            block = jnp.where(offset == 0, taps[first + 1, channel], block)
            block = jnp.where(offset == 1, taps[first + 2, channel], block).astype(jnp.bfloat16)
            for q in range(2):
                down = (q + dz) * NY
                right = (2 * dx + q) * NY
                band[down : down + NY, right : right + NY] = block
    sheets = [before[0, 0]] + [field[0, z] for z in range(planes)] + [after[0, 0]]
    left = jnp.concatenate(
        [jnp.concatenate(sheets[z : z + 4], axis=1) for z in range(0, planes, 2)], axis=0
    )
    x = lax.broadcasted_iota(jnp.int32, (left.shape[0], 1), 0) % NX
    total = dot(left, band[:, 2 * NY : 4 * NY])
    lower = pltpu.roll(dot(left, band[:, : 2 * NY]), 1, axis=0)
    total = total + jnp.where(x == 0, 0.0, lower)
    upper = pltpu.roll(dot(left, band[:, 4 * NY :]), left.shape[0] - 1, axis=0)
    total = (total + jnp.where(x == NX - 1, 0.0, upper)).astype(jnp.bfloat16)
    for z in range(planes):
        at = (z // 2) * NX
        out[0, z] = total[at : at + NX, (z % 2) * NY : (z % 2 + 1) * NY]


def stencil_planes(before, field, after, taps, name):
    channels, planes = field.shape[:2]
    rim = pl.BlockSpec((1, 1, NX, NY), lambda c: (c, 0, 0, 0))
    sheets = pl.BlockSpec((1, planes, NX, NY), lambda c: (c, 0, 0, 0))
    return pl.pallas_call(
        stencil_kernel,
        grid=(channels,),
        in_specs=[pl.BlockSpec(memory_space=pltpu.SMEM), rim, sheets, rim],
        out_specs=sheets,
        out_shape=jax.ShapeDtypeStruct(field.shape, jnp.bfloat16),
        scratch_shapes=[pltpu.VMEM((4 * NY, 6 * NY), jnp.bfloat16)],
        compiler_params=params(),
        cost_estimate=pl.CostEstimate(flops=2 * 10**10, bytes_accessed=2 * 10**7, transcendentals=0),
        name=name,
    )(taps, before, field, after)


def gradient_kernel(depth, part, spectra, duals, first, second, out):
    step = pl.program_id(0)
    samples = spectra.shape[0]
    half = spectra.shape[1] // 2
    lane = lax.broadcasted_iota(jnp.int32, (1, spectra.shape[2]), 1)
    mine = lane % depth == step
    block = 64
    for at in range(0, half, block):
        total = jnp.zeros((block, out.shape[1]), jnp.float32)
        for s in range(samples):
            real_in = jnp.where(mine, spectra[s, at : at + block, :], 0)
            imag_in = jnp.where(mine, spectra[s, half + at : half + at + block, :], 0)
            real_dual = duals[s, at : at + block, :]
            imag_dual = duals[s, half + at : half + at + block, :]
            with_real = jnp.where(part[0] == 0, real_dual, imag_dual)
            with_imag = jnp.where(part[0] == 0, imag_dual, -real_dual)
            with_real = jnp.where(mine, with_real, 0)
            with_imag = jnp.where(mine, with_imag, 0)
            total = total + dot(real_in, first[0]) * dot(with_real, second[...])
            total = total + dot(imag_in, first[0]) * dot(with_imag, second[...])
        out[at : at + block, :] = total * (1.0 / samples)


def weight_gradient(spectra, duals, depth, width, index):
    samples, rows, lines = spectra.shape
    channels = lines // depth
    square = channels * channels
    cuts = square // width
    first = first_table(channels, depth).reshape(lines, cuts, width).transpose(1, 0, 2)
    second = second_table(channels, depth)[:, :width]
    first = constant(first)
    second = constant(second)
    where = jnp.stack([index // cuts, index % cuts]).astype(jnp.int32)
    half = rows // 2
    return pl.pallas_call(
        functools.partial(gradient_kernel, depth),
        grid_spec=pltpu.PrefetchScalarGridSpec(
            num_scalar_prefetch=1,
            grid=(depth,),
            in_specs=[
                pl.BlockSpec(spectra.shape, lambda j, w: (0, 0, 0)),
                pl.BlockSpec(duals.shape, lambda j, w: (0, 0, 0)),
                pl.BlockSpec((1, lines, width), lambda j, w: (w[1], 0, 0)),
                pl.BlockSpec(second.shape, lambda j, w: (0, 0)),
            ],
            out_specs=pl.BlockSpec((half, width), lambda j, w: (j, 0)),
        ),
        out_shape=jax.ShapeDtypeStruct((depth * half, width), jnp.float32),
        compiler_params=params(),
        cost_estimate=pl.CostEstimate(flops=10**10, bytes_accessed=10**7, transcendentals=0),
        name="weight_gradient",
    )(where, spectra, duals, first, second)


def neighbours(field):
    size = lax.axis_size("slab")
    up = [(i, i + 1) for i in range(size - 1)]
    down = [(j, i) for i, j in up]
    planes = field.shape[1]
    before = lax.ppermute(field[:, planes - 1 :], "slab", up)
    after = lax.ppermute(field[:, :1], "slab", down)
    return before, after


def swap(planar):
    return lax.all_to_all(planar, "slab", split_axis=0, concat_axis=0)


def local_fast(feats, grains, spec_weight, taps, point_weight, bias, cotangent):
    slabs = lax.axis_size("slab")
    field = feats[0]
    channels = field.shape[0]
    cell_scale = 1.0 / math.sqrt(NX * NY * NZ)
    mode_scale = 1.0 / math.sqrt(KX * KY * KZ)
    mode_rows = spec_weight.shape[0]
    weight = spec_weight.reshape(mode_rows * KZ, 2 * channels * channels)
    width = weight.shape[1] // lax.axis_size("dp")

    before, after = neighbours(field)
    planar = swap(forward_modes(field, slabs))
    spectrum, planar = mix(planar, weight, cell_scale, mode_scale, False)
    spectra = lax.all_gather(spectrum, "dp")
    planar = swap(planar)
    smooth = stencil_planes(before, field, after, taps, "smooth")
    spread, planar = layer(planar, smooth, cotangent[0], grains[0], bias, point_weight)
    before, after = neighbours(spread)
    planar = swap(planar)
    dual, planar = mix(planar, weight, mode_scale, cell_scale, True)
    duals = lax.all_gather(dual, "dp")
    planar = swap(planar)
    near = stencil_planes(before, spread, after, taps[::-1], "near")
    grad_feats = finish(planar, near)[None]
    grad_spec = weight_gradient(spectra, duals, KX // slabs, width, lax.axis_index("dp"))
    return (grad_feats, grad_spec.reshape(mode_rows, KZ, width))


def local(feats, grains, spec_weight, taps, point_weight, bias, cotangent):
    samples, channels, planes = feats.shape[:3]
    width = spec_weight.shape[2] // lax.axis_size("dp")
    fits = (
        lax.axis_size("slab") * 4 == KX
        and samples == 1
        and channels == 32
        and planes % 2 == 0
        and channels * channels % width == 0
        and width % 128 == 0
    )
    form = local_fast if fits else local_any
    return form(feats, grains, spec_weight, taps, point_weight, bias, cotangent)


def solution(mesh):
    in_specs = (
        P(("grp", "dp"), None, "slab", None, None),
        P(("grp", "dp"), "slab", None, None),
        P("slab", None, None),
        P(),
        P(),
        P(),
        P(("grp", "dp"), None, "slab", None, None),
    )
    out_specs = (P(("grp", "dp"), None, "slab", None, None), P("slab", "grp", "dp"))
    return jax.shard_map(local, mesh=mesh, in_specs=in_specs, out_specs=out_specs, check_vma=False)
```

```python
import functools
import math

import jax
import jax.numpy as jnp
import ml_dtypes
import numpy as np
from jax import lax
from jax.experimental import pallas as pl
from jax.experimental.pallas import tpu as pltpu
from jax.sharding import PartitionSpec as P

NX = 128
NY = 128
NZ = 32
KX = 16
KY = 16
KZ = 16


HIGHEST = lax.Precision.HIGHEST


def extended(shard, sides, width):
    for axis, dim in sides:
        size, length = (lax.axis_size(axis), shard.shape[dim])
        up = [(i, (i + 1) % size) for i in range(size - 1)]
        down = [(j, i) for i, j in up]
        last = lax.slice_in_dim(shard, length - width, length, axis=dim)
        first = lax.slice_in_dim(shard, 0, width, axis=dim)
        before = lax.ppermute(last, axis, up)
        after = lax.ppermute(first, axis, down)
        shard = jnp.concatenate([before, shard, after], axis=dim)
    return shard


def tables(count, length, span):
    indices = jnp.arange(count, dtype=jnp.int32)
    frequency = jnp.where(indices < count // 2, indices, length - count + indices)
    position = jnp.arange(span, dtype=jnp.int32)
    phases = frequency[:, None] * position[None, :] % length
    angles = phases.astype(jnp.float32) * (2.0 * math.pi / length)
    return (jnp.cos(angles), jnp.sin(angles))


def mobility(grains):
    leading = [(0, 0)] * (grains.ndim - 2)
    along_x = (grains[..., 1:, :] != grains[..., :-1, :]).astype(jnp.float32)
    along_y = (grains[..., :, 1:] != grains[..., :, :-1]).astype(jnp.float32)
    differ = jnp.pad(along_x, leading + [(1, 0), (0, 0)]) + jnp.pad(
        along_x, leading + [(0, 1), (0, 0)]
    )
    differ = (
        differ
        + jnp.pad(along_y, leading + [(0, 0), (1, 0)])
        + jnp.pad(along_y, leading + [(0, 0), (0, 1)])
    )
    return 0.25 * (1.0 + differ)


def stencil(padded, taps, adjoint):
    planes = padded.shape[-3] - 2
    rows_x = padded.shape[-2] - 2
    rows_y = padded.shape[-1] - 2
    total = jnp.zeros(padded.shape[:-3] + (planes, rows_x, rows_y), jnp.float32)
    for offset in range(27):
        shift_z, shift_x, shift_y = (offset // 9, offset // 3 % 3, offset % 3)
        if adjoint:
            shift_z, shift_x, shift_y = (2 - shift_z, 2 - shift_x, 2 - shift_y)
        window = padded[
            ..., shift_z : shift_z + planes, shift_x : shift_x + rows_x, shift_y : shift_y + rows_y
        ]
        total = total + taps[offset][:, None, None, None] * window.astype(jnp.float32)
    return total


def plane_forward(field, cos_x, sin_x, cos_y, sin_y):
    real_y = jnp.einsum("...xy,ky->...xk", field, cos_y, precision=HIGHEST)
    imag_y = -jnp.einsum("...xy,ky->...xk", field, sin_y, precision=HIGHEST)
    real_part = jnp.einsum("...xk,jx->...jk", real_y, cos_x, precision=HIGHEST) + jnp.einsum(
        "...xk,jx->...jk", imag_y, sin_x, precision=HIGHEST
    )
    imag_part = jnp.einsum("...xk,jx->...jk", imag_y, cos_x, precision=HIGHEST) - jnp.einsum(
        "...xk,jx->...jk", real_y, sin_x, precision=HIGHEST
    )
    return (real_part, imag_part)


def plane_inverse(real_part, imag_part, cos_x, sin_x, cos_y, sin_y):
    real_x = jnp.einsum("...jk,jx->...xk", real_part, cos_x, precision=HIGHEST) - jnp.einsum(
        "...jk,jx->...xk", imag_part, sin_x, precision=HIGHEST
    )
    imag_x = jnp.einsum("...jk,jx->...xk", imag_part, cos_x, precision=HIGHEST) + jnp.einsum(
        "...jk,jx->...xk", real_part, sin_x, precision=HIGHEST
    )
    return jnp.einsum("...xk,ky->...xy", real_x, cos_y, precision=HIGHEST) - jnp.einsum(
        "...xk,ky->...xy", imag_x, sin_y, precision=HIGHEST
    )


def depth_forward(packed, cos_table, sin_table):
    width = packed.shape[-1] // 2
    real_in = packed[..., :width]
    imag_in = packed[..., width:]
    real_out = jnp.einsum("pszc,kz->pskc", real_in, cos_table, precision=HIGHEST) + jnp.einsum(
        "pszc,kz->pskc", imag_in, sin_table, precision=HIGHEST
    )
    imag_out = jnp.einsum("pszc,kz->pskc", imag_in, cos_table, precision=HIGHEST) - jnp.einsum(
        "pszc,kz->pskc", real_in, sin_table, precision=HIGHEST
    )
    return jnp.concatenate([real_out, imag_out], axis=-1)


def depth_inverse(real_modes, imag_modes, cos_table, sin_table):
    real_out = jnp.einsum("pskc,kz->pszc", real_modes, cos_table, precision=HIGHEST) - jnp.einsum(
        "pskc,kz->pszc", imag_modes, sin_table, precision=HIGHEST
    )
    imag_out = jnp.einsum("pskc,kz->pszc", imag_modes, cos_table, precision=HIGHEST) + jnp.einsum(
        "pskc,kz->pszc", real_modes, sin_table, precision=HIGHEST
    )
    return jnp.concatenate([real_out, imag_out], axis=-1)


def rim_planes(field):
    return extended(field, (("slab", 2),), 1)


def local_any(feats, grains, spec_weight, taps, point_weight, bias, cotangent):
    samples_here = feats.shape[0]
    channels = feats.shape[1]
    planes = feats.shape[2]
    cos_x, sin_x = tables(KX, NX, NX)
    cos_y, sin_y = tables(KY, NY, NY)
    cos_full, sin_full = tables(KZ, NZ, NZ)
    cell_scale = math.sqrt(NX * NY * NZ)
    mode_scale = math.sqrt(KX * KY * KZ)
    mode_rows = spec_weight.shape[0]
    weights = spec_weight.astype(jnp.float32).reshape(mode_rows, KZ, 2, channels, channels)
    w_real = weights[:, :, 0]
    w_imag = weights[:, :, 1]
    moving = mobility(grains)[:, None]

    def to_modes(field):
        real_plane, imag_plane = plane_forward(field, cos_x, sin_x, cos_y, sin_y)
        packed = jnp.stack([real_plane, imag_plane], axis=1)
        packed = packed.transpose(4, 5, 0, 3, 1, 2).reshape(
            KX * KY, samples_here, planes, 2 * channels
        )
        moved = lax.all_to_all(packed, "slab", split_axis=0, concat_axis=2, tiled=True)
        summed = depth_forward(moved, cos_full, sin_full)
        return (summed[..., :channels], summed[..., channels:])

    def from_modes(real_modes, imag_modes):
        planar = depth_inverse(real_modes, imag_modes, cos_full, sin_full)
        packed = lax.all_to_all(planar, "slab", split_axis=2, concat_axis=0, tiled=True)
        grouped = packed.reshape(KX, KY, samples_here, planes, 2, channels).transpose(
            2, 4, 5, 3, 0, 1
        )
        return plane_inverse(grouped[:, 0], grouped[:, 1], cos_x, sin_x, cos_y, sin_y)

    zero_rim = ((0, 0), (0, 0), (0, 0), (1, 1), (1, 1))
    padded = jnp.pad(rim_planes(feats), zero_rim)
    smooth = stencil(padded, taps, False).astype(jnp.bfloat16)
    local_part = moving * jnp.einsum(
        "sczxy,co->sozxy", smooth, point_weight, preferred_element_type=jnp.float32
    )
    spec_real, spec_imag = to_modes(feats.astype(jnp.float32))
    spec_real = spec_real / cell_scale
    spec_imag = spec_imag / cell_scale
    mixed_real = jnp.einsum("pskc,pkco->psko", spec_real, w_real, precision=HIGHEST) - jnp.einsum(
        "pskc,pkco->psko", spec_imag, w_imag, precision=HIGHEST
    )
    mixed_imag = jnp.einsum("pskc,pkco->psko", spec_real, w_imag, precision=HIGHEST) + jnp.einsum(
        "pskc,pkco->psko", spec_imag, w_real, precision=HIGHEST
    )
    spectral = from_modes(mixed_real, mixed_imag) / mode_scale
    pre = spectral + local_part + bias[None, :, None, None, None]
    gate = jax.nn.sigmoid(pre)
    delta = (cotangent.astype(jnp.float32) * gate * (1.0 + pre * (1.0 - gate))).astype(jnp.bfloat16)
    dual_real, dual_imag = to_modes(delta.astype(jnp.float32))
    dual_real = dual_real / mode_scale
    dual_imag = dual_imag / mode_scale
    batch_total = samples_here * lax.axis_size("dp")
    grad_real = jnp.einsum("pskc,psko->pkco", spec_real, dual_real, precision=HIGHEST) + jnp.einsum(
        "pskc,psko->pkco", spec_imag, dual_imag, precision=HIGHEST
    )
    grad_imag = jnp.einsum("pskc,psko->pkco", spec_real, dual_imag, precision=HIGHEST) - jnp.einsum(
        "pskc,psko->pkco", spec_imag, dual_real, precision=HIGHEST
    )
    grad_terms = (jnp.stack([grad_real, grad_imag], axis=2) / batch_total).reshape(
        mode_rows, KZ, 2 * channels * channels
    )
    grad_spec = lax.psum_scatter(
        grad_terms.astype(jnp.bfloat16), "dp", scatter_dimension=2, tiled=True
    ).astype(jnp.float32)
    back_real = jnp.einsum("psko,pkco->pskc", dual_real, w_real, precision=HIGHEST) + jnp.einsum(
        "psko,pkco->pskc", dual_imag, w_imag, precision=HIGHEST
    )
    back_imag = jnp.einsum("psko,pkco->pskc", dual_imag, w_real, precision=HIGHEST) - jnp.einsum(
        "psko,pkco->pskc", dual_real, w_imag, precision=HIGHEST
    )
    spectral_back = from_modes(back_real, back_imag) / cell_scale
    spread = (
        moving
        * jnp.einsum("sozxy,co->sczxy", delta, point_weight, preferred_element_type=jnp.float32)
    ).astype(jnp.bfloat16)
    spread_padded = jnp.pad(rim_planes(spread), zero_rim)
    local_back = stencil(spread_padded, taps, True)
    grad_feats = (spectral_back + local_back).astype(jnp.bfloat16)
    return (grad_feats, grad_spec)


def frequencies(count, length):
    index = np.arange(count)
    return np.where(index < count // 2, index, length - count + index)


def angles(count, length):
    phases = np.outer(frequencies(count, length), np.arange(length)) % length
    return phases * (2.0 * np.pi / length)


def constant(array):
    return jnp.asarray(np.asarray(array, np.float32).astype(ml_dtypes.bfloat16))


def forward_x_table(slabs):
    a = angles(KX, NX).reshape(slabs, KX // slabs, NX)
    trig = np.stack([np.cos(a), np.sin(a)])
    table = np.einsum("tsjx,cd->tscjdx", trig, np.eye(2))
    return table.reshape(2 * slabs * 2 * (KX // slabs), 2 * NX)


def forward_y_table(planes):
    a = angles(KY, NY)
    cos, sin = np.cos(a).T, np.sin(a).T
    block = np.stack([np.stack([cos, -sin], 1), np.stack([-sin, -cos], 1)])
    pick = np.eye(planes).reshape(planes // 2, 2, planes)
    table = np.einsum("pqz,tyrk->pqtyzrk", pick, block)
    return table.reshape(planes // 2, 4 * NY, planes * 2 * KY)


def forward_z_table():
    a = angles(KZ, NZ)
    cos, sin = np.cos(a).T, np.sin(a).T
    block = np.stack([np.stack([cos, -sin], 1), np.stack([sin, cos], 1)], 1)
    table = np.einsum("zrqm,kl->zrkqlm", block, np.eye(KY))
    return table.reshape(NZ * 2 * KY, 2 * KY * KZ)


def inverse_z_table():
    a = angles(KZ, NZ)
    cos, sin = np.cos(a), np.sin(a)
    block = np.stack([np.stack([cos, sin], 2), np.stack([-sin, cos], 2)])
    table = np.einsum("rmzq,kl->rkmzql", block, np.eye(KY))
    return table.reshape(2 * KY * KZ, NZ * 2 * KY)


def inverse_y_table(planes):
    a = angles(KY, NY)
    cos, sin = np.cos(a), np.sin(a)
    block = np.stack([np.stack([cos, -sin], 1), np.stack([-sin, -cos], 1)])
    pick = np.eye(planes).reshape(planes // 2, 2, planes)
    table = np.einsum("pqz,rkty->pzrktqy", pick, block)
    return table.reshape(planes // 2, planes * 2 * KY, 4 * NY)


def inverse_x_table(slabs):
    a = angles(KX, NX).reshape(slabs, KX // slabs, NX)
    trig = np.stack([np.cos(a), np.sin(a)])
    table = np.einsum("tsjx,cd->cxstdj", trig, np.eye(8))
    return table.reshape(8 * NX, 2 * KX * 8)


def first_table(channels, depth):
    table = np.einsum("ac,j,b->ajcb", np.eye(channels), np.ones(depth), np.ones(channels))
    return table.reshape(channels * depth, channels * channels)


def second_table(channels, depth):
    table = np.einsum("ac,j,b->ajbc", np.eye(channels), np.ones(depth), np.ones(channels))
    return table.reshape(channels * depth, channels * channels)


def dot(a, b):
    return jnp.dot(a, b, preferred_element_type=jnp.float32)


def whole(shape):
    return pl.BlockSpec(shape, lambda *_: (0,) * len(shape))


def params(**kw):
    return pltpu.CompilerParams(vmem_limit_bytes=58 * 2**20, **kw)


def modes_step(load, x_table, y_table, rows, total, pair):
    slabs = total.shape[0]
    for i in range(rows.shape[3] // 8):
        part = dot(x_table[...], load(i))
        for t in range(2):
            for s in range(slabs):
                at = 8 * (t * slabs + s)
                for q in range(2):
                    rows[q, t, s, 8 * i : 8 * i + 8, :] = part[at : at + 8, q * NY : q * NY + NY]
    for s in range(slabs):
        left = [rows[q, t, s].astype(jnp.bfloat16) for q in range(2) for t in range(2)]
        step = dot(jnp.concatenate(left, axis=1), y_table[0])
        before = jnp.where(pair == 0, 0.0, total[s])
        total[s] = before + step


def store_rims(field, first, last, pair):
    @pl.when(pair == 0)
    def _():
        first[:, 0] = field[:, 0]

    @pl.when(pair == pl.num_programs(0) - 1)
    def _():
        last[:, 0] = field[:, 1]


def forward_kernel(field, x_table, y_table, out, first, last, rows, total):
    pair = pl.program_id(0)

    def load(i):
        halves = [field[2 * i : 2 * i + 2, q].reshape(2 * NX, NY) for q in range(2)]
        return jnp.concatenate(halves, axis=1)

    store_rims(field, first, last, pair)
    modes_step(load, x_table, y_table, rows, total, pair)

    @pl.when(pair == pl.num_programs(0) - 1)
    def _():
        out[...] = total[...].astype(jnp.bfloat16)


def forward_modes(field, slabs):
    channels, planes = field.shape[:2]
    lines = channels * (KX // slabs)
    x_table = constant(forward_x_table(slabs))
    y_table = constant(forward_y_table(planes))
    shape = (slabs, lines, planes * 2 * KY)
    rim = (channels, 1, NX, NY)
    return pl.pallas_call(
        forward_kernel,
        grid=(planes // 2,),
        in_specs=[
            pl.BlockSpec((channels, 2, NX, NY), lambda p: (0, p, 0, 0)),
            whole(x_table.shape),
            pl.BlockSpec((1,) + y_table.shape[1:], lambda p: (p, 0, 0)),
        ],
        out_specs=[whole(shape), whole(rim), whole(rim)],
        out_shape=[
            jax.ShapeDtypeStruct(shape, jnp.bfloat16),
            jax.ShapeDtypeStruct(rim, jnp.bfloat16),
            jax.ShapeDtypeStruct(rim, jnp.bfloat16),
        ],
        scratch_shapes=[
            pltpu.VMEM((2, 2, slabs, lines, NY), jnp.float32),
            pltpu.VMEM(shape, jnp.float32),
        ],
        compiler_params=params(),
        cost_estimate=pl.CostEstimate(flops=10**10, bytes_accessed=10**7, transcendentals=0),
        name="forward_modes",
    )(field, x_table, y_table)


def mixing_kernel(scale_in, scale_out, adjoint, planar, weight, z_in, z_out, spread_table,
                  sum_table, *rest):
    if adjoint:
        partner, out, send, spectrum, total, wide, product = rest
    else:
        spectrum, out, total, wide, product = rest
    step = pl.program_id(0)
    steps = pl.num_programs(0)
    slabs = planar.shape[0]
    width = planar.shape[2]
    half = spectrum.shape[0] // 2
    lanes = weight.shape[1] // 2

    @pl.when(step == 0)
    def _():
        left = jnp.concatenate([planar[s] for s in range(slabs)], axis=1)
        modes = (dot(left, z_in[...]).T * scale_in).astype(jnp.bfloat16)
        spectrum[...] = modes
        total[...] = jnp.zeros_like(total)
        if adjoint:
            for d in range(send.shape[0]):
                send[d, : 2 * half] = partner[...]
                send[d, 2 * half :] = modes

    lane = lax.broadcasted_iota(jnp.int32, (1, spectrum.shape[1]), 1)
    mine = lane % steps == step
    wide[...] = dot(jnp.where(mine, spectrum[...], 0), spread_table[...])
    block = 32
    for at in range(0, half, block):
        real_wide = wide[at : at + block]
        imag_wide = wide[half + at : half + at + block]
        w_real = weight[at : at + block, :lanes].astype(jnp.float32)
        w_imag = weight[at : at + block, lanes:].astype(jnp.float32)
        if adjoint:
            real = real_wide * w_real + imag_wide * w_imag
            imag = imag_wide * w_real - real_wide * w_imag
        else:
            real = real_wide * w_real - imag_wide * w_imag
            imag = real_wide * w_imag + imag_wide * w_real
        product[at : at + block] = real.astype(jnp.bfloat16)
        product[half + at : half + at + block] = imag.astype(jnp.bfloat16)
    total[...] += jnp.where(mine, dot(product[...], sum_table[...]), 0.0)

    @pl.when(step == steps - 1)
    def _():
        modes = (total[...] * scale_out).T.astype(jnp.bfloat16)
        for s in range(slabs):
            out[s] = dot(modes, z_out[:, s * width : (s + 1) * width]).astype(jnp.bfloat16)


def mix(planar, weight, scale_in, scale_out, partner=None, copies=0):
    slabs, lines, width = planar.shape
    adjoint = partner is not None
    depth = KX // slabs
    channels = lines // depth
    rows = KY * KZ
    z_in = constant(forward_z_table())
    z_out = constant(inverse_z_table())
    first = first_table(channels, depth)
    second = second_table(channels, depth)
    spread_table = constant(second if adjoint else first)
    sum_table = constant((first if adjoint else second).T)
    shape = (2 * rows, lines)
    in_specs = [
        whole(planar.shape),
        pl.BlockSpec((rows, weight.shape[1]), lambda j: (j, 0)),
        whole(z_in.shape),
        whole(z_out.shape),
        whole(spread_table.shape),
        whole(sum_table.shape),
    ]
    operands = [planar, weight, z_in, z_out, spread_table, sum_table]
    scratch = [
        pltpu.VMEM(shape, jnp.float32),
        pltpu.VMEM((2 * rows, channels * channels), jnp.float32),
        pltpu.VMEM((2 * rows, channels * channels), jnp.bfloat16),
    ]
    if adjoint:
        in_specs.append(whole(shape))
        operands.append(partner)
        scratch = [pltpu.VMEM(shape, jnp.bfloat16)] + scratch
        outs = [planar.shape, (copies, 2 * shape[0], lines)]
    else:
        outs = [shape, planar.shape]
    return pl.pallas_call(
        functools.partial(mixing_kernel, scale_in, scale_out, adjoint),
        grid=(depth,),
        in_specs=in_specs,
        out_specs=[whole(out) for out in outs],
        out_shape=[jax.ShapeDtypeStruct(out, jnp.bfloat16) for out in outs],
        scratch_shapes=scratch,
        compiler_params=params(),
        cost_estimate=pl.CostEstimate(flops=4 * 10**9, bytes_accessed=10**7, transcendentals=0),
        name="mix_back" if adjoint else "mix",
    )(*operands)


def inverse_step(planar, x_table, y_table, waves, store):
    slabs = planar.shape[0]
    for s in range(slabs):
        step = dot(planar[s], y_table[0]).astype(jnp.bfloat16)
        for t in range(2):
            waves[s, t] = step[:, 2 * NY * t : 2 * NY * (t + 1)]
    group = 8 * (KX // slabs)
    for g in range(planar.shape[1] // group):
        right = [waves[s, t, g * group : (g + 1) * group, :] for s in range(slabs) for t in range(2)]
        step = dot(x_table[...], jnp.concatenate(right, axis=0))
        store(g, step.reshape(8, NX, 2 * NY))


def plane_mobility(grains):
    same = [
        jnp.concatenate([grains[:1], grains[:-1]], axis=0),
        jnp.concatenate([grains[1:], grains[-1:]], axis=0),
        jnp.concatenate([grains[:, :1], grains[:, :-1]], axis=1),
        jnp.concatenate([grains[:, 1:], grains[:, -1:]], axis=1),
    ]
    total = jnp.full(grains.shape, 0.25, jnp.float32)
    for other in same:
        total = total + jnp.where(grains != other, 0.25, 0.0)
    return total


def layer_kernel(bias, planar, smooth, cotangent, grains, point_weight, repeat, ix_table, iy_table,
                 x_table, y_table, spread, out, first, last, waves, spectral, moving, delta, rows,
                 total, bias_wide, mix_out, mix_in):
    pair = pl.program_id(0)
    channels = smooth.shape[0]

    @pl.when(pair == 0)
    def _():
        for c in range(channels):
            bias_wide[c] = jnp.full(bias_wide.shape[1:], bias[c], jnp.float32)
        tall = dot(repeat[...], point_weight[...]).astype(jnp.bfloat16)
        square = lax.dot_general(
            tall, repeat[...], (((1,), (1,)), ((), ())), preferred_element_type=jnp.float32
        )
        row = lax.broadcasted_iota(jnp.int32, square.shape, 0) % 8
        column = lax.broadcasted_iota(jnp.int32, square.shape, 1) % 8
        square = jnp.where(row == column, square, 0.0)
        mix_in[...] = square.astype(jnp.bfloat16)
        mix_out[...] = square.T.astype(jnp.bfloat16)

    def store(g, value):
        spectral[8 * g : 8 * g + 8] = value

    inverse_step(planar, ix_table, iy_table, waves, store)
    for q in range(2):
        moving[:, q * NY : (q + 1) * NY] = plane_mobility(grains[q])

    def wide(ref, x):
        halves = [ref[:, q, pl.ds(x, 16), :] for q in range(2)]
        return jnp.concatenate(halves, axis=2).astype(jnp.float32)

    def body(i, _):
        x = pl.multiple_of(16 * i, 16)
        smooth_here = wide(smooth, x)
        cotangent_here = wide(cotangent, x)
        deltas = []
        spreads = []
        for h in range(2):
            at = pl.ds(pl.multiple_of(x + 8 * h, 8), 8)
            mobile = moving[at, :][None]
            right = smooth_here[:, 8 * h : 8 * h + 8, :].reshape(8 * channels, 2 * NY)
            local = dot(mix_out[...], right.astype(jnp.bfloat16)).reshape(channels, 8, 2 * NY)
            pre = spectral[:, at, :] + mobile * local + bias_wide[...]
            gate = 0.5 * jnp.tanh(0.5 * pre) + 0.5
            slope = gate * (1.0 + pre * (1.0 - gate))
            change = cotangent_here[:, 8 * h : 8 * h + 8, :] * slope
            deltas.append(change)
            right = change.reshape(8 * channels, 2 * NY).astype(jnp.bfloat16)
            back = dot(mix_in[...], right).reshape(channels, 8, 2 * NY)
            spreads.append(mobile * back)
        delta[:, pl.ds(x, 16), :] = jnp.concatenate(deltas, axis=1).astype(jnp.bfloat16)
        both = jnp.concatenate(spreads, axis=1).astype(jnp.bfloat16)
        for q in range(2):
            spread[:, q, pl.ds(x, 16), :] = both[:, :, q * NY : (q + 1) * NY]
        return 0

    lax.fori_loop(0, NX // 16, body, 0, unroll=2)
    store_rims(spread, first, last, pair)

    def load(i):
        return delta[2 * i : 2 * i + 2].reshape(2 * NX, 2 * NY)

    modes_step(load, x_table, y_table, rows, total, pair)

    @pl.when(pair == pl.num_programs(0) - 1)
    def _():
        out[...] = total[...].astype(jnp.bfloat16)


def layer(planar, smooth, cotangent, grains, bias, point_weight):
    slabs, lines, width = planar.shape
    channels, planes = smooth.shape[:2]
    repeat = constant(np.repeat(np.eye(channels), 8, axis=0))
    tables = [
        constant(inverse_x_table(slabs)),
        constant(inverse_y_table(planes)),
        constant(forward_x_table(slabs)),
        constant(forward_y_table(planes)),
    ]

    def paired(shape):
        return pl.BlockSpec((1,) + shape[1:], lambda p: (p, 0, 0))

    field = pl.BlockSpec((channels, 2, NX, NY), lambda p: (0, p, 0, 0))
    rim = (channels, 1, NX, NY)
    outs = [smooth.shape, planar.shape, rim, rim]
    return pl.pallas_call(
        layer_kernel,
        grid=(planes // 2,),
        in_specs=[
            pl.BlockSpec(memory_space=pltpu.SMEM),
            whole(planar.shape),
            field,
            field,
            pl.BlockSpec((2, NX, NY), lambda p: (p, 0, 0)),
            whole(point_weight.shape),
            whole(repeat.shape),
            whole(tables[0].shape),
            paired(tables[1].shape),
            whole(tables[2].shape),
            paired(tables[3].shape),
        ],
        out_specs=[field, whole(planar.shape), whole(rim), whole(rim)],
        out_shape=[jax.ShapeDtypeStruct(out, jnp.bfloat16) for out in outs],
        scratch_shapes=[
            pltpu.VMEM((slabs, 2, lines, 2 * NY), jnp.bfloat16),
            pltpu.VMEM((channels, NX, 2 * NY), jnp.float32),
            pltpu.VMEM((NX, 2 * NY), jnp.float32),
            pltpu.VMEM((channels, NX, 2 * NY), jnp.bfloat16),
            pltpu.VMEM((2, 2, slabs, lines, NY), jnp.float32),
            pltpu.VMEM(planar.shape, jnp.float32),
            pltpu.VMEM((channels, 8, 2 * NY), jnp.float32),
            pltpu.VMEM((8 * channels, 8 * channels), jnp.bfloat16),
            pltpu.VMEM((8 * channels, 8 * channels), jnp.bfloat16),
        ],
        compiler_params=params(),
        cost_estimate=pl.CostEstimate(flops=3 * 10**10, bytes_accessed=3 * 10**7, transcendentals=4 * 10**6),
        name="layer",
    )(bias, planar, smooth, cotangent, grains, point_weight, repeat, *tables)


def finish_kernel(planar, near, ix_table, iy_table, out, waves):
    def store(g, value):
        for q in range(2):
            here = slice(8 * g, 8 * g + 8)
            total = value[:, :, q * NY : (q + 1) * NY] + near[here, q].astype(jnp.float32)
            out[here, q] = total.astype(jnp.bfloat16)

    inverse_step(planar, ix_table, iy_table, waves, store)


def finish(planar, near):
    slabs, lines, width = planar.shape
    channels, planes = near.shape[:2]
    ix_table = constant(inverse_x_table(slabs))
    iy_table = constant(inverse_y_table(planes))
    field = pl.BlockSpec((channels, 2, NX, NY), lambda p: (0, p, 0, 0))
    return pl.pallas_call(
        finish_kernel,
        grid=(planes // 2,),
        in_specs=[
            whole(planar.shape),
            field,
            whole(ix_table.shape),
            pl.BlockSpec((1,) + iy_table.shape[1:], lambda p: (p, 0, 0)),
        ],
        out_specs=field,
        out_shape=jax.ShapeDtypeStruct(near.shape, jnp.bfloat16),
        scratch_shapes=[pltpu.VMEM((slabs, 2, lines, 2 * NY), jnp.bfloat16)],
        compiler_params=params(),
        cost_estimate=pl.CostEstimate(flops=10**10, bytes_accessed=2 * 10**7, transcendentals=0),
        name="finish",
    )(planar, near, ix_table, iy_table)


def build_band(adjoint, taps, masks, channel, band):
    blocks = masks.shape[1] // 16
    for dz in range(3):
        for dx in range(3):
            block = jnp.zeros((blocks, 16, NY), jnp.bfloat16)
            for dy in range(3):
                number = 9 * dz + 3 * dx + dy
                tap = taps[26 - number if adjoint else number, channel]
                tap = jnp.full((16, NY), tap, jnp.float32).astype(jnp.bfloat16)
                block = block + masks[dy].reshape(blocks, 16, NY) * tap[None]
            block = block.reshape(NY, NY)
            for q in range(2):
                down = (q + dz) * NY
                right = (2 * dx + q) * NY
                band[down : down + NY, right : right + NY] = block


def apply_band(before, field, after, out, band, c):
    planes = field.shape[1]
    sheets = [before[c, 0]] + [field[c, z] for z in range(planes)] + [after[c, 0]]
    pairs = range(planes // 2)
    left = jnp.concatenate(
        [jnp.concatenate(sheets[2 * p : 2 * p + 4], axis=1) for p in pairs], axis=0
    )
    middle = dot(left, band[:, 2 * NY : 4 * NY])
    lower = dot(left, band[:, : 2 * NY])
    upper = dot(left, band[:, 4 * NY :])
    row = lax.broadcasted_iota(jnp.int32, (8, 2 * NY), 0)
    for p in pairs:
        here = slice(p * NX, (p + 1) * NX)
        down = pltpu.roll(lower[here], 1, axis=0)
        up = pltpu.roll(upper[here], NX - 1, axis=0)
        down = jnp.concatenate([jnp.where(row == 0, 0.0, down[:8]), down[8:]], axis=0)
        up = jnp.concatenate([up[:-8], jnp.where(row == 7, 0.0, up[-8:])], axis=0)
        total = (middle[here] + down + up).astype(jnp.bfloat16)
        out[c, 2 * p] = total[:, :NY]
        out[c, 2 * p + 1] = total[:, NY:]


def stencil_kernel(adjoint, taps, masks, before, field, after, out, even, odd):
    step = pl.program_id(0)
    build = functools.partial(build_band, adjoint, taps, masks)

    @pl.when(step == 0)
    def _():
        even[...] = jnp.zeros_like(even)
        odd[...] = jnp.zeros_like(odd)
        build(0, even)

    build(2 * step + 1, odd)
    apply_band(before, field, after, out, even, 0)
    build(jnp.minimum(2 * step + 2, 2 * pl.num_programs(0) - 1), even)
    apply_band(before, field, after, out, odd, 1)


def stencil_planes(before, field, after, taps, adjoint):
    channels, planes = field.shape[:2]
    masks = constant(np.stack([np.eye(NY, k=1 - dy) for dy in range(3)]))
    rim = pl.BlockSpec((2, 1, NX, NY), lambda c: (c, 0, 0, 0))
    sheets = pl.BlockSpec((2, planes, NX, NY), lambda c: (c, 0, 0, 0))
    return pl.pallas_call(
        functools.partial(stencil_kernel, adjoint),
        grid=(channels // 2,),
        in_specs=[pl.BlockSpec(memory_space=pltpu.SMEM), whole(masks.shape), rim, sheets, rim],
        out_specs=sheets,
        out_shape=jax.ShapeDtypeStruct(field.shape, jnp.bfloat16),
        scratch_shapes=[pltpu.VMEM((4 * NY, 6 * NY), jnp.bfloat16) for _ in range(2)],
        compiler_params=params(),
        cost_estimate=pl.CostEstimate(flops=2 * 10**10, bytes_accessed=2 * 10**7, transcendentals=0),
        name="near" if adjoint else "smooth",
    )(taps, masks, before, field, after)


def gradient_kernel(depth, where, gathered, first, second, out):
    step = pl.program_id(0)
    samples, rows, lines = gathered.shape
    half = rows // 4
    lane = lax.broadcasted_iota(jnp.int32, (1, lines), 1)
    mine = lane % depth == step
    total = jnp.zeros(out.shape, jnp.float32)
    for s in range(samples):
        spectrum = jnp.where(mine, gathered[s, : 2 * half], 0)
        real = gathered[s, 2 * half : 3 * half]
        imag = gathered[s, 3 * half :]
        dual = jnp.concatenate(
            [jnp.where(where[0] == 0, real, imag), jnp.where(where[0] == 0, imag, -real)], axis=0
        )
        dual = jnp.where(mine, dual, 0)
        product = dot(spectrum, first[0]) * dot(dual, second[...])
        total = total + product[:half] + product[half:]
    out[...] = total * (1.0 / samples)


def weight_gradient(gathered, depth, width, index):
    samples, rows, lines = gathered.shape
    channels = lines // depth
    square = channels * channels
    cuts = square // width
    first = first_table(channels, depth).reshape(lines, cuts, width).transpose(1, 0, 2)
    second = second_table(channels, depth)[:, :width]
    first = constant(first)
    second = constant(second)
    where = jnp.stack([index // cuts, index % cuts]).astype(jnp.int32)
    half = rows // 4
    return pl.pallas_call(
        functools.partial(gradient_kernel, depth),
        grid_spec=pltpu.PrefetchScalarGridSpec(
            num_scalar_prefetch=1,
            grid=(depth,),
            in_specs=[
                pl.BlockSpec(gathered.shape, lambda j, w: (0, 0, 0)),
                pl.BlockSpec((1, lines, width), lambda j, w: (w[1], 0, 0)),
                pl.BlockSpec(second.shape, lambda j, w: (0, 0)),
            ],
            out_specs=pl.BlockSpec((half, width), lambda j, w: (j, 0)),
        ),
        out_shape=jax.ShapeDtypeStruct((depth * half, width), jnp.float32),
        compiler_params=params(),
        cost_estimate=pl.CostEstimate(flops=10**10, bytes_accessed=10**7, transcendentals=0),
        name="weight_gradient",
    )(where, gathered, first, second)


def neighbours(first, last):
    size = lax.axis_size("slab")
    up = [(i, i + 1) for i in range(size - 1)]
    down = [(j, i) for i, j in up]
    return lax.ppermute(last, "slab", up), lax.ppermute(first, "slab", down)


def swap(planar):
    return lax.all_to_all(planar, "slab", split_axis=0, concat_axis=0)


def local_fast(feats, grains, spec_weight, taps, point_weight, bias, cotangent):
    slabs = lax.axis_size("slab")
    field = feats[0]
    channels = field.shape[0]
    cell_scale = 1.0 / math.sqrt(NX * NY * NZ)
    mode_scale = 1.0 / math.sqrt(KX * KY * KZ)
    mode_rows = spec_weight.shape[0]
    weight = spec_weight.reshape(mode_rows * KZ, 2 * channels * channels)
    width = weight.shape[1] // lax.axis_size("dp")

    planar, first, last = forward_modes(field, slabs)
    planar, first, last = lax.optimization_barrier((swap(planar), first, last))
    before, after = neighbours(first, last)
    spectrum, planar = mix(planar, weight, cell_scale, mode_scale)
    planar = swap(planar)
    smooth = stencil_planes(before, field, after, taps, False)
    spread, planar, first, last = layer(planar, smooth, cotangent[0], grains[0], bias, point_weight)
    planar, first, last = lax.optimization_barrier((swap(planar), first, last))
    before, after = neighbours(first, last)
    copies = lax.axis_size("dp")
    planar, send = mix(planar, weight, mode_scale, cell_scale, spectrum, copies)
    planar = swap(planar)
    gathered = lax.all_to_all(send, "dp", split_axis=0, concat_axis=0)
    near = stencil_planes(before, spread, after, taps, True)
    grad_feats = finish(planar, near)[None]
    grad_spec = weight_gradient(gathered, KX // slabs, width, lax.axis_index("dp"))
    return (grad_feats, grad_spec.reshape(mode_rows, KZ, width))


def local(feats, grains, spec_weight, taps, point_weight, bias, cotangent):
    samples, channels, planes = feats.shape[:3]
    width = spec_weight.shape[2] // lax.axis_size("dp")
    fits = (
        lax.axis_size("slab") * 4 == KX
        and samples == 1
        and channels == 32
        and planes % 2 == 0
        and channels * channels % width == 0
        and width % 128 == 0
    )
    form = local_fast if fits else local_any
    return form(feats, grains, spec_weight, taps, point_weight, bias, cotangent)


def solution(mesh):
    in_specs = (
        P(("grp", "dp"), None, "slab", None, None),
        P(("grp", "dp"), "slab", None, None),
        P("slab", None, None),
        P(),
        P(),
        P(),
        P(("grp", "dp"), None, "slab", None, None),
    )
    out_specs = (P(("grp", "dp"), None, "slab", None, None), P("slab", "grp", "dp"))
    return jax.shard_map(local, mesh=mesh, in_specs=in_specs, out_specs=out_specs, check_vma=False)
```

```python
import functools
import math

import jax
import jax.numpy as jnp
import ml_dtypes
import numpy as np
from jax import lax
from jax.experimental import pallas as pl
from jax.experimental.pallas import tpu as pltpu
from jax.sharding import PartitionSpec as P

NX = 128
NY = 128
NZ = 32
KX = 16
KY = 16
KZ = 16


HIGHEST = lax.Precision.HIGHEST


def extended(shard, sides, width):
    for axis, dim in sides:
        size, length = (lax.axis_size(axis), shard.shape[dim])
        up = [(i, (i + 1) % size) for i in range(size - 1)]
        down = [(j, i) for i, j in up]
        last = lax.slice_in_dim(shard, length - width, length, axis=dim)
        first = lax.slice_in_dim(shard, 0, width, axis=dim)
        before = lax.ppermute(last, axis, up)
        after = lax.ppermute(first, axis, down)
        shard = jnp.concatenate([before, shard, after], axis=dim)
    return shard


def tables(count, length, span):
    indices = jnp.arange(count, dtype=jnp.int32)
    frequency = jnp.where(indices < count // 2, indices, length - count + indices)
    position = jnp.arange(span, dtype=jnp.int32)
    phases = frequency[:, None] * position[None, :] % length
    angles = phases.astype(jnp.float32) * (2.0 * math.pi / length)
    return (jnp.cos(angles), jnp.sin(angles))


def mobility(grains):
    leading = [(0, 0)] * (grains.ndim - 2)
    along_x = (grains[..., 1:, :] != grains[..., :-1, :]).astype(jnp.float32)
    along_y = (grains[..., :, 1:] != grains[..., :, :-1]).astype(jnp.float32)
    differ = jnp.pad(along_x, leading + [(1, 0), (0, 0)]) + jnp.pad(
        along_x, leading + [(0, 1), (0, 0)]
    )
    differ = (
        differ
        + jnp.pad(along_y, leading + [(0, 0), (1, 0)])
        + jnp.pad(along_y, leading + [(0, 0), (0, 1)])
    )
    return 0.25 * (1.0 + differ)


def stencil(padded, taps, adjoint):
    planes = padded.shape[-3] - 2
    rows_x = padded.shape[-2] - 2
    rows_y = padded.shape[-1] - 2
    total = jnp.zeros(padded.shape[:-3] + (planes, rows_x, rows_y), jnp.float32)
    for offset in range(27):
        shift_z, shift_x, shift_y = (offset // 9, offset // 3 % 3, offset % 3)
        if adjoint:
            shift_z, shift_x, shift_y = (2 - shift_z, 2 - shift_x, 2 - shift_y)
        window = padded[
            ..., shift_z : shift_z + planes, shift_x : shift_x + rows_x, shift_y : shift_y + rows_y
        ]
        total = total + taps[offset][:, None, None, None] * window.astype(jnp.float32)
    return total


def plane_forward(field, cos_x, sin_x, cos_y, sin_y):
    real_y = jnp.einsum("...xy,ky->...xk", field, cos_y, precision=HIGHEST)
    imag_y = -jnp.einsum("...xy,ky->...xk", field, sin_y, precision=HIGHEST)
    real_part = jnp.einsum("...xk,jx->...jk", real_y, cos_x, precision=HIGHEST) + jnp.einsum(
        "...xk,jx->...jk", imag_y, sin_x, precision=HIGHEST
    )
    imag_part = jnp.einsum("...xk,jx->...jk", imag_y, cos_x, precision=HIGHEST) - jnp.einsum(
        "...xk,jx->...jk", real_y, sin_x, precision=HIGHEST
    )
    return (real_part, imag_part)


def plane_inverse(real_part, imag_part, cos_x, sin_x, cos_y, sin_y):
    real_x = jnp.einsum("...jk,jx->...xk", real_part, cos_x, precision=HIGHEST) - jnp.einsum(
        "...jk,jx->...xk", imag_part, sin_x, precision=HIGHEST
    )
    imag_x = jnp.einsum("...jk,jx->...xk", imag_part, cos_x, precision=HIGHEST) + jnp.einsum(
        "...jk,jx->...xk", real_part, sin_x, precision=HIGHEST
    )
    return jnp.einsum("...xk,ky->...xy", real_x, cos_y, precision=HIGHEST) - jnp.einsum(
        "...xk,ky->...xy", imag_x, sin_y, precision=HIGHEST
    )


def depth_forward(packed, cos_table, sin_table):
    width = packed.shape[-1] // 2
    real_in = packed[..., :width]
    imag_in = packed[..., width:]
    real_out = jnp.einsum("pszc,kz->pskc", real_in, cos_table, precision=HIGHEST) + jnp.einsum(
        "pszc,kz->pskc", imag_in, sin_table, precision=HIGHEST
    )
    imag_out = jnp.einsum("pszc,kz->pskc", imag_in, cos_table, precision=HIGHEST) - jnp.einsum(
        "pszc,kz->pskc", real_in, sin_table, precision=HIGHEST
    )
    return jnp.concatenate([real_out, imag_out], axis=-1)


def depth_inverse(real_modes, imag_modes, cos_table, sin_table):
    real_out = jnp.einsum("pskc,kz->pszc", real_modes, cos_table, precision=HIGHEST) - jnp.einsum(
        "pskc,kz->pszc", imag_modes, sin_table, precision=HIGHEST
    )
    imag_out = jnp.einsum("pskc,kz->pszc", imag_modes, cos_table, precision=HIGHEST) + jnp.einsum(
        "pskc,kz->pszc", real_modes, sin_table, precision=HIGHEST
    )
    return jnp.concatenate([real_out, imag_out], axis=-1)


def rim_planes(field):
    return extended(field, (("slab", 2),), 1)


def local_any(feats, grains, spec_weight, taps, point_weight, bias, cotangent):
    samples_here = feats.shape[0]
    channels = feats.shape[1]
    planes = feats.shape[2]
    cos_x, sin_x = tables(KX, NX, NX)
    cos_y, sin_y = tables(KY, NY, NY)
    cos_full, sin_full = tables(KZ, NZ, NZ)
    cell_scale = math.sqrt(NX * NY * NZ)
    mode_scale = math.sqrt(KX * KY * KZ)
    mode_rows = spec_weight.shape[0]
    weights = spec_weight.astype(jnp.float32).reshape(mode_rows, KZ, 2, channels, channels)
    w_real = weights[:, :, 0]
    w_imag = weights[:, :, 1]
    moving = mobility(grains)[:, None]

    def to_modes(field):
        real_plane, imag_plane = plane_forward(field, cos_x, sin_x, cos_y, sin_y)
        packed = jnp.stack([real_plane, imag_plane], axis=1)
        packed = packed.transpose(4, 5, 0, 3, 1, 2).reshape(
            KX * KY, samples_here, planes, 2 * channels
        )
        moved = lax.all_to_all(packed, "slab", split_axis=0, concat_axis=2, tiled=True)
        summed = depth_forward(moved, cos_full, sin_full)
        return (summed[..., :channels], summed[..., channels:])

    def from_modes(real_modes, imag_modes):
        planar = depth_inverse(real_modes, imag_modes, cos_full, sin_full)
        packed = lax.all_to_all(planar, "slab", split_axis=2, concat_axis=0, tiled=True)
        grouped = packed.reshape(KX, KY, samples_here, planes, 2, channels).transpose(
            2, 4, 5, 3, 0, 1
        )
        return plane_inverse(grouped[:, 0], grouped[:, 1], cos_x, sin_x, cos_y, sin_y)

    zero_rim = ((0, 0), (0, 0), (0, 0), (1, 1), (1, 1))
    padded = jnp.pad(rim_planes(feats), zero_rim)
    smooth = stencil(padded, taps, False).astype(jnp.bfloat16)
    local_part = moving * jnp.einsum(
        "sczxy,co->sozxy", smooth, point_weight, preferred_element_type=jnp.float32
    )
    spec_real, spec_imag = to_modes(feats.astype(jnp.float32))
    spec_real = spec_real / cell_scale
    spec_imag = spec_imag / cell_scale
    mixed_real = jnp.einsum("pskc,pkco->psko", spec_real, w_real, precision=HIGHEST) - jnp.einsum(
        "pskc,pkco->psko", spec_imag, w_imag, precision=HIGHEST
    )
    mixed_imag = jnp.einsum("pskc,pkco->psko", spec_real, w_imag, precision=HIGHEST) + jnp.einsum(
        "pskc,pkco->psko", spec_imag, w_real, precision=HIGHEST
    )
    spectral = from_modes(mixed_real, mixed_imag) / mode_scale
    pre = spectral + local_part + bias[None, :, None, None, None]
    gate = jax.nn.sigmoid(pre)
    delta = (cotangent.astype(jnp.float32) * gate * (1.0 + pre * (1.0 - gate))).astype(jnp.bfloat16)
    dual_real, dual_imag = to_modes(delta.astype(jnp.float32))
    dual_real = dual_real / mode_scale
    dual_imag = dual_imag / mode_scale
    batch_total = samples_here * lax.axis_size("dp")
    grad_real = jnp.einsum("pskc,psko->pkco", spec_real, dual_real, precision=HIGHEST) + jnp.einsum(
        "pskc,psko->pkco", spec_imag, dual_imag, precision=HIGHEST
    )
    grad_imag = jnp.einsum("pskc,psko->pkco", spec_real, dual_imag, precision=HIGHEST) - jnp.einsum(
        "pskc,psko->pkco", spec_imag, dual_real, precision=HIGHEST
    )
    grad_terms = (jnp.stack([grad_real, grad_imag], axis=2) / batch_total).reshape(
        mode_rows, KZ, 2 * channels * channels
    )
    grad_spec = lax.psum_scatter(
        grad_terms.astype(jnp.bfloat16), "dp", scatter_dimension=2, tiled=True
    ).astype(jnp.float32)
    back_real = jnp.einsum("psko,pkco->pskc", dual_real, w_real, precision=HIGHEST) + jnp.einsum(
        "psko,pkco->pskc", dual_imag, w_imag, precision=HIGHEST
    )
    back_imag = jnp.einsum("psko,pkco->pskc", dual_imag, w_real, precision=HIGHEST) - jnp.einsum(
        "psko,pkco->pskc", dual_real, w_imag, precision=HIGHEST
    )
    spectral_back = from_modes(back_real, back_imag) / cell_scale
    spread = (
        moving
        * jnp.einsum("sozxy,co->sczxy", delta, point_weight, preferred_element_type=jnp.float32)
    ).astype(jnp.bfloat16)
    spread_padded = jnp.pad(rim_planes(spread), zero_rim)
    local_back = stencil(spread_padded, taps, True)
    grad_feats = (spectral_back + local_back).astype(jnp.bfloat16)
    return (grad_feats, grad_spec)


def frequencies(count, length):
    index = np.arange(count)
    return np.where(index < count // 2, index, length - count + index)


def angles(count, length):
    phases = np.outer(frequencies(count, length), np.arange(length)) % length
    return phases * (2.0 * np.pi / length)


def constant(array):
    return jnp.asarray(np.asarray(array, np.float32).astype(ml_dtypes.bfloat16))


def forward_x_table(slabs):
    a = angles(KX, NX).reshape(slabs, KX // slabs, NX)
    trig = np.stack([np.cos(a), np.sin(a)])
    table = np.einsum("tsjx,cd->tscjdx", trig, np.eye(2))
    return table.reshape(2 * slabs * 2 * (KX // slabs), 2 * NX)


def forward_y_table(planes):
    a = angles(KY, NY)
    cos, sin = np.cos(a).T, np.sin(a).T
    block = np.stack([np.stack([cos, -sin], 1), np.stack([-sin, -cos], 1)])
    pick = np.eye(planes).reshape(planes // 2, 2, planes)
    table = np.einsum("pqz,tyrk->pqtyzrk", pick, block)
    return table.reshape(planes // 2, 4 * NY, planes * 2 * KY)


def forward_z_table():
    a = angles(KZ, NZ)
    cos, sin = np.cos(a).T, np.sin(a).T
    block = np.stack([np.stack([cos, -sin], 1), np.stack([sin, cos], 1)], 1)
    table = np.einsum("zrqm,kl->zrkqlm", block, np.eye(KY))
    return table.reshape(NZ * 2 * KY, 2 * KY * KZ)


def inverse_z_table():
    a = angles(KZ, NZ)
    cos, sin = np.cos(a), np.sin(a)
    block = np.stack([np.stack([cos, sin], 2), np.stack([-sin, cos], 2)])
    table = np.einsum("rmzq,kl->rkmzql", block, np.eye(KY))
    return table.reshape(2 * KY * KZ, NZ * 2 * KY)


def inverse_y_table(planes):
    a = angles(KY, NY)
    cos, sin = np.cos(a), np.sin(a)
    block = np.stack([np.stack([cos, -sin], 1), np.stack([-sin, -cos], 1)])
    pick = np.eye(planes).reshape(planes // 2, 2, planes)
    table = np.einsum("pqz,rkty->pzrktqy", pick, block)
    return table.reshape(planes // 2, planes * 2 * KY, 4 * NY)


def inverse_x_table(slabs):
    a = angles(KX, NX).reshape(slabs, KX // slabs, NX)
    trig = np.stack([np.cos(a), np.sin(a)])
    table = np.einsum("tsjx,cd->cxstdj", trig, np.eye(8))
    return table.reshape(8 * NX, 2 * KX * 8)


def first_table(channels, depth):
    table = np.einsum("ac,j,b->ajcb", np.eye(channels), np.ones(depth), np.ones(channels))
    return table.reshape(channels * depth, channels * channels)


def second_table(channels, depth):
    table = np.einsum("ac,j,b->ajbc", np.eye(channels), np.ones(depth), np.ones(channels))
    return table.reshape(channels * depth, channels * channels)


LIGHT = pl.CostEstimate(flops=10**7, bytes_accessed=10**5, transcendentals=0)


def dot(a, b):
    return jnp.dot(a, b, preferred_element_type=jnp.float32)


def whole(shape):
    return pl.BlockSpec(shape, lambda *_: (0,) * len(shape))


def params(**kw):
    return pltpu.CompilerParams(vmem_limit_bytes=58 * 2**20, **kw)


def modes_step(load, x_table, y_table, rows, total, pair):
    slabs = total.shape[0]
    for i in range(rows.shape[3] // 8):
        part = dot(x_table[...], load(i))
        for t in range(2):
            for s in range(slabs):
                at = 8 * (t * slabs + s)
                for q in range(2):
                    rows[q, t, s, 8 * i : 8 * i + 8, :] = part[at : at + 8, q * NY : q * NY + NY]
    for s in range(slabs):
        left = [rows[q, t, s].astype(jnp.bfloat16) for q in range(2) for t in range(2)]
        step = dot(jnp.concatenate(left, axis=1), y_table[0])
        before = jnp.where(pair == 0, 0.0, total[s])
        total[s] = before + step


def forward_kernel(field, x_table, y_table, out, rows, total):
    pair = pl.program_id(0)

    def load(i):
        halves = [field[2 * i : 2 * i + 2, q].reshape(2 * NX, NY) for q in range(2)]
        return jnp.concatenate(halves, axis=1)

    modes_step(load, x_table, y_table, rows, total, pair)

    @pl.when(pair == pl.num_programs(0) - 1)
    def _():
        out[...] = total[...].astype(jnp.bfloat16)


def forward_modes(field, slabs):
    channels, planes = field.shape[:2]
    lines = channels * (KX // slabs)
    x_table = constant(forward_x_table(slabs))
    y_table = constant(forward_y_table(planes))
    shape = (slabs, lines, planes * 2 * KY)
    return pl.pallas_call(
        forward_kernel,
        grid=(planes // 2,),
        in_specs=[
            pl.BlockSpec((channels, 2, NX, NY), lambda p: (0, p, 0, 0)),
            whole(x_table.shape),
            pl.BlockSpec((1,) + y_table.shape[1:], lambda p: (p, 0, 0)),
        ],
        out_specs=whole(shape),
        out_shape=jax.ShapeDtypeStruct(shape, jnp.bfloat16),
        scratch_shapes=[
            pltpu.VMEM((2, 2, slabs, lines, NY), jnp.float32),
            pltpu.VMEM(shape, jnp.float32),
        ],
        compiler_params=params(),
        cost_estimate=LIGHT,
        name="forward_modes",
    )(field, x_table, y_table)


def mixing_kernel(scale_in, scale_out, adjoint, planar, weight, z_in, z_out, spread_table,
                  sum_table, *rest):
    if adjoint:
        partner, out, send, spectrum, total, wide, product = rest
    else:
        spectrum, out, total, wide, product = rest
    step = pl.program_id(0)
    steps = pl.num_programs(0)
    slabs = planar.shape[0]
    width = planar.shape[2]
    half = spectrum.shape[0] // 2
    lanes = weight.shape[1] // 2

    @pl.when(step == 0)
    def _():
        left = jnp.concatenate([planar[s] for s in range(slabs)], axis=1)
        modes = (dot(left, z_in[...]).T * scale_in).astype(jnp.bfloat16)
        spectrum[...] = modes
        total[...] = jnp.zeros_like(total)
        if adjoint:
            for d in range(send.shape[0]):
                send[d, : 2 * half] = partner[...]
                send[d, 2 * half :] = modes

    lane = lax.broadcasted_iota(jnp.int32, (1, spectrum.shape[1]), 1)
    mine = lane % steps == step
    wide[...] = dot(jnp.where(mine, spectrum[...], 0), spread_table[...])
    block = 32
    for at in range(0, half, block):
        real_wide = wide[at : at + block]
        imag_wide = wide[half + at : half + at + block]
        w_real = weight[at : at + block, :lanes].astype(jnp.float32)
        w_imag = weight[at : at + block, lanes:].astype(jnp.float32)
        if adjoint:
            real = real_wide * w_real + imag_wide * w_imag
            imag = imag_wide * w_real - real_wide * w_imag
        else:
            real = real_wide * w_real - imag_wide * w_imag
            imag = real_wide * w_imag + imag_wide * w_real
        product[at : at + block] = real.astype(jnp.bfloat16)
        product[half + at : half + at + block] = imag.astype(jnp.bfloat16)
    total[...] += jnp.where(mine, dot(product[...], sum_table[...]), 0.0)

    @pl.when(step == steps - 1)
    def _():
        modes = (total[...] * scale_out).T.astype(jnp.bfloat16)
        for s in range(slabs):
            out[s] = dot(modes, z_out[:, s * width : (s + 1) * width]).astype(jnp.bfloat16)


def mix(planar, weight, scale_in, scale_out, partner=None, copies=0):
    slabs, lines, width = planar.shape
    adjoint = partner is not None
    depth = KX // slabs
    channels = lines // depth
    rows = KY * KZ
    z_in = constant(forward_z_table())
    z_out = constant(inverse_z_table())
    first = first_table(channels, depth)
    second = second_table(channels, depth)
    spread_table = constant(second if adjoint else first)
    sum_table = constant((first if adjoint else second).T)
    shape = (2 * rows, lines)
    in_specs = [
        whole(planar.shape),
        pl.BlockSpec((rows, weight.shape[1]), lambda j: (j, 0)),
        whole(z_in.shape),
        whole(z_out.shape),
        whole(spread_table.shape),
        whole(sum_table.shape),
    ]
    operands = [planar, weight, z_in, z_out, spread_table, sum_table]
    scratch = [
        pltpu.VMEM(shape, jnp.float32),
        pltpu.VMEM((2 * rows, channels * channels), jnp.float32),
        pltpu.VMEM((2 * rows, channels * channels), jnp.bfloat16),
    ]
    if adjoint:
        in_specs.append(whole(shape))
        operands.append(partner)
        scratch = [pltpu.VMEM(shape, jnp.bfloat16)] + scratch
        outs = [planar.shape, (copies, 2 * shape[0], lines)]
    else:
        outs = [shape, planar.shape]
    return pl.pallas_call(
        functools.partial(mixing_kernel, scale_in, scale_out, adjoint),
        grid=(depth,),
        in_specs=in_specs,
        out_specs=[whole(out) for out in outs],
        out_shape=[jax.ShapeDtypeStruct(out, jnp.bfloat16) for out in outs],
        scratch_shapes=scratch,
        compiler_params=params(),
        cost_estimate=LIGHT,
        name="mix_back" if adjoint else "mix",
    )(*operands)


def inverse_step(planar, x_table, y_table, waves, store):
    slabs = planar.shape[0]
    for s in range(slabs):
        step = dot(planar[s], y_table[0]).astype(jnp.bfloat16)
        for t in range(2):
            waves[s, t] = step[:, 2 * NY * t : 2 * NY * (t + 1)]
    group = 8 * (KX // slabs)
    for g in range(planar.shape[1] // group):
        right = [waves[s, t, g * group : (g + 1) * group, :] for s in range(slabs) for t in range(2)]
        step = dot(x_table[...], jnp.concatenate(right, axis=0))
        store(g, step.reshape(8, NX, 2 * NY))


def plane_mobility(grains):
    same = [
        jnp.concatenate([grains[:1], grains[:-1]], axis=0),
        jnp.concatenate([grains[1:], grains[-1:]], axis=0),
        jnp.concatenate([grains[:, :1], grains[:, :-1]], axis=1),
        jnp.concatenate([grains[:, 1:], grains[:, -1:]], axis=1),
    ]
    total = jnp.full(grains.shape, 0.25, jnp.float32)
    for other in same:
        total = total + jnp.where(grains != other, 0.25, 0.0)
    return total


def layer_kernel(bias, planar, smooth, cotangent, grains, point_weight, repeat, ix_table, iy_table,
                 x_table, y_table, spread, out, waves, spectral, moving, delta, rows, total,
                 bias_wide, mix_out, mix_in):
    pair = pl.program_id(0)
    channels = smooth.shape[0]

    @pl.when(pair == 0)
    def _():
        for c in range(channels):
            bias_wide[c] = jnp.full(bias_wide.shape[1:], bias[c], jnp.float32)
        tall = dot(repeat[...], point_weight[...]).astype(jnp.bfloat16)
        square = lax.dot_general(
            tall, repeat[...], (((1,), (1,)), ((), ())), preferred_element_type=jnp.float32
        )
        row = lax.broadcasted_iota(jnp.int32, square.shape, 0) % 8
        column = lax.broadcasted_iota(jnp.int32, square.shape, 1) % 8
        square = jnp.where(row == column, square, 0.0)
        mix_in[...] = square.astype(jnp.bfloat16)
        mix_out[...] = square.T.astype(jnp.bfloat16)

    def store(g, value):
        spectral[8 * g : 8 * g + 8] = value

    inverse_step(planar, ix_table, iy_table, waves, store)
    for q in range(2):
        moving[:, q * NY : (q + 1) * NY] = plane_mobility(grains[q])

    def wide(ref, x):
        halves = [ref[:, q, pl.ds(x, 16), :] for q in range(2)]
        return jnp.concatenate(halves, axis=2).astype(jnp.float32)

    def body(i, _):
        x = pl.multiple_of(16 * i, 16)
        smooth_here = wide(smooth, x)
        cotangent_here = wide(cotangent, x)
        deltas = []
        spreads = []
        for h in range(2):
            at = pl.ds(pl.multiple_of(x + 8 * h, 8), 8)
            mobile = moving[at, :][None]
            right = smooth_here[:, 8 * h : 8 * h + 8, :].reshape(8 * channels, 2 * NY)
            local = dot(mix_out[...], right.astype(jnp.bfloat16)).reshape(channels, 8, 2 * NY)
            pre = spectral[:, at, :] + mobile * local + bias_wide[...]
            gate = 0.5 * jnp.tanh(0.5 * pre) + 0.5
            slope = gate * (1.0 + pre * (1.0 - gate))
            change = cotangent_here[:, 8 * h : 8 * h + 8, :] * slope
            deltas.append(change)
            right = change.reshape(8 * channels, 2 * NY).astype(jnp.bfloat16)
            back = dot(mix_in[...], right).reshape(channels, 8, 2 * NY)
            spreads.append(mobile * back)
        delta[:, pl.ds(x, 16), :] = jnp.concatenate(deltas, axis=1).astype(jnp.bfloat16)
        both = jnp.concatenate(spreads, axis=1).astype(jnp.bfloat16)
        for q in range(2):
            spread[:, q, pl.ds(x, 16), :] = both[:, :, q * NY : (q + 1) * NY]
        return 0

    lax.fori_loop(0, NX // 16, body, 0, unroll=4)

    def load(i):
        return delta[2 * i : 2 * i + 2].reshape(2 * NX, 2 * NY)

    modes_step(load, x_table, y_table, rows, total, pair)

    @pl.when(pair == pl.num_programs(0) - 1)
    def _():
        out[...] = total[...].astype(jnp.bfloat16)


def layer(planar, smooth, cotangent, grains, bias, point_weight):
    slabs, lines, width = planar.shape
    channels, planes = smooth.shape[:2]
    repeat = constant(np.repeat(np.eye(channels), 8, axis=0))
    tables = [
        constant(inverse_x_table(slabs)),
        constant(inverse_y_table(planes)),
        constant(forward_x_table(slabs)),
        constant(forward_y_table(planes)),
    ]

    def paired(shape):
        return pl.BlockSpec((1,) + shape[1:], lambda p: (p, 0, 0))

    field = pl.BlockSpec((channels, 2, NX, NY), lambda p: (0, p, 0, 0))
    outs = [smooth.shape, planar.shape]
    return pl.pallas_call(
        layer_kernel,
        grid=(planes // 2,),
        in_specs=[
            pl.BlockSpec(memory_space=pltpu.SMEM),
            whole(planar.shape),
            pl.BlockSpec((channels, 2, NX, NY), lambda p: (0, kept(p, planes // 2), 0, 0)),
            field,
            pl.BlockSpec((2, NX, NY), lambda p: (p, 0, 0)),
            whole(point_weight.shape),
            whole(repeat.shape),
            whole(tables[0].shape),
            paired(tables[1].shape),
            whole(tables[2].shape),
            paired(tables[3].shape),
        ],
        out_specs=[field, whole(planar.shape)],
        out_shape=[jax.ShapeDtypeStruct(out, jnp.bfloat16) for out in outs],
        scratch_shapes=[
            pltpu.VMEM((slabs, 2, lines, 2 * NY), jnp.bfloat16),
            pltpu.VMEM((channels, NX, 2 * NY), jnp.float32),
            pltpu.VMEM((NX, 2 * NY), jnp.float32),
            pltpu.VMEM((channels, NX, 2 * NY), jnp.bfloat16),
            pltpu.VMEM((2, 2, slabs, lines, NY), jnp.float32),
            pltpu.VMEM(planar.shape, jnp.float32),
            pltpu.VMEM((channels, 8, 2 * NY), jnp.float32),
            pltpu.VMEM((8 * channels, 8 * channels), jnp.bfloat16),
            pltpu.VMEM((8 * channels, 8 * channels), jnp.bfloat16),
        ],
        compiler_params=params(),
        cost_estimate=LIGHT,
        name="layer",
    )(bias, planar, smooth, cotangent, grains, point_weight, repeat, *tables)


def finish_kernel(planar, near, ix_table, iy_table, out, waves):
    def store(g, value):
        for q in range(2):
            here = slice(8 * g, 8 * g + 8)
            total = value[:, :, q * NY : (q + 1) * NY] + near[here, q].astype(jnp.float32)
            out[here, q] = total.astype(jnp.bfloat16)

    inverse_step(planar, ix_table, iy_table, waves, store)


def finish(planar, near):
    slabs, lines, width = planar.shape
    channels, planes = near.shape[:2]
    ix_table = constant(inverse_x_table(slabs))
    iy_table = constant(inverse_y_table(planes))
    field = pl.BlockSpec((channels, 2, NX, NY), lambda p: (0, p, 0, 0))
    return pl.pallas_call(
        finish_kernel,
        grid=(planes // 2,),
        in_specs=[
            whole(planar.shape),
            pl.BlockSpec((channels, 2, NX, NY), lambda p: (0, kept(p, planes // 2), 0, 0)),
            whole(ix_table.shape),
            pl.BlockSpec((1,) + iy_table.shape[1:], lambda p: (p, 0, 0)),
        ],
        out_specs=field,
        out_shape=jax.ShapeDtypeStruct(near.shape, jnp.bfloat16),
        scratch_shapes=[pltpu.VMEM((slabs, 2, lines, 2 * NY), jnp.bfloat16)],
        compiler_params=params(),
        cost_estimate=LIGHT,
        name="finish",
    )(planar, near, ix_table, iy_table)


def build_band(adjoint, taps, masks, channel, band):
    blocks = masks.shape[1] // 16
    for dz in range(3):
        for dx in range(3):
            block = jnp.zeros((blocks, 16, NY), jnp.bfloat16)
            for dy in range(3):
                number = 9 * dz + 3 * dx + dy
                tap = taps[26 - number if adjoint else number, channel]
                tap = jnp.full((16, NY), tap, jnp.float32).astype(jnp.bfloat16)
                block = block + masks[dy].reshape(blocks, 16, NY) * tap[None]
            block = block.reshape(NY, NY)
            for q in range(2):
                down = (q + dz) * NY
                right = (2 * dx + q) * NY
                band[down : down + NY, right : right + NY] = block


def kept(pair, pairs):
    return jnp.where(pair == 0, pairs - 2, jnp.where(pair == pairs - 1, pair, pair - 1))


def apply_band(quads, out, band, c):
    left = jnp.concatenate([jnp.concatenate(quad, axis=1) for quad in quads], axis=0)
    middle = dot(left, band[:, 2 * NY : 4 * NY])
    lower = dot(left, band[:, : 2 * NY])
    upper = dot(left, band[:, 4 * NY :])
    row = lax.broadcasted_iota(jnp.int32, (8, 2 * NY), 0)
    for p in range(len(quads)):
        here = slice(p * NX, (p + 1) * NX)
        down = pltpu.roll(lower[here], 1, axis=0)
        up = pltpu.roll(upper[here], NX - 1, axis=0)
        down = jnp.concatenate([jnp.where(row == 0, 0.0, down[:8]), down[8:]], axis=0)
        up = jnp.concatenate([up[:-8], jnp.where(row == 7, 0.0, up[-8:])], axis=0)
        total = (middle[here] + down + up).astype(jnp.bfloat16)
        out[c, 2 * p] = total[:, :NY]
        out[c, 2 * p + 1] = total[:, NY:]


def inner_quads(field, c):
    planes = field.shape[1]
    return [[field[c, z + k] for k in range(4)] for z in range(1, planes - 3, 2)]


def outer_quads(before, field, after, c):
    planes = field.shape[1]
    low = [before[c, 0]] + [field[c, z] for z in range(3)]
    high = [field[c, z] for z in range(planes - 3, planes)] + [after[c, 0]]
    return [low, high]


def stencil_kernel(adjoint, rims, inner, start, taps, masks, *refs):
    if rims:
        low, high, field, out, first, last, even, odd = refs
        first[...] = low[...]
        last[...] = high[...]
    elif inner:
        _, field, out, even, odd = refs
    else:
        _, field, before, after, out, even, odd = refs
    step = pl.program_id(0)
    steps = pl.num_programs(0)
    build = functools.partial(build_band, adjoint, taps, masks)

    def quads(c):
        return inner_quads(field, c) if inner else outer_quads(before, field, after, c)

    @pl.when(step == 0)
    def _():
        even[...] = jnp.zeros_like(even)
        odd[...] = jnp.zeros_like(odd)
        build(start, even)

    build(start + 2 * step + 1, odd)
    apply_band(quads(0), out, even, 0)
    build(start + jnp.minimum(2 * step + 2, 2 * steps - 1), even)
    apply_band(quads(1), out, odd, 1)


def stencil_planes(kind, taps, adjoint, field, near=None, rims=None):
    channels, planes = field.shape[:2]
    masks = constant(np.stack([np.eye(NY, k=1 - dy) for dy in range(3)]))
    quarter = channels // 4
    start = quarter if kind == "inner" else 0
    count = {"rims": quarter, "inner": channels - quarter, "outer": channels}[kind]
    steps = count // 2
    skip = start // 2
    sheets = pl.BlockSpec((2, planes, NX, NY), lambda c: (c + skip, 0, 0, 0))
    if kind == "outer":
        out_spec = pl.BlockSpec((2, 4, NX, NY), lambda c: (c, planes // 4 - 1, 0, 0))
    else:
        out_spec = pl.BlockSpec((2, planes - 4, NX, NY), lambda c: (c + skip, 0, 0, 0))
    in_specs = [pl.BlockSpec(memory_space=pltpu.SMEM), whole(masks.shape)]
    operands = [taps, masks]
    out_specs = [out_spec]
    out_shape = [jax.ShapeDtypeStruct(field.shape, jnp.bfloat16)]
    aliases = {}
    if kind == "rims":
        wide = channels // steps
        rim = (wide, 1, NX, NY)
        in_specs.append(pl.BlockSpec(rim, lambda c: (c, 0, 0, 0)))
        in_specs.append(pl.BlockSpec(rim, lambda c: (c, planes - 1, 0, 0)))
        operands += [field, field]
        for _ in range(2):
            out_specs.append(pl.BlockSpec(rim, lambda c: (c, 0, 0, 0)))
            out_shape.append(jax.ShapeDtypeStruct((channels, 1, NX, NY), jnp.bfloat16))
    else:
        in_specs.append(pl.BlockSpec(memory_space=pl.ANY))
        operands.append(near)
        aliases = {2: 0}
    in_specs.append(sheets)
    operands.append(field)
    if kind == "outer":
        in_specs += [pl.BlockSpec((2, 1, NX, NY), lambda c: (c, 0, 0, 0))] * 2
        operands += list(rims)
    result = pl.pallas_call(
        functools.partial(stencil_kernel, adjoint, kind == "rims", kind != "outer", start),
        grid=(steps,),
        in_specs=in_specs,
        out_specs=out_specs,
        out_shape=out_shape,
        input_output_aliases=aliases,
        scratch_shapes=[pltpu.VMEM((4 * NY, 6 * NY), jnp.bfloat16) for _ in range(2)],
        compiler_params=params(),
        cost_estimate=LIGHT,
        name=("near_" if adjoint else "smooth_") + kind,
    )(*operands)
    return result if kind == "rims" else result[0]


def gradient_kernel(depth, where, gathered, first, second, out):
    step = pl.program_id(0)
    samples, rows, lines = gathered.shape
    half = rows // 4
    lane = lax.broadcasted_iota(jnp.int32, (1, lines), 1)
    mine = lane % depth == step
    total = jnp.zeros(out.shape, jnp.float32)
    for s in range(samples):
        spectrum = jnp.where(mine, gathered[s, : 2 * half], 0)
        real = gathered[s, 2 * half : 3 * half]
        imag = gathered[s, 3 * half :]
        dual = jnp.concatenate(
            [jnp.where(where[0] == 0, real, imag), jnp.where(where[0] == 0, imag, -real)], axis=0
        )
        dual = jnp.where(mine, dual, 0)
        product = dot(spectrum, first[0]) * dot(dual, second[...])
        total = total + product[:half] + product[half:]
    out[...] = total * (1.0 / samples)


def weight_gradient(gathered, depth, width, index):
    samples, rows, lines = gathered.shape
    channels = lines // depth
    square = channels * channels
    cuts = square // width
    first = first_table(channels, depth).reshape(lines, cuts, width).transpose(1, 0, 2)
    second = second_table(channels, depth)[:, :width]
    first = constant(first)
    second = constant(second)
    where = jnp.stack([index // cuts, index % cuts]).astype(jnp.int32)
    half = rows // 4
    return pl.pallas_call(
        functools.partial(gradient_kernel, depth),
        grid_spec=pltpu.PrefetchScalarGridSpec(
            num_scalar_prefetch=1,
            grid=(depth,),
            in_specs=[
                pl.BlockSpec(gathered.shape, lambda j, w: (0, 0, 0)),
                pl.BlockSpec((1, lines, width), lambda j, w: (w[1], 0, 0)),
                pl.BlockSpec(second.shape, lambda j, w: (0, 0)),
            ],
            out_specs=pl.BlockSpec((half, width), lambda j, w: (j, 0)),
        ),
        out_shape=jax.ShapeDtypeStruct((depth * half, width), jnp.float32),
        compiler_params=params(),
        cost_estimate=LIGHT,
        name="weight_gradient",
    )(where, gathered, first, second)


def neighbours(first, last):
    size = lax.axis_size("slab")
    up = [(i, i + 1) for i in range(size - 1)]
    down = [(j, i) for i, j in up]
    return lax.ppermute(last, "slab", up), lax.ppermute(first, "slab", down)


def swap(planar):
    return lax.all_to_all(planar, "slab", split_axis=0, concat_axis=0)


def local_fast(feats, grains, spec_weight, taps, point_weight, bias, cotangent):
    slabs = lax.axis_size("slab")
    field = feats[0]
    channels = field.shape[0]
    cell_scale = 1.0 / math.sqrt(NX * NY * NZ)
    mode_scale = 1.0 / math.sqrt(KX * KY * KZ)
    mode_rows = spec_weight.shape[0]
    weight = spec_weight.reshape(mode_rows * KZ, 2 * channels * channels)
    width = weight.shape[1] // lax.axis_size("dp")

    copies = lax.axis_size("dp")
    barrier = lax.optimization_barrier

    planar, field = barrier((forward_modes(field, slabs), field))
    smooth, first, last = stencil_planes("rims", taps, False, field)
    rims = neighbours(first, last)
    smooth = stencil_planes("inner", taps, False, field, smooth)
    planar, smooth = barrier((swap(planar), smooth))
    spectrum, planar = mix(planar, weight, cell_scale, mode_scale)
    planar, smooth = barrier((planar, smooth))
    planar = swap(planar)
    smooth = stencil_planes("outer", taps, False, field, smooth, rims)
    planar, smooth = barrier((planar, smooth))
    spread, planar = layer(planar, smooth, cotangent[0], grains[0], bias, point_weight)
    near, first, last = stencil_planes("rims", taps, True, spread)
    rims = neighbours(first, last)
    near = stencil_planes("inner", taps, True, spread, near)
    planar, near = barrier((swap(planar), near))
    planar, send = mix(planar, weight, mode_scale, cell_scale, spectrum, copies)
    planar, near = barrier((planar, near))
    planar = swap(planar)
    near = stencil_planes("outer", taps, True, spread, near, rims)
    planar, near, send = barrier((planar, near, send))
    gathered = lax.all_to_all(send, "dp", split_axis=0, concat_axis=0)
    grad_feats = finish(planar, near)[None]
    grad_spec = weight_gradient(gathered, KX // slabs, width, lax.axis_index("dp"))
    return (grad_feats, grad_spec.reshape(mode_rows, KZ, width))


def local(feats, grains, spec_weight, taps, point_weight, bias, cotangent):
    samples, channels, planes = feats.shape[:3]
    width = spec_weight.shape[2] // lax.axis_size("dp")
    fits = (
        lax.axis_size("slab") * 4 == KX
        and samples == 1
        and channels == 32
        and planes == 8
        and channels * channels % width == 0
        and width % 128 == 0
    )
    form = local_fast if fits else local_any
    return form(feats, grains, spec_weight, taps, point_weight, bias, cotangent)


def solution(mesh):
    in_specs = (
        P(("grp", "dp"), None, "slab", None, None),
        P(("grp", "dp"), "slab", None, None),
        P("slab", None, None),
        P(),
        P(),
        P(),
        P(("grp", "dp"), None, "slab", None, None),
    )
    out_specs = (P(("grp", "dp"), None, "slab", None, None), P("slab", "grp", "dp"))
    return jax.shard_map(local, mesh=mesh, in_specs=in_specs, out_specs=out_specs, check_vma=False)
```

```python
import functools
import math

import jax
import jax.numpy as jnp
import ml_dtypes
import numpy as np
from jax import lax
from jax.experimental import pallas as pl
from jax.experimental.pallas import tpu as pltpu
from jax.sharding import PartitionSpec as P

NX = 128
NY = 128
NZ = 32
KX = 16
KY = 16
KZ = 16


HIGHEST = lax.Precision.HIGHEST


def extended(shard, sides, width):
    for axis, dim in sides:
        size, length = (lax.axis_size(axis), shard.shape[dim])
        up = [(i, (i + 1) % size) for i in range(size - 1)]
        down = [(j, i) for i, j in up]
        last = lax.slice_in_dim(shard, length - width, length, axis=dim)
        first = lax.slice_in_dim(shard, 0, width, axis=dim)
        before = lax.ppermute(last, axis, up)
        after = lax.ppermute(first, axis, down)
        shard = jnp.concatenate([before, shard, after], axis=dim)
    return shard


def tables(count, length, span):
    indices = jnp.arange(count, dtype=jnp.int32)
    frequency = jnp.where(indices < count // 2, indices, length - count + indices)
    position = jnp.arange(span, dtype=jnp.int32)
    phases = frequency[:, None] * position[None, :] % length
    angles = phases.astype(jnp.float32) * (2.0 * math.pi / length)
    return (jnp.cos(angles), jnp.sin(angles))


def mobility(grains):
    leading = [(0, 0)] * (grains.ndim - 2)
    along_x = (grains[..., 1:, :] != grains[..., :-1, :]).astype(jnp.float32)
    along_y = (grains[..., :, 1:] != grains[..., :, :-1]).astype(jnp.float32)
    differ = jnp.pad(along_x, leading + [(1, 0), (0, 0)]) + jnp.pad(
        along_x, leading + [(0, 1), (0, 0)]
    )
    differ = (
        differ
        + jnp.pad(along_y, leading + [(0, 0), (1, 0)])
        + jnp.pad(along_y, leading + [(0, 0), (0, 1)])
    )
    return 0.25 * (1.0 + differ)


def stencil(padded, taps, adjoint):
    planes = padded.shape[-3] - 2
    rows_x = padded.shape[-2] - 2
    rows_y = padded.shape[-1] - 2
    total = jnp.zeros(padded.shape[:-3] + (planes, rows_x, rows_y), jnp.float32)
    for offset in range(27):
        shift_z, shift_x, shift_y = (offset // 9, offset // 3 % 3, offset % 3)
        if adjoint:
            shift_z, shift_x, shift_y = (2 - shift_z, 2 - shift_x, 2 - shift_y)
        window = padded[
            ..., shift_z : shift_z + planes, shift_x : shift_x + rows_x, shift_y : shift_y + rows_y
        ]
        total = total + taps[offset][:, None, None, None] * window.astype(jnp.float32)
    return total


def plane_forward(field, cos_x, sin_x, cos_y, sin_y):
    real_y = jnp.einsum("...xy,ky->...xk", field, cos_y, precision=HIGHEST)
    imag_y = -jnp.einsum("...xy,ky->...xk", field, sin_y, precision=HIGHEST)
    real_part = jnp.einsum("...xk,jx->...jk", real_y, cos_x, precision=HIGHEST) + jnp.einsum(
        "...xk,jx->...jk", imag_y, sin_x, precision=HIGHEST
    )
    imag_part = jnp.einsum("...xk,jx->...jk", imag_y, cos_x, precision=HIGHEST) - jnp.einsum(
        "...xk,jx->...jk", real_y, sin_x, precision=HIGHEST
    )
    return (real_part, imag_part)


def plane_inverse(real_part, imag_part, cos_x, sin_x, cos_y, sin_y):
    real_x = jnp.einsum("...jk,jx->...xk", real_part, cos_x, precision=HIGHEST) - jnp.einsum(
        "...jk,jx->...xk", imag_part, sin_x, precision=HIGHEST
    )
    imag_x = jnp.einsum("...jk,jx->...xk", imag_part, cos_x, precision=HIGHEST) + jnp.einsum(
        "...jk,jx->...xk", real_part, sin_x, precision=HIGHEST
    )
    return jnp.einsum("...xk,ky->...xy", real_x, cos_y, precision=HIGHEST) - jnp.einsum(
        "...xk,ky->...xy", imag_x, sin_y, precision=HIGHEST
    )


def depth_forward(packed, cos_table, sin_table):
    width = packed.shape[-1] // 2
    real_in = packed[..., :width]
    imag_in = packed[..., width:]
    real_out = jnp.einsum("pszc,kz->pskc", real_in, cos_table, precision=HIGHEST) + jnp.einsum(
        "pszc,kz->pskc", imag_in, sin_table, precision=HIGHEST
    )
    imag_out = jnp.einsum("pszc,kz->pskc", imag_in, cos_table, precision=HIGHEST) - jnp.einsum(
        "pszc,kz->pskc", real_in, sin_table, precision=HIGHEST
    )
    return jnp.concatenate([real_out, imag_out], axis=-1)


def depth_inverse(real_modes, imag_modes, cos_table, sin_table):
    real_out = jnp.einsum("pskc,kz->pszc", real_modes, cos_table, precision=HIGHEST) - jnp.einsum(
        "pskc,kz->pszc", imag_modes, sin_table, precision=HIGHEST
    )
    imag_out = jnp.einsum("pskc,kz->pszc", imag_modes, cos_table, precision=HIGHEST) + jnp.einsum(
        "pskc,kz->pszc", real_modes, sin_table, precision=HIGHEST
    )
    return jnp.concatenate([real_out, imag_out], axis=-1)


def rim_planes(field):
    return extended(field, (("slab", 2),), 1)


def local_any(feats, grains, spec_weight, taps, point_weight, bias, cotangent):
    samples_here = feats.shape[0]
    channels = feats.shape[1]
    planes = feats.shape[2]
    cos_x, sin_x = tables(KX, NX, NX)
    cos_y, sin_y = tables(KY, NY, NY)
    cos_full, sin_full = tables(KZ, NZ, NZ)
    cell_scale = math.sqrt(NX * NY * NZ)
    mode_scale = math.sqrt(KX * KY * KZ)
    mode_rows = spec_weight.shape[0]
    weights = spec_weight.astype(jnp.float32).reshape(mode_rows, KZ, 2, channels, channels)
    w_real = weights[:, :, 0]
    w_imag = weights[:, :, 1]
    moving = mobility(grains)[:, None]

    def to_modes(field):
        real_plane, imag_plane = plane_forward(field, cos_x, sin_x, cos_y, sin_y)
        packed = jnp.stack([real_plane, imag_plane], axis=1)
        packed = packed.transpose(4, 5, 0, 3, 1, 2).reshape(
            KX * KY, samples_here, planes, 2 * channels
        )
        moved = lax.all_to_all(packed, "slab", split_axis=0, concat_axis=2, tiled=True)
        summed = depth_forward(moved, cos_full, sin_full)
        return (summed[..., :channels], summed[..., channels:])

    def from_modes(real_modes, imag_modes):
        planar = depth_inverse(real_modes, imag_modes, cos_full, sin_full)
        packed = lax.all_to_all(planar, "slab", split_axis=2, concat_axis=0, tiled=True)
        grouped = packed.reshape(KX, KY, samples_here, planes, 2, channels).transpose(
            2, 4, 5, 3, 0, 1
        )
        return plane_inverse(grouped[:, 0], grouped[:, 1], cos_x, sin_x, cos_y, sin_y)

    zero_rim = ((0, 0), (0, 0), (0, 0), (1, 1), (1, 1))
    padded = jnp.pad(rim_planes(feats), zero_rim)
    smooth = stencil(padded, taps, False).astype(jnp.bfloat16)
    local_part = moving * jnp.einsum(
        "sczxy,co->sozxy", smooth, point_weight, preferred_element_type=jnp.float32
    )
    spec_real, spec_imag = to_modes(feats.astype(jnp.float32))
    spec_real = spec_real / cell_scale
    spec_imag = spec_imag / cell_scale
    mixed_real = jnp.einsum("pskc,pkco->psko", spec_real, w_real, precision=HIGHEST) - jnp.einsum(
        "pskc,pkco->psko", spec_imag, w_imag, precision=HIGHEST
    )
    mixed_imag = jnp.einsum("pskc,pkco->psko", spec_real, w_imag, precision=HIGHEST) + jnp.einsum(
        "pskc,pkco->psko", spec_imag, w_real, precision=HIGHEST
    )
    spectral = from_modes(mixed_real, mixed_imag) / mode_scale
    pre = spectral + local_part + bias[None, :, None, None, None]
    gate = jax.nn.sigmoid(pre)
    delta = (cotangent.astype(jnp.float32) * gate * (1.0 + pre * (1.0 - gate))).astype(jnp.bfloat16)
    dual_real, dual_imag = to_modes(delta.astype(jnp.float32))
    dual_real = dual_real / mode_scale
    dual_imag = dual_imag / mode_scale
    batch_total = samples_here * lax.axis_size("dp")
    grad_real = jnp.einsum("pskc,psko->pkco", spec_real, dual_real, precision=HIGHEST) + jnp.einsum(
        "pskc,psko->pkco", spec_imag, dual_imag, precision=HIGHEST
    )
    grad_imag = jnp.einsum("pskc,psko->pkco", spec_real, dual_imag, precision=HIGHEST) - jnp.einsum(
        "pskc,psko->pkco", spec_imag, dual_real, precision=HIGHEST
    )
    grad_terms = (jnp.stack([grad_real, grad_imag], axis=2) / batch_total).reshape(
        mode_rows, KZ, 2 * channels * channels
    )
    grad_spec = lax.psum_scatter(
        grad_terms.astype(jnp.bfloat16), "dp", scatter_dimension=2, tiled=True
    ).astype(jnp.float32)
    back_real = jnp.einsum("psko,pkco->pskc", dual_real, w_real, precision=HIGHEST) + jnp.einsum(
        "psko,pkco->pskc", dual_imag, w_imag, precision=HIGHEST
    )
    back_imag = jnp.einsum("psko,pkco->pskc", dual_imag, w_real, precision=HIGHEST) - jnp.einsum(
        "psko,pkco->pskc", dual_real, w_imag, precision=HIGHEST
    )
    spectral_back = from_modes(back_real, back_imag) / cell_scale
    spread = (
        moving
        * jnp.einsum("sozxy,co->sczxy", delta, point_weight, preferred_element_type=jnp.float32)
    ).astype(jnp.bfloat16)
    spread_padded = jnp.pad(rim_planes(spread), zero_rim)
    local_back = stencil(spread_padded, taps, True)
    grad_feats = (spectral_back + local_back).astype(jnp.bfloat16)
    return (grad_feats, grad_spec)


def frequencies(count, length):
    index = np.arange(count)
    return np.where(index < count // 2, index, length - count + index)


def angles(count, length):
    phases = np.outer(frequencies(count, length), np.arange(length)) % length
    return phases * (2.0 * np.pi / length)


def constant(array):
    return jnp.asarray(np.asarray(array, np.float32).astype(ml_dtypes.bfloat16))


def forward_x_table(slabs, split):
    a = angles(KX, NX).reshape(slabs, KX // slabs, NX)
    trig = np.stack([np.cos(a), np.sin(a)])
    table = np.einsum("tsjx,cd->tscjdx", trig, np.eye(2)).reshape(-1, 2, NX // 8, 8)
    if split:
        table = table.transpose(0, 2, 1, 3)
    return table.reshape(4 * KX, 2 * NX)


def forward_y_table(planes):
    a = angles(KY, NY)
    trig = np.stack([np.cos(a), np.sin(a)])
    table = np.einsum("zw,tky->zywtk", np.eye(planes), trig)
    return table.reshape(planes * NY, planes * 2 * KY)


def forward_z_table():
    a = angles(KZ, NZ)
    cos, sin = np.cos(a).T, np.sin(a).T
    block = np.stack([np.stack([cos, -sin], 1), np.stack([sin, cos], 1)], 1)
    table = np.einsum("zrqm,kl->zrkqlm", block, np.eye(KY))
    return table.reshape(NZ * 2 * KY, 2 * KY * KZ)


def inverse_z_table():
    a = angles(KZ, NZ)
    cos, sin = np.cos(a), np.sin(a)
    block = np.stack([np.stack([cos, sin], 2), np.stack([-sin, cos], 2)])
    table = np.einsum("rmzq,kl->rkmzql", block, np.eye(KY))
    return table.reshape(2 * KY * KZ, NZ * 2 * KY)


def inverse_y_table(planes, group):
    a = angles(KY, NY)
    cos, sin = np.cos(a), np.sin(a)
    block = np.stack([np.stack([cos, -sin], 1), np.stack([-sin, -cos], 1)])
    pick = np.eye(planes).reshape(planes // group, group, planes)
    table = np.einsum("pqz,rkty->pzrktqy", pick, block)
    return table.reshape(planes // group, planes * 2 * KY, 2 * group * NY)


def inverse_x_table(slabs, group):
    a = angles(KX, NX).reshape(slabs, KX // slabs, NX)
    trig = np.stack([np.cos(a), np.sin(a)])
    table = np.einsum("tsjx,cd->cxstdj", trig, np.eye(group))
    return table.reshape(group * NX, 2 * KX * group)


def first_table(channels, depth):
    table = np.einsum("ac,j,b->ajcb", np.eye(channels), np.ones(depth), np.ones(channels))
    return table.reshape(channels * depth, channels * channels)


def second_table(channels, depth):
    table = np.einsum("ac,j,b->ajbc", np.eye(channels), np.ones(depth), np.ones(channels))
    return table.reshape(channels * depth, channels * channels)


LIGHT = pl.CostEstimate(flops=10**7, bytes_accessed=10**5, transcendentals=0)


def dot(a, b):
    return jnp.dot(a, b, preferred_element_type=jnp.float32)


def whole(shape):
    return pl.BlockSpec(shape, lambda *_: (0,) * len(shape))


def params(**kw):
    return pltpu.CompilerParams(vmem_limit_bytes=58 * 2**20, **kw)


def modes_of(left, y_table, x_table):
    waves = dot(left, y_table[...]).astype(jnp.bfloat16)
    both = dot(x_table[...], waves)
    half = both.shape[0] // 2
    lane = lax.broadcasted_iota(jnp.int32, (half, 128), 1)
    real = (lane // KY) % 2 == 0
    parts = []
    for at in range(0, both.shape[1], 128):
        cos = both[:half, at : at + 128]
        sin = both[half:, at : at + 128]
        other = jnp.where(real, pltpu.roll(sin, 128 - KY, axis=1), pltpu.roll(sin, KY, axis=1))
        parts.append(jnp.where(real, cos, -cos) - other)
    return jnp.concatenate(parts, axis=1)


def store_modes(out, at, first, second):
    rows = first.shape[0] // out.shape[0]
    for s in range(out.shape[0]):
        here = slice(s * rows, (s + 1) * rows)
        both = jnp.concatenate([first[here], second[here]], axis=0)
        out[s, pl.ds(at, 2 * rows), :] = both.astype(jnp.bfloat16)


def forward_kernel(field, x_table, y_table, out, first, last):
    step = pl.program_id(0)
    planes = field.shape[1]
    first[:, 0] = field[:, 0]
    last[:, 0] = field[:, planes - 1]
    modes = []
    for i in range(2):
        sheets = [field[2 * i : 2 * i + 2, z].reshape(2 * NX, NY) for z in range(planes)]
        modes.append(modes_of(jnp.concatenate(sheets, axis=1), y_table, x_table))
    store_modes(out, pl.multiple_of(16 * step, 16), *modes)


def forward_modes(field, slabs):
    channels, planes = field.shape[:2]
    lines = channels * (KX // slabs)
    x_table = constant(forward_x_table(slabs, False))
    y_table = constant(forward_y_table(planes))
    shape = (slabs, lines, planes * 2 * KY)
    rim = pl.BlockSpec((4, 1, NX, NY), lambda c: (c, 0, 0, 0))
    rims = jax.ShapeDtypeStruct((channels, 1, NX, NY), jnp.bfloat16)
    return pl.pallas_call(
        forward_kernel,
        grid=(channels // 4,),
        in_specs=[
            pl.BlockSpec((4, planes, NX, NY), lambda c: (c, 0, 0, 0)),
            whole(x_table.shape),
            whole(y_table.shape),
        ],
        out_specs=[whole(shape), rim, rim],
        out_shape=[jax.ShapeDtypeStruct(shape, jnp.bfloat16), rims, rims],
        compiler_params=params(),
        cost_estimate=LIGHT,
        name="forward_modes",
    )(field, x_table, y_table)


def mixing_kernel(scale_in, scale_out, adjoint, planar, weight, z_in, z_out, spread_table,
                  sum_table, *rest):
    if adjoint:
        partner, out, send, spectrum, total, wide, product = rest
    else:
        spectrum, out, total, wide, product = rest
    step = pl.program_id(0)
    steps = pl.num_programs(0)
    slabs = planar.shape[0]
    width = planar.shape[2]
    half = spectrum.shape[0] // 2
    lanes = weight.shape[1] // 2

    @pl.when(step == 0)
    def _():
        left = jnp.concatenate([planar[s] for s in range(slabs)], axis=1)
        modes = (dot(left, z_in[...]).T * scale_in).astype(jnp.bfloat16)
        spectrum[...] = modes
        total[...] = jnp.zeros_like(total)
        if adjoint:
            for d in range(send.shape[0]):
                send[d, : 2 * half] = partner[...]
                send[d, 2 * half :] = modes

    lane = lax.broadcasted_iota(jnp.int32, (1, spectrum.shape[1]), 1)
    mine = lane % steps == step
    wide[...] = dot(jnp.where(mine, spectrum[...], 0), spread_table[...])
    block = 32
    for at in range(0, half, block):
        real_wide = wide[at : at + block]
        imag_wide = wide[half + at : half + at + block]
        w_real = weight[at : at + block, :lanes].astype(jnp.float32)
        w_imag = weight[at : at + block, lanes:].astype(jnp.float32)
        if adjoint:
            real = real_wide * w_real + imag_wide * w_imag
            imag = imag_wide * w_real - real_wide * w_imag
        else:
            real = real_wide * w_real - imag_wide * w_imag
            imag = real_wide * w_imag + imag_wide * w_real
        product[at : at + block] = real.astype(jnp.bfloat16)
        product[half + at : half + at + block] = imag.astype(jnp.bfloat16)
    total[...] += jnp.where(mine, dot(product[...], sum_table[...]), 0.0)

    @pl.when(step == steps - 1)
    def _():
        modes = (total[...] * scale_out).T.astype(jnp.bfloat16)
        for s in range(slabs):
            out[s] = dot(modes, z_out[:, s * width : (s + 1) * width]).astype(jnp.bfloat16)


def mix(planar, weight, scale_in, scale_out, partner=None, copies=0):
    slabs, lines, width = planar.shape
    adjoint = partner is not None
    depth = KX // slabs
    channels = lines // depth
    rows = KY * KZ
    z_in = constant(forward_z_table())
    z_out = constant(inverse_z_table())
    first = first_table(channels, depth)
    second = second_table(channels, depth)
    spread_table = constant(second if adjoint else first)
    sum_table = constant((first if adjoint else second).T)
    shape = (2 * rows, lines)
    in_specs = [
        whole(planar.shape),
        pl.BlockSpec((rows, weight.shape[1]), lambda j: (j, 0)),
        whole(z_in.shape),
        whole(z_out.shape),
        whole(spread_table.shape),
        whole(sum_table.shape),
    ]
    operands = [planar, weight, z_in, z_out, spread_table, sum_table]
    scratch = [
        pltpu.VMEM(shape, jnp.float32),
        pltpu.VMEM((2 * rows, channels * channels), jnp.float32),
        pltpu.VMEM((2 * rows, channels * channels), jnp.bfloat16),
    ]
    if adjoint:
        in_specs.append(whole(shape))
        operands.append(partner)
        scratch = [pltpu.VMEM(shape, jnp.bfloat16)] + scratch
        outs = [planar.shape, (copies, 2 * shape[0], lines)]
    else:
        outs = [shape, planar.shape]
    return pl.pallas_call(
        functools.partial(mixing_kernel, scale_in, scale_out, adjoint),
        grid=(depth,),
        in_specs=in_specs,
        out_specs=[whole(out) for out in outs],
        out_shape=[jax.ShapeDtypeStruct(out, jnp.bfloat16) for out in outs],
        scratch_shapes=scratch,
        compiler_params=params(),
        cost_estimate=LIGHT,
        name="mix_back" if adjoint else "mix",
    )(*operands)


def plane_mobility(grains):
    same = [
        jnp.concatenate([grains[:1], grains[:-1]], axis=0),
        jnp.concatenate([grains[1:], grains[-1:]], axis=0),
        jnp.concatenate([grains[:, :1], grains[:, :-1]], axis=1),
        jnp.concatenate([grains[:, 1:], grains[:, -1:]], axis=1),
    ]
    total = jnp.full(grains.shape, 0.25, jnp.float32)
    for other in same:
        total = total + jnp.where(grains != other, 0.25, 0.0)
    return total


def layer_kernel(bias, planar, smooth, cotangent, grains, point_weight, repeat, ix_table, iy_table,
                 x_table, y_table, spread, out, first, last, waves, spectral, moving, delta,
                 bias_wide, mix_out, mix_in):
    pair = pl.program_id(0)
    pairs = delta.shape[0]
    channels = cotangent.shape[0]
    slabs = planar.shape[0]

    @pl.when(pair == 0)
    def _():
        for c in range(channels):
            bias_wide[c] = jnp.full(bias_wide.shape[1:], 0.5 * bias[c], jnp.float32)
        tall = dot(repeat[...], point_weight[...]).astype(jnp.bfloat16)
        square = lax.dot_general(
            tall, repeat[...], (((1,), (1,)), ((), ())), preferred_element_type=jnp.float32
        )
        row = lax.broadcasted_iota(jnp.int32, square.shape, 0) % 8
        column = lax.broadcasted_iota(jnp.int32, square.shape, 1) % 8
        square = jnp.where(row == column, square, 0.0)
        mix_in[...] = square.astype(jnp.bfloat16)
        mix_out[...] = square.T.astype(jnp.bfloat16)

    for s in range(slabs):
        step = dot(planar[s], iy_table[0]).astype(jnp.bfloat16)
        for t in range(2):
            waves[s, t] = step[:, 2 * NY * t : 2 * NY * (t + 1)]
    group = 8 * (KX // slabs)
    for g in range(channels // 8):
        right = [waves[s, t, g * group : (g + 1) * group, :] for s in range(slabs) for t in range(2)]
        step = dot(ix_table[...], jnp.concatenate(right, axis=0))
        spectral[8 * g : 8 * g + 8] = step.reshape(8, NX, 2 * NY)
    for q in range(2):
        moving[:, q * NY : (q + 1) * NY] = 0.5 * plane_mobility(grains[q])

    def body(i, _):
        x = pl.multiple_of(16 * i, 16)
        halves = [cotangent[:, q, pl.ds(x, 16), :] for q in range(2)]
        cotangent_here = jnp.concatenate(halves, axis=2).astype(jnp.float32)
        spreads = []
        for h in range(2):
            at = pl.ds(pl.multiple_of(x + 8 * h, 8), 8)
            mobile = moving[at, :][None]
            local = dot(mix_out[...], smooth[0, 2 * i + h]).reshape(channels, 8, 2 * NY)
            half = spectral[:, at, :] + mobile * local + bias_wide[...]
            wave = jnp.tanh(half)
            slope = (1.0 + wave) * (1.0 + (half - half * wave))
            change = cotangent_here[:, 8 * h : 8 * h + 8, :] * slope
            right = change.reshape(8 * channels, 2 * NY).astype(jnp.bfloat16)
            delta[pair, 2 * i + h] = right
            back = dot(mix_in[...], right).reshape(channels, 8, 2 * NY)
            spreads.append(mobile * back)
        both = jnp.concatenate(spreads, axis=1).astype(jnp.bfloat16)
        for q in range(2):
            spread[:, q, pl.ds(x, 16), :] = both[:, :, q * NY : (q + 1) * NY]
        return 0

    lax.fori_loop(0, NX // 16, body, 0, unroll=4)

    @pl.when(pair == 0)
    def _():
        first[:, 0] = spread[:, 0]

    @pl.when(pair == pairs - 1)
    def _():
        last[:, 0] = spread[:, 1]
        for step in range(channels // 4):
            modes = []
            for i in range(2):
                here = slice(32 * step + 16 * i, 32 * step + 16 * i + 16)
                sheets = [delta[p, :, here, :].reshape(2 * NX, 2 * NY) for p in range(pairs)]
                modes.append(modes_of(jnp.concatenate(sheets, axis=1), y_table, x_table))
            store_modes(out, 16 * step, *modes)


def layer(planar, smooth, cotangent, grains, bias, point_weight):
    slabs, lines, width = planar.shape
    channels, planes = cotangent.shape[:2]
    pairs = planes // 2
    repeat = constant(np.repeat(np.eye(channels), 8, axis=0))
    ix_table = constant(inverse_x_table(slabs, 8))
    iy_table = constant(inverse_y_table(planes, 2))
    x_table = constant(forward_x_table(slabs, True))
    y_table = constant(forward_y_table(planes))
    field = pl.BlockSpec((channels, 2, NX, NY), lambda p: (0, p, 0, 0))
    rim = (channels, 1, NX, NY)
    outs = [cotangent.shape, planar.shape, rim, rim]
    return pl.pallas_call(
        layer_kernel,
        grid=(pairs,),
        in_specs=[
            pl.BlockSpec(memory_space=pltpu.SMEM),
            whole(planar.shape),
            pl.BlockSpec((1,) + smooth.shape[1:], lambda p: (kept(p, pairs), 0, 0, 0)),
            field,
            pl.BlockSpec((2, NX, NY), lambda p: (p, 0, 0)),
            whole(point_weight.shape),
            whole(repeat.shape),
            whole(ix_table.shape),
            pl.BlockSpec((1,) + iy_table.shape[1:], lambda p: (p, 0, 0)),
            whole(x_table.shape),
            whole(y_table.shape),
        ],
        out_specs=[field, whole(planar.shape), whole(rim), whole(rim)],
        out_shape=[jax.ShapeDtypeStruct(out, jnp.bfloat16) for out in outs],
        scratch_shapes=[
            pltpu.VMEM((slabs, 2, lines, 2 * NY), jnp.bfloat16),
            pltpu.VMEM((channels, NX, 2 * NY), jnp.float32),
            pltpu.VMEM((NX, 2 * NY), jnp.float32),
            pltpu.VMEM((pairs, NX // 8, 8 * channels, 2 * NY), jnp.bfloat16),
            pltpu.VMEM((channels, 8, 2 * NY), jnp.float32),
            pltpu.VMEM((8 * channels, 8 * channels), jnp.bfloat16),
            pltpu.VMEM((8 * channels, 8 * channels), jnp.bfloat16),
        ],
        compiler_params=params(),
        cost_estimate=LIGHT,
        name="layer",
    )(bias, planar, smooth, cotangent, grains, point_weight, repeat, ix_table, iy_table, x_table,
      y_table)


def kept(pair, pairs):
    return jnp.where(pair == 0, pairs - 2, jnp.where(pair == pairs - 1, pair, pair - 1))


def build_band(adjoint, taps, channel, band):
    row = lax.broadcasted_iota(jnp.int32, (8, NY), 0)
    lane = lax.broadcasted_iota(jnp.int32, (8, NY), 1)
    offset = row - lane
    for dz in range(3):
        for dx in range(3):
            tile = jnp.zeros((8, NY), jnp.float32)
            for dy in range(3):
                number = 9 * dz + 3 * dx + dy
                tap = taps[26 - number if adjoint else number, channel]
                hit = (offset == dy - 1) | (offset == dy - 1 - NY)
                tile = jnp.where(hit, tap, tile)
            tiles = [pltpu.roll(tile, 8 * k, axis=1) if k > 0 else tile for k in range(NY // 8)]
            tiles[0] = jnp.where((row == 0) & (lane == NY - 1), 0.0, tiles[0])
            tiles[-1] = jnp.where((row == 7) & (lane == 0), 0.0, tiles[-1])
            block = jnp.concatenate(tiles, axis=0).astype(jnp.bfloat16)
            for q in range(2):
                down = (q + dz) * NY
                right = (2 * dx + q) * NY
                band[down : down + NY, right : right + NY] = block


def apply_band(quads, band):
    left = jnp.concatenate([jnp.concatenate(quad, axis=1) for quad in quads], axis=0)
    middle = dot(left, band[:, 2 * NY : 4 * NY])
    lower = dot(left, band[:, : 2 * NY])
    upper = dot(left, band[:, 4 * NY :])
    row = lax.broadcasted_iota(jnp.int32, (8, 2 * NY), 0)
    totals = []
    for p in range(len(quads)):
        here = slice(p * NX, (p + 1) * NX)
        down = pltpu.roll(lower[here], 1, axis=0)
        up = pltpu.roll(upper[here], NX - 1, axis=0)
        down = jnp.concatenate([jnp.where(row == 0, 0.0, down[:8]), down[8:]], axis=0)
        up = jnp.concatenate([up[:-8], jnp.where(row == 7, 0.0, up[-8:])], axis=0)
        totals.append(middle[here] + down + up)
    return totals


def banded(adjoint, taps, even, odd, channels):
    step = pl.program_id(0)
    final = channels * pl.num_programs(0) - 1
    bands = (even, odd)

    @pl.when(step == 0)
    def _():
        even[...] = jnp.zeros_like(even)
        odd[...] = jnp.zeros_like(odd)
        build_band(adjoint, taps, 0, even)

    def run(visit):
        for c in range(channels):
            following = jnp.minimum(channels * step + c + 1, final)
            build_band(adjoint, taps, following, bands[(c + 1) % 2])
            visit(c, bands[c % 2])

    return run


def smooth_kernel(inner, taps, field, *refs):
    if inner:
        out, even, odd = refs
    else:
        _, before, after, out, even, odd = refs
    planes = field.shape[1]
    totals = []

    def visit(c, band):
        if inner:
            quads = [[field[c, z + k] for k in range(4)] for z in range(1, planes - 3, 2)]
        else:
            low = [before[c, 0]] + [field[c, z] for z in range(3)]
            high = [field[c, z] for z in range(planes - 3, planes)] + [after[c, 0]]
            quads = [low, high]
        totals.append(apply_band(quads, band))

    banded(False, taps, even, odd, 2)(visit)
    for p in range(len(totals[0])):
        both = [totals[c][p].reshape(NX // 8, 8, 2 * NY) for c in range(2)]
        out[p] = jnp.concatenate(both, axis=1).astype(jnp.bfloat16)


def smooth_planes(field, taps, inner=None, rims=None):
    channels, planes = field.shape[:2]
    pairs = planes // 2
    shape = (pairs, NX // 8, 8 * channels, 2 * NY)
    in_specs = [
        pl.BlockSpec(memory_space=pltpu.SMEM),
        pl.BlockSpec((2, planes, NX, NY), lambda c: (c, 0, 0, 0)),
    ]
    operands = [taps, field]
    place = 0
    if inner is not None:
        in_specs.append(pl.BlockSpec(memory_space=pl.ANY))
        in_specs += [pl.BlockSpec((2, 1, NX, NY), lambda c: (c, 0, 0, 0))] * 2
        operands += [inner, *rims]
        place = 1
    return pl.pallas_call(
        functools.partial(smooth_kernel, inner is None),
        grid=(channels // 2,),
        in_specs=in_specs,
        out_specs=pl.BlockSpec((pairs // 2, NX // 8, 16, 2 * NY), lambda c: (place, 0, c, 0)),
        out_shape=jax.ShapeDtypeStruct(shape, jnp.bfloat16),
        input_output_aliases={} if inner is None else {2: 0},
        scratch_shapes=[pltpu.VMEM((4 * NY, 6 * NY), jnp.bfloat16) for _ in range(2)],
        compiler_params=params(),
        cost_estimate=LIGHT,
        name="smooth_inner" if inner is None else "smooth_outer",
    )(*operands)


def finish_kernel(taps, before, field, after, planar, ix_table, iy_table, out, waves, spectral,
                  even, odd):
    step = pl.program_id(0)
    slabs = planar.shape[0]
    planes = field.shape[1]
    span = planes * NY

    @pl.when(step == 0)
    def _():
        for s in range(slabs):
            for t in range(2):
                right = iy_table[0, :, t * span : (t + 1) * span]
                waves[s, t] = dot(planar[s], right).astype(jnp.bfloat16)

    rows = 4 * (KX // slabs)
    here = pl.ds(pl.multiple_of(rows * step, rows), rows)
    right = [waves[s, t, here, :] for s in range(slabs) for t in range(2)]
    spectral[...] = dot(ix_table[...], jnp.concatenate(right, axis=0))

    def visit(c, band):
        sheets = [before[c, 0]] + [field[c, z] for z in range(planes)] + [after[c, 0]]
        totals = apply_band([sheets[z : z + 4] for z in range(0, planes, 2)], band)
        for p in range(planes // 2):
            wide = slice(2 * p * NY, 2 * (p + 1) * NY)
            total = (totals[p] + spectral[c * NX : (c + 1) * NX, wide]).astype(jnp.bfloat16)
            out[c, 2 * p] = total[:, :NY]
            out[c, 2 * p + 1] = total[:, NY:]

    banded(True, taps, even, odd, 4)(visit)


def finish(planar, spread, rims, taps):
    slabs, lines, width = planar.shape
    channels, planes = spread.shape[:2]
    ix_table = constant(inverse_x_table(slabs, 4))
    iy_table = constant(inverse_y_table(planes, planes))
    rim = pl.BlockSpec((4, 1, NX, NY), lambda c: (c, 0, 0, 0))
    sheets = pl.BlockSpec((4, planes, NX, NY), lambda c: (c, 0, 0, 0))
    return pl.pallas_call(
        finish_kernel,
        grid=(channels // 4,),
        in_specs=[
            pl.BlockSpec(memory_space=pltpu.SMEM),
            rim,
            sheets,
            rim,
            whole(planar.shape),
            whole(ix_table.shape),
            whole(iy_table.shape),
        ],
        out_specs=sheets,
        out_shape=jax.ShapeDtypeStruct(spread.shape, jnp.bfloat16),
        scratch_shapes=[
            pltpu.VMEM((slabs, 2, lines, planes * NY), jnp.bfloat16),
            pltpu.VMEM((4 * NX, planes * NY), jnp.float32),
            pltpu.VMEM((4 * NY, 6 * NY), jnp.bfloat16),
            pltpu.VMEM((4 * NY, 6 * NY), jnp.bfloat16),
        ],
        compiler_params=params(),
        cost_estimate=LIGHT,
        name="finish",
    )(taps, rims[0], spread, rims[1], planar, ix_table, iy_table)


def gradient_kernel(depth, where, gathered, first, second, out):
    step = pl.program_id(0)
    samples, rows, lines = gathered.shape
    half = rows // 4
    lane = lax.broadcasted_iota(jnp.int32, (1, lines), 1)
    mine = lane % depth == step
    total = jnp.zeros(out.shape, jnp.float32)
    for s in range(samples):
        spectrum = jnp.where(mine, gathered[s, : 2 * half], 0)
        real = gathered[s, 2 * half : 3 * half]
        imag = gathered[s, 3 * half :]
        dual = jnp.concatenate(
            [jnp.where(where[0] == 0, real, imag), jnp.where(where[0] == 0, imag, -real)], axis=0
        )
        dual = jnp.where(mine, dual, 0)
        product = dot(spectrum, first[0]) * dot(dual, second[...])
        total = total + product[:half] + product[half:]
    out[...] = total * (1.0 / samples)


def weight_gradient(gathered, depth, width, index):
    samples, rows, lines = gathered.shape
    channels = lines // depth
    square = channels * channels
    cuts = square // width
    first = first_table(channels, depth).reshape(lines, cuts, width).transpose(1, 0, 2)
    second = second_table(channels, depth)[:, :width]
    first = constant(first)
    second = constant(second)
    where = jnp.stack([index // cuts, index % cuts]).astype(jnp.int32)
    half = rows // 4
    return pl.pallas_call(
        functools.partial(gradient_kernel, depth),
        grid_spec=pltpu.PrefetchScalarGridSpec(
            num_scalar_prefetch=1,
            grid=(depth,),
            in_specs=[
                pl.BlockSpec(gathered.shape, lambda j, w: (0, 0, 0)),
                pl.BlockSpec((1, lines, width), lambda j, w: (w[1], 0, 0)),
                pl.BlockSpec(second.shape, lambda j, w: (0, 0)),
            ],
            out_specs=pl.BlockSpec((half, width), lambda j, w: (j, 0)),
        ),
        out_shape=jax.ShapeDtypeStruct((depth * half, width), jnp.float32),
        compiler_params=params(),
        cost_estimate=LIGHT,
        name="weight_gradient",
    )(where, gathered, first, second)


def neighbours(first, last):
    size = lax.axis_size("slab")
    up = [(i, i + 1) for i in range(size - 1)]
    down = [(j, i) for i, j in up]
    return lax.ppermute(last, "slab", up), lax.ppermute(first, "slab", down)


def swap(planar):
    return lax.all_to_all(planar, "slab", split_axis=0, concat_axis=0)


def local_fast(feats, grains, spec_weight, taps, point_weight, bias, cotangent):
    slabs = lax.axis_size("slab")
    copies = lax.axis_size("dp")
    barrier = lax.optimization_barrier
    field = feats[0]
    channels = field.shape[0]
    cell_scale = 1.0 / math.sqrt(NX * NY * NZ)
    mode_scale = 1.0 / math.sqrt(KX * KY * KZ)
    mode_rows = spec_weight.shape[0]
    weight = spec_weight.reshape(mode_rows * KZ, 2 * channels * channels)
    width = weight.shape[1] // copies

    planar, first, last = forward_modes(field, slabs)
    rims = neighbours(first, last)
    spectrum, planar = mix(swap(planar), weight, cell_scale, 0.5 * mode_scale)
    planar, field = barrier((planar, field))
    planar = swap(planar)
    smooth = smooth_planes(field, taps)
    smooth = smooth_planes(field, taps, smooth, rims)
    planar, smooth = barrier((planar, smooth))
    spread, planar, first, last = layer(planar, smooth, cotangent[0], grains[0], bias, point_weight)
    rims = neighbours(first, last)
    planar, send = mix(swap(planar), weight, 0.5 * mode_scale, cell_scale, spectrum, copies)
    planar = swap(planar)
    gathered = lax.all_to_all(send, "dp", split_axis=0, concat_axis=0)
    grad_spec = weight_gradient(gathered, KX // slabs, width, lax.axis_index("dp"))
    planar, grad_spec = barrier((planar, grad_spec))
    grad_feats = finish(planar, spread, rims, taps)[None]
    return (grad_feats, grad_spec.reshape(mode_rows, KZ, width))


def local(feats, grains, spec_weight, taps, point_weight, bias, cotangent):
    samples, channels, planes = feats.shape[:3]
    width = spec_weight.shape[2] // lax.axis_size("dp")
    fits = (
        lax.axis_size("slab") * 4 == KX
        and samples == 1
        and channels == 32
        and planes == 8
        and channels * channels % width == 0
        and width % 128 == 0
    )
    form = local_fast if fits else local_any
    return form(feats, grains, spec_weight, taps, point_weight, bias, cotangent)


def solution(mesh):
    in_specs = (
        P(("grp", "dp"), None, "slab", None, None),
        P(("grp", "dp"), "slab", None, None),
        P("slab", None, None),
        P(),
        P(),
        P(),
        P(("grp", "dp"), None, "slab", None, None),
    )
    out_specs = (P(("grp", "dp"), None, "slab", None, None), P("slab", "grp", "dp"))
    return jax.shard_map(local, mesh=mesh, in_specs=in_specs, out_specs=out_specs, check_vma=False)
```

```python
import functools
import math

import jax
import jax.numpy as jnp
import ml_dtypes
import numpy as np
from jax import lax
from jax.experimental import pallas as pl
from jax.experimental.pallas import tpu as pltpu
from jax.sharding import PartitionSpec as P

NX = 128
NY = 128
NZ = 32
KX = 16
KY = 16
KZ = 16


HIGHEST = lax.Precision.HIGHEST


def extended(shard, sides, width):
    for axis, dim in sides:
        size, length = (lax.axis_size(axis), shard.shape[dim])
        up = [(i, (i + 1) % size) for i in range(size - 1)]
        down = [(j, i) for i, j in up]
        last = lax.slice_in_dim(shard, length - width, length, axis=dim)
        first = lax.slice_in_dim(shard, 0, width, axis=dim)
        before = lax.ppermute(last, axis, up)
        after = lax.ppermute(first, axis, down)
        shard = jnp.concatenate([before, shard, after], axis=dim)
    return shard


def tables(count, length, span):
    indices = jnp.arange(count, dtype=jnp.int32)
    frequency = jnp.where(indices < count // 2, indices, length - count + indices)
    position = jnp.arange(span, dtype=jnp.int32)
    phases = frequency[:, None] * position[None, :] % length
    angles = phases.astype(jnp.float32) * (2.0 * math.pi / length)
    return (jnp.cos(angles), jnp.sin(angles))


def mobility(grains):
    leading = [(0, 0)] * (grains.ndim - 2)
    along_x = (grains[..., 1:, :] != grains[..., :-1, :]).astype(jnp.float32)
    along_y = (grains[..., :, 1:] != grains[..., :, :-1]).astype(jnp.float32)
    differ = jnp.pad(along_x, leading + [(1, 0), (0, 0)]) + jnp.pad(
        along_x, leading + [(0, 1), (0, 0)]
    )
    differ = (
        differ
        + jnp.pad(along_y, leading + [(0, 0), (1, 0)])
        + jnp.pad(along_y, leading + [(0, 0), (0, 1)])
    )
    return 0.25 * (1.0 + differ)


def stencil(padded, taps, adjoint):
    planes = padded.shape[-3] - 2
    rows_x = padded.shape[-2] - 2
    rows_y = padded.shape[-1] - 2
    total = jnp.zeros(padded.shape[:-3] + (planes, rows_x, rows_y), jnp.float32)
    for offset in range(27):
        shift_z, shift_x, shift_y = (offset // 9, offset // 3 % 3, offset % 3)
        if adjoint:
            shift_z, shift_x, shift_y = (2 - shift_z, 2 - shift_x, 2 - shift_y)
        window = padded[
            ..., shift_z : shift_z + planes, shift_x : shift_x + rows_x, shift_y : shift_y + rows_y
        ]
        total = total + taps[offset][:, None, None, None] * window.astype(jnp.float32)
    return total


def plane_forward(field, cos_x, sin_x, cos_y, sin_y):
    real_y = jnp.einsum("...xy,ky->...xk", field, cos_y, precision=HIGHEST)
    imag_y = -jnp.einsum("...xy,ky->...xk", field, sin_y, precision=HIGHEST)
    real_part = jnp.einsum("...xk,jx->...jk", real_y, cos_x, precision=HIGHEST) + jnp.einsum(
        "...xk,jx->...jk", imag_y, sin_x, precision=HIGHEST
    )
    imag_part = jnp.einsum("...xk,jx->...jk", imag_y, cos_x, precision=HIGHEST) - jnp.einsum(
        "...xk,jx->...jk", real_y, sin_x, precision=HIGHEST
    )
    return (real_part, imag_part)


def plane_inverse(real_part, imag_part, cos_x, sin_x, cos_y, sin_y):
    real_x = jnp.einsum("...jk,jx->...xk", real_part, cos_x, precision=HIGHEST) - jnp.einsum(
        "...jk,jx->...xk", imag_part, sin_x, precision=HIGHEST
    )
    imag_x = jnp.einsum("...jk,jx->...xk", imag_part, cos_x, precision=HIGHEST) + jnp.einsum(
        "...jk,jx->...xk", real_part, sin_x, precision=HIGHEST
    )
    return jnp.einsum("...xk,ky->...xy", real_x, cos_y, precision=HIGHEST) - jnp.einsum(
        "...xk,ky->...xy", imag_x, sin_y, precision=HIGHEST
    )


def depth_forward(packed, cos_table, sin_table):
    width = packed.shape[-1] // 2
    real_in = packed[..., :width]
    imag_in = packed[..., width:]
    real_out = jnp.einsum("pszc,kz->pskc", real_in, cos_table, precision=HIGHEST) + jnp.einsum(
        "pszc,kz->pskc", imag_in, sin_table, precision=HIGHEST
    )
    imag_out = jnp.einsum("pszc,kz->pskc", imag_in, cos_table, precision=HIGHEST) - jnp.einsum(
        "pszc,kz->pskc", real_in, sin_table, precision=HIGHEST
    )
    return jnp.concatenate([real_out, imag_out], axis=-1)


def depth_inverse(real_modes, imag_modes, cos_table, sin_table):
    real_out = jnp.einsum("pskc,kz->pszc", real_modes, cos_table, precision=HIGHEST) - jnp.einsum(
        "pskc,kz->pszc", imag_modes, sin_table, precision=HIGHEST
    )
    imag_out = jnp.einsum("pskc,kz->pszc", imag_modes, cos_table, precision=HIGHEST) + jnp.einsum(
        "pskc,kz->pszc", real_modes, sin_table, precision=HIGHEST
    )
    return jnp.concatenate([real_out, imag_out], axis=-1)


def rim_planes(field):
    return extended(field, (("slab", 2),), 1)


def local_any(feats, grains, spec_weight, taps, point_weight, bias, cotangent):
    samples_here = feats.shape[0]
    channels = feats.shape[1]
    planes = feats.shape[2]
    cos_x, sin_x = tables(KX, NX, NX)
    cos_y, sin_y = tables(KY, NY, NY)
    cos_full, sin_full = tables(KZ, NZ, NZ)
    cell_scale = math.sqrt(NX * NY * NZ)
    mode_scale = math.sqrt(KX * KY * KZ)
    mode_rows = spec_weight.shape[0]
    weights = spec_weight.astype(jnp.float32).reshape(mode_rows, KZ, 2, channels, channels)
    w_real = weights[:, :, 0]
    w_imag = weights[:, :, 1]
    moving = mobility(grains)[:, None]

    def to_modes(field):
        real_plane, imag_plane = plane_forward(field, cos_x, sin_x, cos_y, sin_y)
        packed = jnp.stack([real_plane, imag_plane], axis=1)
        packed = packed.transpose(4, 5, 0, 3, 1, 2).reshape(
            KX * KY, samples_here, planes, 2 * channels
        )
        moved = lax.all_to_all(packed, "slab", split_axis=0, concat_axis=2, tiled=True)
        summed = depth_forward(moved, cos_full, sin_full)
        return (summed[..., :channels], summed[..., channels:])

    def from_modes(real_modes, imag_modes):
        planar = depth_inverse(real_modes, imag_modes, cos_full, sin_full)
        packed = lax.all_to_all(planar, "slab", split_axis=2, concat_axis=0, tiled=True)
        grouped = packed.reshape(KX, KY, samples_here, planes, 2, channels).transpose(
            2, 4, 5, 3, 0, 1
        )
        return plane_inverse(grouped[:, 0], grouped[:, 1], cos_x, sin_x, cos_y, sin_y)

    zero_rim = ((0, 0), (0, 0), (0, 0), (1, 1), (1, 1))
    padded = jnp.pad(rim_planes(feats), zero_rim)
    smooth = stencil(padded, taps, False).astype(jnp.bfloat16)
    local_part = moving * jnp.einsum(
        "sczxy,co->sozxy", smooth, point_weight, preferred_element_type=jnp.float32
    )
    spec_real, spec_imag = to_modes(feats.astype(jnp.float32))
    spec_real = spec_real / cell_scale
    spec_imag = spec_imag / cell_scale
    mixed_real = jnp.einsum("pskc,pkco->psko", spec_real, w_real, precision=HIGHEST) - jnp.einsum(
        "pskc,pkco->psko", spec_imag, w_imag, precision=HIGHEST
    )
    mixed_imag = jnp.einsum("pskc,pkco->psko", spec_real, w_imag, precision=HIGHEST) + jnp.einsum(
        "pskc,pkco->psko", spec_imag, w_real, precision=HIGHEST
    )
    spectral = from_modes(mixed_real, mixed_imag) / mode_scale
    pre = spectral + local_part + bias[None, :, None, None, None]
    gate = jax.nn.sigmoid(pre)
    delta = (cotangent.astype(jnp.float32) * gate * (1.0 + pre * (1.0 - gate))).astype(jnp.bfloat16)
    dual_real, dual_imag = to_modes(delta.astype(jnp.float32))
    dual_real = dual_real / mode_scale
    dual_imag = dual_imag / mode_scale
    batch_total = samples_here * lax.axis_size("dp")
    grad_real = jnp.einsum("pskc,psko->pkco", spec_real, dual_real, precision=HIGHEST) + jnp.einsum(
        "pskc,psko->pkco", spec_imag, dual_imag, precision=HIGHEST
    )
    grad_imag = jnp.einsum("pskc,psko->pkco", spec_real, dual_imag, precision=HIGHEST) - jnp.einsum(
        "pskc,psko->pkco", spec_imag, dual_real, precision=HIGHEST
    )
    grad_terms = (jnp.stack([grad_real, grad_imag], axis=2) / batch_total).reshape(
        mode_rows, KZ, 2 * channels * channels
    )
    grad_spec = lax.psum_scatter(
        grad_terms.astype(jnp.bfloat16), "dp", scatter_dimension=2, tiled=True
    ).astype(jnp.float32)
    back_real = jnp.einsum("psko,pkco->pskc", dual_real, w_real, precision=HIGHEST) + jnp.einsum(
        "psko,pkco->pskc", dual_imag, w_imag, precision=HIGHEST
    )
    back_imag = jnp.einsum("psko,pkco->pskc", dual_imag, w_real, precision=HIGHEST) - jnp.einsum(
        "psko,pkco->pskc", dual_real, w_imag, precision=HIGHEST
    )
    spectral_back = from_modes(back_real, back_imag) / cell_scale
    spread = (
        moving
        * jnp.einsum("sozxy,co->sczxy", delta, point_weight, preferred_element_type=jnp.float32)
    ).astype(jnp.bfloat16)
    spread_padded = jnp.pad(rim_planes(spread), zero_rim)
    local_back = stencil(spread_padded, taps, True)
    grad_feats = (spectral_back + local_back).astype(jnp.bfloat16)
    return (grad_feats, grad_spec)


def frequencies(count, length):
    index = np.arange(count)
    return np.where(index < count // 2, index, length - count + index)


def angles(count, length):
    phases = np.outer(frequencies(count, length), np.arange(length)) % length
    return phases * (2.0 * np.pi / length)


def constant(array):
    return jnp.asarray(np.asarray(array, np.float32).astype(ml_dtypes.bfloat16))


def forward_x_table(slabs, split):
    a = angles(KX, NX).reshape(slabs, KX // slabs, NX)
    trig = np.stack([np.cos(a), np.sin(a)])
    table = np.einsum("tsjx,cd->tscjdx", trig, np.eye(2)).reshape(-1, 2, NX // 8, 8)
    if split:
        table = table.transpose(0, 2, 1, 3)
    return table.reshape(4 * KX, 2 * NX)


def forward_y_table(planes):
    a = angles(KY, NY)
    cos, sin = np.cos(a).T, np.sin(a).T
    block = np.stack([np.stack([cos, -sin], 1), np.stack([-sin, -cos], 1)])
    pick = np.eye(planes).reshape(planes // 2, 2, planes)
    table = np.einsum("pqz,tyrk->ptqyzrk", pick, block)
    return table.reshape(planes * 2 * NY, planes * 2 * KY)


def forward_z_table():
    a = angles(KZ, NZ)
    cos, sin = np.cos(a).T, np.sin(a).T
    block = np.stack([np.stack([cos, -sin], 1), np.stack([sin, cos], 1)], 1)
    table = np.einsum("zrqm,kl->zrkqlm", block, np.eye(KY))
    return table.reshape(NZ * 2 * KY, 2 * KY * KZ)


def inverse_z_table():
    a = angles(KZ, NZ)
    cos, sin = np.cos(a), np.sin(a)
    block = np.stack([np.stack([cos, sin], 2), np.stack([-sin, cos], 2)])
    table = np.einsum("rmzq,kl->rkmzql", block, np.eye(KY))
    return table.reshape(2 * KY * KZ, NZ * 2 * KY)


def inverse_y_table(planes, group):
    a = angles(KY, NY)
    cos, sin = np.cos(a), np.sin(a)
    block = np.stack([np.stack([cos, -sin], 1), np.stack([-sin, -cos], 1)])
    pick = np.eye(planes).reshape(planes // group, group, planes)
    table = np.einsum("pqz,rkty->pzrktqy", pick, block)
    return table.reshape(planes // group, planes * 2 * KY, 2 * group * NY)


def inverse_x_table(slabs, group):
    a = angles(KX, NX).reshape(slabs, KX // slabs, NX)
    trig = np.stack([np.cos(a), np.sin(a)])
    table = np.einsum("tsjx,cd->cxstdj", trig, np.eye(group))
    return table.reshape(group * NX, 2 * KX * group)


def first_table(channels, depth):
    table = np.einsum("ac,j,b->ajcb", np.eye(channels), np.ones(depth), np.ones(channels))
    return table.reshape(channels * depth, channels * channels)


def second_table(channels, depth):
    table = np.einsum("ac,j,b->ajbc", np.eye(channels), np.ones(depth), np.ones(channels))
    return table.reshape(channels * depth, channels * channels)


LIGHT = pl.CostEstimate(flops=10**7, bytes_accessed=10**5, transcendentals=0)
HEAVY = pl.CostEstimate(flops=10**11, bytes_accessed=10**8, transcendentals=0)


def dot(a, b):
    return jnp.dot(a, b, preferred_element_type=jnp.float32)


def whole(shape):
    return pl.BlockSpec(shape, lambda *_: (0,) * len(shape))


def params(**kw):
    return pltpu.CompilerParams(vmem_limit_bytes=58 * 2**20, **kw)


def store_rows(rows, at, parts):
    for p, part in parts:
        for t in range(2):
            for s in range(rows.shape[2]):
                here = slice(8 * (t * rows.shape[2] + s), 8 * (t * rows.shape[2] + s) + 8)
                both = jnp.concatenate([part[0][here], part[1][here]], axis=0)
                rows[p, t, s, pl.ds(at, 16), :] = both.astype(jnp.bfloat16)


def store_modes(rows, y_table, out):
    pairs, _, slabs, lines, _ = rows.shape
    left = [
        jnp.concatenate([rows[p, t, s] for p in range(pairs) for t in range(2)], axis=1)
        for s in range(slabs)
    ]
    modes = dot(jnp.concatenate(left, axis=0), y_table[...])
    for s in range(slabs):
        out[s] = modes[s * lines : (s + 1) * lines].astype(jnp.bfloat16)


def forward_kernel(field, x_table, y_table, out, first, last, rows):
    step = pl.program_id(0)
    planes = field.shape[1]
    first[:, 0] = field[:, 0]
    last[:, 0] = field[:, planes - 1]
    products = []
    for i in range(2):
        sheets = [field[2 * i : 2 * i + 2, z].reshape(2 * NX, NY) for z in range(planes)]
        products.append(dot(x_table[...], jnp.concatenate(sheets, axis=1)))
    parts = [
        (p, [product[:, 2 * NY * p : 2 * NY * (p + 1)] for product in products])
        for p in range(planes // 2)
    ]
    store_rows(rows, pl.multiple_of(16 * step, 16), parts)

    @pl.when(step == pl.num_programs(0) - 1)
    def _():
        store_modes(rows, y_table, out)


def forward_modes(field, slabs):
    channels, planes = field.shape[:2]
    lines = channels * (KX // slabs)
    x_table = constant(forward_x_table(slabs, False))
    y_table = constant(forward_y_table(planes))
    shape = (slabs, lines, planes * 2 * KY)
    rim = pl.BlockSpec((4, 1, NX, NY), lambda c: (c, 0, 0, 0))
    rims = jax.ShapeDtypeStruct((channels, 1, NX, NY), jnp.bfloat16)
    return pl.pallas_call(
        forward_kernel,
        grid=(channels // 4,),
        in_specs=[
            pl.BlockSpec((4, planes, NX, NY), lambda c: (c, 0, 0, 0)),
            whole(x_table.shape),
            whole(y_table.shape),
        ],
        out_specs=[whole(shape), rim, rim],
        out_shape=[jax.ShapeDtypeStruct(shape, jnp.bfloat16), rims, rims],
        scratch_shapes=[pltpu.VMEM((planes // 2, 2, slabs, lines, 2 * NY), jnp.bfloat16)],
        compiler_params=params(),
        cost_estimate=LIGHT,
        name="forward_modes",
    )(field, x_table, y_table)


def mixing_kernel(scale_in, scale_out, adjoint, planar, weight, z_in, z_out, spread_table,
                  sum_table, *rest):
    if adjoint:
        partner, out, send, spectrum, total, wide, product = rest
    else:
        spectrum, out, total, wide, product = rest
    step = pl.program_id(0)
    steps = pl.num_programs(0)
    slabs = planar.shape[0]
    width = planar.shape[2]
    half = spectrum.shape[0] // 2
    lanes = weight.shape[1] // 2

    @pl.when(step == 0)
    def _():
        left = jnp.concatenate([planar[s] for s in range(slabs)], axis=1)
        modes = (dot(left, z_in[...]).T * scale_in).astype(jnp.bfloat16)
        spectrum[...] = modes
        total[...] = jnp.zeros_like(total)
        if adjoint:
            for d in range(send.shape[0]):
                send[d, : 2 * half] = partner[...]
                send[d, 2 * half :] = modes

    lane = lax.broadcasted_iota(jnp.int32, (1, spectrum.shape[1]), 1)
    mine = lane % steps == step
    wide[...] = dot(jnp.where(mine, spectrum[...], 0), spread_table[...])
    block = 32
    for at in range(0, half, block):
        real_wide = wide[at : at + block]
        imag_wide = wide[half + at : half + at + block]
        w_real = weight[at : at + block, :lanes].astype(jnp.float32)
        w_imag = weight[at : at + block, lanes:].astype(jnp.float32)
        if adjoint:
            real = real_wide * w_real + imag_wide * w_imag
            imag = imag_wide * w_real - real_wide * w_imag
        else:
            real = real_wide * w_real - imag_wide * w_imag
            imag = real_wide * w_imag + imag_wide * w_real
        product[at : at + block] = real.astype(jnp.bfloat16)
        product[half + at : half + at + block] = imag.astype(jnp.bfloat16)
    total[...] += jnp.where(mine, dot(product[...], sum_table[...]), 0.0)

    @pl.when(step == steps - 1)
    def _():
        modes = dot((total[...] * scale_out).T.astype(jnp.bfloat16), z_out[...])
        for s in range(slabs):
            out[s] = modes[:, s * width : (s + 1) * width].astype(jnp.bfloat16)


def mix(planar, weight, scale_in, scale_out, partner=None, copies=0):
    slabs, lines, width = planar.shape
    adjoint = partner is not None
    depth = KX // slabs
    channels = lines // depth
    rows = KY * KZ
    z_in = constant(forward_z_table())
    z_out = constant(inverse_z_table())
    first = first_table(channels, depth)
    second = second_table(channels, depth)
    spread_table = constant(second if adjoint else first)
    sum_table = constant((first if adjoint else second).T)
    shape = (2 * rows, lines)
    in_specs = [
        whole(planar.shape),
        pl.BlockSpec((rows, weight.shape[1]), lambda j: (j, 0)),
        whole(z_in.shape),
        whole(z_out.shape),
        whole(spread_table.shape),
        whole(sum_table.shape),
    ]
    operands = [planar, weight, z_in, z_out, spread_table, sum_table]
    scratch = [
        pltpu.VMEM(shape, jnp.float32),
        pltpu.VMEM((2 * rows, channels * channels), jnp.float32),
        pltpu.VMEM((2 * rows, channels * channels), jnp.bfloat16),
    ]
    if adjoint:
        in_specs.append(whole(shape))
        operands.append(partner)
        scratch = [pltpu.VMEM(shape, jnp.bfloat16)] + scratch
        outs = [planar.shape, (copies, 2 * shape[0], lines)]
    else:
        outs = [shape, planar.shape]
    return pl.pallas_call(
        functools.partial(mixing_kernel, scale_in, scale_out, adjoint),
        grid=(depth,),
        in_specs=in_specs,
        out_specs=[whole(out) for out in outs],
        out_shape=[jax.ShapeDtypeStruct(out, jnp.bfloat16) for out in outs],
        scratch_shapes=scratch,
        compiler_params=params(),
        cost_estimate=HEAVY,
        name="mix_back" if adjoint else "mix",
    )(*operands)


def plane_mobility(grains):
    same = [
        jnp.concatenate([grains[:1], grains[:-1]], axis=0),
        jnp.concatenate([grains[1:], grains[-1:]], axis=0),
        jnp.concatenate([grains[:, :1], grains[:, :-1]], axis=1),
        jnp.concatenate([grains[:, 1:], grains[:, -1:]], axis=1),
    ]
    total = jnp.full(grains.shape, 0.25, jnp.float32)
    for other in same:
        total = total + jnp.where(grains != other, 0.25, 0.0)
    return total


def layer_kernel(bias, planar, smooth, cotangent, grains, point_weight, repeat, ix_table, iy_table,
                 x_table, y_table, spread, out, first, last, waves, spectral, moving, delta,
                 rows, bias_wide, mix_out, mix_in):
    pair = pl.program_id(0)
    pairs = rows.shape[0]
    channels = cotangent.shape[0]
    slabs = planar.shape[0]

    @pl.when(pair == 0)
    def _():
        for c in range(channels):
            bias_wide[c] = jnp.full(bias_wide.shape[1:], 0.5 * bias[c], jnp.float32)
        tall = dot(repeat[...], point_weight[...]).astype(jnp.bfloat16)
        square = lax.dot_general(
            tall, repeat[...], (((1,), (1,)), ((), ())), preferred_element_type=jnp.float32
        )
        row = lax.broadcasted_iota(jnp.int32, square.shape, 0) % 8
        column = lax.broadcasted_iota(jnp.int32, square.shape, 1) % 8
        square = jnp.where(row == column, square, 0.0)
        mix_in[...] = square.astype(jnp.bfloat16)
        mix_out[...] = square.T.astype(jnp.bfloat16)

    lines = planar.shape[1]
    step = jnp.concatenate([planar[s] for s in range(slabs)], axis=0)
    step = dot(step, iy_table[0]).astype(jnp.bfloat16)
    for s in range(slabs):
        for t in range(2):
            waves[s, t] = step[s * lines : (s + 1) * lines, 2 * NY * t : 2 * NY * (t + 1)]
    group = 8 * (KX // slabs)
    right = []
    for g in range(channels // 8):
        here = slice(g * group, (g + 1) * group)
        wave = [waves[s, t, here, :] for s in range(slabs) for t in range(2)]
        right.append(jnp.concatenate(wave, axis=0))
    step = dot(ix_table[...], jnp.concatenate(right, axis=1))
    for g in range(channels // 8):
        here = step[:, 2 * NY * g : 2 * NY * (g + 1)]
        spectral[8 * g : 8 * g + 8] = here.reshape(8, NX, 2 * NY)
    for q in range(2):
        moving[:, q * NY : (q + 1) * NY] = 0.5 * plane_mobility(grains[q])

    def body(i, _):
        x = pl.multiple_of(16 * i, 16)
        halves = [cotangent[:, q, pl.ds(x, 16), :] for q in range(2)]
        cotangent_here = jnp.concatenate(halves, axis=2).astype(jnp.float32)
        rights = []
        mobiles = []
        right = jnp.concatenate([smooth[0, 2 * i + h] for h in range(2)], axis=1)
        local = dot(mix_out[...], right).reshape(channels, 8, 4 * NY)
        for h in range(2):
            at = pl.ds(pl.multiple_of(x + 8 * h, 8), 8)
            mobile = moving[at, :][None]
            local_here = local[:, :, 2 * NY * h : 2 * NY * (h + 1)]
            half = spectral[:, at, :] + mobile * local_here + bias_wide[...]
            wave = jnp.tanh(half)
            slope = (1.0 + wave) * (1.0 + (half - half * wave))
            change = cotangent_here[:, 8 * h : 8 * h + 8, :] * slope
            right = change.reshape(8 * channels, 2 * NY).astype(jnp.bfloat16)
            delta[2 * i + h] = right
            rights.append(right)
            mobiles.append(mobile)
        back = dot(mix_in[...], jnp.concatenate(rights, axis=1)).reshape(channels, 8, 4 * NY)
        spreads = [mobiles[h] * back[:, :, 2 * NY * h : 2 * NY * (h + 1)] for h in range(2)]
        both = jnp.concatenate(spreads, axis=1).astype(jnp.bfloat16)
        for q in range(2):
            spread[:, q, pl.ds(x, 16), :] = both[:, :, q * NY : (q + 1) * NY]
        return 0

    lax.fori_loop(0, NX // 16, body, 0, unroll=4)

    for step in range(channels // 8):
        right = [
            delta[:, 16 * i : 16 * i + 16, :].reshape(2 * NX, 2 * NY)
            for i in range(4 * step, 4 * step + 4)
        ]
        product = dot(x_table[...], jnp.concatenate(right, axis=1))
        parts = [product[:, 2 * NY * i : 2 * NY * (i + 1)] for i in range(4)]
        for i in range(2):
            store_rows(rows, 32 * step + 16 * i, [(pair, parts[2 * i : 2 * i + 2])])

    @pl.when(pair == 0)
    def _():
        first[:, 0] = spread[:, 0]

    @pl.when(pair == pairs - 1)
    def _():
        last[:, 0] = spread[:, 1]
        store_modes(rows, y_table, out)


def layer(planar, smooth, cotangent, grains, bias, point_weight):
    slabs, lines, width = planar.shape
    channels, planes = cotangent.shape[:2]
    pairs = planes // 2
    repeat = constant(np.repeat(np.eye(channels), 8, axis=0))
    ix_table = constant(inverse_x_table(slabs, 8))
    iy_table = constant(inverse_y_table(planes, 2))
    x_table = constant(forward_x_table(slabs, True))
    y_table = constant(forward_y_table(planes))
    field = pl.BlockSpec((channels, 2, NX, NY), lambda p: (0, p, 0, 0))
    rim = (channels, 1, NX, NY)
    outs = [cotangent.shape, planar.shape, rim, rim]
    return pl.pallas_call(
        layer_kernel,
        grid=(pairs,),
        in_specs=[
            pl.BlockSpec(memory_space=pltpu.SMEM),
            whole(planar.shape),
            pl.BlockSpec((1,) + smooth.shape[1:], lambda p: (p, 0, 0, 0)),
            field,
            pl.BlockSpec((2, NX, NY), lambda p: (p, 0, 0)),
            whole(point_weight.shape),
            whole(repeat.shape),
            whole(ix_table.shape),
            pl.BlockSpec((1,) + iy_table.shape[1:], lambda p: (p, 0, 0)),
            whole(x_table.shape),
            whole(y_table.shape),
        ],
        out_specs=[field, whole(planar.shape), whole(rim), whole(rim)],
        out_shape=[jax.ShapeDtypeStruct(out, jnp.bfloat16) for out in outs],
        scratch_shapes=[
            pltpu.VMEM((slabs, 2, lines, 2 * NY), jnp.bfloat16),
            pltpu.VMEM((channels, NX, 2 * NY), jnp.float32),
            pltpu.VMEM((NX, 2 * NY), jnp.float32),
            pltpu.VMEM((NX // 8, 8 * channels, 2 * NY), jnp.bfloat16),
            pltpu.VMEM((pairs, 2, slabs, lines, 2 * NY), jnp.bfloat16),
            pltpu.VMEM((channels, 8, 2 * NY), jnp.float32),
            pltpu.VMEM((8 * channels, 8 * channels), jnp.bfloat16),
            pltpu.VMEM((8 * channels, 8 * channels), jnp.bfloat16),
        ],
        compiler_params=params(),
        cost_estimate=LIGHT,
        name="layer",
    )(bias, planar, smooth, cotangent, grains, point_weight, repeat, ix_table, iy_table, x_table,
      y_table)


def build_band(adjoint, taps, channel, band):
    row = lax.broadcasted_iota(jnp.int32, (8, NY), 0)
    lane = lax.broadcasted_iota(jnp.int32, (8, NY), 1)
    offset = row - lane
    for dz in range(3):
        for dx in range(3):
            tile = jnp.zeros((8, NY), jnp.float32)
            for dy in range(3):
                number = 9 * dz + 3 * dx + dy
                tap = taps[26 - number if adjoint else number, channel]
                hit = (offset == dy - 1) | (offset == dy - 1 - NY)
                tile = jnp.where(hit, tap, tile)
            tiles = [pltpu.roll(tile, 8 * k, axis=1) if k > 0 else tile for k in range(NY // 8)]
            tiles[0] = jnp.where((row == 0) & (lane == NY - 1), 0.0, tiles[0])
            tiles[-1] = jnp.where((row == 7) & (lane == 0), 0.0, tiles[-1])
            block = jnp.concatenate(tiles, axis=0).astype(jnp.bfloat16)
            for q in range(2):
                down = (q + dz) * NY
                right = (2 * dx + q) * NY
                band[down : down + NY, right : right + NY] = block


def apply_band(quads, band):
    left = jnp.concatenate([jnp.concatenate(quad, axis=1) for quad in quads], axis=0)
    wide = dot(left, band[...])
    lower, middle, upper = (wide[:, 2 * NY * dx : 2 * NY * (dx + 1)] for dx in range(3))
    row = lax.broadcasted_iota(jnp.int32, (8, 2 * NY), 0)
    totals = []
    for p in range(len(quads)):
        here = slice(p * NX, (p + 1) * NX)
        down = pltpu.roll(lower[here], 1, axis=0)
        up = pltpu.roll(upper[here], NX - 1, axis=0)
        down = jnp.concatenate([jnp.where(row == 0, 0.0, down[:8]), down[8:]], axis=0)
        up = jnp.concatenate([up[:-8], jnp.where(row == 7, 0.0, up[-8:])], axis=0)
        totals.append(middle[here] + down + up)
    return totals


def banded(adjoint, taps, even, odd, channels):
    step = pl.program_id(0)
    final = channels * pl.num_programs(0) - 1
    bands = (even, odd)

    @pl.when(step == 0)
    def _():
        even[...] = jnp.zeros_like(even)
        odd[...] = jnp.zeros_like(odd)
        build_band(adjoint, taps, 0, even)

    def run(visit):
        for c in range(channels):
            following = jnp.minimum(channels * step + c + 1, final)
            build_band(adjoint, taps, following, bands[(c + 1) % 2])
            visit(c, bands[c % 2])

    return run


def smooth_kernel(taps, before, field, after, out, even, odd):
    planes = field.shape[1]
    totals = []

    def visit(c, band):
        sheets = [before[c, 0]] + [field[c, z] for z in range(planes)] + [after[c, 0]]
        totals.append(apply_band([sheets[z : z + 4] for z in range(0, planes, 2)], band))

    banded(False, taps, even, odd, 2)(visit)
    for p in range(planes // 2):
        both = [totals[c][p].reshape(NX // 8, 8, 2 * NY) for c in range(2)]
        out[p] = jnp.concatenate(both, axis=1).astype(jnp.bfloat16)


def smooth_planes(field, rims, taps):
    channels, planes = field.shape[:2]
    pairs = planes // 2
    rim = pl.BlockSpec((2, 1, NX, NY), lambda c: (c, 0, 0, 0))
    return pl.pallas_call(
        smooth_kernel,
        grid=(channels // 2,),
        in_specs=[
            pl.BlockSpec(memory_space=pltpu.SMEM),
            rim,
            pl.BlockSpec((2, planes, NX, NY), lambda c: (c, 0, 0, 0)),
            rim,
        ],
        out_specs=pl.BlockSpec((pairs, NX // 8, 16, 2 * NY), lambda c: (0, 0, c, 0)),
        out_shape=jax.ShapeDtypeStruct((pairs, NX // 8, 8 * channels, 2 * NY), jnp.bfloat16),
        scratch_shapes=[pltpu.VMEM((4 * NY, 6 * NY), jnp.bfloat16) for _ in range(2)],
        compiler_params=params(),
        cost_estimate=LIGHT,
        name="smooth",
    )(taps, rims[0], field, rims[1])


def finish_kernel(taps, before, field, after, planar, ix_table, iy_table, out, waves, spectral,
                  even, odd):
    step = pl.program_id(0)
    slabs = planar.shape[0]
    planes = field.shape[1]
    span = planes * NY

    @pl.when(step == 0)
    def _():
        lines = planar.shape[1]
        left = jnp.concatenate([planar[s] for s in range(slabs)], axis=0)
        for t in range(2):
            wave = dot(left, iy_table[0, :, t * span : (t + 1) * span]).astype(jnp.bfloat16)
            for s in range(slabs):
                waves[s, t] = wave[s * lines : (s + 1) * lines]

    rows = 4 * (KX // slabs)
    here = pl.ds(pl.multiple_of(rows * step, rows), rows)
    right = [waves[s, t, here, :] for s in range(slabs) for t in range(2)]
    spectral[...] = dot(ix_table[...], jnp.concatenate(right, axis=0))

    def visit(c, band):
        sheets = [before[c, 0]] + [field[c, z] for z in range(planes)] + [after[c, 0]]
        totals = apply_band([sheets[z : z + 4] for z in range(0, planes, 2)], band)
        for p in range(planes // 2):
            wide = slice(2 * p * NY, 2 * (p + 1) * NY)
            total = (totals[p] + spectral[c * NX : (c + 1) * NX, wide]).astype(jnp.bfloat16)
            out[c, 2 * p] = total[:, :NY]
            out[c, 2 * p + 1] = total[:, NY:]

    banded(True, taps, even, odd, 4)(visit)


def finish(planar, spread, rims, taps):
    slabs, lines, width = planar.shape
    channels, planes = spread.shape[:2]
    ix_table = constant(inverse_x_table(slabs, 4))
    iy_table = constant(inverse_y_table(planes, planes))
    rim = pl.BlockSpec((4, 1, NX, NY), lambda c: (c, 0, 0, 0))
    sheets = pl.BlockSpec((4, planes, NX, NY), lambda c: (c, 0, 0, 0))
    return pl.pallas_call(
        finish_kernel,
        grid=(channels // 4,),
        in_specs=[
            pl.BlockSpec(memory_space=pltpu.SMEM),
            rim,
            sheets,
            rim,
            whole(planar.shape),
            whole(ix_table.shape),
            whole(iy_table.shape),
        ],
        out_specs=sheets,
        out_shape=jax.ShapeDtypeStruct(spread.shape, jnp.bfloat16),
        scratch_shapes=[
            pltpu.VMEM((slabs, 2, lines, planes * NY), jnp.bfloat16),
            pltpu.VMEM((4 * NX, planes * NY), jnp.float32),
            pltpu.VMEM((4 * NY, 6 * NY), jnp.bfloat16),
            pltpu.VMEM((4 * NY, 6 * NY), jnp.bfloat16),
        ],
        compiler_params=params(),
        cost_estimate=HEAVY,
        name="finish",
    )(taps, rims[0], spread, rims[1], planar, ix_table, iy_table)


def gradient_kernel(depth, where, gathered, first, second, out):
    step = pl.program_id(0)
    samples, rows, lines = gathered.shape
    half = rows // 4
    lane = lax.broadcasted_iota(jnp.int32, (1, lines), 1)
    mine = lane % depth == step
    total = jnp.zeros(out.shape, jnp.float32)
    for s in range(samples):
        spectrum = jnp.where(mine, gathered[s, : 2 * half], 0)
        real = gathered[s, 2 * half : 3 * half]
        imag = gathered[s, 3 * half :]
        dual = jnp.concatenate(
            [jnp.where(where[0] == 0, real, imag), jnp.where(where[0] == 0, imag, -real)], axis=0
        )
        dual = jnp.where(mine, dual, 0)
        product = dot(spectrum, first[0]) * dot(dual, second[...])
        total = total + product[:half] + product[half:]
    out[...] = total * (1.0 / samples)


def weight_gradient(gathered, depth, width, index):
    samples, rows, lines = gathered.shape
    channels = lines // depth
    square = channels * channels
    cuts = square // width
    first = first_table(channels, depth).reshape(lines, cuts, width).transpose(1, 0, 2)
    second = second_table(channels, depth)[:, :width]
    first = constant(first)
    second = constant(second)
    where = jnp.stack([index // cuts, index % cuts]).astype(jnp.int32)
    half = rows // 4
    return pl.pallas_call(
        functools.partial(gradient_kernel, depth),
        grid_spec=pltpu.PrefetchScalarGridSpec(
            num_scalar_prefetch=1,
            grid=(depth,),
            in_specs=[
                pl.BlockSpec(gathered.shape, lambda j, w: (0, 0, 0)),
                pl.BlockSpec((1, lines, width), lambda j, w: (w[1], 0, 0)),
                pl.BlockSpec(second.shape, lambda j, w: (0, 0)),
            ],
            out_specs=pl.BlockSpec((half, width), lambda j, w: (j, 0)),
        ),
        out_shape=jax.ShapeDtypeStruct((depth * half, width), jnp.float32),
        compiler_params=params(),
        cost_estimate=LIGHT,
        name="weight_gradient",
    )(where, gathered, first, second)


def neighbours(first, last):
    size = lax.axis_size("slab")
    up = [(i, i + 1) for i in range(size - 1)]
    down = [(j, i) for i, j in up]
    return lax.ppermute(last, "slab", up), lax.ppermute(first, "slab", down)


def swap(planar):
    return lax.all_to_all(planar, "slab", split_axis=0, concat_axis=0)


def local_fast(feats, grains, spec_weight, taps, point_weight, bias, cotangent):
    slabs = lax.axis_size("slab")
    copies = lax.axis_size("dp")
    barrier = lax.optimization_barrier
    field = feats[0]
    channels = field.shape[0]
    cell_scale = 1.0 / math.sqrt(NX * NY * NZ)
    mode_scale = 1.0 / math.sqrt(KX * KY * KZ)
    mode_rows = spec_weight.shape[0]
    weight = spec_weight.reshape(mode_rows * KZ, 2 * channels * channels)
    width = weight.shape[1] // copies

    planar, first, last = forward_modes(field, slabs)
    planar, first, last = barrier((swap(planar), first, last))
    rims = neighbours(first, last)
    spectrum, planar = mix(planar, weight, cell_scale, 0.5 * mode_scale)
    planar = swap(planar)
    smooth = smooth_planes(field, rims, taps)
    spread, planar, first, last = layer(planar, smooth, cotangent[0], grains[0], bias, point_weight)
    rims = neighbours(first, last)
    planar, send = mix(swap(planar), weight, 0.5 * mode_scale, cell_scale, spectrum, copies)
    planar = swap(planar)
    gathered = lax.all_to_all(send, "dp", split_axis=0, concat_axis=0)
    grad_feats = finish(planar, spread, rims, taps)
    grad_feats, gathered = barrier((grad_feats, gathered))
    grad_feats = grad_feats[None]
    grad_spec = weight_gradient(gathered, KX // slabs, width, lax.axis_index("dp"))
    return (grad_feats, grad_spec.reshape(mode_rows, KZ, width))


def local(feats, grains, spec_weight, taps, point_weight, bias, cotangent):
    samples, channels, planes = feats.shape[:3]
    width = spec_weight.shape[2] // lax.axis_size("dp")
    fits = (
        lax.axis_size("slab") * 4 == KX
        and samples == 1
        and channels == 32
        and planes == 8
        and channels * channels % width == 0
        and width % 128 == 0
    )
    form = local_fast if fits else local_any
    return form(feats, grains, spec_weight, taps, point_weight, bias, cotangent)


def solution(mesh):
    in_specs = (
        P(("grp", "dp"), None, "slab", None, None),
        P(("grp", "dp"), "slab", None, None),
        P("slab", None, None),
        P(),
        P(),
        P(),
        P(("grp", "dp"), None, "slab", None, None),
    )
    out_specs = (P(("grp", "dp"), None, "slab", None, None), P("slab", "grp", "dp"))
    return jax.shard_map(local, mesh=mesh, in_specs=in_specs, out_specs=out_specs, check_vma=False)
```

```python
import functools
import math

import jax
import jax.numpy as jnp
import ml_dtypes
import numpy as np
from jax import lax
from jax.experimental import pallas as pl
from jax.experimental.pallas import tpu as pltpu
from jax.sharding import PartitionSpec as P

NX = 128
NY = 128
NZ = 32
KX = 16
KY = 16
KZ = 16


HIGHEST = lax.Precision.HIGHEST


def extended(shard, sides, width):
    for axis, dim in sides:
        size, length = (lax.axis_size(axis), shard.shape[dim])
        up = [(i, (i + 1) % size) for i in range(size - 1)]
        down = [(j, i) for i, j in up]
        last = lax.slice_in_dim(shard, length - width, length, axis=dim)
        first = lax.slice_in_dim(shard, 0, width, axis=dim)
        before = lax.ppermute(last, axis, up)
        after = lax.ppermute(first, axis, down)
        shard = jnp.concatenate([before, shard, after], axis=dim)
    return shard


def tables(count, length, span):
    indices = jnp.arange(count, dtype=jnp.int32)
    frequency = jnp.where(indices < count // 2, indices, length - count + indices)
    position = jnp.arange(span, dtype=jnp.int32)
    phases = frequency[:, None] * position[None, :] % length
    angles = phases.astype(jnp.float32) * (2.0 * math.pi / length)
    return (jnp.cos(angles), jnp.sin(angles))


def mobility(grains):
    leading = [(0, 0)] * (grains.ndim - 2)
    along_x = (grains[..., 1:, :] != grains[..., :-1, :]).astype(jnp.float32)
    along_y = (grains[..., :, 1:] != grains[..., :, :-1]).astype(jnp.float32)
    differ = jnp.pad(along_x, leading + [(1, 0), (0, 0)]) + jnp.pad(
        along_x, leading + [(0, 1), (0, 0)]
    )
    differ = (
        differ
        + jnp.pad(along_y, leading + [(0, 0), (1, 0)])
        + jnp.pad(along_y, leading + [(0, 0), (0, 1)])
    )
    return 0.25 * (1.0 + differ)


def stencil(padded, taps, adjoint):
    planes = padded.shape[-3] - 2
    rows_x = padded.shape[-2] - 2
    rows_y = padded.shape[-1] - 2
    total = jnp.zeros(padded.shape[:-3] + (planes, rows_x, rows_y), jnp.float32)
    for offset in range(27):
        shift_z, shift_x, shift_y = (offset // 9, offset // 3 % 3, offset % 3)
        if adjoint:
            shift_z, shift_x, shift_y = (2 - shift_z, 2 - shift_x, 2 - shift_y)
        window = padded[
            ..., shift_z : shift_z + planes, shift_x : shift_x + rows_x, shift_y : shift_y + rows_y
        ]
        total = total + taps[offset][:, None, None, None] * window.astype(jnp.float32)
    return total


def plane_forward(field, cos_x, sin_x, cos_y, sin_y):
    real_y = jnp.einsum("...xy,ky->...xk", field, cos_y, precision=HIGHEST)
    imag_y = -jnp.einsum("...xy,ky->...xk", field, sin_y, precision=HIGHEST)
    real_part = jnp.einsum("...xk,jx->...jk", real_y, cos_x, precision=HIGHEST) + jnp.einsum(
        "...xk,jx->...jk", imag_y, sin_x, precision=HIGHEST
    )
    imag_part = jnp.einsum("...xk,jx->...jk", imag_y, cos_x, precision=HIGHEST) - jnp.einsum(
        "...xk,jx->...jk", real_y, sin_x, precision=HIGHEST
    )
    return (real_part, imag_part)


def plane_inverse(real_part, imag_part, cos_x, sin_x, cos_y, sin_y):
    real_x = jnp.einsum("...jk,jx->...xk", real_part, cos_x, precision=HIGHEST) - jnp.einsum(
        "...jk,jx->...xk", imag_part, sin_x, precision=HIGHEST
    )
    imag_x = jnp.einsum("...jk,jx->...xk", imag_part, cos_x, precision=HIGHEST) + jnp.einsum(
        "...jk,jx->...xk", real_part, sin_x, precision=HIGHEST
    )
    return jnp.einsum("...xk,ky->...xy", real_x, cos_y, precision=HIGHEST) - jnp.einsum(
        "...xk,ky->...xy", imag_x, sin_y, precision=HIGHEST
    )


def depth_forward(packed, cos_table, sin_table):
    width = packed.shape[-1] // 2
    real_in = packed[..., :width]
    imag_in = packed[..., width:]
    real_out = jnp.einsum("pszc,kz->pskc", real_in, cos_table, precision=HIGHEST) + jnp.einsum(
        "pszc,kz->pskc", imag_in, sin_table, precision=HIGHEST
    )
    imag_out = jnp.einsum("pszc,kz->pskc", imag_in, cos_table, precision=HIGHEST) - jnp.einsum(
        "pszc,kz->pskc", real_in, sin_table, precision=HIGHEST
    )
    return jnp.concatenate([real_out, imag_out], axis=-1)


def depth_inverse(real_modes, imag_modes, cos_table, sin_table):
    real_out = jnp.einsum("pskc,kz->pszc", real_modes, cos_table, precision=HIGHEST) - jnp.einsum(
        "pskc,kz->pszc", imag_modes, sin_table, precision=HIGHEST
    )
    imag_out = jnp.einsum("pskc,kz->pszc", imag_modes, cos_table, precision=HIGHEST) + jnp.einsum(
        "pskc,kz->pszc", real_modes, sin_table, precision=HIGHEST
    )
    return jnp.concatenate([real_out, imag_out], axis=-1)


def rim_planes(field):
    return extended(field, (("slab", 2),), 1)


def local_any(feats, grains, spec_weight, taps, point_weight, bias, cotangent):
    samples_here = feats.shape[0]
    channels = feats.shape[1]
    planes = feats.shape[2]
    cos_x, sin_x = tables(KX, NX, NX)
    cos_y, sin_y = tables(KY, NY, NY)
    cos_full, sin_full = tables(KZ, NZ, NZ)
    cell_scale = math.sqrt(NX * NY * NZ)
    mode_scale = math.sqrt(KX * KY * KZ)
    mode_rows = spec_weight.shape[0]
    weights = spec_weight.astype(jnp.float32).reshape(mode_rows, KZ, 2, channels, channels)
    w_real = weights[:, :, 0]
    w_imag = weights[:, :, 1]
    moving = mobility(grains)[:, None]

    def to_modes(field):
        real_plane, imag_plane = plane_forward(field, cos_x, sin_x, cos_y, sin_y)
        packed = jnp.stack([real_plane, imag_plane], axis=1)
        packed = packed.transpose(4, 5, 0, 3, 1, 2).reshape(
            KX * KY, samples_here, planes, 2 * channels
        )
        moved = lax.all_to_all(packed, "slab", split_axis=0, concat_axis=2, tiled=True)
        summed = depth_forward(moved, cos_full, sin_full)
        return (summed[..., :channels], summed[..., channels:])

    def from_modes(real_modes, imag_modes):
        planar = depth_inverse(real_modes, imag_modes, cos_full, sin_full)
        packed = lax.all_to_all(planar, "slab", split_axis=2, concat_axis=0, tiled=True)
        grouped = packed.reshape(KX, KY, samples_here, planes, 2, channels).transpose(
            2, 4, 5, 3, 0, 1
        )
        return plane_inverse(grouped[:, 0], grouped[:, 1], cos_x, sin_x, cos_y, sin_y)

    zero_rim = ((0, 0), (0, 0), (0, 0), (1, 1), (1, 1))
    padded = jnp.pad(rim_planes(feats), zero_rim)
    smooth = stencil(padded, taps, False).astype(jnp.bfloat16)
    local_part = moving * jnp.einsum(
        "sczxy,co->sozxy", smooth, point_weight, preferred_element_type=jnp.float32
    )
    spec_real, spec_imag = to_modes(feats.astype(jnp.float32))
    spec_real = spec_real / cell_scale
    spec_imag = spec_imag / cell_scale
    mixed_real = jnp.einsum("pskc,pkco->psko", spec_real, w_real, precision=HIGHEST) - jnp.einsum(
        "pskc,pkco->psko", spec_imag, w_imag, precision=HIGHEST
    )
    mixed_imag = jnp.einsum("pskc,pkco->psko", spec_real, w_imag, precision=HIGHEST) + jnp.einsum(
        "pskc,pkco->psko", spec_imag, w_real, precision=HIGHEST
    )
    spectral = from_modes(mixed_real, mixed_imag) / mode_scale
    pre = spectral + local_part + bias[None, :, None, None, None]
    gate = jax.nn.sigmoid(pre)
    delta = (cotangent.astype(jnp.float32) * gate * (1.0 + pre * (1.0 - gate))).astype(jnp.bfloat16)
    dual_real, dual_imag = to_modes(delta.astype(jnp.float32))
    dual_real = dual_real / mode_scale
    dual_imag = dual_imag / mode_scale
    batch_total = samples_here * lax.axis_size("dp")
    grad_real = jnp.einsum("pskc,psko->pkco", spec_real, dual_real, precision=HIGHEST) + jnp.einsum(
        "pskc,psko->pkco", spec_imag, dual_imag, precision=HIGHEST
    )
    grad_imag = jnp.einsum("pskc,psko->pkco", spec_real, dual_imag, precision=HIGHEST) - jnp.einsum(
        "pskc,psko->pkco", spec_imag, dual_real, precision=HIGHEST
    )
    grad_terms = (jnp.stack([grad_real, grad_imag], axis=2) / batch_total).reshape(
        mode_rows, KZ, 2 * channels * channels
    )
    grad_spec = lax.psum_scatter(
        grad_terms.astype(jnp.bfloat16), "dp", scatter_dimension=2, tiled=True
    ).astype(jnp.float32)
    back_real = jnp.einsum("psko,pkco->pskc", dual_real, w_real, precision=HIGHEST) + jnp.einsum(
        "psko,pkco->pskc", dual_imag, w_imag, precision=HIGHEST
    )
    back_imag = jnp.einsum("psko,pkco->pskc", dual_imag, w_real, precision=HIGHEST) - jnp.einsum(
        "psko,pkco->pskc", dual_real, w_imag, precision=HIGHEST
    )
    spectral_back = from_modes(back_real, back_imag) / cell_scale
    spread = (
        moving
        * jnp.einsum("sozxy,co->sczxy", delta, point_weight, preferred_element_type=jnp.float32)
    ).astype(jnp.bfloat16)
    spread_padded = jnp.pad(rim_planes(spread), zero_rim)
    local_back = stencil(spread_padded, taps, True)
    grad_feats = (spectral_back + local_back).astype(jnp.bfloat16)
    return (grad_feats, grad_spec)


def frequencies(count, length):
    index = np.arange(count)
    return np.where(index < count // 2, index, length - count + index)


def angles(count, length):
    phases = np.outer(frequencies(count, length), np.arange(length)) % length
    return phases * (2.0 * np.pi / length)


def constant(array):
    return jnp.asarray(np.asarray(array, np.float32).astype(ml_dtypes.bfloat16))


def forward_x_table(slabs, split):
    a = angles(KX, NX).reshape(slabs, KX // slabs, NX)
    trig = np.stack([np.cos(a), np.sin(a)])
    table = np.einsum("tsjx,cd->tscjdx", trig, np.eye(2)).reshape(-1, 2, NX // 8, 8)
    if split:
        table = table.transpose(0, 2, 1, 3)
    return table.reshape(4 * KX, 2 * NX)


def forward_y_table(planes):
    a = angles(KY, NY)
    cos, sin = np.cos(a).T, np.sin(a).T
    block = np.stack([np.stack([cos, -sin], 1), np.stack([-sin, -cos], 1)])
    pick = np.eye(planes).reshape(planes // 2, 2, planes)
    table = np.einsum("pqz,tyrk->ptqyzrk", pick, block)
    return table.reshape(planes * 2 * NY, planes * 2 * KY)


def forward_z_table():
    a = angles(KZ, NZ)
    cos, sin = np.cos(a).T, np.sin(a).T
    block = np.stack([np.stack([cos, -sin], 1), np.stack([sin, cos], 1)], 1)
    table = np.einsum("zrqm,kl->zrkqlm", block, np.eye(KY))
    return table.reshape(NZ * 2 * KY, 2 * KY * KZ)


def inverse_z_table():
    a = angles(KZ, NZ)
    cos, sin = np.cos(a), np.sin(a)
    block = np.stack([np.stack([cos, sin], 2), np.stack([-sin, cos], 2)])
    table = np.einsum("rmzq,kl->rkmzql", block, np.eye(KY))
    return table.reshape(2 * KY * KZ, NZ * 2 * KY)


def inverse_y_table(planes, group):
    a = angles(KY, NY)
    cos, sin = np.cos(a), np.sin(a)
    block = np.stack([np.stack([cos, -sin], 1), np.stack([-sin, -cos], 1)])
    pick = np.eye(planes).reshape(planes // group, group, planes)
    table = np.einsum("pqz,rkty->pzrktqy", pick, block)
    return table.reshape(planes // group, planes * 2 * KY, 2 * group * NY)


def inverse_x_table(slabs, group):
    a = angles(KX, NX).reshape(slabs, KX // slabs, NX)
    trig = np.stack([np.cos(a), np.sin(a)])
    table = np.einsum("tsjx,cd->cxstdj", trig, np.eye(group))
    return table.reshape(group * NX, 2 * KX * group)


def first_table(channels, depth):
    table = np.einsum("ac,j,b->ajcb", np.eye(channels), np.ones(depth), np.ones(channels))
    return table.reshape(channels * depth, channels * channels)


def second_table(channels, depth):
    table = np.einsum("ac,j,b->ajbc", np.eye(channels), np.ones(depth), np.ones(channels))
    return table.reshape(channels * depth, channels * channels)


LIGHT = pl.CostEstimate(flops=10**7, bytes_accessed=10**5, transcendentals=0)
HEAVY = pl.CostEstimate(flops=10**11, bytes_accessed=10**8, transcendentals=0)


def dot(a, b):
    return jnp.dot(a, b, preferred_element_type=jnp.float32)


def whole(shape):
    return pl.BlockSpec(shape, lambda *_: (0,) * len(shape))


def params(**kw):
    return pltpu.CompilerParams(vmem_limit_bytes=58 * 2**20, **kw)


def store_rows(rows, pair, x_table, load):
    slabs, lines = rows.shape[2:4]
    for i in range(lines // 16):
        parts = [dot(x_table[...], load(2 * i + k)) for k in range(2)]
        for t in range(2):
            for s in range(slabs):
                here = slice(8 * (t * slabs + s), 8 * (t * slabs + s) + 8)
                both = jnp.concatenate([part[here] for part in parts], axis=0)
                rows[pair, t, s, 16 * i : 16 * i + 16, :] = both.astype(jnp.bfloat16)


def store_modes(rows, y_table, out):
    pairs, _, slabs, lines, _ = rows.shape
    left = [
        jnp.concatenate([rows[p, t, s] for p in range(pairs) for t in range(2)], axis=1)
        for s in range(slabs)
    ]
    modes = dot(jnp.concatenate(left, axis=0), y_table[...])
    for s in range(slabs):
        out[s] = modes[s * lines : (s + 1) * lines].astype(jnp.bfloat16)


def store_rims(field, rims, pair, pairs):
    half = field.shape[0] // 2

    @pl.when(pair == 0)
    def _():
        for i in range(2):
            rims[i][:, 0] = field[half * i : half * (i + 1), 0]

    @pl.when(pair == pairs - 1)
    def _():
        for i in range(2):
            rims[2 + i][:, 0] = field[half * i : half * (i + 1), 1]


def forward_kernel(field, x_table, y_table, out, *rest):
    *rims, rows = rest
    pair = pl.program_id(0)
    pairs = rows.shape[0]
    store_rims(field, rims, pair, pairs)

    def load(i):
        halves = [field[2 * i : 2 * i + 2, q].reshape(2 * NX, NY) for q in range(2)]
        return jnp.concatenate(halves, axis=1)

    store_rows(rows, pair, x_table, load)

    @pl.when(pair == pairs - 1)
    def _():
        store_modes(rows, y_table, out)


def forward_modes(field, slabs):
    channels, planes = field.shape[:2]
    lines = channels * (KX // slabs)
    x_table = constant(forward_x_table(slabs, False))
    y_table = constant(forward_y_table(planes))
    outs = [(slabs, lines, planes * 2 * KY)] + [(channels // 2, 1, NX, NY)] * 4
    return pl.pallas_call(
        forward_kernel,
        grid=(planes // 2,),
        in_specs=[
            pl.BlockSpec((channels, 2, NX, NY), lambda p: (0, p, 0, 0)),
            whole(x_table.shape),
            whole(y_table.shape),
        ],
        out_specs=[whole(out) for out in outs],
        out_shape=[jax.ShapeDtypeStruct(out, jnp.bfloat16) for out in outs],
        scratch_shapes=[pltpu.VMEM((planes // 2, 2, slabs, lines, 2 * NY), jnp.bfloat16)],
        compiler_params=params(),
        cost_estimate=LIGHT,
        name="forward_modes",
    )(field, x_table, y_table)


def mixing_kernel(scale_in, scale_out, adjoint, planar, weight, z_in, z_out, spread_table,
                  sum_table, *rest):
    if adjoint:
        partner, out, send, spectrum, total, wide, product = rest
    else:
        spectrum, out, total, wide, product = rest
    step = pl.program_id(0)
    steps = pl.num_programs(0)
    slabs = planar.shape[0]
    width = planar.shape[2]
    half = spectrum.shape[0] // 2
    lanes = weight.shape[1] // 2

    @pl.when(step == 0)
    def _():
        left = jnp.concatenate([planar[s] for s in range(slabs)], axis=1)
        modes = (dot(left, z_in[...]).T * scale_in).astype(jnp.bfloat16)
        spectrum[...] = modes
        total[...] = jnp.zeros_like(total)
        if adjoint:
            for d in range(send.shape[0]):
                send[d, : 2 * half] = partner[...]
                send[d, 2 * half :] = modes

    lane = lax.broadcasted_iota(jnp.int32, (1, spectrum.shape[1]), 1)
    mine = lane % steps == step
    wide[...] = dot(jnp.where(mine, spectrum[...], 0), spread_table[...])
    block = 32
    tile = wide.shape[1]
    for at in range(0, half, block):
        sums = [0.0, 0.0]
        for column in range(0, lanes, 128):
            here = slice(column, column + 128) if tile == lanes else slice(None)
            real_wide = wide[at : at + block, here]
            imag_wide = wide[half + at : half + at + block, here]
            w_real = weight[at : at + block, column : column + 128].astype(jnp.float32)
            imag_column = lanes + column
            w_imag = weight[at : at + block, imag_column : imag_column + 128].astype(jnp.float32)
            if adjoint:
                real = real_wide * w_real + imag_wide * w_imag
                imag = imag_wide * w_real - real_wide * w_imag
                product[at : at + block, column : column + 128] = real.astype(jnp.bfloat16)
                product[half + at : half + at + block, column : column + 128] = imag.astype(
                    jnp.bfloat16
                )
            else:
                sums[0] = sums[0] + (real_wide * w_real - imag_wide * w_imag)
                sums[1] = sums[1] + (real_wide * w_imag + imag_wide * w_real)
        if not adjoint:
            product[at : at + block] = sums[0].astype(jnp.bfloat16)
            product[half + at : half + at + block] = sums[1].astype(jnp.bfloat16)
    total[...] += jnp.where(mine, dot(product[...], sum_table[...]), 0.0)

    @pl.when(step == steps - 1)
    def _():
        modes = dot((total[...] * scale_out).T.astype(jnp.bfloat16), z_out[...])
        for s in range(slabs):
            out[s] = modes[:, s * width : (s + 1) * width].astype(jnp.bfloat16)


def mix(planar, weight, scale_in, scale_out, partner=None, copies=0):
    slabs, lines, width = planar.shape
    adjoint = partner is not None
    depth = KX // slabs
    channels = lines // depth
    rows = KY * KZ
    z_in = constant(forward_z_table())
    z_out = constant(inverse_z_table())
    first = first_table(channels, depth)
    second = second_table(channels, depth)
    spread_table = constant(second[:, :128] if adjoint else first)
    sum_table = constant(first.T if adjoint else second[:, :128].T)
    shape = (2 * rows, lines)
    in_specs = [
        whole(planar.shape),
        pl.BlockSpec((rows, weight.shape[1]), lambda j: (j, 0)),
        whole(z_in.shape),
        whole(z_out.shape),
        whole(spread_table.shape),
        whole(sum_table.shape),
    ]
    operands = [planar, weight, z_in, z_out, spread_table, sum_table]
    scratch = [
        pltpu.VMEM(shape, jnp.float32),
        pltpu.VMEM((2 * rows, spread_table.shape[1]), jnp.float32),
        pltpu.VMEM((2 * rows, sum_table.shape[0]), jnp.bfloat16),
    ]
    if adjoint:
        in_specs.append(whole(shape))
        operands.append(partner)
        scratch = [pltpu.VMEM(shape, jnp.bfloat16)] + scratch
        outs = [planar.shape, (copies, 2 * shape[0], lines)]
    else:
        outs = [shape, planar.shape]
    return pl.pallas_call(
        functools.partial(mixing_kernel, scale_in, scale_out, adjoint),
        grid=(depth,),
        in_specs=in_specs,
        out_specs=[whole(out) for out in outs],
        out_shape=[jax.ShapeDtypeStruct(out, jnp.bfloat16) for out in outs],
        scratch_shapes=scratch,
        compiler_params=params(),
        cost_estimate=HEAVY,
        name="mix_back" if adjoint else "mix",
    )(*operands)


def plane_mobility(grains):
    same = [
        jnp.concatenate([grains[:1], grains[:-1]], axis=0),
        jnp.concatenate([grains[1:], grains[-1:]], axis=0),
        jnp.concatenate([grains[:, :1], grains[:, :-1]], axis=1),
        jnp.concatenate([grains[:, 1:], grains[:, -1:]], axis=1),
    ]
    total = jnp.full(grains.shape, 0.25, jnp.float32)
    for other in same:
        total = total + jnp.where(grains != other, 0.25, 0.0)
    return total


def layer_kernel(bias, planar, smooth, cotangent, grains, point_weight, repeat, ix_table, iy_table,
                 x_table, y_table, spread, out, *rest):
    pair = pl.program_id(0)
    rims, rest = rest[:4], rest[4:]
    waves, spectral, moving, delta, rows, bias_wide, mix_out, mix_in = rest
    pairs = rows.shape[0]
    channels = cotangent.shape[0]
    slabs = planar.shape[0]

    @pl.when(pair == 0)
    def _():
        for c in range(channels):
            bias_wide[c] = jnp.full(bias_wide.shape[1:], 0.5 * bias[c], jnp.float32)
        tall = dot(repeat[...], point_weight[...]).astype(jnp.bfloat16)
        square = lax.dot_general(
            tall, repeat[...], (((1,), (1,)), ((), ())), preferred_element_type=jnp.float32
        )
        row = lax.broadcasted_iota(jnp.int32, square.shape, 0) % 8
        column = lax.broadcasted_iota(jnp.int32, square.shape, 1) % 8
        square = jnp.where(row == column, square, 0.0)
        mix_in[...] = square.astype(jnp.bfloat16)
        mix_out[...] = square.T.astype(jnp.bfloat16)

    lines = planar.shape[1]
    step = jnp.concatenate([planar[s] for s in range(slabs)], axis=0)
    step = dot(step, iy_table[0]).astype(jnp.bfloat16)
    for s in range(slabs):
        for t in range(2):
            waves[s, t] = step[s * lines : (s + 1) * lines, 2 * NY * t : 2 * NY * (t + 1)]
    group = 8 * (KX // slabs)
    for g in range(channels // 8):
        here = slice(g * group, (g + 1) * group)
        wave = [waves[s, t, here, :] for s in range(slabs) for t in range(2)]
        step = dot(ix_table[...], jnp.concatenate(wave, axis=0))
        spectral[8 * g : 8 * g + 8] = step.reshape(8, NX, 2 * NY)
    for q in range(2):
        moving[:, q * NY : (q + 1) * NY] = 0.5 * plane_mobility(grains[q])

    def body(i, _):
        x = pl.multiple_of(16 * i, 16)
        halves = [cotangent[:, q, pl.ds(x, 16), :] for q in range(2)]
        cotangent_here = jnp.concatenate(halves, axis=2).astype(jnp.float32)
        spreads = []
        for h in range(2):
            at = pl.ds(pl.multiple_of(x + 8 * h, 8), 8)
            mobile = moving[at, :][None]
            local = dot(mix_out[...], smooth[0, 2 * i + h]).reshape(channels, 8, 2 * NY)
            half = spectral[:, at, :] + mobile * local + bias_wide[...]
            wave = jnp.tanh(half)
            slope = (1.0 + wave) * (1.0 + (half - half * wave))
            change = cotangent_here[:, 8 * h : 8 * h + 8, :] * slope
            right = change.reshape(8 * channels, 2 * NY).astype(jnp.bfloat16)
            delta[2 * i + h] = right
            back = dot(mix_in[...], right).reshape(channels, 8, 2 * NY)
            spreads.append(mobile * back)
        both = jnp.concatenate(spreads, axis=1).astype(jnp.bfloat16)
        for q in range(2):
            spread[:, q, pl.ds(x, 16), :] = both[:, :, q * NY : (q + 1) * NY]
        return 0

    lax.fori_loop(0, NX // 16, body, 0, unroll=4)

    store_rims(spread, rims, pair, pairs)

    def load(i):
        return delta[:, 16 * i : 16 * i + 16, :].reshape(2 * NX, 2 * NY)

    store_rows(rows, pair, x_table, load)

    @pl.when(pair == pairs - 1)
    def _():
        store_modes(rows, y_table, out)


def layer(planar, smooth, cotangent, grains, bias, point_weight):
    slabs, lines, width = planar.shape
    channels, planes = cotangent.shape[:2]
    pairs = planes // 2
    repeat = constant(np.repeat(np.eye(channels), 8, axis=0))
    ix_table = constant(inverse_x_table(slabs, 8))
    iy_table = constant(inverse_y_table(planes, 2))
    x_table = constant(forward_x_table(slabs, True))
    y_table = constant(forward_y_table(planes))
    field = pl.BlockSpec((channels, 2, NX, NY), lambda p: (0, p, 0, 0))
    outs = [cotangent.shape, planar.shape] + [(channels // 2, 1, NX, NY)] * 4
    return pl.pallas_call(
        layer_kernel,
        grid=(pairs,),
        in_specs=[
            pl.BlockSpec(memory_space=pltpu.SMEM),
            whole(planar.shape),
            pl.BlockSpec((1,) + smooth.shape[1:], lambda p: (p, 0, 0, 0)),
            field,
            pl.BlockSpec((2, NX, NY), lambda p: (p, 0, 0)),
            whole(point_weight.shape),
            whole(repeat.shape),
            whole(ix_table.shape),
            pl.BlockSpec((1,) + iy_table.shape[1:], lambda p: (p, 0, 0)),
            whole(x_table.shape),
            whole(y_table.shape),
        ],
        out_specs=[field] + [whole(out) for out in outs[1:]],
        out_shape=[jax.ShapeDtypeStruct(out, jnp.bfloat16) for out in outs],
        scratch_shapes=[
            pltpu.VMEM((slabs, 2, lines, 2 * NY), jnp.bfloat16),
            pltpu.VMEM((channels, NX, 2 * NY), jnp.float32),
            pltpu.VMEM((NX, 2 * NY), jnp.float32),
            pltpu.VMEM((NX // 8, 8 * channels, 2 * NY), jnp.bfloat16),
            pltpu.VMEM((pairs, 2, slabs, lines, 2 * NY), jnp.bfloat16),
            pltpu.VMEM((channels, 8, 2 * NY), jnp.float32),
            pltpu.VMEM((8 * channels, 8 * channels), jnp.bfloat16),
            pltpu.VMEM((8 * channels, 8 * channels), jnp.bfloat16),
        ],
        compiler_params=params(),
        cost_estimate=LIGHT,
        name="layer",
    )(bias, planar, smooth, cotangent, grains, point_weight, repeat, ix_table, iy_table, x_table,
      y_table)


def build_band(adjoint, taps, channel, band):
    row = lax.broadcasted_iota(jnp.int32, (8, NY), 0)
    lane = lax.broadcasted_iota(jnp.int32, (8, NY), 1)
    offset = row - lane
    for dz in range(3):
        for dx in range(3):
            tile = jnp.zeros((8, NY), jnp.float32)
            for dy in range(3):
                number = 9 * dz + 3 * dx + dy
                tap = taps[26 - number if adjoint else number, channel]
                hit = (offset == dy - 1) | (offset == dy - 1 - NY)
                tile = jnp.where(hit, tap, tile)
            tiles = [pltpu.roll(tile, 8 * k, axis=1) if k > 0 else tile for k in range(NY // 8)]
            tiles[0] = jnp.where((row == 0) & (lane == NY - 1), 0.0, tiles[0])
            tiles[-1] = jnp.where((row == 7) & (lane == 0), 0.0, tiles[-1])
            block = jnp.concatenate(tiles, axis=0).astype(jnp.bfloat16)
            for q in range(2):
                down = (q + dz) * NY
                right = (2 * dx + q) * NY
                band[down : down + NY, right : right + NY] = block


def apply_band(quads, band):
    left = jnp.concatenate([jnp.concatenate(quad, axis=1) for quad in quads], axis=0)
    wide = dot(left, band[...])
    lower, middle, upper = (wide[:, 2 * NY * dx : 2 * NY * (dx + 1)] for dx in range(3))
    row = lax.broadcasted_iota(jnp.int32, (8, 2 * NY), 0)
    totals = []
    for p in range(len(quads)):
        here = slice(p * NX, (p + 1) * NX)
        down = pltpu.roll(lower[here], 1, axis=0)
        up = pltpu.roll(upper[here], NX - 1, axis=0)
        down = jnp.concatenate([jnp.where(row == 0, 0.0, down[:8]), down[8:]], axis=0)
        up = jnp.concatenate([up[:-8], jnp.where(row == 7, 0.0, up[-8:])], axis=0)
        totals.append(middle[here] + down + up)
    return totals


def banded(adjoint, taps, start, even, odd, channels):
    step = pl.program_id(0)
    final = start + channels * pl.num_programs(0) - 1
    bands = (even, odd)

    @pl.when(step == 0)
    def _():
        even[...] = jnp.zeros_like(even)
        odd[...] = jnp.zeros_like(odd)
        build_band(adjoint, taps, start, even)

    def run(visit):
        for c in range(channels):
            following = jnp.minimum(start + channels * step + c + 1, final)
            build_band(adjoint, taps, following, bands[(c + 1) % 2])
            visit(c, bands[c % 2])

    return run


def stencil_kernel(adjoint, start, taps, before, field, after, *rest):
    out, even, odd = rest[-3:]
    planes = field.shape[1]
    totals = []

    def visit(c, band):
        sheets = [before[c, 0]] + [field[c, z] for z in range(planes)] + [after[c, 0]]
        pairs = apply_band([sheets[z : z + 4] for z in range(0, planes, 2)], band)
        if adjoint:
            for p, total in enumerate(pairs):
                total = total.astype(jnp.bfloat16)
                out[c, 2 * p] = total[:, :NY]
                out[c, 2 * p + 1] = total[:, NY:]
        else:
            totals.append(pairs)

    banded(adjoint, taps, start, even, odd, 2)(visit)
    if not adjoint:
        for p in range(planes // 2):
            both = [totals[c][p].reshape(NX // 8, 8, 2 * NY) for c in range(2)]
            out[p] = jnp.concatenate(both, axis=1).astype(jnp.bfloat16)


def stencil_planes(field, rims, taps, adjoint, done=None):
    channels, planes = field.shape[:2]
    pairs = planes // 2
    start = 0 if done is None else channels // 2
    skip = start // 2
    rim = pl.BlockSpec((2, 1, NX, NY), lambda c: (c, 0, 0, 0))
    sheets = pl.BlockSpec((2, planes, NX, NY), lambda c: (c + skip, 0, 0, 0))
    in_specs = [pl.BlockSpec(memory_space=pltpu.SMEM), rim, sheets, rim]
    operands = [taps, rims[0], field, rims[1]]
    if done is not None:
        in_specs.append(pl.BlockSpec(memory_space=pl.ANY))
        operands.append(done)
    if adjoint:
        out_spec, shape = sheets, field.shape
    else:
        out_spec = pl.BlockSpec((pairs, NX // 8, 16, 2 * NY), lambda c: (0, 0, c + skip, 0))
        shape = (pairs, NX // 8, 8 * channels, 2 * NY)
    name = "near" if adjoint else "smooth"
    return pl.pallas_call(
        functools.partial(stencil_kernel, adjoint, start),
        grid=(channels // 4,),
        in_specs=in_specs,
        out_specs=out_spec,
        out_shape=jax.ShapeDtypeStruct(shape, jnp.bfloat16),
        input_output_aliases={} if done is None else {4: 0},
        scratch_shapes=[pltpu.VMEM((4 * NY, 6 * NY), jnp.bfloat16) for _ in range(2)],
        compiler_params=params(),
        cost_estimate=LIGHT,
        name=name + ("_low" if done is None else "_high"),
    )(*operands)


def finish_kernel(planar, near, ix_table, iy_table, out, waves):
    step = pl.program_id(0)
    slabs, lines = planar.shape[:2]
    planes = near.shape[1]
    span = planes * NY

    @pl.when(step == 0)
    def _():
        left = jnp.concatenate([planar[s] for s in range(slabs)], axis=0)
        for t in range(2):
            wave = dot(left, iy_table[0, :, t * span : (t + 1) * span]).astype(jnp.bfloat16)
            for s in range(slabs):
                waves[s, t] = wave[s * lines : (s + 1) * lines]

    rows = 4 * (KX // slabs)
    here = pl.ds(pl.multiple_of(rows * step, rows), rows)
    right = [waves[s, t, here, :] for s in range(slabs) for t in range(2)]
    right = jnp.concatenate(right, axis=0)
    for p in range(planes // 2):
        spectral = dot(ix_table[...], right[:, 2 * p * NY : 2 * (p + 1) * NY])
        for c in range(4):
            for q in range(2):
                far = spectral[c * NX : (c + 1) * NX, q * NY : (q + 1) * NY]
                total = far + near[c, 2 * p + q].astype(jnp.float32)
                out[c, 2 * p + q] = total.astype(jnp.bfloat16)


def finish(planar, near):
    slabs, lines, width = planar.shape
    channels, planes = near.shape[:2]
    ix_table = constant(inverse_x_table(slabs, 4))
    iy_table = constant(inverse_y_table(planes, planes))
    sheets = pl.BlockSpec((4, planes, NX, NY), lambda c: (c, 0, 0, 0))
    return pl.pallas_call(
        finish_kernel,
        grid=(channels // 4,),
        in_specs=[whole(planar.shape), sheets, whole(ix_table.shape), whole(iy_table.shape)],
        out_specs=sheets,
        out_shape=jax.ShapeDtypeStruct(near.shape, jnp.bfloat16),
        scratch_shapes=[pltpu.VMEM((slabs, 2, lines, planes * NY), jnp.bfloat16)],
        compiler_params=params(),
        cost_estimate=HEAVY,
        name="finish",
    )(planar, near, ix_table, iy_table)


def gradient_kernel(depth, where, gathered, first, second, out):
    step = pl.program_id(0)
    samples, rows, lines = gathered.shape
    half = rows // 4
    lane = lax.broadcasted_iota(jnp.int32, (1, lines), 1)
    mine = lane % depth == step
    spectra = [gathered[s, : 2 * half] for s in range(samples)]
    duals = []
    for s in range(samples):
        real = gathered[s, 2 * half : 3 * half]
        imag = gathered[s, 3 * half :]
        duals.append(jnp.where(where[0] == 0, real, imag))
        duals.append(jnp.where(where[0] == 0, imag, -real))
    spectra = jnp.where(mine, jnp.concatenate(spectra, axis=0), 0)
    duals = jnp.where(mine, jnp.concatenate(duals, axis=0), 0)
    wide = dot(duals, second[...])
    for column in range(0, out.shape[1], 256):
        product = dot(spectra, first[0, :, column : column + 256])
        for at in range(0, 256, 128):
            total = 0.0
            for s in range(2 * samples):
                here = slice(s * half, (s + 1) * half)
                total = total + product[here, at : at + 128] * wide[here]
            out[:, column + at : column + at + 128] = total * (1.0 / samples)


def weight_gradient(gathered, depth, width, index):
    samples, rows, lines = gathered.shape
    channels = lines // depth
    square = channels * channels
    cuts = square // width
    first = first_table(channels, depth).reshape(lines, cuts, width).transpose(1, 0, 2)
    first = constant(first)
    second = constant(second_table(channels, depth)[:, :128])
    where = jnp.stack([index // cuts, index % cuts]).astype(jnp.int32)
    half = rows // 4
    return pl.pallas_call(
        functools.partial(gradient_kernel, depth),
        grid_spec=pltpu.PrefetchScalarGridSpec(
            num_scalar_prefetch=1,
            grid=(depth,),
            in_specs=[
                pl.BlockSpec(gathered.shape, lambda j, w: (0, 0, 0)),
                pl.BlockSpec((1, lines, width), lambda j, w: (w[1], 0, 0)),
                pl.BlockSpec(second.shape, lambda j, w: (0, 0)),
            ],
            out_specs=pl.BlockSpec((half, width), lambda j, w: (j, 0)),
        ),
        out_shape=jax.ShapeDtypeStruct((depth * half, width), jnp.float32),
        compiler_params=params(),
        cost_estimate=LIGHT,
        name="weight_gradient",
    )(where, gathered, first, second)


def exchange(first, last):
    size = lax.axis_size("slab")
    up = [(i, i + 1) for i in range(size - 1)]
    down = [(j, i) for i, j in up]
    return lax.ppermute(last, "slab", up), lax.ppermute(first, "slab", down)


def swap(planar):
    return lax.all_to_all(planar, "slab", split_axis=0, concat_axis=0)


def local_fast(feats, grains, spec_weight, taps, point_weight, bias, cotangent):
    slabs = lax.axis_size("slab")
    copies = lax.axis_size("dp")
    barrier = lax.optimization_barrier
    field = feats[0]
    channels = field.shape[0]
    cell_scale = 1.0 / math.sqrt(NX * NY * NZ)
    mode_scale = 1.0 / math.sqrt(KX * KY * KZ)
    mode_rows = spec_weight.shape[0]
    weight = spec_weight.reshape(mode_rows * KZ, 2 * channels * channels)
    width = weight.shape[1] // copies

    planar, first, first_high, last, last_high = forward_modes(field, slabs)
    planar, first, last = barrier((swap(planar), first, last))
    rims = exchange(first, last)
    spectrum, planar = mix(planar, weight, cell_scale, 0.5 * mode_scale)
    planar = swap(planar)
    rims, first, last, spectrum = barrier((rims, first_high, last_high, spectrum))
    rims_high = exchange(first, last)
    smooth = stencil_planes(field, rims, taps, False)
    smooth = stencil_planes(field, rims_high, taps, False, smooth)
    spread, planar, first, first_high, last, last_high = layer(
        planar, smooth, cotangent[0], grains[0], bias, point_weight
    )
    rims = exchange(first, last)
    planar, send = mix(swap(planar), weight, 0.5 * mode_scale, cell_scale, spectrum, copies)
    planar = swap(planar)
    rims, first, last, send = barrier((rims, first_high, last_high, send))
    rims_high = exchange(first, last)
    near, send = barrier((stencil_planes(spread, rims, taps, True), send))
    near = stencil_planes(spread, rims_high, taps, True, near)
    gathered = lax.all_to_all(send, "dp", split_axis=0, concat_axis=0)
    grad_feats = finish(planar, near)
    grad_feats, gathered = barrier((grad_feats, gathered))
    grad_feats = grad_feats[None]
    grad_spec = weight_gradient(gathered, KX // slabs, width, lax.axis_index("dp"))
    return (grad_feats, grad_spec.reshape(mode_rows, KZ, width))


def local(feats, grains, spec_weight, taps, point_weight, bias, cotangent):
    samples, channels, planes = feats.shape[:3]
    width = spec_weight.shape[2] // lax.axis_size("dp")
    fits = (
        lax.axis_size("slab") * 4 == KX
        and samples == 1
        and channels == 32
        and planes == 8
        and channels * channels % width == 0
        and width % 128 == 0
    )
    form = local_fast if fits else local_any
    return form(feats, grains, spec_weight, taps, point_weight, bias, cotangent)


def solution(mesh):
    in_specs = (
        P(("grp", "dp"), None, "slab", None, None),
        P(("grp", "dp"), "slab", None, None),
        P("slab", None, None),
        P(),
        P(),
        P(),
        P(("grp", "dp"), None, "slab", None, None),
    )
    out_specs = (P(("grp", "dp"), None, "slab", None, None), P("slab", "grp", "dp"))
    return jax.shard_map(local, mesh=mesh, in_specs=in_specs, out_specs=out_specs, check_vma=False)
```

```python
import functools
import math

import jax
import jax.numpy as jnp
import ml_dtypes
import numpy as np
from jax import lax
from jax.experimental import pallas as pl
from jax.experimental.pallas import tpu as pltpu
from jax.sharding import PartitionSpec as P

NX = 128
NY = 128
NZ = 32
KX = 16
KY = 16
KZ = 16


HIGHEST = lax.Precision.HIGHEST


def extended(shard, sides, width):
    for axis, dim in sides:
        size, length = (lax.axis_size(axis), shard.shape[dim])
        up = [(i, (i + 1) % size) for i in range(size - 1)]
        down = [(j, i) for i, j in up]
        last = lax.slice_in_dim(shard, length - width, length, axis=dim)
        first = lax.slice_in_dim(shard, 0, width, axis=dim)
        before = lax.ppermute(last, axis, up)
        after = lax.ppermute(first, axis, down)
        shard = jnp.concatenate([before, shard, after], axis=dim)
    return shard


def tables(count, length, span):
    indices = jnp.arange(count, dtype=jnp.int32)
    frequency = jnp.where(indices < count // 2, indices, length - count + indices)
    position = jnp.arange(span, dtype=jnp.int32)
    phases = frequency[:, None] * position[None, :] % length
    angles = phases.astype(jnp.float32) * (2.0 * math.pi / length)
    return (jnp.cos(angles), jnp.sin(angles))


def mobility(grains):
    leading = [(0, 0)] * (grains.ndim - 2)
    along_x = (grains[..., 1:, :] != grains[..., :-1, :]).astype(jnp.float32)
    along_y = (grains[..., :, 1:] != grains[..., :, :-1]).astype(jnp.float32)
    differ = jnp.pad(along_x, leading + [(1, 0), (0, 0)]) + jnp.pad(
        along_x, leading + [(0, 1), (0, 0)]
    )
    differ = (
        differ
        + jnp.pad(along_y, leading + [(0, 0), (1, 0)])
        + jnp.pad(along_y, leading + [(0, 0), (0, 1)])
    )
    return 0.25 * (1.0 + differ)


def stencil(padded, taps, adjoint):
    planes = padded.shape[-3] - 2
    rows_x = padded.shape[-2] - 2
    rows_y = padded.shape[-1] - 2
    total = jnp.zeros(padded.shape[:-3] + (planes, rows_x, rows_y), jnp.float32)
    for offset in range(27):
        shift_z, shift_x, shift_y = (offset // 9, offset // 3 % 3, offset % 3)
        if adjoint:
            shift_z, shift_x, shift_y = (2 - shift_z, 2 - shift_x, 2 - shift_y)
        window = padded[
            ..., shift_z : shift_z + planes, shift_x : shift_x + rows_x, shift_y : shift_y + rows_y
        ]
        total = total + taps[offset][:, None, None, None] * window.astype(jnp.float32)
    return total


def plane_forward(field, cos_x, sin_x, cos_y, sin_y):
    real_y = jnp.einsum("...xy,ky->...xk", field, cos_y, precision=HIGHEST)
    imag_y = -jnp.einsum("...xy,ky->...xk", field, sin_y, precision=HIGHEST)
    real_part = jnp.einsum("...xk,jx->...jk", real_y, cos_x, precision=HIGHEST) + jnp.einsum(
        "...xk,jx->...jk", imag_y, sin_x, precision=HIGHEST
    )
    imag_part = jnp.einsum("...xk,jx->...jk", imag_y, cos_x, precision=HIGHEST) - jnp.einsum(
        "...xk,jx->...jk", real_y, sin_x, precision=HIGHEST
    )
    return (real_part, imag_part)


def plane_inverse(real_part, imag_part, cos_x, sin_x, cos_y, sin_y):
    real_x = jnp.einsum("...jk,jx->...xk", real_part, cos_x, precision=HIGHEST) - jnp.einsum(
        "...jk,jx->...xk", imag_part, sin_x, precision=HIGHEST
    )
    imag_x = jnp.einsum("...jk,jx->...xk", imag_part, cos_x, precision=HIGHEST) + jnp.einsum(
        "...jk,jx->...xk", real_part, sin_x, precision=HIGHEST
    )
    return jnp.einsum("...xk,ky->...xy", real_x, cos_y, precision=HIGHEST) - jnp.einsum(
        "...xk,ky->...xy", imag_x, sin_y, precision=HIGHEST
    )


def depth_forward(packed, cos_table, sin_table):
    width = packed.shape[-1] // 2
    real_in = packed[..., :width]
    imag_in = packed[..., width:]
    real_out = jnp.einsum("pszc,kz->pskc", real_in, cos_table, precision=HIGHEST) + jnp.einsum(
        "pszc,kz->pskc", imag_in, sin_table, precision=HIGHEST
    )
    imag_out = jnp.einsum("pszc,kz->pskc", imag_in, cos_table, precision=HIGHEST) - jnp.einsum(
        "pszc,kz->pskc", real_in, sin_table, precision=HIGHEST
    )
    return jnp.concatenate([real_out, imag_out], axis=-1)


def depth_inverse(real_modes, imag_modes, cos_table, sin_table):
    real_out = jnp.einsum("pskc,kz->pszc", real_modes, cos_table, precision=HIGHEST) - jnp.einsum(
        "pskc,kz->pszc", imag_modes, sin_table, precision=HIGHEST
    )
    imag_out = jnp.einsum("pskc,kz->pszc", imag_modes, cos_table, precision=HIGHEST) + jnp.einsum(
        "pskc,kz->pszc", real_modes, sin_table, precision=HIGHEST
    )
    return jnp.concatenate([real_out, imag_out], axis=-1)


def rim_planes(field):
    return extended(field, (("slab", 2),), 1)


def local_any(feats, grains, spec_weight, taps, point_weight, bias, cotangent):
    samples_here = feats.shape[0]
    channels = feats.shape[1]
    planes = feats.shape[2]
    cos_x, sin_x = tables(KX, NX, NX)
    cos_y, sin_y = tables(KY, NY, NY)
    cos_full, sin_full = tables(KZ, NZ, NZ)
    cell_scale = math.sqrt(NX * NY * NZ)
    mode_scale = math.sqrt(KX * KY * KZ)
    mode_rows = spec_weight.shape[0]
    weights = spec_weight.astype(jnp.float32).reshape(mode_rows, KZ, 2, channels, channels)
    w_real = weights[:, :, 0]
    w_imag = weights[:, :, 1]
    moving = mobility(grains)[:, None]

    def to_modes(field):
        real_plane, imag_plane = plane_forward(field, cos_x, sin_x, cos_y, sin_y)
        packed = jnp.stack([real_plane, imag_plane], axis=1)
        packed = packed.transpose(4, 5, 0, 3, 1, 2).reshape(
            KX * KY, samples_here, planes, 2 * channels
        )
        moved = lax.all_to_all(packed, "slab", split_axis=0, concat_axis=2, tiled=True)
        summed = depth_forward(moved, cos_full, sin_full)
        return (summed[..., :channels], summed[..., channels:])

    def from_modes(real_modes, imag_modes):
        planar = depth_inverse(real_modes, imag_modes, cos_full, sin_full)
        packed = lax.all_to_all(planar, "slab", split_axis=2, concat_axis=0, tiled=True)
        grouped = packed.reshape(KX, KY, samples_here, planes, 2, channels).transpose(
            2, 4, 5, 3, 0, 1
        )
        return plane_inverse(grouped[:, 0], grouped[:, 1], cos_x, sin_x, cos_y, sin_y)

    zero_rim = ((0, 0), (0, 0), (0, 0), (1, 1), (1, 1))
    padded = jnp.pad(rim_planes(feats), zero_rim)
    smooth = stencil(padded, taps, False).astype(jnp.bfloat16)
    local_part = moving * jnp.einsum(
        "sczxy,co->sozxy", smooth, point_weight, preferred_element_type=jnp.float32
    )
    spec_real, spec_imag = to_modes(feats.astype(jnp.float32))
    spec_real = spec_real / cell_scale
    spec_imag = spec_imag / cell_scale
    mixed_real = jnp.einsum("pskc,pkco->psko", spec_real, w_real, precision=HIGHEST) - jnp.einsum(
        "pskc,pkco->psko", spec_imag, w_imag, precision=HIGHEST
    )
    mixed_imag = jnp.einsum("pskc,pkco->psko", spec_real, w_imag, precision=HIGHEST) + jnp.einsum(
        "pskc,pkco->psko", spec_imag, w_real, precision=HIGHEST
    )
    spectral = from_modes(mixed_real, mixed_imag) / mode_scale
    pre = spectral + local_part + bias[None, :, None, None, None]
    gate = jax.nn.sigmoid(pre)
    delta = (cotangent.astype(jnp.float32) * gate * (1.0 + pre * (1.0 - gate))).astype(jnp.bfloat16)
    dual_real, dual_imag = to_modes(delta.astype(jnp.float32))
    dual_real = dual_real / mode_scale
    dual_imag = dual_imag / mode_scale
    batch_total = samples_here * lax.axis_size("dp")
    grad_real = jnp.einsum("pskc,psko->pkco", spec_real, dual_real, precision=HIGHEST) + jnp.einsum(
        "pskc,psko->pkco", spec_imag, dual_imag, precision=HIGHEST
    )
    grad_imag = jnp.einsum("pskc,psko->pkco", spec_real, dual_imag, precision=HIGHEST) - jnp.einsum(
        "pskc,psko->pkco", spec_imag, dual_real, precision=HIGHEST
    )
    grad_terms = (jnp.stack([grad_real, grad_imag], axis=2) / batch_total).reshape(
        mode_rows, KZ, 2 * channels * channels
    )
    grad_spec = lax.psum_scatter(
        grad_terms.astype(jnp.bfloat16), "dp", scatter_dimension=2, tiled=True
    ).astype(jnp.float32)
    back_real = jnp.einsum("psko,pkco->pskc", dual_real, w_real, precision=HIGHEST) + jnp.einsum(
        "psko,pkco->pskc", dual_imag, w_imag, precision=HIGHEST
    )
    back_imag = jnp.einsum("psko,pkco->pskc", dual_imag, w_real, precision=HIGHEST) - jnp.einsum(
        "psko,pkco->pskc", dual_real, w_imag, precision=HIGHEST
    )
    spectral_back = from_modes(back_real, back_imag) / cell_scale
    spread = (
        moving
        * jnp.einsum("sozxy,co->sczxy", delta, point_weight, preferred_element_type=jnp.float32)
    ).astype(jnp.bfloat16)
    spread_padded = jnp.pad(rim_planes(spread), zero_rim)
    local_back = stencil(spread_padded, taps, True)
    grad_feats = (spectral_back + local_back).astype(jnp.bfloat16)
    return (grad_feats, grad_spec)


def frequencies(count, length):
    index = np.arange(count)
    return np.where(index < count // 2, index, length - count + index)


def angles(count, length):
    phases = np.outer(frequencies(count, length), np.arange(length)) % length
    return phases * (2.0 * np.pi / length)


def constant(array):
    return jnp.asarray(np.asarray(array, np.float32).astype(ml_dtypes.bfloat16))


def forward_x_table(slabs, split):
    a = angles(KX, NX).reshape(slabs, KX // slabs, NX)
    trig = np.stack([np.cos(a), np.sin(a)])
    table = np.einsum("tsjx,cd->tscjdx", trig, np.eye(2)).reshape(-1, 2, NX // 8, 8)
    if split:
        table = table.transpose(0, 2, 1, 3)
    return table.reshape(4 * KX, 2 * NX)


def forward_y_table(planes):
    a = angles(KY, NY)
    cos, sin = np.cos(a).T, np.sin(a).T
    block = np.stack([np.stack([cos, -sin], 1), np.stack([-sin, -cos], 1)])
    pick = np.eye(planes).reshape(planes // 2, 2, planes)
    table = np.einsum("pqz,tyrk->ptqyzrk", pick, block)
    return table.reshape(planes * 2 * NY, planes * 2 * KY)


def forward_z_table():
    a = angles(KZ, NZ)
    cos, sin = np.cos(a).T, np.sin(a).T
    block = np.stack([np.stack([cos, -sin], 1), np.stack([sin, cos], 1)], 1)
    table = np.einsum("zrqm,kl->zrkqlm", block, np.eye(KY))
    return table.reshape(NZ * 2 * KY, 2 * KY * KZ)


def inverse_z_table():
    a = angles(KZ, NZ)
    cos, sin = np.cos(a), np.sin(a)
    block = np.stack([np.stack([cos, sin], 2), np.stack([-sin, cos], 2)])
    table = np.einsum("rmzq,kl->rkmzql", block, np.eye(KY))
    return table.reshape(2 * KY * KZ, NZ * 2 * KY)


def inverse_y_table(planes, group):
    a = angles(KY, NY)
    cos, sin = np.cos(a), np.sin(a)
    block = np.stack([np.stack([cos, -sin], 1), np.stack([-sin, -cos], 1)])
    pick = np.eye(planes).reshape(planes // group, group, planes)
    table = np.einsum("pqz,rkty->pzrktqy", pick, block)
    return table.reshape(planes // group, planes * 2 * KY, 2 * group * NY)


def inverse_x_table(slabs, group):
    a = angles(KX, NX).reshape(slabs, KX // slabs, NX)
    trig = np.stack([np.cos(a), np.sin(a)])
    table = np.einsum("tsjx,cd->cxstdj", trig, np.eye(group))
    return table.reshape(group * NX, 2 * KX * group)


def first_table(channels, depth):
    table = np.einsum("ac,j,b->ajcb", np.eye(channels), np.ones(depth), np.ones(channels))
    return table.reshape(channels * depth, channels * channels)


def second_table(channels, depth):
    table = np.einsum("ac,j,b->ajbc", np.eye(channels), np.ones(depth), np.ones(channels))
    return table.reshape(channels * depth, channels * channels)


LIGHT = pl.CostEstimate(flops=10**7, bytes_accessed=10**5, transcendentals=0)
HEAVY = pl.CostEstimate(flops=10**11, bytes_accessed=10**8, transcendentals=0)


def dot(a, b):
    return jnp.dot(a, b, preferred_element_type=jnp.float32)


def whole(shape):
    return pl.BlockSpec(shape, lambda *_: (0,) * len(shape))


def params(**kw):
    return pltpu.CompilerParams(vmem_limit_bytes=58 * 2**20, **kw)


def store_rows(rows, pair, x_table, load):
    slabs, lines = rows.shape[2:4]
    for i in range(lines // 16):
        parts = [dot(x_table[...], load(2 * i + k)) for k in range(2)]
        for t in range(2):
            for s in range(slabs):
                here = slice(8 * (t * slabs + s), 8 * (t * slabs + s) + 8)
                both = jnp.concatenate([part[here] for part in parts], axis=0)
                rows[pair, t, s, 16 * i : 16 * i + 16, :] = both.astype(jnp.bfloat16)


def store_modes(rows, y_table, out):
    pairs, _, slabs, lines, _ = rows.shape
    left = [
        jnp.concatenate([rows[p, t, s] for p in range(pairs) for t in range(2)], axis=1)
        for s in range(slabs)
    ]
    modes = dot(jnp.concatenate(left, axis=0), y_table[...])
    for s in range(slabs):
        out[s] = modes[s * lines : (s + 1) * lines].astype(jnp.bfloat16)


def rims_kernel(field, *refs):
    rims, done = refs[:4], refs[4]
    half = field.shape[0] // 2
    last = field.shape[1] - 1
    copies = []
    for k in range(4):
        source = field.at[pl.ds(half * (k % 2), half), pl.ds(last * (k // 2), 1)]
        copies.append(pltpu.make_async_copy(source, rims[k], done.at[k]))
    for copy in copies:
        copy.start()
    for copy in copies:
        copy.wait()


def cut_rims(field):
    channels = field.shape[0]
    rim = jax.ShapeDtypeStruct((channels // 2, 1, NX, NY), jnp.bfloat16)
    return pl.pallas_call(
        rims_kernel,
        in_specs=[pl.BlockSpec(memory_space=pl.ANY)],
        out_specs=[pl.BlockSpec(memory_space=pl.ANY)] * 4,
        out_shape=[rim] * 4,
        scratch_shapes=[pltpu.SemaphoreType.DMA((4,))],
        compiler_params=params(),
        cost_estimate=LIGHT,
        name="rims",
    )(field)


def forward_kernel(field, x_table, y_table, out, rows):
    pair = pl.program_id(0)
    pairs = rows.shape[0]

    def load(i):
        halves = [field[2 * i : 2 * i + 2, q].reshape(2 * NX, NY) for q in range(2)]
        return jnp.concatenate(halves, axis=1)

    store_rows(rows, pair, x_table, load)

    @pl.when(pair == pairs - 1)
    def _():
        store_modes(rows, y_table, out)


def forward_modes(field, slabs):
    channels, planes = field.shape[:2]
    lines = channels * (KX // slabs)
    x_table = constant(forward_x_table(slabs, False))
    y_table = constant(forward_y_table(planes))
    shape = (slabs, lines, planes * 2 * KY)
    return pl.pallas_call(
        forward_kernel,
        grid=(planes // 2,),
        in_specs=[
            pl.BlockSpec((channels, 2, NX, NY), lambda p: (0, p, 0, 0)),
            whole(x_table.shape),
            whole(y_table.shape),
        ],
        out_specs=whole(shape),
        out_shape=jax.ShapeDtypeStruct(shape, jnp.bfloat16),
        scratch_shapes=[pltpu.VMEM((planes // 2, 2, slabs, lines, 2 * NY), jnp.bfloat16)],
        compiler_params=params(),
        cost_estimate=LIGHT,
        name="forward_modes",
    )(field, x_table, y_table)


def mixing_kernel(scale_in, scale_out, adjoint, planar, weight, z_in, z_out, spread_table,
                  sum_table, *rest):
    if adjoint:
        partner, out, send, spectrum, total, wide, product = rest
    else:
        spectrum, out, total, wide, product = rest
    step = pl.program_id(0)
    steps = pl.num_programs(0)
    slabs = planar.shape[0]
    width = planar.shape[2]
    half = spectrum.shape[0] // 2
    lanes = weight.shape[1] // 2

    @pl.when(step == 0)
    def _():
        left = jnp.concatenate([planar[s] for s in range(slabs)], axis=1)
        modes = (dot(left, z_in[...]).T * scale_in).astype(jnp.bfloat16)
        spectrum[...] = modes
        total[...] = jnp.zeros_like(total)
        if adjoint:
            send[: 2 * half] = partner[...]
            send[2 * half :] = modes

    lane = lax.broadcasted_iota(jnp.int32, (1, spectrum.shape[1]), 1)
    mine = lane % steps == step
    wide[...] = dot(jnp.where(mine, spectrum[...], 0), spread_table[...])
    block = 32
    tile = wide.shape[1]
    for at in range(0, half, block):
        sums = [0.0, 0.0]
        for column in range(0, lanes, 128):
            here = slice(column, column + 128) if tile == lanes else slice(None)
            real_wide = wide[at : at + block, here]
            imag_wide = wide[half + at : half + at + block, here]
            w_real = weight[at : at + block, column : column + 128].astype(jnp.float32)
            imag_column = lanes + column
            w_imag = weight[at : at + block, imag_column : imag_column + 128].astype(jnp.float32)
            if adjoint:
                real = real_wide * w_real + imag_wide * w_imag
                imag = imag_wide * w_real - real_wide * w_imag
                product[at : at + block, column : column + 128] = real.astype(jnp.bfloat16)
                product[half + at : half + at + block, column : column + 128] = imag.astype(
                    jnp.bfloat16
                )
            else:
                sums[0] = sums[0] + (real_wide * w_real - imag_wide * w_imag)
                sums[1] = sums[1] + (real_wide * w_imag + imag_wide * w_real)
        if not adjoint:
            product[at : at + block] = sums[0].astype(jnp.bfloat16)
            product[half + at : half + at + block] = sums[1].astype(jnp.bfloat16)
    total[...] += jnp.where(mine, dot(product[...], sum_table[...]), 0.0)

    @pl.when(step == steps - 1)
    def _():
        modes = dot((total[...] * scale_out).T.astype(jnp.bfloat16), z_out[...])
        for s in range(slabs):
            out[s] = modes[:, s * width : (s + 1) * width].astype(jnp.bfloat16)


def mix(planar, weight, scale_in, scale_out, partner=None):
    slabs, lines, width = planar.shape
    adjoint = partner is not None
    depth = KX // slabs
    channels = lines // depth
    rows = KY * KZ
    z_in = constant(forward_z_table())
    z_out = constant(inverse_z_table())
    first = first_table(channels, depth)
    second = second_table(channels, depth)
    spread_table = constant(second[:, :128] if adjoint else first)
    sum_table = constant(first.T if adjoint else second[:, :128].T)
    shape = (2 * rows, lines)
    in_specs = [
        whole(planar.shape),
        pl.BlockSpec((rows, weight.shape[1]), lambda j: (j, 0)),
        whole(z_in.shape),
        whole(z_out.shape),
        whole(spread_table.shape),
        whole(sum_table.shape),
    ]
    operands = [planar, weight, z_in, z_out, spread_table, sum_table]
    scratch = [
        pltpu.VMEM(shape, jnp.float32),
        pltpu.VMEM((2 * rows, spread_table.shape[1]), jnp.float32),
        pltpu.VMEM((2 * rows, sum_table.shape[0]), jnp.bfloat16),
    ]
    if adjoint:
        in_specs.append(whole(shape))
        operands.append(partner)
        scratch = [pltpu.VMEM(shape, jnp.bfloat16)] + scratch
        outs = [planar.shape, (2 * shape[0], lines)]
    else:
        outs = [shape, planar.shape]
    return pl.pallas_call(
        functools.partial(mixing_kernel, scale_in, scale_out, adjoint),
        grid=(depth,),
        in_specs=in_specs,
        out_specs=[whole(out) for out in outs],
        out_shape=[jax.ShapeDtypeStruct(out, jnp.bfloat16) for out in outs],
        scratch_shapes=scratch,
        compiler_params=params(),
        cost_estimate=HEAVY,
        name="mix_back" if adjoint else "mix",
    )(*operands)


def plane_mobility(grains):
    same = [
        jnp.concatenate([grains[:1], grains[:-1]], axis=0),
        jnp.concatenate([grains[1:], grains[-1:]], axis=0),
        jnp.concatenate([grains[:, :1], grains[:, :-1]], axis=1),
        jnp.concatenate([grains[:, 1:], grains[:, -1:]], axis=1),
    ]
    total = jnp.full(grains.shape, 0.25, jnp.float32)
    for other in same:
        total = total + jnp.where(grains != other, 0.25, 0.0)
    return total


def layer_kernel(bias, planar, smooth, cotangent, grains, point_weight, repeat, ix_table, iy_table,
                 x_table, y_table, spread, out, first, last, *rest):
    pair = pl.program_id(0)
    waves, spectral, moving, delta, rows, bias_wide, mix_out, mix_in = rest
    pairs = rows.shape[0]
    channels = cotangent.shape[0]
    slabs = planar.shape[0]

    @pl.when(pair == 0)
    def _():
        for c in range(channels):
            bias_wide[c] = jnp.full(bias_wide.shape[1:], 0.5 * bias[c], jnp.float32)
        tall = dot(repeat[...], point_weight[...]).astype(jnp.bfloat16)
        square = lax.dot_general(
            tall, repeat[...], (((1,), (1,)), ((), ())), preferred_element_type=jnp.float32
        )
        row = lax.broadcasted_iota(jnp.int32, square.shape, 0) % 8
        column = lax.broadcasted_iota(jnp.int32, square.shape, 1) % 8
        square = jnp.where(row == column, square, 0.0)
        mix_in[...] = square.astype(jnp.bfloat16)
        mix_out[...] = square.T.astype(jnp.bfloat16)

    lines = planar.shape[1]
    step = jnp.concatenate([planar[s] for s in range(slabs)], axis=0)
    step = dot(step, iy_table[0]).astype(jnp.bfloat16)
    for s in range(slabs):
        for t in range(2):
            waves[s, t] = step[s * lines : (s + 1) * lines, 2 * NY * t : 2 * NY * (t + 1)]
    group = 8 * (KX // slabs)
    for g in range(channels // 8):
        here = slice(g * group, (g + 1) * group)
        wave = [waves[s, t, here, :] for s in range(slabs) for t in range(2)]
        step = dot(ix_table[...], jnp.concatenate(wave, axis=0))
        spectral[8 * g : 8 * g + 8] = step.reshape(8, NX, 2 * NY)
    for q in range(2):
        moving[:, q * NY : (q + 1) * NY] = 0.5 * plane_mobility(grains[q])

    def body(i, _):
        x = pl.multiple_of(16 * i, 16)
        halves = [cotangent[:, q, pl.ds(x, 16), :] for q in range(2)]
        cotangent_here = jnp.concatenate(halves, axis=2).astype(jnp.float32)
        spreads = []
        for h in range(2):
            at = pl.ds(pl.multiple_of(x + 8 * h, 8), 8)
            mobile = moving[at, :][None]
            local = dot(mix_out[...], smooth[0, 2 * i + h]).reshape(channels, 8, 2 * NY)
            half = spectral[:, at, :] + mobile * local + bias_wide[...]
            wave = jnp.tanh(half)
            slope = (1.0 + wave) * (1.0 + (half - half * wave))
            change = cotangent_here[:, 8 * h : 8 * h + 8, :] * slope
            right = change.reshape(8 * channels, 2 * NY).astype(jnp.bfloat16)
            delta[2 * i + h] = right
            back = dot(mix_in[...], right).reshape(channels, 8, 2 * NY)
            spreads.append(mobile * back)
        both = jnp.concatenate(spreads, axis=1).astype(jnp.bfloat16)
        for q in range(2):
            spread[:, q, pl.ds(x, 16), :] = both[:, :, q * NY : (q + 1) * NY]
        return 0

    lax.fori_loop(0, NX // 16, body, 0, unroll=4)


    @pl.when(pair == 0)
    def _():
        first[:, 0] = spread[:, 0]

    @pl.when(pair == pairs - 1)
    def _():
        last[:, 0] = spread[:, 1]

    def load(i):
        return delta[:, 16 * i : 16 * i + 16, :].reshape(2 * NX, 2 * NY)

    store_rows(rows, pair, x_table, load)

    @pl.when(pair == pairs - 1)
    def _():
        store_modes(rows, y_table, out)


def layer(planar, smooth, cotangent, grains, bias, point_weight):
    slabs, lines, width = planar.shape
    channels, planes = cotangent.shape[:2]
    pairs = planes // 2
    repeat = constant(np.repeat(np.eye(channels), 8, axis=0))
    ix_table = constant(inverse_x_table(slabs, 8))
    iy_table = constant(inverse_y_table(planes, 2))
    x_table = constant(forward_x_table(slabs, True))
    y_table = constant(forward_y_table(planes))
    field = pl.BlockSpec((channels, 2, NX, NY), lambda p: (0, p, 0, 0))
    outs = [cotangent.shape, planar.shape] + [(channels, 1, NX, NY)] * 2
    return pl.pallas_call(
        layer_kernel,
        grid=(pairs,),
        in_specs=[
            pl.BlockSpec(memory_space=pltpu.SMEM),
            whole(planar.shape),
            pl.BlockSpec((1,) + smooth.shape[1:], lambda p: (p, 0, 0, 0)),
            field,
            pl.BlockSpec((2, NX, NY), lambda p: (p, 0, 0)),
            whole(point_weight.shape),
            whole(repeat.shape),
            whole(ix_table.shape),
            pl.BlockSpec((1,) + iy_table.shape[1:], lambda p: (p, 0, 0)),
            whole(x_table.shape),
            whole(y_table.shape),
        ],
        out_specs=[field] + [whole(out) for out in outs[1:]],
        out_shape=[jax.ShapeDtypeStruct(out, jnp.bfloat16) for out in outs],
        scratch_shapes=[
            pltpu.VMEM((slabs, 2, lines, 2 * NY), jnp.bfloat16),
            pltpu.VMEM((channels, NX, 2 * NY), jnp.float32),
            pltpu.VMEM((NX, 2 * NY), jnp.float32),
            pltpu.VMEM((NX // 8, 8 * channels, 2 * NY), jnp.bfloat16),
            pltpu.VMEM((pairs, 2, slabs, lines, 2 * NY), jnp.bfloat16),
            pltpu.VMEM((channels, 8, 2 * NY), jnp.float32),
            pltpu.VMEM((8 * channels, 8 * channels), jnp.bfloat16),
            pltpu.VMEM((8 * channels, 8 * channels), jnp.bfloat16),
        ],
        compiler_params=params(),
        cost_estimate=LIGHT,
        name="layer",
    )(bias, planar, smooth, cotangent, grains, point_weight, repeat, ix_table, iy_table, x_table,
      y_table)


def build_band(adjoint, taps, channel, band):
    row = lax.broadcasted_iota(jnp.int32, (8, 128), 0)
    lane = lax.broadcasted_iota(jnp.int32, (8, 128), 1)
    for dy in range(3):
        for q in range(2):
            halves = []
            for side in range(2):
                tile = jnp.zeros((8, 128), jnp.float32)
                for k in range(2):
                    dz = 2 * side + k - q
                    if not 0 <= dz <= 2:
                        continue
                    for dx in range(3):
                        number = 9 * dz + 3 * dx + dy
                        tap = taps[26 - number if adjoint else number, channel]
                        hit = lane == (64 * k + row + (dx - 1)) % 128
                        tile = jnp.where(hit, tap, tile)
                tiles = [pltpu.roll(tile, 8 * k, axis=1) if k > 0 else tile for k in range(8)]
                low = (row == 0) & (lane % 64 == 63)
                high = (row == 7) & (lane % 64 == 0)
                tiles[0] = jnp.where(low, 0.0, tiles[0])
                tiles[7] = jnp.where(high, 0.0, tiles[7])
                halves.append(jnp.concatenate(tiles[1:7] + [tiles[0], tiles[7]], axis=0))
            at = 64 * (2 * dy + q)
            band[at : at + 64, :] = jnp.concatenate(halves, axis=1).astype(jnp.bfloat16)


def apply_band(sheets, band):
    blocks = range(6)
    lefts = [
        band[...],
        jnp.concatenate([band[64 * b : 64 * b + 48, :] for b in blocks], axis=0),
        jnp.concatenate([band[64 * b + 32 : 64 * b + 64, :] for b in blocks], axis=0),
    ]
    lane = lax.broadcasted_iota(jnp.int32, (NX, NY), 1)
    totals = []
    for group in range(0, len(sheets) - 2, 4):
        products = []
        for left, x in zip(lefts, (0, 48, 64)):
            right = [
                jnp.concatenate([sheets[group + 2 * p + k][x : x + 64] for k in range(4)], axis=0)
                for p in range(2)
            ]
            products.append(dot(left, jnp.concatenate(right, axis=1)))
        for p in range(2):
            wide = slice(NY * p, NY * (p + 1))
            pair = []
            for q in range(2):
                shifted = []
                for dy in range(3):
                    b = 2 * dy + q
                    pieces = [
                        products[0][64 * b + 48 : 64 * b + 56, wide],
                        products[0][64 * b : 64 * b + 48, wide],
                        products[1][48 * b : 48 * b + 48, wide],
                        products[2][32 * b : 32 * b + 16, wide],
                        products[2][32 * b + 24 : 32 * b + 32, wide],
                    ]
                    shifted.append(jnp.concatenate(pieces, axis=0))
                before = jnp.where(lane == 0, 0.0, pltpu.roll(shifted[0], 1, axis=1))
                after = jnp.where(lane == NY - 1, 0.0, pltpu.roll(shifted[2], NY - 1, axis=1))
                pair.append(shifted[1] + before + after)
            totals.append(jnp.concatenate(pair, axis=1))
    return totals


def banded(adjoint, taps, start, even, odd, channels):
    step = pl.program_id(0)
    final = start + channels * pl.num_programs(0) - 1
    bands = (even, odd)

    @pl.when(step == 0)
    def _():
        even[...] = jnp.zeros_like(even)
        odd[...] = jnp.zeros_like(odd)
        build_band(adjoint, taps, start, even)

    def run(visit):
        for c in range(channels):
            following = jnp.minimum(start + channels * step + c + 1, final)
            build_band(adjoint, taps, following, bands[(c + 1) % 2])
            visit(c, bands[c % 2])

    return run


def smooth_kernel(start, taps, before, field, after, *rest):
    out, even, odd = rest[-3:]
    planes = field.shape[1]
    totals = []

    def visit(c, band):
        sheets = [before[c, 0]] + [field[c, z] for z in range(planes)] + [after[c, 0]]
        totals.append(apply_band(sheets, band))

    banded(False, taps, start, even, odd, 2)(visit)
    for p in range(planes // 2):
        both = [totals[c][p].reshape(NX // 8, 8, 2 * NY) for c in range(2)]
        out[p] = jnp.concatenate(both, axis=1).astype(jnp.bfloat16)


def smooth_planes(field, rims, taps, done=None):
    channels, planes = field.shape[:2]
    pairs = planes // 2
    start = 0 if done is None else channels // 2
    skip = start // 2
    rim = pl.BlockSpec((2, 1, NX, NY), lambda c: (c, 0, 0, 0))
    sheets = pl.BlockSpec((2, planes, NX, NY), lambda c: (c + skip, 0, 0, 0))
    in_specs = [pl.BlockSpec(memory_space=pltpu.SMEM), rim, sheets, rim]
    operands = [taps, rims[0], field, rims[1]]
    if done is not None:
        in_specs.append(pl.BlockSpec(memory_space=pl.ANY))
        operands.append(done)
    return pl.pallas_call(
        functools.partial(smooth_kernel, start),
        grid=(channels // 4,),
        in_specs=in_specs,
        out_specs=pl.BlockSpec((pairs, NX // 8, 16, 2 * NY), lambda c: (0, 0, c + skip, 0)),
        out_shape=jax.ShapeDtypeStruct((pairs, NX // 8, 8 * channels, 2 * NY), jnp.bfloat16),
        input_output_aliases={} if done is None else {4: 0},
        scratch_shapes=[pltpu.VMEM((6 * 64, 4 * 64), jnp.bfloat16) for _ in range(2)],
        compiler_params=params(),
        cost_estimate=LIGHT,
        name="smooth_low" if done is None else "smooth_high",
    )(*operands)


def finish_kernel(taps, before, field, after, planar, ix_table, iy_table, out, waves, even, odd):
    step = pl.program_id(0)
    slabs, lines = planar.shape[:2]
    planes = field.shape[1]
    span = planes * NY

    @pl.when(step == 0)
    def _():
        left = jnp.concatenate([planar[s] for s in range(slabs)], axis=0)
        for t in range(2):
            wave = dot(left, iy_table[0, :, t * span : (t + 1) * span]).astype(jnp.bfloat16)
            for s in range(slabs):
                waves[s, t] = wave[s * lines : (s + 1) * lines]

    rows = 4 * (KX // slabs)
    here = pl.ds(pl.multiple_of(rows * step, rows), rows)
    right = [waves[s, t, here, :] for s in range(slabs) for t in range(2)]
    right = jnp.concatenate(right, axis=0)
    far = [
        dot(ix_table[...], right[:, 2 * p * NY : 2 * (p + 1) * NY]) for p in range(planes // 2)
    ]

    def visit(c, band):
        sheets = [before[c, 0]] + [field[c, z] for z in range(planes)] + [after[c, 0]]
        for p, near in enumerate(apply_band(sheets, band)):
            total = (near + far[p][c * NX : (c + 1) * NX]).astype(jnp.bfloat16)
            out[c, 2 * p] = total[:, :NY]
            out[c, 2 * p + 1] = total[:, NY:]

    banded(True, taps, 0, even, odd, 4)(visit)


def finish(planar, spread, rims, taps):
    slabs, lines, width = planar.shape
    channels, planes = spread.shape[:2]
    ix_table = constant(inverse_x_table(slabs, 4))
    iy_table = constant(inverse_y_table(planes, planes))
    rim = pl.BlockSpec((4, 1, NX, NY), lambda c: (c, 0, 0, 0))
    sheets = pl.BlockSpec((4, planes, NX, NY), lambda c: (c, 0, 0, 0))
    return pl.pallas_call(
        finish_kernel,
        grid=(channels // 4,),
        in_specs=[
            pl.BlockSpec(memory_space=pltpu.SMEM),
            rim,
            sheets,
            rim,
            whole(planar.shape),
            whole(ix_table.shape),
            whole(iy_table.shape),
        ],
        out_specs=sheets,
        out_shape=jax.ShapeDtypeStruct(spread.shape, jnp.bfloat16),
        scratch_shapes=[
            pltpu.VMEM((slabs, 2, lines, planes * NY), jnp.bfloat16),
            pltpu.VMEM((6 * 64, 4 * 64), jnp.bfloat16),
            pltpu.VMEM((6 * 64, 4 * 64), jnp.bfloat16),
        ],
        compiler_params=params(),
        cost_estimate=HEAVY,
        name="finish",
    )(taps, rims[0], spread, rims[1], planar, ix_table, iy_table)


def gradient_kernel(depth, where, gathered, first, second, out):
    step = pl.program_id(0)
    samples, rows, lines = gathered.shape
    half = rows // 4
    lane = lax.broadcasted_iota(jnp.int32, (1, lines), 1)
    mine = lane % depth == step
    spectra = [gathered[s, : 2 * half] for s in range(samples)]
    duals = []
    for s in range(samples):
        real = gathered[s, 2 * half : 3 * half]
        imag = gathered[s, 3 * half :]
        duals.append(jnp.where(where[0] == 0, real, imag))
        duals.append(jnp.where(where[0] == 0, imag, -real))
    spectra = jnp.where(mine, jnp.concatenate(spectra, axis=0), 0)
    duals = jnp.where(mine, jnp.concatenate(duals, axis=0), 0)
    wide = dot(duals, second[...])
    for column in range(0, out.shape[1], 256):
        product = dot(spectra, first[0, :, column : column + 256])
        for at in range(0, 256, 128):
            total = 0.0
            for s in range(2 * samples):
                here = slice(s * half, (s + 1) * half)
                total = total + product[here, at : at + 128] * wide[here]
            out[:, column + at : column + at + 128] = total * (1.0 / samples)


def weight_gradient(gathered, depth, width, index):
    samples, rows, lines = gathered.shape
    channels = lines // depth
    square = channels * channels
    cuts = square // width
    first = first_table(channels, depth).reshape(lines, cuts, width).transpose(1, 0, 2)
    first = constant(first)
    second = constant(second_table(channels, depth)[:, :128])
    where = jnp.stack([index // cuts, index % cuts]).astype(jnp.int32)
    half = rows // 4
    return pl.pallas_call(
        functools.partial(gradient_kernel, depth),
        grid_spec=pltpu.PrefetchScalarGridSpec(
            num_scalar_prefetch=1,
            grid=(depth,),
            in_specs=[
                pl.BlockSpec(gathered.shape, lambda j, w: (0, 0, 0)),
                pl.BlockSpec((1, lines, width), lambda j, w: (w[1], 0, 0)),
                pl.BlockSpec(second.shape, lambda j, w: (0, 0)),
            ],
            out_specs=pl.BlockSpec((half, width), lambda j, w: (j, 0)),
        ),
        out_shape=jax.ShapeDtypeStruct((depth * half, width), jnp.float32),
        compiler_params=params(),
        cost_estimate=LIGHT,
        name="weight_gradient",
    )(where, gathered, first, second)


def exchange(first, last):
    size = lax.axis_size("slab")
    up = [(i, i + 1) for i in range(size - 1)]
    down = [(j, i) for i, j in up]
    return lax.ppermute(last, "slab", up), lax.ppermute(first, "slab", down)


def swap(planar):
    return lax.all_to_all(planar, "slab", split_axis=0, concat_axis=0)


def local_fast(feats, grains, spec_weight, taps, point_weight, bias, cotangent):
    slabs = lax.axis_size("slab")
    copies = lax.axis_size("dp")
    barrier = lax.optimization_barrier
    field = feats[0]
    channels = field.shape[0]
    cell_scale = 1.0 / math.sqrt(NX * NY * NZ)
    mode_scale = 1.0 / math.sqrt(KX * KY * KZ)
    mode_rows = spec_weight.shape[0]
    weight = spec_weight.reshape(mode_rows * KZ, 2 * channels * channels)
    width = weight.shape[1] // copies

    first, first_high, last, last_high = cut_rims(field)
    rims = exchange(first, last)
    planar = swap(forward_modes(field, slabs))
    rims, first, last = barrier((rims, first_high, last_high))
    rims_high = exchange(first, last)
    planar, smooth = barrier((planar, smooth_planes(field, rims, taps)))
    spectrum, planar = mix(planar, weight, cell_scale, 0.5 * mode_scale)
    smooth, spectrum = barrier((smooth, spectrum))
    planar = swap(planar)
    smooth = smooth_planes(field, rims_high, taps, smooth)
    spread, planar, first, last = layer(planar, smooth, cotangent[0], grains[0], bias, point_weight)
    rims = exchange(first, last)
    planar, send = mix(swap(planar), weight, 0.5 * mode_scale, cell_scale, spectrum)
    planar = swap(planar)
    gathered = lax.all_gather(send, "dp")
    grad_spec = weight_gradient(gathered, KX // slabs, width, lax.axis_index("dp"))
    planar, grad_spec = barrier((planar, grad_spec))
    grad_feats = finish(planar, spread, rims, taps)[None]
    return (grad_feats, grad_spec.reshape(mode_rows, KZ, width))


def local(feats, grains, spec_weight, taps, point_weight, bias, cotangent):
    samples, channels, planes = feats.shape[:3]
    width = spec_weight.shape[2] // lax.axis_size("dp")
    fits = (
        lax.axis_size("slab") * 4 == KX
        and samples == 1
        and channels == 32
        and planes == 8
        and channels * channels % width == 0
        and width % 128 == 0
    )
    form = local_fast if fits else local_any
    return form(feats, grains, spec_weight, taps, point_weight, bias, cotangent)


def solution(mesh):
    in_specs = (
        P(("grp", "dp"), None, "slab", None, None),
        P(("grp", "dp"), "slab", None, None),
        P("slab", None, None),
        P(),
        P(),
        P(),
        P(("grp", "dp"), None, "slab", None, None),
    )
    out_specs = (P(("grp", "dp"), None, "slab", None, None), P("slab", "grp", "dp"))
    return jax.shard_map(local, mesh=mesh, in_specs=in_specs, out_specs=out_specs, check_vma=False)
```

```python
import functools
import math

import jax
import jax.numpy as jnp
import ml_dtypes
import numpy as np
from jax import lax
from jax.experimental import pallas as pl
from jax.experimental.pallas import tpu as pltpu
from jax.sharding import PartitionSpec as P

NX = 128
NY = 128
NZ = 32
KX = 16
KY = 16
KZ = 16


HIGHEST = lax.Precision.HIGHEST


def extended(shard, sides, width):
    for axis, dim in sides:
        size, length = (lax.axis_size(axis), shard.shape[dim])
        up = [(i, (i + 1) % size) for i in range(size - 1)]
        down = [(j, i) for i, j in up]
        last = lax.slice_in_dim(shard, length - width, length, axis=dim)
        first = lax.slice_in_dim(shard, 0, width, axis=dim)
        before = lax.ppermute(last, axis, up)
        after = lax.ppermute(first, axis, down)
        shard = jnp.concatenate([before, shard, after], axis=dim)
    return shard


def tables(count, length, span):
    indices = jnp.arange(count, dtype=jnp.int32)
    frequency = jnp.where(indices < count // 2, indices, length - count + indices)
    position = jnp.arange(span, dtype=jnp.int32)
    phases = frequency[:, None] * position[None, :] % length
    angles = phases.astype(jnp.float32) * (2.0 * math.pi / length)
    return (jnp.cos(angles), jnp.sin(angles))


def mobility(grains):
    leading = [(0, 0)] * (grains.ndim - 2)
    along_x = (grains[..., 1:, :] != grains[..., :-1, :]).astype(jnp.float32)
    along_y = (grains[..., :, 1:] != grains[..., :, :-1]).astype(jnp.float32)
    differ = jnp.pad(along_x, leading + [(1, 0), (0, 0)]) + jnp.pad(
        along_x, leading + [(0, 1), (0, 0)]
    )
    differ = (
        differ
        + jnp.pad(along_y, leading + [(0, 0), (1, 0)])
        + jnp.pad(along_y, leading + [(0, 0), (0, 1)])
    )
    return 0.25 * (1.0 + differ)


def stencil(padded, taps, adjoint):
    planes = padded.shape[-3] - 2
    rows_x = padded.shape[-2] - 2
    rows_y = padded.shape[-1] - 2
    total = jnp.zeros(padded.shape[:-3] + (planes, rows_x, rows_y), jnp.float32)
    for offset in range(27):
        shift_z, shift_x, shift_y = (offset // 9, offset // 3 % 3, offset % 3)
        if adjoint:
            shift_z, shift_x, shift_y = (2 - shift_z, 2 - shift_x, 2 - shift_y)
        window = padded[
            ..., shift_z : shift_z + planes, shift_x : shift_x + rows_x, shift_y : shift_y + rows_y
        ]
        total = total + taps[offset][:, None, None, None] * window.astype(jnp.float32)
    return total


def plane_forward(field, cos_x, sin_x, cos_y, sin_y):
    real_y = jnp.einsum("...xy,ky->...xk", field, cos_y, precision=HIGHEST)
    imag_y = -jnp.einsum("...xy,ky->...xk", field, sin_y, precision=HIGHEST)
    real_part = jnp.einsum("...xk,jx->...jk", real_y, cos_x, precision=HIGHEST) + jnp.einsum(
        "...xk,jx->...jk", imag_y, sin_x, precision=HIGHEST
    )
    imag_part = jnp.einsum("...xk,jx->...jk", imag_y, cos_x, precision=HIGHEST) - jnp.einsum(
        "...xk,jx->...jk", real_y, sin_x, precision=HIGHEST
    )
    return (real_part, imag_part)


def plane_inverse(real_part, imag_part, cos_x, sin_x, cos_y, sin_y):
    real_x = jnp.einsum("...jk,jx->...xk", real_part, cos_x, precision=HIGHEST) - jnp.einsum(
        "...jk,jx->...xk", imag_part, sin_x, precision=HIGHEST
    )
    imag_x = jnp.einsum("...jk,jx->...xk", imag_part, cos_x, precision=HIGHEST) + jnp.einsum(
        "...jk,jx->...xk", real_part, sin_x, precision=HIGHEST
    )
    return jnp.einsum("...xk,ky->...xy", real_x, cos_y, precision=HIGHEST) - jnp.einsum(
        "...xk,ky->...xy", imag_x, sin_y, precision=HIGHEST
    )


def depth_forward(packed, cos_table, sin_table):
    width = packed.shape[-1] // 2
    real_in = packed[..., :width]
    imag_in = packed[..., width:]
    real_out = jnp.einsum("pszc,kz->pskc", real_in, cos_table, precision=HIGHEST) + jnp.einsum(
        "pszc,kz->pskc", imag_in, sin_table, precision=HIGHEST
    )
    imag_out = jnp.einsum("pszc,kz->pskc", imag_in, cos_table, precision=HIGHEST) - jnp.einsum(
        "pszc,kz->pskc", real_in, sin_table, precision=HIGHEST
    )
    return jnp.concatenate([real_out, imag_out], axis=-1)


def depth_inverse(real_modes, imag_modes, cos_table, sin_table):
    real_out = jnp.einsum("pskc,kz->pszc", real_modes, cos_table, precision=HIGHEST) - jnp.einsum(
        "pskc,kz->pszc", imag_modes, sin_table, precision=HIGHEST
    )
    imag_out = jnp.einsum("pskc,kz->pszc", imag_modes, cos_table, precision=HIGHEST) + jnp.einsum(
        "pskc,kz->pszc", real_modes, sin_table, precision=HIGHEST
    )
    return jnp.concatenate([real_out, imag_out], axis=-1)


def rim_planes(field):
    return extended(field, (("slab", 2),), 1)


def local_any(feats, grains, spec_weight, taps, point_weight, bias, cotangent):
    samples_here = feats.shape[0]
    channels = feats.shape[1]
    planes = feats.shape[2]
    cos_x, sin_x = tables(KX, NX, NX)
    cos_y, sin_y = tables(KY, NY, NY)
    cos_full, sin_full = tables(KZ, NZ, NZ)
    cell_scale = math.sqrt(NX * NY * NZ)
    mode_scale = math.sqrt(KX * KY * KZ)
    mode_rows = spec_weight.shape[0]
    weights = spec_weight.astype(jnp.float32).reshape(mode_rows, KZ, 2, channels, channels)
    w_real = weights[:, :, 0]
    w_imag = weights[:, :, 1]
    moving = mobility(grains)[:, None]

    def to_modes(field):
        real_plane, imag_plane = plane_forward(field, cos_x, sin_x, cos_y, sin_y)
        packed = jnp.stack([real_plane, imag_plane], axis=1)
        packed = packed.transpose(4, 5, 0, 3, 1, 2).reshape(
            KX * KY, samples_here, planes, 2 * channels
        )
        moved = lax.all_to_all(packed, "slab", split_axis=0, concat_axis=2, tiled=True)
        summed = depth_forward(moved, cos_full, sin_full)
        return (summed[..., :channels], summed[..., channels:])

    def from_modes(real_modes, imag_modes):
        planar = depth_inverse(real_modes, imag_modes, cos_full, sin_full)
        packed = lax.all_to_all(planar, "slab", split_axis=2, concat_axis=0, tiled=True)
        grouped = packed.reshape(KX, KY, samples_here, planes, 2, channels).transpose(
            2, 4, 5, 3, 0, 1
        )
        return plane_inverse(grouped[:, 0], grouped[:, 1], cos_x, sin_x, cos_y, sin_y)

    zero_rim = ((0, 0), (0, 0), (0, 0), (1, 1), (1, 1))
    padded = jnp.pad(rim_planes(feats), zero_rim)
    smooth = stencil(padded, taps, False).astype(jnp.bfloat16)
    local_part = moving * jnp.einsum(
        "sczxy,co->sozxy", smooth, point_weight, preferred_element_type=jnp.float32
    )
    spec_real, spec_imag = to_modes(feats.astype(jnp.float32))
    spec_real = spec_real / cell_scale
    spec_imag = spec_imag / cell_scale
    mixed_real = jnp.einsum("pskc,pkco->psko", spec_real, w_real, precision=HIGHEST) - jnp.einsum(
        "pskc,pkco->psko", spec_imag, w_imag, precision=HIGHEST
    )
    mixed_imag = jnp.einsum("pskc,pkco->psko", spec_real, w_imag, precision=HIGHEST) + jnp.einsum(
        "pskc,pkco->psko", spec_imag, w_real, precision=HIGHEST
    )
    spectral = from_modes(mixed_real, mixed_imag) / mode_scale
    pre = spectral + local_part + bias[None, :, None, None, None]
    gate = jax.nn.sigmoid(pre)
    delta = (cotangent.astype(jnp.float32) * gate * (1.0 + pre * (1.0 - gate))).astype(jnp.bfloat16)
    dual_real, dual_imag = to_modes(delta.astype(jnp.float32))
    dual_real = dual_real / mode_scale
    dual_imag = dual_imag / mode_scale
    batch_total = samples_here * lax.axis_size("dp")
    grad_real = jnp.einsum("pskc,psko->pkco", spec_real, dual_real, precision=HIGHEST) + jnp.einsum(
        "pskc,psko->pkco", spec_imag, dual_imag, precision=HIGHEST
    )
    grad_imag = jnp.einsum("pskc,psko->pkco", spec_real, dual_imag, precision=HIGHEST) - jnp.einsum(
        "pskc,psko->pkco", spec_imag, dual_real, precision=HIGHEST
    )
    grad_terms = (jnp.stack([grad_real, grad_imag], axis=2) / batch_total).reshape(
        mode_rows, KZ, 2 * channels * channels
    )
    grad_spec = lax.psum_scatter(
        grad_terms.astype(jnp.bfloat16), "dp", scatter_dimension=2, tiled=True
    ).astype(jnp.float32)
    back_real = jnp.einsum("psko,pkco->pskc", dual_real, w_real, precision=HIGHEST) + jnp.einsum(
        "psko,pkco->pskc", dual_imag, w_imag, precision=HIGHEST
    )
    back_imag = jnp.einsum("psko,pkco->pskc", dual_imag, w_real, precision=HIGHEST) - jnp.einsum(
        "psko,pkco->pskc", dual_real, w_imag, precision=HIGHEST
    )
    spectral_back = from_modes(back_real, back_imag) / cell_scale
    spread = (
        moving
        * jnp.einsum("sozxy,co->sczxy", delta, point_weight, preferred_element_type=jnp.float32)
    ).astype(jnp.bfloat16)
    spread_padded = jnp.pad(rim_planes(spread), zero_rim)
    local_back = stencil(spread_padded, taps, True)
    grad_feats = (spectral_back + local_back).astype(jnp.bfloat16)
    return (grad_feats, grad_spec)


def frequencies(count, length):
    index = np.arange(count)
    return np.where(index < count // 2, index, length - count + index)


def angles(count, length):
    phases = np.outer(frequencies(count, length), np.arange(length)) % length
    return phases * (2.0 * np.pi / length)


def constant(array):
    return jnp.asarray(np.asarray(array, np.float32).astype(ml_dtypes.bfloat16))


def forward_x_table(slabs, split):
    a = angles(KX, NX).reshape(slabs, KX // slabs, NX)
    trig = np.stack([np.cos(a), np.sin(a)])
    table = np.einsum("tsjx,cd->tscjdx", trig, np.eye(2)).reshape(-1, 2, NX // 8, 8)
    if split:
        table = table.transpose(0, 2, 1, 3)
    return table.reshape(4 * KX, 2 * NX)


def forward_y_table(planes):
    a = angles(KY, NY)
    cos, sin = np.cos(a).T, np.sin(a).T
    block = np.stack([np.stack([cos, -sin], 1), np.stack([-sin, -cos], 1)])
    pick = np.eye(planes).reshape(planes // 2, 2, planes)
    table = np.einsum("pqz,tyrk->ptqyzrk", pick, block)
    return table.reshape(planes * 2 * NY, planes * 2 * KY)


def forward_z_table():
    a = angles(KZ, NZ)
    cos, sin = np.cos(a).T, np.sin(a).T
    block = np.stack([np.stack([cos, -sin], 1), np.stack([sin, cos], 1)], 1)
    table = np.einsum("zrqm,kl->zrkqlm", block, np.eye(KY))
    return table.reshape(NZ * 2 * KY, 2 * KY * KZ)


def inverse_z_table():
    a = angles(KZ, NZ)
    cos, sin = np.cos(a), np.sin(a)
    block = np.stack([np.stack([cos, sin], 2), np.stack([-sin, cos], 2)])
    table = np.einsum("rmzq,kl->rkmzql", block, np.eye(KY))
    return table.reshape(2 * KY * KZ, NZ * 2 * KY)


def inverse_y_table(planes, group):
    a = angles(KY, NY)
    cos, sin = np.cos(a), np.sin(a)
    block = np.stack([np.stack([cos, -sin], 1), np.stack([-sin, -cos], 1)])
    pick = np.eye(planes).reshape(planes // group, group, planes)
    table = np.einsum("pqz,rkty->pzrktqy", pick, block)
    return table.reshape(planes // group, planes * 2 * KY, 2 * group * NY)


def inverse_x_table(slabs, group):
    a = angles(KX, NX).reshape(slabs, KX // slabs, NX)
    trig = np.stack([np.cos(a), np.sin(a)])
    table = np.einsum("tsjx,cd->cxstdj", trig, np.eye(group))
    return table.reshape(group * NX, 2 * KX * group)


def first_table(channels, depth):
    table = np.einsum("ac,j,b->ajcb", np.eye(channels), np.ones(depth), np.ones(channels))
    return table.reshape(channels * depth, channels * channels)


def second_table(channels, depth):
    table = np.einsum("ac,j,b->ajbc", np.eye(channels), np.ones(depth), np.ones(channels))
    return table.reshape(channels * depth, channels * channels)


LIGHT = pl.CostEstimate(flops=10**7, bytes_accessed=10**5, transcendentals=0)
HEAVY = pl.CostEstimate(flops=10**11, bytes_accessed=10**8, transcendentals=0)


def dot(a, b):
    return jnp.dot(a, b, preferred_element_type=jnp.float32)


def whole(shape):
    return pl.BlockSpec(shape, lambda *_: (0,) * len(shape))


def params(**kw):
    return pltpu.CompilerParams(vmem_limit_bytes=58 * 2**20, **kw)


def store_rows(rows, pair, x_table, load):
    slabs, lines = rows.shape[2:4]
    for i in range(lines // 16):
        parts = [dot(x_table[...], load(2 * i + k)) for k in range(2)]
        for t in range(2):
            for s in range(slabs):
                here = slice(8 * (t * slabs + s), 8 * (t * slabs + s) + 8)
                both = jnp.concatenate([part[here] for part in parts], axis=0)
                rows[pair, t, s, 16 * i : 16 * i + 16, :] = both.astype(jnp.bfloat16)


def store_modes(rows, y_table, out):
    pairs, _, slabs, lines, _ = rows.shape
    left = [
        jnp.concatenate([rows[p, t, s] for p in range(pairs) for t in range(2)], axis=1)
        for s in range(slabs)
    ]
    modes = dot(jnp.concatenate(left, axis=0), y_table[...])
    for s in range(slabs):
        out[s] = modes[s * lines : (s + 1) * lines].astype(jnp.bfloat16)


def rims_kernel(low, high, *rims):
    step = pl.program_id(0)
    half = pl.num_programs(0) // 2
    for k, source in enumerate((low, high)):

        @pl.when(step < half)
        def _():
            rims[2 * k][...] = source[...]

        @pl.when(step >= half)
        def _():
            rims[2 * k + 1][...] = source[...]


def cut_rims(field):
    channels, planes = field.shape[:2]
    steps = 4
    rim = jax.ShapeDtypeStruct((channels // 2, 1, NX, NY), jnp.bfloat16)
    block = (channels // steps, 1, NX, NY)
    outs = [
        pl.BlockSpec(block, lambda c: (jnp.minimum(c, steps // 2 - 1), 0, 0, 0)),
        pl.BlockSpec(block, lambda c: (jnp.maximum(c - steps // 2, 0), 0, 0, 0)),
    ]
    return pl.pallas_call(
        rims_kernel,
        grid=(steps,),
        in_specs=[
            pl.BlockSpec(block, lambda c: (c, 0, 0, 0)),
            pl.BlockSpec(block, lambda c: (c, planes - 1, 0, 0)),
        ],
        out_specs=outs + outs,
        out_shape=[rim] * 4,
        compiler_params=params(),
        cost_estimate=LIGHT,
        name="rims",
    )(field, field)


def forward_kernel(field, x_table, y_table, out, rows):
    pair = pl.program_id(0)
    pairs = rows.shape[0]

    def load(i):
        halves = [field[2 * i : 2 * i + 2, q].reshape(2 * NX, NY) for q in range(2)]
        return jnp.concatenate(halves, axis=1)

    store_rows(rows, pair, x_table, load)

    @pl.when(pair == pairs - 1)
    def _():
        store_modes(rows, y_table, out)


def forward_modes(field, slabs):
    channels, planes = field.shape[:2]
    lines = channels * (KX // slabs)
    x_table = constant(forward_x_table(slabs, False))
    y_table = constant(forward_y_table(planes))
    shape = (slabs, lines, planes * 2 * KY)
    return pl.pallas_call(
        forward_kernel,
        grid=(planes // 2,),
        in_specs=[
            pl.BlockSpec((channels, 2, NX, NY), lambda p: (0, p, 0, 0)),
            whole(x_table.shape),
            whole(y_table.shape),
        ],
        out_specs=whole(shape),
        out_shape=jax.ShapeDtypeStruct(shape, jnp.bfloat16),
        scratch_shapes=[pltpu.VMEM((planes // 2, 2, slabs, lines, 2 * NY), jnp.bfloat16)],
        compiler_params=params(),
        cost_estimate=LIGHT,
        name="forward_modes",
    )(field, x_table, y_table)


def mixing_kernel(scale_in, scale_out, adjoint, planar, weight, z_in, z_out, spread_table,
                  sum_table, *rest):
    if adjoint:
        partner, out, send, spectrum, total, wide, product = rest
    else:
        spectrum, out, total, wide, product = rest
    step = pl.program_id(0)
    steps = pl.num_programs(0)
    slabs = planar.shape[0]
    width = planar.shape[2]
    half = spectrum.shape[0] // 2
    lanes = weight.shape[1] // 2

    @pl.when(step == 0)
    def _():
        left = jnp.concatenate([planar[s] for s in range(slabs)], axis=1)
        modes = (dot(left, z_in[...]).T * scale_in).astype(jnp.bfloat16)
        spectrum[...] = modes
        total[...] = jnp.zeros_like(total)
        if adjoint:
            send[: 2 * half] = partner[...]
            send[2 * half :] = modes

    lane = lax.broadcasted_iota(jnp.int32, (1, spectrum.shape[1]), 1)
    mine = lane % steps == step
    wide[...] = dot(jnp.where(mine, spectrum[...], 0), spread_table[...])
    block = 32
    tile = wide.shape[1]
    for at in range(0, half, block):
        sums = [0.0, 0.0]
        for column in range(0, lanes, 128):
            here = slice(column, column + 128) if tile == lanes else slice(None)
            real_wide = wide[at : at + block, here]
            imag_wide = wide[half + at : half + at + block, here]
            w_real = weight[at : at + block, column : column + 128].astype(jnp.float32)
            imag_column = lanes + column
            w_imag = weight[at : at + block, imag_column : imag_column + 128].astype(jnp.float32)
            if adjoint:
                real = real_wide * w_real + imag_wide * w_imag
                imag = imag_wide * w_real - real_wide * w_imag
                product[at : at + block, column : column + 128] = real.astype(jnp.bfloat16)
                product[half + at : half + at + block, column : column + 128] = imag.astype(
                    jnp.bfloat16
                )
            else:
                sums[0] = sums[0] + (real_wide * w_real - imag_wide * w_imag)
                sums[1] = sums[1] + (real_wide * w_imag + imag_wide * w_real)
        if not adjoint:
            product[at : at + block] = sums[0].astype(jnp.bfloat16)
            product[half + at : half + at + block] = sums[1].astype(jnp.bfloat16)
    total[...] += jnp.where(mine, dot(product[...], sum_table[...]), 0.0)

    @pl.when(step == steps - 1)
    def _():
        modes = dot((total[...] * scale_out).T.astype(jnp.bfloat16), z_out[...])
        for s in range(slabs):
            out[s] = modes[:, s * width : (s + 1) * width].astype(jnp.bfloat16)


def mix(planar, weight, scale_in, scale_out, partner=None):
    slabs, lines, width = planar.shape
    adjoint = partner is not None
    depth = KX // slabs
    channels = lines // depth
    rows = KY * KZ
    z_in = constant(forward_z_table())
    z_out = constant(inverse_z_table())
    first = first_table(channels, depth)
    second = second_table(channels, depth)
    spread_table = constant(second[:, :128] if adjoint else first)
    sum_table = constant(first.T if adjoint else second[:, :128].T)
    shape = (2 * rows, lines)
    in_specs = [
        whole(planar.shape),
        pl.BlockSpec((rows, weight.shape[1]), lambda j: (j, 0)),
        whole(z_in.shape),
        whole(z_out.shape),
        whole(spread_table.shape),
        whole(sum_table.shape),
    ]
    operands = [planar, weight, z_in, z_out, spread_table, sum_table]
    scratch = [
        pltpu.VMEM(shape, jnp.float32),
        pltpu.VMEM((2 * rows, spread_table.shape[1]), jnp.float32),
        pltpu.VMEM((2 * rows, sum_table.shape[0]), jnp.bfloat16),
    ]
    if adjoint:
        in_specs.append(whole(shape))
        operands.append(partner)
        scratch = [pltpu.VMEM(shape, jnp.bfloat16)] + scratch
        outs = [planar.shape, (2 * shape[0], lines)]
    else:
        outs = [shape, planar.shape]
    return pl.pallas_call(
        functools.partial(mixing_kernel, scale_in, scale_out, adjoint),
        grid=(depth,),
        in_specs=in_specs,
        out_specs=[whole(out) for out in outs],
        out_shape=[jax.ShapeDtypeStruct(out, jnp.bfloat16) for out in outs],
        scratch_shapes=scratch,
        compiler_params=params(),
        cost_estimate=HEAVY,
        name="mix_back" if adjoint else "mix",
    )(*operands)


def plane_mobility(grains):
    same = [
        jnp.concatenate([grains[:1], grains[:-1]], axis=0),
        jnp.concatenate([grains[1:], grains[-1:]], axis=0),
        jnp.concatenate([grains[:, :1], grains[:, :-1]], axis=1),
        jnp.concatenate([grains[:, 1:], grains[:, -1:]], axis=1),
    ]
    total = jnp.full(grains.shape, 0.25, jnp.float32)
    for other in same:
        total = total + jnp.where(grains != other, 0.25, 0.0)
    return total


def layer_kernel(bias, planar, smooth, cotangent, grains, point_weight, repeat, ix_table, iy_table,
                 x_table, y_table, spread, out, first, last, *rest):
    pair = pl.program_id(0)
    waves, spectral, moving, delta, rows, bias_wide, mix_out, mix_in = rest
    pairs = rows.shape[0]
    channels = cotangent.shape[0]
    slabs = planar.shape[0]

    @pl.when(pair == 0)
    def _():
        for c in range(channels):
            bias_wide[c] = jnp.full(bias_wide.shape[1:], 0.5 * bias[c], jnp.float32)
        tall = dot(repeat[...], point_weight[...]).astype(jnp.bfloat16)
        square = lax.dot_general(
            tall, repeat[...], (((1,), (1,)), ((), ())), preferred_element_type=jnp.float32
        )
        row = lax.broadcasted_iota(jnp.int32, square.shape, 0) % 8
        column = lax.broadcasted_iota(jnp.int32, square.shape, 1) % 8
        square = jnp.where(row == column, square, 0.0)
        mix_in[...] = square.astype(jnp.bfloat16)
        mix_out[...] = square.T.astype(jnp.bfloat16)

    lines = planar.shape[1]
    step = jnp.concatenate([planar[s] for s in range(slabs)], axis=0)
    step = dot(step, iy_table[0]).astype(jnp.bfloat16)
    for s in range(slabs):
        for t in range(2):
            waves[s, t] = step[s * lines : (s + 1) * lines, 2 * NY * t : 2 * NY * (t + 1)]
    group = 8 * (KX // slabs)
    for g in range(channels // 8):
        here = slice(g * group, (g + 1) * group)
        wave = [waves[s, t, here, :] for s in range(slabs) for t in range(2)]
        step = dot(ix_table[...], jnp.concatenate(wave, axis=0))
        spectral[8 * g : 8 * g + 8] = step.reshape(8, NX, 2 * NY)
    for q in range(2):
        moving[:, q * NY : (q + 1) * NY] = 0.5 * plane_mobility(grains[q])

    def body(i, _):
        x = pl.multiple_of(16 * i, 16)
        halves = [cotangent[:, q, pl.ds(x, 16), :] for q in range(2)]
        cotangent_here = jnp.concatenate(halves, axis=2).astype(jnp.float32)
        spreads = []
        for h in range(2):
            at = pl.ds(pl.multiple_of(x + 8 * h, 8), 8)
            mobile = moving[at, :][None]
            local = dot(mix_out[...], smooth[0, 2 * i + h]).reshape(channels, 8, 2 * NY)
            half = spectral[:, at, :] + mobile * local + bias_wide[...]
            wave = jnp.tanh(half)
            slope = (1.0 + wave) * (1.0 + (half - half * wave))
            change = cotangent_here[:, 8 * h : 8 * h + 8, :] * slope
            right = change.reshape(8 * channels, 2 * NY).astype(jnp.bfloat16)
            delta[2 * i + h] = right
            back = dot(mix_in[...], right).reshape(channels, 8, 2 * NY)
            spreads.append(mobile * back)
        both = jnp.concatenate(spreads, axis=1).astype(jnp.bfloat16)
        for q in range(2):
            spread[:, q, pl.ds(x, 16), :] = both[:, :, q * NY : (q + 1) * NY]
        return 0

    lax.fori_loop(0, NX // 16, body, 0, unroll=4)


    @pl.when(pair == 0)
    def _():
        first[:, 0] = spread[:, 0]

    @pl.when(pair == pairs - 1)
    def _():
        last[:, 0] = spread[:, 1]

    def load(i):
        return delta[:, 16 * i : 16 * i + 16, :].reshape(2 * NX, 2 * NY)

    store_rows(rows, pair, x_table, load)

    @pl.when(pair == pairs - 1)
    def _():
        store_modes(rows, y_table, out)


def layer(planar, smooth, cotangent, grains, bias, point_weight):
    slabs, lines, width = planar.shape
    channels, planes = cotangent.shape[:2]
    pairs = planes // 2
    repeat = constant(np.repeat(np.eye(channels), 8, axis=0))
    ix_table = constant(inverse_x_table(slabs, 8))
    iy_table = constant(inverse_y_table(planes, 2))
    x_table = constant(forward_x_table(slabs, True))
    y_table = constant(forward_y_table(planes))
    field = pl.BlockSpec((channels, 2, NX, NY), lambda p: (0, p, 0, 0))
    outs = [cotangent.shape, planar.shape] + [(channels, 1, NX, NY)] * 2
    return pl.pallas_call(
        layer_kernel,
        grid=(pairs,),
        in_specs=[
            pl.BlockSpec(memory_space=pltpu.SMEM),
            whole(planar.shape),
            pl.BlockSpec((1,) + smooth.shape[1:], lambda p: (p, 0, 0, 0)),
            field,
            pl.BlockSpec((2, NX, NY), lambda p: (p, 0, 0)),
            whole(point_weight.shape),
            whole(repeat.shape),
            whole(ix_table.shape),
            pl.BlockSpec((1,) + iy_table.shape[1:], lambda p: (p, 0, 0)),
            whole(x_table.shape),
            whole(y_table.shape),
        ],
        out_specs=[field] + [whole(out) for out in outs[1:]],
        out_shape=[jax.ShapeDtypeStruct(out, jnp.bfloat16) for out in outs],
        scratch_shapes=[
            pltpu.VMEM((slabs, 2, lines, 2 * NY), jnp.bfloat16),
            pltpu.VMEM((channels, NX, 2 * NY), jnp.float32),
            pltpu.VMEM((NX, 2 * NY), jnp.float32),
            pltpu.VMEM((NX // 8, 8 * channels, 2 * NY), jnp.bfloat16),
            pltpu.VMEM((pairs, 2, slabs, lines, 2 * NY), jnp.bfloat16),
            pltpu.VMEM((channels, 8, 2 * NY), jnp.float32),
            pltpu.VMEM((8 * channels, 8 * channels), jnp.bfloat16),
            pltpu.VMEM((8 * channels, 8 * channels), jnp.bfloat16),
        ],
        compiler_params=params(),
        cost_estimate=LIGHT,
        name="layer",
    )(bias, planar, smooth, cotangent, grains, point_weight, repeat, ix_table, iy_table, x_table,
      y_table)


def build_band(adjoint, taps, channel, band):
    row = lax.broadcasted_iota(jnp.int32, (8, 128), 0)
    lane = lax.broadcasted_iota(jnp.int32, (8, 128), 1)
    for dy in range(3):
        for q in range(2):
            halves = []
            for side in range(2):
                tile = jnp.zeros((8, 128), jnp.float32)
                for k in range(2):
                    dz = 2 * side + k - q
                    if not 0 <= dz <= 2:
                        continue
                    for dx in range(3):
                        number = 9 * dz + 3 * dx + dy
                        tap = taps[26 - number if adjoint else number, channel]
                        hit = lane == (64 * k + row + (dx - 1)) % 128
                        tile = jnp.where(hit, tap, tile)
                tiles = [pltpu.roll(tile, 8 * k, axis=1) if k > 0 else tile for k in range(8)]
                low = (row == 0) & (lane % 64 == 63)
                high = (row == 7) & (lane % 64 == 0)
                tiles[0] = jnp.where(low, 0.0, tiles[0])
                tiles[7] = jnp.where(high, 0.0, tiles[7])
                halves.append(jnp.concatenate(tiles[1:7] + [tiles[0], tiles[7]], axis=0))
            at = 64 * (2 * dy + q)
            band[at : at + 64, :] = jnp.concatenate(halves, axis=1).astype(jnp.bfloat16)


def apply_band(quads, band):
    blocks = range(6)
    lefts = [
        band[...],
        jnp.concatenate([band[64 * b : 64 * b + 48, :] for b in blocks], axis=0),
        jnp.concatenate([band[64 * b + 32 : 64 * b + 64, :] for b in blocks], axis=0),
    ]
    lane = lax.broadcasted_iota(jnp.int32, (NX, NY), 1)
    totals = []
    for group in range(0, len(quads), 2):
        products = []
        for left, x in zip(lefts, (0, 48, 64)):
            right = [
                jnp.concatenate([sheet[x : x + 64] for sheet in quads[group + p]], axis=0)
                for p in range(2)
            ]
            products.append(dot(left, jnp.concatenate(right, axis=1)))
        for p in range(2):
            wide = slice(NY * p, NY * (p + 1))
            pair = []
            for q in range(2):
                shifted = []
                for dy in range(3):
                    b = 2 * dy + q
                    pieces = [
                        products[0][64 * b + 48 : 64 * b + 56, wide],
                        products[0][64 * b : 64 * b + 48, wide],
                        products[1][48 * b : 48 * b + 48, wide],
                        products[2][32 * b : 32 * b + 16, wide],
                        products[2][32 * b + 24 : 32 * b + 32, wide],
                    ]
                    shifted.append(jnp.concatenate(pieces, axis=0))
                before = jnp.where(lane == 0, 0.0, pltpu.roll(shifted[0], 1, axis=1))
                after = jnp.where(lane == NY - 1, 0.0, pltpu.roll(shifted[2], NY - 1, axis=1))
                pair.append(shifted[1] + before + after)
            totals.append(jnp.concatenate(pair, axis=1))
    return totals


def banded(adjoint, taps, start, even, odd, channels):
    step = pl.program_id(0)
    final = start + channels * pl.num_programs(0) - 1
    bands = (even, odd)

    @pl.when(step == 0)
    def _():
        even[...] = jnp.zeros_like(even)
        odd[...] = jnp.zeros_like(odd)
        build_band(adjoint, taps, start, even)

    def run(visit):
        for c in range(channels):
            following = jnp.minimum(start + channels * step + c + 1, final)
            build_band(adjoint, taps, following, bands[(c + 1) % 2])
            visit(c, bands[c % 2])

    return run


def smooth_kernel(start, taps, before, field, after, *rest):
    out, even, odd = rest[-3:]
    planes = field.shape[1]
    totals = []

    def visit(c, band):
        sheets = [before[c, 0]] + [field[c, z] for z in range(planes)] + [after[c, 0]]
        totals.append(apply_band([sheets[z : z + 4] for z in range(0, planes, 2)], band))

    banded(False, taps, start, even, odd, 2)(visit)
    for p in range(planes // 2):
        both = [totals[c][p].reshape(NX // 8, 8, 2 * NY) for c in range(2)]
        out[p] = jnp.concatenate(both, axis=1).astype(jnp.bfloat16)


def smooth_planes(field, rims, taps, done=None):
    channels, planes = field.shape[:2]
    pairs = planes // 2
    start = 0 if done is None else channels // 2
    skip = start // 2
    rim = pl.BlockSpec((2, 1, NX, NY), lambda c: (c, 0, 0, 0))
    sheets = pl.BlockSpec((2, planes, NX, NY), lambda c: (c + skip, 0, 0, 0))
    in_specs = [pl.BlockSpec(memory_space=pltpu.SMEM), rim, sheets, rim]
    operands = [taps, rims[0], field, rims[1]]
    if done is not None:
        in_specs.append(pl.BlockSpec(memory_space=pl.ANY))
        operands.append(done)
    return pl.pallas_call(
        functools.partial(smooth_kernel, start),
        grid=(channels // 4,),
        in_specs=in_specs,
        out_specs=pl.BlockSpec((pairs, NX // 8, 16, 2 * NY), lambda c: (0, 0, c + skip, 0)),
        out_shape=jax.ShapeDtypeStruct((pairs, NX // 8, 8 * channels, 2 * NY), jnp.bfloat16),
        input_output_aliases={} if done is None else {4: 0},
        scratch_shapes=[pltpu.VMEM((6 * 64, 4 * 64), jnp.bfloat16) for _ in range(2)],
        compiler_params=params(),
        cost_estimate=LIGHT,
        name="smooth_low" if done is None else "smooth_high",
    )(*operands)


def inner_kernel(taps, field, out, even, odd):
    planes = field.shape[1]

    def visit(c, band):
        quads = [[field[c, z + k] for k in range(4)] for z in range(1, planes - 3, 2)]
        for p, near in enumerate(apply_band(quads, band)):
            total = near.astype(jnp.bfloat16)
            out[c, 2 * p] = total[:, :NY]
            out[c, 2 * p + 1] = total[:, NY:]

    banded(True, taps, 0, even, odd, 2)(visit)


def near_inner(field, taps):
    channels, planes = field.shape[:2]
    shape = (channels, planes - 4, NX, NY)
    return pl.pallas_call(
        inner_kernel,
        grid=(channels // 2,),
        in_specs=[
            pl.BlockSpec(memory_space=pltpu.SMEM),
            pl.BlockSpec((2, planes, NX, NY), lambda c: (c, 0, 0, 0)),
        ],
        out_specs=pl.BlockSpec((2,) + shape[1:], lambda c: (c, 0, 0, 0)),
        out_shape=jax.ShapeDtypeStruct(shape, jnp.bfloat16),
        scratch_shapes=[pltpu.VMEM((6 * 64, 4 * 64), jnp.bfloat16) for _ in range(2)],
        compiler_params=params(),
        cost_estimate=LIGHT,
        name="near_inner",
    )(taps, field)


def finish_kernel(taps, before, field, after, inner, planar, ix_table, iy_table, out, waves, even,
                  odd):
    step = pl.program_id(0)
    slabs, lines = planar.shape[:2]
    planes = field.shape[1]
    span = planes * NY

    @pl.when(step == 0)
    def _():
        left = jnp.concatenate([planar[s] for s in range(slabs)], axis=0)
        for t in range(2):
            wave = dot(left, iy_table[0, :, t * span : (t + 1) * span]).astype(jnp.bfloat16)
            for s in range(slabs):
                waves[s, t] = wave[s * lines : (s + 1) * lines]

    rows = 4 * (KX // slabs)
    here = pl.ds(pl.multiple_of(rows * step, rows), rows)
    right = [waves[s, t, here, :] for s in range(slabs) for t in range(2)]
    right = jnp.concatenate(right, axis=0)
    far = [
        dot(ix_table[...], right[:, 2 * p * NY : 2 * (p + 1) * NY]) for p in range(planes // 2)
    ]

    def store(c, p, near):
        for q in range(2):
            total = near[q] + far[p][c * NX : (c + 1) * NX, q * NY : (q + 1) * NY]
            out[c, 2 * p + q] = total.astype(jnp.bfloat16)

    def visit(c, band):
        low = [before[c, 0]] + [field[c, z] for z in range(3)]
        high = [field[c, z] for z in range(planes - 3, planes)] + [after[c, 0]]
        for p, near in zip((0, planes // 2 - 1), apply_band([low, high], band)):
            store(c, p, [near[:, :NY], near[:, NY:]])
        for p in range(1, planes // 2 - 1):
            store(c, p, [inner[c, 2 * p - 2 + q].astype(jnp.float32) for q in range(2)])

    banded(True, taps, 0, even, odd, 4)(visit)


def finish(planar, spread, rims, inner, taps):
    slabs, lines, width = planar.shape
    channels, planes = spread.shape[:2]
    ix_table = constant(inverse_x_table(slabs, 4))
    iy_table = constant(inverse_y_table(planes, planes))
    rim = pl.BlockSpec((4, 1, NX, NY), lambda c: (c, 0, 0, 0))
    sheets = pl.BlockSpec((4, planes, NX, NY), lambda c: (c, 0, 0, 0))
    return pl.pallas_call(
        finish_kernel,
        grid=(channels // 4,),
        in_specs=[
            pl.BlockSpec(memory_space=pltpu.SMEM),
            rim,
            sheets,
            rim,
            pl.BlockSpec((4,) + inner.shape[1:], lambda c: (c, 0, 0, 0)),
            whole(planar.shape),
            whole(ix_table.shape),
            whole(iy_table.shape),
        ],
        out_specs=sheets,
        out_shape=jax.ShapeDtypeStruct(spread.shape, jnp.bfloat16),
        scratch_shapes=[
            pltpu.VMEM((slabs, 2, lines, planes * NY), jnp.bfloat16),
            pltpu.VMEM((6 * 64, 4 * 64), jnp.bfloat16),
            pltpu.VMEM((6 * 64, 4 * 64), jnp.bfloat16),
        ],
        compiler_params=params(),
        cost_estimate=HEAVY,
        name="finish",
    )(taps, rims[0], spread, rims[1], inner, planar, ix_table, iy_table)


def gradient_kernel(depth, where, gathered, first, second, out):
    step = pl.program_id(0)
    samples, rows, lines = gathered.shape
    half = rows // 4
    lane = lax.broadcasted_iota(jnp.int32, (1, lines), 1)
    mine = lane % depth == step
    spectra = [gathered[s, : 2 * half] for s in range(samples)]
    duals = []
    for s in range(samples):
        real = gathered[s, 2 * half : 3 * half]
        imag = gathered[s, 3 * half :]
        duals.append(jnp.where(where[0] == 0, real, imag))
        duals.append(jnp.where(where[0] == 0, imag, -real))
    spectra = jnp.where(mine, jnp.concatenate(spectra, axis=0), 0)
    duals = jnp.where(mine, jnp.concatenate(duals, axis=0), 0)
    wide = dot(duals, second[...])
    for column in range(0, out.shape[1], 256):
        product = dot(spectra, first[0, :, column : column + 256])
        for at in range(0, 256, 128):
            total = 0.0
            for s in range(2 * samples):
                here = slice(s * half, (s + 1) * half)
                total = total + product[here, at : at + 128] * wide[here]
            out[:, column + at : column + at + 128] = total * (1.0 / samples)


def weight_gradient(gathered, depth, width, index):
    samples, rows, lines = gathered.shape
    channels = lines // depth
    square = channels * channels
    cuts = square // width
    first = first_table(channels, depth).reshape(lines, cuts, width).transpose(1, 0, 2)
    first = constant(first)
    second = constant(second_table(channels, depth)[:, :128])
    where = jnp.stack([index // cuts, index % cuts]).astype(jnp.int32)
    half = rows // 4
    return pl.pallas_call(
        functools.partial(gradient_kernel, depth),
        grid_spec=pltpu.PrefetchScalarGridSpec(
            num_scalar_prefetch=1,
            grid=(depth,),
            in_specs=[
                pl.BlockSpec(gathered.shape, lambda j, w: (0, 0, 0)),
                pl.BlockSpec((1, lines, width), lambda j, w: (w[1], 0, 0)),
                pl.BlockSpec(second.shape, lambda j, w: (0, 0)),
            ],
            out_specs=pl.BlockSpec((half, width), lambda j, w: (j, 0)),
        ),
        out_shape=jax.ShapeDtypeStruct((depth * half, width), jnp.float32),
        compiler_params=params(),
        cost_estimate=LIGHT,
        name="weight_gradient",
    )(where, gathered, first, second)


def exchange(first, last):
    size = lax.axis_size("slab")
    up = [(i, i + 1) for i in range(size - 1)]
    down = [(j, i) for i, j in up]
    return lax.ppermute(last, "slab", up), lax.ppermute(first, "slab", down)


def swap(planar):
    return lax.all_to_all(planar, "slab", split_axis=0, concat_axis=0)


def local_fast(feats, grains, spec_weight, taps, point_weight, bias, cotangent):
    slabs = lax.axis_size("slab")
    copies = lax.axis_size("dp")
    barrier = lax.optimization_barrier
    field = feats[0]
    channels = field.shape[0]
    cell_scale = 1.0 / math.sqrt(NX * NY * NZ)
    mode_scale = 1.0 / math.sqrt(KX * KY * KZ)
    mode_rows = spec_weight.shape[0]
    weight = spec_weight.reshape(mode_rows * KZ, 2 * channels * channels)
    width = weight.shape[1] // copies

    first, first_high, last, last_high = cut_rims(field)
    rims = exchange(first, last)
    planar = swap(forward_modes(field, slabs))
    rims, first, last = barrier((rims, first_high, last_high))
    rims_high = exchange(first, last)
    planar, smooth = barrier((planar, smooth_planes(field, rims, taps)))
    spectrum, planar = mix(planar, weight, cell_scale, 0.5 * mode_scale)
    smooth, spectrum = barrier((smooth, spectrum))
    planar = swap(planar)
    smooth = smooth_planes(field, rims_high, taps, smooth)
    spread, planar, first, last = layer(planar, smooth, cotangent[0], grains[0], bias, point_weight)
    rims = exchange(first, last)
    planar, send = mix(swap(planar), weight, 0.5 * mode_scale, cell_scale, spectrum)
    planar = swap(planar)
    send, spread = barrier((send, spread))
    inner = near_inner(spread, taps)
    grad_feats = finish(planar, spread, rims, inner, taps)
    gathered = lax.all_gather(send, "dp")
    grad_feats, gathered = barrier((grad_feats, gathered))
    grad_feats = grad_feats[None]
    grad_spec = weight_gradient(gathered, KX // slabs, width, lax.axis_index("dp"))
    return (grad_feats, grad_spec.reshape(mode_rows, KZ, width))


def local(feats, grains, spec_weight, taps, point_weight, bias, cotangent):
    samples, channels, planes = feats.shape[:3]
    width = spec_weight.shape[2] // lax.axis_size("dp")
    fits = (
        lax.axis_size("slab") * 4 == KX
        and samples == 1
        and channels == 32
        and planes == 8
        and channels * channels % width == 0
        and width % 128 == 0
    )
    form = local_fast if fits else local_any
    return form(feats, grains, spec_weight, taps, point_weight, bias, cotangent)


def solution(mesh):
    in_specs = (
        P(("grp", "dp"), None, "slab", None, None),
        P(("grp", "dp"), "slab", None, None),
        P("slab", None, None),
        P(),
        P(),
        P(),
        P(("grp", "dp"), None, "slab", None, None),
    )
    out_specs = (P(("grp", "dp"), None, "slab", None, None), P("slab", "grp", "dp"))
    return jax.shard_map(local, mesh=mesh, in_specs=in_specs, out_specs=out_specs, check_vma=False)
```

```python
import functools
import math

import jax
import jax.numpy as jnp
import ml_dtypes
import numpy as np
from jax import lax
from jax.experimental import pallas as pl
from jax.experimental.pallas import tpu as pltpu
from jax.sharding import PartitionSpec as P

NX = 128
NY = 128
NZ = 32
KX = 16
KY = 16
KZ = 16


HIGHEST = lax.Precision.HIGHEST


def extended(shard, sides, width):
    for axis, dim in sides:
        size, length = (lax.axis_size(axis), shard.shape[dim])
        up = [(i, (i + 1) % size) for i in range(size - 1)]
        down = [(j, i) for i, j in up]
        last = lax.slice_in_dim(shard, length - width, length, axis=dim)
        first = lax.slice_in_dim(shard, 0, width, axis=dim)
        before = lax.ppermute(last, axis, up)
        after = lax.ppermute(first, axis, down)
        shard = jnp.concatenate([before, shard, after], axis=dim)
    return shard


def tables(count, length, span):
    indices = jnp.arange(count, dtype=jnp.int32)
    frequency = jnp.where(indices < count // 2, indices, length - count + indices)
    position = jnp.arange(span, dtype=jnp.int32)
    phases = frequency[:, None] * position[None, :] % length
    angles = phases.astype(jnp.float32) * (2.0 * math.pi / length)
    return (jnp.cos(angles), jnp.sin(angles))


def mobility(grains):
    leading = [(0, 0)] * (grains.ndim - 2)
    along_x = (grains[..., 1:, :] != grains[..., :-1, :]).astype(jnp.float32)
    along_y = (grains[..., :, 1:] != grains[..., :, :-1]).astype(jnp.float32)
    differ = jnp.pad(along_x, leading + [(1, 0), (0, 0)]) + jnp.pad(
        along_x, leading + [(0, 1), (0, 0)]
    )
    differ = (
        differ
        + jnp.pad(along_y, leading + [(0, 0), (1, 0)])
        + jnp.pad(along_y, leading + [(0, 0), (0, 1)])
    )
    return 0.25 * (1.0 + differ)


def stencil(padded, taps, adjoint):
    planes = padded.shape[-3] - 2
    rows_x = padded.shape[-2] - 2
    rows_y = padded.shape[-1] - 2
    total = jnp.zeros(padded.shape[:-3] + (planes, rows_x, rows_y), jnp.float32)
    for offset in range(27):
        shift_z, shift_x, shift_y = (offset // 9, offset // 3 % 3, offset % 3)
        if adjoint:
            shift_z, shift_x, shift_y = (2 - shift_z, 2 - shift_x, 2 - shift_y)
        window = padded[
            ..., shift_z : shift_z + planes, shift_x : shift_x + rows_x, shift_y : shift_y + rows_y
        ]
        total = total + taps[offset][:, None, None, None] * window.astype(jnp.float32)
    return total


def plane_forward(field, cos_x, sin_x, cos_y, sin_y):
    real_y = jnp.einsum("...xy,ky->...xk", field, cos_y, precision=HIGHEST)
    imag_y = -jnp.einsum("...xy,ky->...xk", field, sin_y, precision=HIGHEST)
    real_part = jnp.einsum("...xk,jx->...jk", real_y, cos_x, precision=HIGHEST) + jnp.einsum(
        "...xk,jx->...jk", imag_y, sin_x, precision=HIGHEST
    )
    imag_part = jnp.einsum("...xk,jx->...jk", imag_y, cos_x, precision=HIGHEST) - jnp.einsum(
        "...xk,jx->...jk", real_y, sin_x, precision=HIGHEST
    )
    return (real_part, imag_part)


def plane_inverse(real_part, imag_part, cos_x, sin_x, cos_y, sin_y):
    real_x = jnp.einsum("...jk,jx->...xk", real_part, cos_x, precision=HIGHEST) - jnp.einsum(
        "...jk,jx->...xk", imag_part, sin_x, precision=HIGHEST
    )
    imag_x = jnp.einsum("...jk,jx->...xk", imag_part, cos_x, precision=HIGHEST) + jnp.einsum(
        "...jk,jx->...xk", real_part, sin_x, precision=HIGHEST
    )
    return jnp.einsum("...xk,ky->...xy", real_x, cos_y, precision=HIGHEST) - jnp.einsum(
        "...xk,ky->...xy", imag_x, sin_y, precision=HIGHEST
    )


def depth_forward(packed, cos_table, sin_table):
    width = packed.shape[-1] // 2
    real_in = packed[..., :width]
    imag_in = packed[..., width:]
    real_out = jnp.einsum("pszc,kz->pskc", real_in, cos_table, precision=HIGHEST) + jnp.einsum(
        "pszc,kz->pskc", imag_in, sin_table, precision=HIGHEST
    )
    imag_out = jnp.einsum("pszc,kz->pskc", imag_in, cos_table, precision=HIGHEST) - jnp.einsum(
        "pszc,kz->pskc", real_in, sin_table, precision=HIGHEST
    )
    return jnp.concatenate([real_out, imag_out], axis=-1)


def depth_inverse(real_modes, imag_modes, cos_table, sin_table):
    real_out = jnp.einsum("pskc,kz->pszc", real_modes, cos_table, precision=HIGHEST) - jnp.einsum(
        "pskc,kz->pszc", imag_modes, sin_table, precision=HIGHEST
    )
    imag_out = jnp.einsum("pskc,kz->pszc", imag_modes, cos_table, precision=HIGHEST) + jnp.einsum(
        "pskc,kz->pszc", real_modes, sin_table, precision=HIGHEST
    )
    return jnp.concatenate([real_out, imag_out], axis=-1)


def rim_planes(field):
    return extended(field, (("slab", 2),), 1)


def local_any(feats, grains, spec_weight, taps, point_weight, bias, cotangent):
    samples_here = feats.shape[0]
    channels = feats.shape[1]
    planes = feats.shape[2]
    cos_x, sin_x = tables(KX, NX, NX)
    cos_y, sin_y = tables(KY, NY, NY)
    cos_full, sin_full = tables(KZ, NZ, NZ)
    cell_scale = math.sqrt(NX * NY * NZ)
    mode_scale = math.sqrt(KX * KY * KZ)
    mode_rows = spec_weight.shape[0]
    weights = spec_weight.astype(jnp.float32).reshape(mode_rows, KZ, 2, channels, channels)
    w_real = weights[:, :, 0]
    w_imag = weights[:, :, 1]
    moving = mobility(grains)[:, None]

    def to_modes(field):
        real_plane, imag_plane = plane_forward(field, cos_x, sin_x, cos_y, sin_y)
        packed = jnp.stack([real_plane, imag_plane], axis=1)
        packed = packed.transpose(4, 5, 0, 3, 1, 2).reshape(
            KX * KY, samples_here, planes, 2 * channels
        )
        moved = lax.all_to_all(packed, "slab", split_axis=0, concat_axis=2, tiled=True)
        summed = depth_forward(moved, cos_full, sin_full)
        return (summed[..., :channels], summed[..., channels:])

    def from_modes(real_modes, imag_modes):
        planar = depth_inverse(real_modes, imag_modes, cos_full, sin_full)
        packed = lax.all_to_all(planar, "slab", split_axis=2, concat_axis=0, tiled=True)
        grouped = packed.reshape(KX, KY, samples_here, planes, 2, channels).transpose(
            2, 4, 5, 3, 0, 1
        )
        return plane_inverse(grouped[:, 0], grouped[:, 1], cos_x, sin_x, cos_y, sin_y)

    zero_rim = ((0, 0), (0, 0), (0, 0), (1, 1), (1, 1))
    padded = jnp.pad(rim_planes(feats), zero_rim)
    smooth = stencil(padded, taps, False).astype(jnp.bfloat16)
    local_part = moving * jnp.einsum(
        "sczxy,co->sozxy", smooth, point_weight, preferred_element_type=jnp.float32
    )
    spec_real, spec_imag = to_modes(feats.astype(jnp.float32))
    spec_real = spec_real / cell_scale
    spec_imag = spec_imag / cell_scale
    mixed_real = jnp.einsum("pskc,pkco->psko", spec_real, w_real, precision=HIGHEST) - jnp.einsum(
        "pskc,pkco->psko", spec_imag, w_imag, precision=HIGHEST
    )
    mixed_imag = jnp.einsum("pskc,pkco->psko", spec_real, w_imag, precision=HIGHEST) + jnp.einsum(
        "pskc,pkco->psko", spec_imag, w_real, precision=HIGHEST
    )
    spectral = from_modes(mixed_real, mixed_imag) / mode_scale
    pre = spectral + local_part + bias[None, :, None, None, None]
    gate = jax.nn.sigmoid(pre)
    delta = (cotangent.astype(jnp.float32) * gate * (1.0 + pre * (1.0 - gate))).astype(jnp.bfloat16)
    dual_real, dual_imag = to_modes(delta.astype(jnp.float32))
    dual_real = dual_real / mode_scale
    dual_imag = dual_imag / mode_scale
    batch_total = samples_here * lax.axis_size("dp")
    grad_real = jnp.einsum("pskc,psko->pkco", spec_real, dual_real, precision=HIGHEST) + jnp.einsum(
        "pskc,psko->pkco", spec_imag, dual_imag, precision=HIGHEST
    )
    grad_imag = jnp.einsum("pskc,psko->pkco", spec_real, dual_imag, precision=HIGHEST) - jnp.einsum(
        "pskc,psko->pkco", spec_imag, dual_real, precision=HIGHEST
    )
    grad_terms = (jnp.stack([grad_real, grad_imag], axis=2) / batch_total).reshape(
        mode_rows, KZ, 2 * channels * channels
    )
    grad_spec = lax.psum_scatter(
        grad_terms.astype(jnp.bfloat16), "dp", scatter_dimension=2, tiled=True
    ).astype(jnp.float32)
    back_real = jnp.einsum("psko,pkco->pskc", dual_real, w_real, precision=HIGHEST) + jnp.einsum(
        "psko,pkco->pskc", dual_imag, w_imag, precision=HIGHEST
    )
    back_imag = jnp.einsum("psko,pkco->pskc", dual_imag, w_real, precision=HIGHEST) - jnp.einsum(
        "psko,pkco->pskc", dual_real, w_imag, precision=HIGHEST
    )
    spectral_back = from_modes(back_real, back_imag) / cell_scale
    spread = (
        moving
        * jnp.einsum("sozxy,co->sczxy", delta, point_weight, preferred_element_type=jnp.float32)
    ).astype(jnp.bfloat16)
    spread_padded = jnp.pad(rim_planes(spread), zero_rim)
    local_back = stencil(spread_padded, taps, True)
    grad_feats = (spectral_back + local_back).astype(jnp.bfloat16)
    return (grad_feats, grad_spec)


def frequencies(count, length):
    index = np.arange(count)
    return np.where(index < count // 2, index, length - count + index)


def angles(count, length):
    phases = np.outer(frequencies(count, length), np.arange(length)) % length
    return phases * (2.0 * np.pi / length)


def constant(array):
    return jnp.asarray(np.asarray(array, np.float32).astype(ml_dtypes.bfloat16))


def forward_x_table(slabs, split):
    a = angles(KX, NX).reshape(slabs, KX // slabs, NX)
    trig = np.stack([np.cos(a), np.sin(a)])
    table = np.einsum("tsjx,cd->tscjdx", trig, np.eye(2)).reshape(-1, 2, NX // 8, 8)
    if split:
        table = table.transpose(0, 2, 1, 3)
    return table.reshape(4 * KX, 2 * NX)


def forward_y_table(planes):
    a = angles(KY, NY)
    cos, sin = np.cos(a).T, np.sin(a).T
    block = np.stack([np.stack([cos, -sin], 1), np.stack([-sin, -cos], 1)])
    pick = np.eye(planes).reshape(planes // 2, 2, planes)
    table = np.einsum("pqz,tyrk->ptqyzrk", pick, block)
    return table.reshape(planes * 2 * NY, planes * 2 * KY)


def forward_z_table():
    a = angles(KZ, NZ)
    cos, sin = np.cos(a).T, np.sin(a).T
    block = np.stack([np.stack([cos, -sin], 1), np.stack([sin, cos], 1)], 1)
    table = np.einsum("zrqm,kl->zrkqlm", block, np.eye(KY))
    return table.reshape(NZ * 2 * KY, 2 * KY * KZ)


def inverse_z_table():
    a = angles(KZ, NZ)
    cos, sin = np.cos(a), np.sin(a)
    block = np.stack([np.stack([cos, sin], 2), np.stack([-sin, cos], 2)])
    table = np.einsum("rmzq,kl->rkmzql", block, np.eye(KY))
    return table.reshape(2 * KY * KZ, NZ * 2 * KY)


def inverse_y_table(planes, group):
    a = angles(KY, NY)
    cos, sin = np.cos(a), np.sin(a)
    block = np.stack([np.stack([cos, -sin], 1), np.stack([-sin, -cos], 1)])
    pick = np.eye(planes).reshape(planes // group, group, planes)
    table = np.einsum("pqz,rkty->pzrktqy", pick, block)
    return table.reshape(planes // group, planes * 2 * KY, 2 * group * NY)


def inverse_x_table(slabs, group):
    a = angles(KX, NX).reshape(slabs, KX // slabs, NX)
    trig = np.stack([np.cos(a), np.sin(a)])
    table = np.einsum("tsjx,cd->cxstdj", trig, np.eye(group))
    return table.reshape(group * NX, 2 * KX * group)


def first_table(channels, depth):
    table = np.einsum("ac,j,b->ajcb", np.eye(channels), np.ones(depth), np.ones(channels))
    return table.reshape(channels * depth, channels * channels)


def second_table(channels, depth):
    table = np.einsum("ac,j,b->ajbc", np.eye(channels), np.ones(depth), np.ones(channels))
    return table.reshape(channels * depth, channels * channels)


LIGHT = pl.CostEstimate(flops=10**7, bytes_accessed=10**5, transcendentals=0)
HEAVY = pl.CostEstimate(flops=10**11, bytes_accessed=10**8, transcendentals=0)


def dot(a, b):
    return jnp.dot(a, b, preferred_element_type=jnp.float32)


def whole(shape):
    return pl.BlockSpec(shape, lambda *_: (0,) * len(shape))


def params(**kw):
    return pltpu.CompilerParams(vmem_limit_bytes=58 * 2**20, **kw)


def store_rows(rows, pair, x_table, load):
    slabs, lines = rows.shape[2:4]
    for i in range(lines // 16):
        parts = [dot(x_table[...], load(2 * i + k)) for k in range(2)]
        for t in range(2):
            for s in range(slabs):
                here = slice(8 * (t * slabs + s), 8 * (t * slabs + s) + 8)
                both = jnp.concatenate([part[here] for part in parts], axis=0)
                rows[pair, t, s, 16 * i : 16 * i + 16, :] = both.astype(jnp.bfloat16)


def store_modes(rows, y_table, out):
    pairs, _, slabs, lines, _ = rows.shape
    left = [
        jnp.concatenate([rows[p, t, s] for p in range(pairs) for t in range(2)], axis=1)
        for s in range(slabs)
    ]
    modes = dot(jnp.concatenate(left, axis=0), y_table[...])
    for s in range(slabs):
        out[s] = modes[s * lines : (s + 1) * lines].astype(jnp.bfloat16)


def rims_kernel(low, high, *rims):
    step = pl.program_id(0)
    half = pl.num_programs(0) // 2
    for k, source in enumerate((low, high)):

        @pl.when(step < half)
        def _():
            rims[2 * k][...] = source[...]

        @pl.when(step >= half)
        def _():
            rims[2 * k + 1][...] = source[...]


def cut_rims(field):
    channels, planes = field.shape[:2]
    steps = 2
    rim = jax.ShapeDtypeStruct((channels // 2, 1, NX, NY), jnp.bfloat16)
    block = (channels // steps, 1, NX, NY)
    outs = [
        pl.BlockSpec(block, lambda c: (jnp.minimum(c, steps // 2 - 1), 0, 0, 0)),
        pl.BlockSpec(block, lambda c: (jnp.maximum(c - steps // 2, 0), 0, 0, 0)),
    ]
    return pl.pallas_call(
        rims_kernel,
        grid=(steps,),
        in_specs=[
            pl.BlockSpec(block, lambda c: (c, 0, 0, 0)),
            pl.BlockSpec(block, lambda c: (c, planes - 1, 0, 0)),
        ],
        out_specs=outs + outs,
        out_shape=[rim] * 4,
        compiler_params=params(),
        cost_estimate=LIGHT,
        name="rims",
    )(field, field)


def forward_kernel(field, x_table, y_table, out, rows):
    pair = pl.program_id(0)
    pairs = rows.shape[0]

    def load(i):
        halves = [field[2 * i : 2 * i + 2, q].reshape(2 * NX, NY) for q in range(2)]
        return jnp.concatenate(halves, axis=1)

    store_rows(rows, pair, x_table, load)

    @pl.when(pair == pairs - 1)
    def _():
        store_modes(rows, y_table, out)


def forward_modes(field, slabs):
    channels, planes = field.shape[:2]
    lines = channels * (KX // slabs)
    x_table = constant(forward_x_table(slabs, False))
    y_table = constant(forward_y_table(planes))
    shape = (slabs, lines, planes * 2 * KY)
    return pl.pallas_call(
        forward_kernel,
        grid=(planes // 2,),
        in_specs=[
            pl.BlockSpec((channels, 2, NX, NY), lambda p: (0, p, 0, 0)),
            whole(x_table.shape),
            whole(y_table.shape),
        ],
        out_specs=whole(shape),
        out_shape=jax.ShapeDtypeStruct(shape, jnp.bfloat16),
        scratch_shapes=[pltpu.VMEM((planes // 2, 2, slabs, lines, 2 * NY), jnp.bfloat16)],
        compiler_params=params(),
        cost_estimate=LIGHT,
        name="forward_modes",
    )(field, x_table, y_table)


def mixing_kernel(scale_in, scale_out, adjoint, planar, weight, z_in, z_out, spread_table,
                  sum_table, *rest):
    if adjoint:
        partner, out, send, spectrum, total, wide, product = rest
    else:
        spectrum, out, total, wide, product = rest
    step = pl.program_id(0)
    steps = pl.num_programs(0)
    slabs = planar.shape[0]
    width = planar.shape[2]
    half = spectrum.shape[0] // 2
    lanes = weight.shape[1] // 2

    @pl.when(step == 0)
    def _():
        left = jnp.concatenate([planar[s] for s in range(slabs)], axis=1)
        modes = (dot(left, z_in[...]).T * scale_in).astype(jnp.bfloat16)
        spectrum[...] = modes
        total[...] = jnp.zeros_like(total)
        if adjoint:
            for d in range(send.shape[0]):
                send[d, : 2 * half] = partner[...]
                send[d, 2 * half :] = modes

    lane = lax.broadcasted_iota(jnp.int32, (1, spectrum.shape[1]), 1)
    mine = lane % steps == step
    wide[...] = dot(jnp.where(mine, spectrum[...], 0), spread_table[...])
    block = 32
    tile = wide.shape[1]
    for at in range(0, half, block):
        sums = [0.0, 0.0]
        for column in range(0, lanes, 128):
            here = slice(column, column + 128) if tile == lanes else slice(None)
            real_wide = wide[at : at + block, here]
            imag_wide = wide[half + at : half + at + block, here]
            w_real = weight[at : at + block, column : column + 128].astype(jnp.float32)
            imag_column = lanes + column
            w_imag = weight[at : at + block, imag_column : imag_column + 128].astype(jnp.float32)
            if adjoint:
                real = real_wide * w_real + imag_wide * w_imag
                imag = imag_wide * w_real - real_wide * w_imag
                product[at : at + block, column : column + 128] = real.astype(jnp.bfloat16)
                product[half + at : half + at + block, column : column + 128] = imag.astype(
                    jnp.bfloat16
                )
            else:
                sums[0] = sums[0] + (real_wide * w_real - imag_wide * w_imag)
                sums[1] = sums[1] + (real_wide * w_imag + imag_wide * w_real)
        if not adjoint:
            product[at : at + block] = sums[0].astype(jnp.bfloat16)
            product[half + at : half + at + block] = sums[1].astype(jnp.bfloat16)
    total[...] += jnp.where(mine, dot(product[...], sum_table[...]), 0.0)

    @pl.when(step == steps - 1)
    def _():
        modes = dot((total[...] * scale_out).T.astype(jnp.bfloat16), z_out[...])
        for s in range(slabs):
            out[s] = modes[:, s * width : (s + 1) * width].astype(jnp.bfloat16)


def mix(planar, weight, scale_in, scale_out, partner=None, copies=0):
    slabs, lines, width = planar.shape
    adjoint = partner is not None
    depth = KX // slabs
    channels = lines // depth
    rows = KY * KZ
    z_in = constant(forward_z_table())
    z_out = constant(inverse_z_table())
    first = first_table(channels, depth)
    second = second_table(channels, depth)
    spread_table = constant(second[:, :128] if adjoint else first)
    sum_table = constant(first.T if adjoint else second[:, :128].T)
    shape = (2 * rows, lines)
    in_specs = [
        whole(planar.shape),
        pl.BlockSpec((rows, weight.shape[1]), lambda j: (j, 0)),
        whole(z_in.shape),
        whole(z_out.shape),
        whole(spread_table.shape),
        whole(sum_table.shape),
    ]
    operands = [planar, weight, z_in, z_out, spread_table, sum_table]
    scratch = [
        pltpu.VMEM(shape, jnp.float32),
        pltpu.VMEM((2 * rows, spread_table.shape[1]), jnp.float32),
        pltpu.VMEM((2 * rows, sum_table.shape[0]), jnp.bfloat16),
    ]
    if adjoint:
        in_specs.append(whole(shape))
        operands.append(partner)
        scratch = [pltpu.VMEM(shape, jnp.bfloat16)] + scratch
        outs = [planar.shape, (copies, 2 * shape[0], lines)]
    else:
        outs = [shape, planar.shape]
    return pl.pallas_call(
        functools.partial(mixing_kernel, scale_in, scale_out, adjoint),
        grid=(depth,),
        in_specs=in_specs,
        out_specs=[whole(out) for out in outs],
        out_shape=[jax.ShapeDtypeStruct(out, jnp.bfloat16) for out in outs],
        scratch_shapes=scratch,
        compiler_params=params(),
        cost_estimate=HEAVY,
        name="mix_back" if adjoint else "mix",
    )(*operands)


def plane_mobility(grains):
    same = [
        jnp.concatenate([grains[:1], grains[:-1]], axis=0),
        jnp.concatenate([grains[1:], grains[-1:]], axis=0),
        jnp.concatenate([grains[:, :1], grains[:, :-1]], axis=1),
        jnp.concatenate([grains[:, 1:], grains[:, -1:]], axis=1),
    ]
    total = jnp.full(grains.shape, 0.25, jnp.float32)
    for other in same:
        total = total + jnp.where(grains != other, 0.25, 0.0)
    return total


def layer_kernel(bias, planar, smooth, cotangent, grains, point_weight, repeat, ix_table, iy_table,
                 x_table, y_table, spread, out, first, last, *rest):
    pair = pl.program_id(0)
    waves, spectral, moving, delta, rows, bias_wide, mix_out, mix_in = rest
    pairs = rows.shape[0]
    channels = cotangent.shape[0]
    slabs = planar.shape[0]

    @pl.when(pair == 0)
    def _():
        for c in range(channels):
            bias_wide[c] = jnp.full(bias_wide.shape[1:], 0.5 * bias[c], jnp.float32)
        tall = dot(repeat[...], point_weight[...]).astype(jnp.bfloat16)
        square = lax.dot_general(
            tall, repeat[...], (((1,), (1,)), ((), ())), preferred_element_type=jnp.float32
        )
        row = lax.broadcasted_iota(jnp.int32, square.shape, 0) % 8
        column = lax.broadcasted_iota(jnp.int32, square.shape, 1) % 8
        square = jnp.where(row == column, square, 0.0)
        mix_in[...] = square.astype(jnp.bfloat16)
        mix_out[...] = square.T.astype(jnp.bfloat16)

    lines = planar.shape[1]
    step = jnp.concatenate([planar[s] for s in range(slabs)], axis=0)
    step = dot(step, iy_table[0]).astype(jnp.bfloat16)
    for s in range(slabs):
        for t in range(2):
            waves[s, t] = step[s * lines : (s + 1) * lines, 2 * NY * t : 2 * NY * (t + 1)]
    group = 8 * (KX // slabs)
    for g in range(channels // 8):
        here = slice(g * group, (g + 1) * group)
        wave = [waves[s, t, here, :] for s in range(slabs) for t in range(2)]
        step = dot(ix_table[...], jnp.concatenate(wave, axis=0))
        spectral[8 * g : 8 * g + 8] = step.reshape(8, NX, 2 * NY)
    for q in range(2):
        moving[:, q * NY : (q + 1) * NY] = 0.5 * plane_mobility(grains[q])

    def body(i, _):
        x = pl.multiple_of(16 * i, 16)
        halves = [cotangent[:, q, pl.ds(x, 16), :] for q in range(2)]
        cotangent_here = jnp.concatenate(halves, axis=2).astype(jnp.float32)
        spreads = []
        for h in range(2):
            at = pl.ds(pl.multiple_of(x + 8 * h, 8), 8)
            mobile = moving[at, :][None]
            local = dot(mix_out[...], smooth[0, 2 * i + h]).reshape(channels, 8, 2 * NY)
            half = spectral[:, at, :] + mobile * local + bias_wide[...]
            wave = jnp.tanh(half)
            slope = (1.0 + wave) * (1.0 + (half - half * wave))
            change = cotangent_here[:, 8 * h : 8 * h + 8, :] * slope
            right = change.reshape(8 * channels, 2 * NY).astype(jnp.bfloat16)
            delta[2 * i + h] = right
            back = dot(mix_in[...], right).reshape(channels, 8, 2 * NY)
            spreads.append(mobile * back)
        both = jnp.concatenate(spreads, axis=1).astype(jnp.bfloat16)
        for q in range(2):
            spread[:, q, pl.ds(x, 16), :] = both[:, :, q * NY : (q + 1) * NY]
        return 0

    lax.fori_loop(0, NX // 16, body, 0, unroll=4)


    @pl.when(pair == 0)
    def _():
        first[:, 0] = spread[:, 0]

    @pl.when(pair == pairs - 1)
    def _():
        last[:, 0] = spread[:, 1]

    def load(i):
        return delta[:, 16 * i : 16 * i + 16, :].reshape(2 * NX, 2 * NY)

    store_rows(rows, pair, x_table, load)

    @pl.when(pair == pairs - 1)
    def _():
        store_modes(rows, y_table, out)


def layer(planar, smooth, cotangent, grains, bias, point_weight):
    slabs, lines, width = planar.shape
    channels, planes = cotangent.shape[:2]
    pairs = planes // 2
    repeat = constant(np.repeat(np.eye(channels), 8, axis=0))
    ix_table = constant(inverse_x_table(slabs, 8))
    iy_table = constant(inverse_y_table(planes, 2))
    x_table = constant(forward_x_table(slabs, True))
    y_table = constant(forward_y_table(planes))
    field = pl.BlockSpec((channels, 2, NX, NY), lambda p: (0, p, 0, 0))
    outs = [cotangent.shape, planar.shape] + [(channels, 1, NX, NY)] * 2
    return pl.pallas_call(
        layer_kernel,
        grid=(pairs,),
        in_specs=[
            pl.BlockSpec(memory_space=pltpu.SMEM),
            whole(planar.shape),
            pl.BlockSpec((1,) + smooth.shape[1:], lambda p: (p, 0, 0, 0)),
            field,
            pl.BlockSpec((2, NX, NY), lambda p: (p, 0, 0)),
            whole(point_weight.shape),
            whole(repeat.shape),
            whole(ix_table.shape),
            pl.BlockSpec((1,) + iy_table.shape[1:], lambda p: (p, 0, 0)),
            whole(x_table.shape),
            whole(y_table.shape),
        ],
        out_specs=[field] + [whole(out) for out in outs[1:]],
        out_shape=[jax.ShapeDtypeStruct(out, jnp.bfloat16) for out in outs],
        scratch_shapes=[
            pltpu.VMEM((slabs, 2, lines, 2 * NY), jnp.bfloat16),
            pltpu.VMEM((channels, NX, 2 * NY), jnp.float32),
            pltpu.VMEM((NX, 2 * NY), jnp.float32),
            pltpu.VMEM((NX // 8, 8 * channels, 2 * NY), jnp.bfloat16),
            pltpu.VMEM((pairs, 2, slabs, lines, 2 * NY), jnp.bfloat16),
            pltpu.VMEM((channels, 8, 2 * NY), jnp.float32),
            pltpu.VMEM((8 * channels, 8 * channels), jnp.bfloat16),
            pltpu.VMEM((8 * channels, 8 * channels), jnp.bfloat16),
        ],
        compiler_params=params(),
        cost_estimate=LIGHT,
        name="layer",
    )(bias, planar, smooth, cotangent, grains, point_weight, repeat, ix_table, iy_table, x_table,
      y_table)


def build_band(adjoint, taps, channel, band):
    row = lax.broadcasted_iota(jnp.int32, (8, 128), 0)
    lane = lax.broadcasted_iota(jnp.int32, (8, 128), 1)
    for dy in range(3):
        for q in range(2):
            halves = []
            for side in range(2):
                tile = jnp.zeros((8, 128), jnp.float32)
                for k in range(2):
                    dz = 2 * side + k - q
                    if not 0 <= dz <= 2:
                        continue
                    for dx in range(3):
                        number = 9 * dz + 3 * dx + dy
                        tap = taps[26 - number if adjoint else number, channel]
                        hit = lane == (64 * k + row + (dx - 1)) % 128
                        tile = jnp.where(hit, tap, tile)
                tiles = [pltpu.roll(tile, 8 * k, axis=1) if k > 0 else tile for k in range(8)]
                low = (row == 0) & (lane % 64 == 63)
                high = (row == 7) & (lane % 64 == 0)
                tiles[0] = jnp.where(low, 0.0, tiles[0])
                tiles[7] = jnp.where(high, 0.0, tiles[7])
                halves.append(jnp.concatenate(tiles[1:7] + [tiles[0], tiles[7]], axis=0))
            at = 64 * (2 * dy + q)
            band[at : at + 64, :] = jnp.concatenate(halves, axis=1).astype(jnp.bfloat16)


def apply_band(quads, band):
    blocks = range(6)
    lefts = [
        band[...],
        jnp.concatenate([band[64 * b : 64 * b + 48, :] for b in blocks], axis=0),
        jnp.concatenate([band[64 * b + 32 : 64 * b + 64, :] for b in blocks], axis=0),
    ]
    lane = lax.broadcasted_iota(jnp.int32, (NX, NY), 1)
    totals = []
    for group in range(0, len(quads), 2):
        products = []
        for left, x in zip(lefts, (0, 48, 64)):
            right = [
                jnp.concatenate([sheet[x : x + 64] for sheet in quads[group + p]], axis=0)
                for p in range(2)
            ]
            products.append(dot(left, jnp.concatenate(right, axis=1)))
        for p in range(2):
            wide = slice(NY * p, NY * (p + 1))
            pair = []
            for q in range(2):
                shifted = []
                for dy in range(3):
                    b = 2 * dy + q
                    pieces = [
                        products[0][64 * b + 48 : 64 * b + 56, wide],
                        products[0][64 * b : 64 * b + 48, wide],
                        products[1][48 * b : 48 * b + 48, wide],
                        products[2][32 * b : 32 * b + 16, wide],
                        products[2][32 * b + 24 : 32 * b + 32, wide],
                    ]
                    shifted.append(jnp.concatenate(pieces, axis=0))
                before = jnp.where(lane == 0, 0.0, pltpu.roll(shifted[0], 1, axis=1))
                after = jnp.where(lane == NY - 1, 0.0, pltpu.roll(shifted[2], NY - 1, axis=1))
                pair.append(shifted[1] + before + after)
            totals.append(jnp.concatenate(pair, axis=1))
    return totals


def banded(adjoint, taps, start, even, odd, channels):
    step = pl.program_id(0)
    final = start + channels * pl.num_programs(0) - 1
    bands = (even, odd)

    @pl.when(step == 0)
    def _():
        even[...] = jnp.zeros_like(even)
        odd[...] = jnp.zeros_like(odd)
        build_band(adjoint, taps, start, even)

    def run(visit):
        for c in range(channels):
            following = jnp.minimum(start + channels * step + c + 1, final)
            build_band(adjoint, taps, following, bands[(c + 1) % 2])
            visit(c, bands[c % 2])

    return run


def smooth_kernel(start, taps, before, field, after, *rest):
    out, even, odd = rest[-3:]
    planes = field.shape[1]
    totals = []

    def visit(c, band):
        sheets = [before[c, 0]] + [field[c, z] for z in range(planes)] + [after[c, 0]]
        totals.append(apply_band([sheets[z : z + 4] for z in range(0, planes, 2)], band))

        if c % 2 == 1:
            for p in range(planes // 2):
                both = [total[p].reshape(NX // 8, 8, 2 * NY) for total in totals[c - 1 : c + 1]]
                both = jnp.concatenate(both, axis=1).astype(jnp.bfloat16)
                out[p, :, 8 * (c - 1) : 8 * (c + 1), :] = both

    banded(False, taps, start, even, odd, field.shape[0])(visit)


def smooth_planes(field, rims, taps, done=None):
    channels, planes = field.shape[:2]
    pairs = planes // 2
    start = 0 if done is None else channels // 2
    step = 4
    skip = start // step
    rim = pl.BlockSpec((step, 1, NX, NY), lambda c: (c, 0, 0, 0))
    sheets = pl.BlockSpec((step, planes, NX, NY), lambda c: (c + skip, 0, 0, 0))
    in_specs = [pl.BlockSpec(memory_space=pltpu.SMEM), rim, sheets, rim]
    operands = [taps, rims[0], field, rims[1]]
    if done is not None:
        in_specs.append(pl.BlockSpec(memory_space=pl.ANY))
        operands.append(done)
    return pl.pallas_call(
        functools.partial(smooth_kernel, start),
        grid=(channels // 2 // step,),
        in_specs=in_specs,
        out_specs=pl.BlockSpec((pairs, NX // 8, 8 * step, 2 * NY), lambda c: (0, 0, c + skip, 0)),
        out_shape=jax.ShapeDtypeStruct((pairs, NX // 8, 8 * channels, 2 * NY), jnp.bfloat16),
        input_output_aliases={} if done is None else {4: 0},
        scratch_shapes=[pltpu.VMEM((6 * 64, 4 * 64), jnp.bfloat16) for _ in range(2)],
        compiler_params=params(),
        cost_estimate=LIGHT,
        name="smooth_low" if done is None else "smooth_high",
    )(*operands)


def inner_kernel(taps, field, out, even, odd):
    planes = field.shape[1]

    def visit(c, band):
        quads = [[field[c, z + k] for k in range(4)] for z in range(1, planes - 3, 2)]
        for p, near in enumerate(apply_band(quads, band)):
            total = near.astype(jnp.bfloat16)
            out[c, 2 * p] = total[:, :NY]
            out[c, 2 * p + 1] = total[:, NY:]

    banded(True, taps, 0, even, odd, field.shape[0])(visit)


def near_inner(field, taps):
    channels, planes = field.shape[:2]
    step = 8
    shape = (channels, planes - 4, NX, NY)
    return pl.pallas_call(
        inner_kernel,
        grid=(channels // step,),
        in_specs=[
            pl.BlockSpec(memory_space=pltpu.SMEM),
            pl.BlockSpec((step, planes, NX, NY), lambda c: (c, 0, 0, 0)),
        ],
        out_specs=pl.BlockSpec((step,) + shape[1:], lambda c: (c, 0, 0, 0)),
        out_shape=jax.ShapeDtypeStruct(shape, jnp.bfloat16),
        scratch_shapes=[pltpu.VMEM((6 * 64, 4 * 64), jnp.bfloat16) for _ in range(2)],
        compiler_params=params(),
        cost_estimate=LIGHT,
        name="near_inner",
    )(taps, field)


def finish_kernel(taps, before, field, after, inner, planar, ix_table, iy_table, out, waves, even,
                  odd):
    step = pl.program_id(0)
    slabs, lines = planar.shape[:2]
    planes = field.shape[1]
    span = planes * NY

    @pl.when(step == 0)
    def _():
        left = jnp.concatenate([planar[s] for s in range(slabs)], axis=0)
        for t in range(2):
            wave = dot(left, iy_table[0, :, t * span : (t + 1) * span]).astype(jnp.bfloat16)
            for s in range(slabs):
                waves[s, t] = wave[s * lines : (s + 1) * lines]

    rows = field.shape[0] * (KX // slabs)
    here = pl.ds(pl.multiple_of(rows * step, rows), rows)
    right = [waves[s, t, here, :] for s in range(slabs) for t in range(2)]
    right = jnp.concatenate(right, axis=0)
    far = [
        dot(ix_table[...], right[:, 2 * p * NY : 2 * (p + 1) * NY]) for p in range(planes // 2)
    ]

    def store(c, p, near):
        for q in range(2):
            total = near[q] + far[p][c * NX : (c + 1) * NX, q * NY : (q + 1) * NY]
            out[c, 2 * p + q] = total.astype(jnp.bfloat16)

    def visit(c, band):
        low = [before[c, 0]] + [field[c, z] for z in range(3)]
        high = [field[c, z] for z in range(planes - 3, planes)] + [after[c, 0]]
        for p, near in zip((0, planes // 2 - 1), apply_band([low, high], band)):
            store(c, p, [near[:, :NY], near[:, NY:]])
        for p in range(1, planes // 2 - 1):
            store(c, p, [inner[c, 2 * p - 2 + q].astype(jnp.float32) for q in range(2)])

    banded(True, taps, 0, even, odd, field.shape[0])(visit)


def finish(planar, spread, rims, inner, taps):
    slabs, lines, width = planar.shape
    channels, planes = spread.shape[:2]
    step = 8
    ix_table = constant(inverse_x_table(slabs, step))
    iy_table = constant(inverse_y_table(planes, planes))
    rim = pl.BlockSpec((step, 1, NX, NY), lambda c: (c, 0, 0, 0))
    sheets = pl.BlockSpec((step, planes, NX, NY), lambda c: (c, 0, 0, 0))
    return pl.pallas_call(
        finish_kernel,
        grid=(channels // step,),
        in_specs=[
            pl.BlockSpec(memory_space=pltpu.SMEM),
            rim,
            sheets,
            rim,
            pl.BlockSpec((step,) + inner.shape[1:], lambda c: (c, 0, 0, 0)),
            whole(planar.shape),
            whole(ix_table.shape),
            whole(iy_table.shape),
        ],
        out_specs=sheets,
        out_shape=jax.ShapeDtypeStruct(spread.shape, jnp.bfloat16),
        scratch_shapes=[
            pltpu.VMEM((slabs, 2, lines, planes * NY), jnp.bfloat16),
            pltpu.VMEM((6 * 64, 4 * 64), jnp.bfloat16),
            pltpu.VMEM((6 * 64, 4 * 64), jnp.bfloat16),
        ],
        compiler_params=params(),
        cost_estimate=HEAVY,
        name="finish",
    )(taps, rims[0], spread, rims[1], inner, planar, ix_table, iy_table)


def gradient_kernel(depth, where, gathered, first, second, out):
    step = pl.program_id(0)
    samples, rows, lines = gathered.shape
    half = rows // 4
    lane = lax.broadcasted_iota(jnp.int32, (1, lines), 1)
    mine = lane % depth == step
    spectra = [gathered[s, : 2 * half] for s in range(samples)]
    duals = []
    for s in range(samples):
        real = gathered[s, 2 * half : 3 * half]
        imag = gathered[s, 3 * half :]
        duals.append(jnp.where(where[0] == 0, real, imag))
        duals.append(jnp.where(where[0] == 0, imag, -real))
    spectra = jnp.where(mine, jnp.concatenate(spectra, axis=0), 0)
    duals = jnp.where(mine, jnp.concatenate(duals, axis=0), 0)
    wide = dot(duals, second[...])
    for column in range(0, out.shape[1], 256):
        product = dot(spectra, first[0, :, column : column + 256])
        for at in range(0, 256, 128):
            total = 0.0
            for s in range(2 * samples):
                here = slice(s * half, (s + 1) * half)
                total = total + product[here, at : at + 128] * wide[here]
            out[:, column + at : column + at + 128] = total * (1.0 / samples)


def weight_gradient(gathered, depth, width, index):
    samples, rows, lines = gathered.shape
    channels = lines // depth
    square = channels * channels
    cuts = square // width
    first = first_table(channels, depth).reshape(lines, cuts, width).transpose(1, 0, 2)
    first = constant(first)
    second = constant(second_table(channels, depth)[:, :128])
    where = jnp.stack([index // cuts, index % cuts]).astype(jnp.int32)
    half = rows // 4
    return pl.pallas_call(
        functools.partial(gradient_kernel, depth),
        grid_spec=pltpu.PrefetchScalarGridSpec(
            num_scalar_prefetch=1,
            grid=(depth,),
            in_specs=[
                pl.BlockSpec(gathered.shape, lambda j, w: (0, 0, 0)),
                pl.BlockSpec((1, lines, width), lambda j, w: (w[1], 0, 0)),
                pl.BlockSpec(second.shape, lambda j, w: (0, 0)),
            ],
            out_specs=pl.BlockSpec((half, width), lambda j, w: (j, 0)),
        ),
        out_shape=jax.ShapeDtypeStruct((depth * half, width), jnp.float32),
        compiler_params=params(),
        cost_estimate=LIGHT,
        name="weight_gradient",
    )(where, gathered, first, second)


def exchange(first, last):
    size = lax.axis_size("slab")
    up = [(i, i + 1) for i in range(size - 1)]
    down = [(j, i) for i, j in up]
    return lax.ppermute(last, "slab", up), lax.ppermute(first, "slab", down)


def swap(planar):
    return lax.all_to_all(planar, "slab", split_axis=0, concat_axis=0)


def local_fast(feats, grains, spec_weight, taps, point_weight, bias, cotangent):
    slabs = lax.axis_size("slab")
    copies = lax.axis_size("dp")
    barrier = lax.optimization_barrier
    field = feats[0]
    channels = field.shape[0]
    cell_scale = 1.0 / math.sqrt(NX * NY * NZ)
    mode_scale = 1.0 / math.sqrt(KX * KY * KZ)
    mode_rows = spec_weight.shape[0]
    weight = spec_weight.reshape(mode_rows * KZ, 2 * channels * channels)
    width = weight.shape[1] // copies

    first, first_high, last, last_high = cut_rims(field)
    rims = exchange(first, last)
    planar = swap(forward_modes(field, slabs))
    rims, first, last = barrier((rims, first_high, last_high))
    rims_high = exchange(first, last)
    planar, smooth = barrier((planar, smooth_planes(field, rims, taps)))
    spectrum, planar = mix(planar, weight, cell_scale, 0.5 * mode_scale)
    smooth, spectrum = barrier((smooth, spectrum))
    planar = swap(planar)
    smooth = smooth_planes(field, rims_high, taps, smooth)
    spread, planar, first, last = layer(planar, smooth, cotangent[0], grains[0], bias, point_weight)
    rims = exchange(first, last)
    planar, send = mix(swap(planar), weight, 0.5 * mode_scale, cell_scale, spectrum, copies)
    planar = swap(planar)
    send, spread = barrier((send, spread))
    inner = near_inner(spread, taps)
    grad_feats = finish(planar, spread, rims, inner, taps)
    gathered = lax.all_to_all(send, "dp", split_axis=0, concat_axis=0)
    grad_feats, gathered = barrier((grad_feats, gathered))
    grad_feats = grad_feats[None]
    grad_spec = weight_gradient(gathered, KX // slabs, width, lax.axis_index("dp"))
    return (grad_feats, grad_spec.reshape(mode_rows, KZ, width))


def local(feats, grains, spec_weight, taps, point_weight, bias, cotangent):
    samples, channels, planes = feats.shape[:3]
    width = spec_weight.shape[2] // lax.axis_size("dp")
    fits = (
        lax.axis_size("slab") * 4 == KX
        and samples == 1
        and channels == 32
        and planes == 8
        and channels * channels % width == 0
        and width % 128 == 0
    )
    form = local_fast if fits else local_any
    return form(feats, grains, spec_weight, taps, point_weight, bias, cotangent)


def solution(mesh):
    in_specs = (
        P(("grp", "dp"), None, "slab", None, None),
        P(("grp", "dp"), "slab", None, None),
        P("slab", None, None),
        P(),
        P(),
        P(),
        P(("grp", "dp"), None, "slab", None, None),
    )
    out_specs = (P(("grp", "dp"), None, "slab", None, None), P("slab", "grp", "dp"))
    return jax.shard_map(local, mesh=mesh, in_specs=in_specs, out_specs=out_specs, check_vma=False)
```

```python
import functools
import math

import jax
import jax.numpy as jnp
import ml_dtypes
import numpy as np
from jax import lax
from jax.experimental import pallas as pl
from jax.experimental.pallas import tpu as pltpu
from jax.sharding import PartitionSpec as P

NX = 128
NY = 128
NZ = 32
KX = 16
KY = 16
KZ = 16


HIGHEST = lax.Precision.HIGHEST


def extended(shard, sides, width):
    for axis, dim in sides:
        size, length = (lax.axis_size(axis), shard.shape[dim])
        up = [(i, (i + 1) % size) for i in range(size - 1)]
        down = [(j, i) for i, j in up]
        last = lax.slice_in_dim(shard, length - width, length, axis=dim)
        first = lax.slice_in_dim(shard, 0, width, axis=dim)
        before = lax.ppermute(last, axis, up)
        after = lax.ppermute(first, axis, down)
        shard = jnp.concatenate([before, shard, after], axis=dim)
    return shard


def tables(count, length, span):
    indices = jnp.arange(count, dtype=jnp.int32)
    frequency = jnp.where(indices < count // 2, indices, length - count + indices)
    position = jnp.arange(span, dtype=jnp.int32)
    phases = frequency[:, None] * position[None, :] % length
    angles = phases.astype(jnp.float32) * (2.0 * math.pi / length)
    return (jnp.cos(angles), jnp.sin(angles))


def mobility(grains):
    leading = [(0, 0)] * (grains.ndim - 2)
    along_x = (grains[..., 1:, :] != grains[..., :-1, :]).astype(jnp.float32)
    along_y = (grains[..., :, 1:] != grains[..., :, :-1]).astype(jnp.float32)
    differ = jnp.pad(along_x, leading + [(1, 0), (0, 0)]) + jnp.pad(
        along_x, leading + [(0, 1), (0, 0)]
    )
    differ = (
        differ
        + jnp.pad(along_y, leading + [(0, 0), (1, 0)])
        + jnp.pad(along_y, leading + [(0, 0), (0, 1)])
    )
    return 0.25 * (1.0 + differ)


def stencil(padded, taps, adjoint):
    planes = padded.shape[-3] - 2
    rows_x = padded.shape[-2] - 2
    rows_y = padded.shape[-1] - 2
    total = jnp.zeros(padded.shape[:-3] + (planes, rows_x, rows_y), jnp.float32)
    for offset in range(27):
        shift_z, shift_x, shift_y = (offset // 9, offset // 3 % 3, offset % 3)
        if adjoint:
            shift_z, shift_x, shift_y = (2 - shift_z, 2 - shift_x, 2 - shift_y)
        window = padded[
            ..., shift_z : shift_z + planes, shift_x : shift_x + rows_x, shift_y : shift_y + rows_y
        ]
        total = total + taps[offset][:, None, None, None] * window.astype(jnp.float32)
    return total


def plane_forward(field, cos_x, sin_x, cos_y, sin_y):
    real_y = jnp.einsum("...xy,ky->...xk", field, cos_y, precision=HIGHEST)
    imag_y = -jnp.einsum("...xy,ky->...xk", field, sin_y, precision=HIGHEST)
    real_part = jnp.einsum("...xk,jx->...jk", real_y, cos_x, precision=HIGHEST) + jnp.einsum(
        "...xk,jx->...jk", imag_y, sin_x, precision=HIGHEST
    )
    imag_part = jnp.einsum("...xk,jx->...jk", imag_y, cos_x, precision=HIGHEST) - jnp.einsum(
        "...xk,jx->...jk", real_y, sin_x, precision=HIGHEST
    )
    return (real_part, imag_part)


def plane_inverse(real_part, imag_part, cos_x, sin_x, cos_y, sin_y):
    real_x = jnp.einsum("...jk,jx->...xk", real_part, cos_x, precision=HIGHEST) - jnp.einsum(
        "...jk,jx->...xk", imag_part, sin_x, precision=HIGHEST
    )
    imag_x = jnp.einsum("...jk,jx->...xk", imag_part, cos_x, precision=HIGHEST) + jnp.einsum(
        "...jk,jx->...xk", real_part, sin_x, precision=HIGHEST
    )
    return jnp.einsum("...xk,ky->...xy", real_x, cos_y, precision=HIGHEST) - jnp.einsum(
        "...xk,ky->...xy", imag_x, sin_y, precision=HIGHEST
    )


def depth_forward(packed, cos_table, sin_table):
    width = packed.shape[-1] // 2
    real_in = packed[..., :width]
    imag_in = packed[..., width:]
    real_out = jnp.einsum("pszc,kz->pskc", real_in, cos_table, precision=HIGHEST) + jnp.einsum(
        "pszc,kz->pskc", imag_in, sin_table, precision=HIGHEST
    )
    imag_out = jnp.einsum("pszc,kz->pskc", imag_in, cos_table, precision=HIGHEST) - jnp.einsum(
        "pszc,kz->pskc", real_in, sin_table, precision=HIGHEST
    )
    return jnp.concatenate([real_out, imag_out], axis=-1)


def depth_inverse(real_modes, imag_modes, cos_table, sin_table):
    real_out = jnp.einsum("pskc,kz->pszc", real_modes, cos_table, precision=HIGHEST) - jnp.einsum(
        "pskc,kz->pszc", imag_modes, sin_table, precision=HIGHEST
    )
    imag_out = jnp.einsum("pskc,kz->pszc", imag_modes, cos_table, precision=HIGHEST) + jnp.einsum(
        "pskc,kz->pszc", real_modes, sin_table, precision=HIGHEST
    )
    return jnp.concatenate([real_out, imag_out], axis=-1)


def rim_planes(field):
    return extended(field, (("slab", 2),), 1)


def local_any(feats, grains, spec_weight, taps, point_weight, bias, cotangent):
    samples_here = feats.shape[0]
    channels = feats.shape[1]
    planes = feats.shape[2]
    cos_x, sin_x = tables(KX, NX, NX)
    cos_y, sin_y = tables(KY, NY, NY)
    cos_full, sin_full = tables(KZ, NZ, NZ)
    cell_scale = math.sqrt(NX * NY * NZ)
    mode_scale = math.sqrt(KX * KY * KZ)
    mode_rows = spec_weight.shape[0]
    weights = spec_weight.astype(jnp.float32).reshape(mode_rows, KZ, 2, channels, channels)
    w_real = weights[:, :, 0]
    w_imag = weights[:, :, 1]
    moving = mobility(grains)[:, None]

    def to_modes(field):
        real_plane, imag_plane = plane_forward(field, cos_x, sin_x, cos_y, sin_y)
        packed = jnp.stack([real_plane, imag_plane], axis=1)
        packed = packed.transpose(4, 5, 0, 3, 1, 2).reshape(
            KX * KY, samples_here, planes, 2 * channels
        )
        moved = lax.all_to_all(packed, "slab", split_axis=0, concat_axis=2, tiled=True)
        summed = depth_forward(moved, cos_full, sin_full)
        return (summed[..., :channels], summed[..., channels:])

    def from_modes(real_modes, imag_modes):
        planar = depth_inverse(real_modes, imag_modes, cos_full, sin_full)
        packed = lax.all_to_all(planar, "slab", split_axis=2, concat_axis=0, tiled=True)
        grouped = packed.reshape(KX, KY, samples_here, planes, 2, channels).transpose(
            2, 4, 5, 3, 0, 1
        )
        return plane_inverse(grouped[:, 0], grouped[:, 1], cos_x, sin_x, cos_y, sin_y)

    zero_rim = ((0, 0), (0, 0), (0, 0), (1, 1), (1, 1))
    padded = jnp.pad(rim_planes(feats), zero_rim)
    smooth = stencil(padded, taps, False).astype(jnp.bfloat16)
    local_part = moving * jnp.einsum(
        "sczxy,co->sozxy", smooth, point_weight, preferred_element_type=jnp.float32
    )
    spec_real, spec_imag = to_modes(feats.astype(jnp.float32))
    spec_real = spec_real / cell_scale
    spec_imag = spec_imag / cell_scale
    mixed_real = jnp.einsum("pskc,pkco->psko", spec_real, w_real, precision=HIGHEST) - jnp.einsum(
        "pskc,pkco->psko", spec_imag, w_imag, precision=HIGHEST
    )
    mixed_imag = jnp.einsum("pskc,pkco->psko", spec_real, w_imag, precision=HIGHEST) + jnp.einsum(
        "pskc,pkco->psko", spec_imag, w_real, precision=HIGHEST
    )
    spectral = from_modes(mixed_real, mixed_imag) / mode_scale
    pre = spectral + local_part + bias[None, :, None, None, None]
    gate = jax.nn.sigmoid(pre)
    delta = (cotangent.astype(jnp.float32) * gate * (1.0 + pre * (1.0 - gate))).astype(jnp.bfloat16)
    dual_real, dual_imag = to_modes(delta.astype(jnp.float32))
    dual_real = dual_real / mode_scale
    dual_imag = dual_imag / mode_scale
    batch_total = samples_here * lax.axis_size("dp")
    grad_real = jnp.einsum("pskc,psko->pkco", spec_real, dual_real, precision=HIGHEST) + jnp.einsum(
        "pskc,psko->pkco", spec_imag, dual_imag, precision=HIGHEST
    )
    grad_imag = jnp.einsum("pskc,psko->pkco", spec_real, dual_imag, precision=HIGHEST) - jnp.einsum(
        "pskc,psko->pkco", spec_imag, dual_real, precision=HIGHEST
    )
    grad_terms = (jnp.stack([grad_real, grad_imag], axis=2) / batch_total).reshape(
        mode_rows, KZ, 2 * channels * channels
    )
    grad_spec = lax.psum_scatter(
        grad_terms.astype(jnp.bfloat16), "dp", scatter_dimension=2, tiled=True
    ).astype(jnp.float32)
    back_real = jnp.einsum("psko,pkco->pskc", dual_real, w_real, precision=HIGHEST) + jnp.einsum(
        "psko,pkco->pskc", dual_imag, w_imag, precision=HIGHEST
    )
    back_imag = jnp.einsum("psko,pkco->pskc", dual_imag, w_real, precision=HIGHEST) - jnp.einsum(
        "psko,pkco->pskc", dual_real, w_imag, precision=HIGHEST
    )
    spectral_back = from_modes(back_real, back_imag) / cell_scale
    spread = (
        moving
        * jnp.einsum("sozxy,co->sczxy", delta, point_weight, preferred_element_type=jnp.float32)
    ).astype(jnp.bfloat16)
    spread_padded = jnp.pad(rim_planes(spread), zero_rim)
    local_back = stencil(spread_padded, taps, True)
    grad_feats = (spectral_back + local_back).astype(jnp.bfloat16)
    return (grad_feats, grad_spec)


def frequencies(count, length):
    index = np.arange(count)
    return np.where(index < count // 2, index, length - count + index)


def angles(count, length):
    phases = np.outer(frequencies(count, length), np.arange(length)) % length
    return phases * (2.0 * np.pi / length)


def constant(array):
    return jnp.asarray(np.asarray(array, np.float32).astype(ml_dtypes.bfloat16))


def forward_x_table(slabs, split):
    a = angles(KX, NX).reshape(slabs, KX // slabs, NX)
    trig = np.stack([np.cos(a), np.sin(a)])
    table = np.einsum("tsjx,cd->tscjdx", trig, np.eye(2)).reshape(-1, 2, NX // 8, 8)
    if split:
        table = table.transpose(0, 2, 1, 3)
    return table.reshape(4 * KX, 2 * NX)


def halved(table, planes):
    table = table.reshape(-1, planes * 2, 2, KY // 2).transpose(0, 2, 1, 3)
    return table.reshape(-1, planes * 2 * KY)


def forward_y_table(planes):
    a = angles(KY, NY)
    cos, sin = np.cos(a).T, np.sin(a).T
    block = np.stack([np.stack([cos, -sin], 1), np.stack([-sin, -cos], 1)])
    pick = np.eye(planes).reshape(planes // 2, 2, planes)
    table = np.einsum("pqz,tyrk->ptqyzrk", pick, block)
    return halved(table.reshape(planes * 2 * NY, planes * 2 * KY), planes)


def forward_z_table():
    a = angles(KZ, NZ)
    cos, sin = np.cos(a).T, np.sin(a).T
    block = np.stack([np.stack([cos, -sin], 1), np.stack([sin, cos], 1)], 1)
    table = np.einsum("zrqm,kl->zrkqlm", block, np.eye(KY // 2))
    return table.reshape(NZ * KY, KY * KZ)


def inverse_z_table():
    a = angles(KZ, NZ)
    cos, sin = np.cos(a), np.sin(a)
    block = np.stack([np.stack([cos, sin], 2), np.stack([-sin, cos], 2)])
    table = np.einsum("rmzq,kl->rkmzql", block, np.eye(KY // 2))
    return table.reshape(KY * KZ, NZ * KY)


def inverse_y_table(planes, group):
    a = angles(KY, NY)
    cos, sin = np.cos(a), np.sin(a)
    block = np.stack([np.stack([cos, -sin], 1), np.stack([-sin, -cos], 1)])
    pick = np.eye(planes).reshape(planes // group, group, planes)
    table = np.einsum("pqz,rkty->ptqyzrk", pick, block)
    table = halved(table.reshape(-1, planes * 2 * KY), planes)
    return table.reshape(planes // group, 2 * group * NY, planes * 2 * KY).transpose(0, 2, 1)


def inverse_x_table(slabs, group):
    a = angles(KX, NX).reshape(slabs, KX // slabs, NX)
    trig = np.stack([np.cos(a), np.sin(a)])
    table = np.einsum("tsjx,cd->cxstdj", trig, np.eye(group))
    return table.reshape(group * NX, 2 * KX * group)


def first_table(channels, depth):
    table = np.einsum("ac,j,b->ajcb", np.eye(channels), np.ones(depth), np.ones(channels))
    return table.reshape(channels * depth, channels * channels)


def second_table(channels, depth):
    table = np.einsum("ac,j,b->ajbc", np.eye(channels), np.ones(depth), np.ones(channels))
    return table.reshape(channels * depth, channels * channels)


LIGHT = pl.CostEstimate(flops=10**7, bytes_accessed=10**5, transcendentals=0)
HEAVY = pl.CostEstimate(flops=10**11, bytes_accessed=10**8, transcendentals=0)


def dot(a, b):
    return jnp.dot(a, b, preferred_element_type=jnp.float32)


def whole(shape):
    return pl.BlockSpec(shape, lambda *_: (0,) * len(shape))


def params(**kw):
    return pltpu.CompilerParams(vmem_limit_bytes=63438848, **kw)


def store_rows(rows, pair, x_table, load):
    slabs, lines = rows.shape[2:4]
    for i in range(lines // 16):
        parts = [dot(x_table[...], load(2 * i + k)) for k in range(2)]
        for t in range(2):
            for s in range(slabs):
                here = slice(8 * (t * slabs + s), 8 * (t * slabs + s) + 8)
                both = jnp.concatenate([part[here] for part in parts], axis=0)
                rows[pair, t, s, 16 * i : 16 * i + 16, :] = both.astype(jnp.bfloat16)


def store_modes(rows, y_table, out):
    pairs, _, slabs, lines, _ = rows.shape
    left = [
        jnp.concatenate([rows[p, t, s] for p in range(pairs) for t in range(2)], axis=1)
        for s in range(slabs)
    ]
    modes = dot(jnp.concatenate(left, axis=0), y_table[...])
    for s in range(slabs):
        out[s] = modes[s * lines : (s + 1) * lines].astype(jnp.bfloat16)


def rims_kernel(low, high, *rims):
    step = pl.program_id(0)
    half = pl.num_programs(0) // 2
    for k, source in enumerate((low, high)):

        @pl.when(step < half)
        def _():
            rims[2 * k][...] = source[...]

        @pl.when(step >= half)
        def _():
            rims[2 * k + 1][...] = source[...]


def cut_rims(field):
    channels, planes = field.shape[:2]
    steps = 2
    rim = jax.ShapeDtypeStruct((channels // 2, 1, NX, NY), jnp.bfloat16)
    block = (channels // steps, 1, NX, NY)
    outs = [
        pl.BlockSpec(block, lambda c: (jnp.minimum(c, steps // 2 - 1), 0, 0, 0)),
        pl.BlockSpec(block, lambda c: (jnp.maximum(c - steps // 2, 0), 0, 0, 0)),
    ]
    return pl.pallas_call(
        rims_kernel,
        grid=(steps,),
        in_specs=[
            pl.BlockSpec(block, lambda c: (c, 0, 0, 0)),
            pl.BlockSpec(block, lambda c: (c, planes - 1, 0, 0)),
        ],
        out_specs=outs + outs,
        out_shape=[rim] * 4,
        compiler_params=params(),
        cost_estimate=LIGHT,
        name="rims",
    )(field, field)


def forward_kernel(field, x_table, y_table, out, rows):
    pair = pl.program_id(0)
    pairs = rows.shape[0]

    def load(i):
        halves = [field[2 * i : 2 * i + 2, q].reshape(2 * NX, NY) for q in range(2)]
        return jnp.concatenate(halves, axis=1)

    store_rows(rows, pair, x_table, load)

    @pl.when(pair == pairs - 1)
    def _():
        store_modes(rows, y_table, out)


def forward_modes(field, slabs):
    channels, planes = field.shape[:2]
    lines = channels * (KX // slabs)
    x_table = constant(forward_x_table(slabs, False))
    y_table = constant(forward_y_table(planes))
    shape = (slabs, lines, planes * 2 * KY)
    return pl.pallas_call(
        forward_kernel,
        grid=(planes // 2,),
        in_specs=[
            pl.BlockSpec((channels, 2, NX, NY), lambda p: (0, p, 0, 0)),
            whole(x_table.shape),
            whole(y_table.shape),
        ],
        out_specs=whole(shape),
        out_shape=jax.ShapeDtypeStruct(shape, jnp.bfloat16),
        scratch_shapes=[pltpu.VMEM((planes // 2, 2, slabs, lines, 2 * NY), jnp.bfloat16)],
        compiler_params=params(),
        cost_estimate=LIGHT,
        name="forward_modes",
    )(field, x_table, y_table)


def mixing_kernel(scale_in, scale_out, adjoint, planar, weight, z_in, z_out, spread_table,
                  sum_table, *rest):
    if adjoint:
        partner, out, send, spectrum, total, wide, product = rest
    else:
        spectrum, out, total, wide, product = rest
    step = pl.program_id(0)
    steps = pl.num_programs(0)
    slabs, lines, width = planar.shape
    half = width // 2
    quarter = spectrum.shape[0] // 4
    lanes = weight.shape[1] // 2
    depth = weight.shape[0] // (2 * quarter)

    @pl.when(step == 0)
    def _():
        left = [
            jnp.concatenate([planar[s, :, h : h + half] for s in range(slabs)], axis=1)
            for h in (0, half)
        ]
        modes = dot(jnp.concatenate(left, axis=0), z_in[...]) * scale_in
        for h in range(2):
            here = modes[h * lines : (h + 1) * lines].T.astype(jnp.bfloat16)
            spectrum[2 * h * quarter : 2 * (h + 1) * quarter] = here
            if adjoint:
                for d in range(send.shape[0]):
                    send[d, 2 * (h + 2) * quarter : 2 * (h + 3) * quarter] = here
        if adjoint:
            for d in range(send.shape[0]):
                send[d, : 4 * quarter] = partner[...]
        total[...] = jnp.zeros_like(total)

    lane = lax.broadcasted_iota(jnp.int32, (1, lines), 1) % (depth * steps)
    block = 32
    tile = wide.shape[1]
    for j in range(depth):
        mine = lane == depth * step + j
        wide[...] = dot(jnp.where(mine, spectrum[...], 0), spread_table[...])
        for at in range(0, 2 * quarter, block):
            row = 2 * j * quarter + at
            real_at = at + (at // quarter) * quarter
            imag_at = real_at + quarter
            sums = [0.0, 0.0]
            for column in range(0, lanes, 128):
                here = slice(column, column + 128) if tile == lanes else slice(None)
                real_wide = wide[real_at : real_at + block, here]
                imag_wide = wide[imag_at : imag_at + block, here]
                w_real = weight[row : row + block, column : column + 128]
                w_imag = weight[row : row + block, lanes + column : lanes + column + 128]
                w_real = w_real.astype(jnp.float32)
                w_imag = w_imag.astype(jnp.float32)
                if adjoint:
                    real = real_wide * w_real + imag_wide * w_imag
                    imag = imag_wide * w_real - real_wide * w_imag
                    there = slice(column, column + 128)
                    product[real_at : real_at + block, there] = real.astype(jnp.bfloat16)
                    product[imag_at : imag_at + block, there] = imag.astype(jnp.bfloat16)
                else:
                    sums[0] = sums[0] + (real_wide * w_real - imag_wide * w_imag)
                    sums[1] = sums[1] + (real_wide * w_imag + imag_wide * w_real)
            if not adjoint:
                product[real_at : real_at + block] = sums[0].astype(jnp.bfloat16)
                product[imag_at : imag_at + block] = sums[1].astype(jnp.bfloat16)
        total[...] += jnp.where(mine, dot(product[...], sum_table[...]), 0.0)

    @pl.when(step == steps - 1)
    def _():
        modes = total[...] * scale_out
        left = [modes[2 * h * quarter : 2 * (h + 1) * quarter].T for h in range(2)]
        modes = dot(jnp.concatenate(left, axis=0).astype(jnp.bfloat16), z_out[...])
        for s in range(slabs):
            for h in range(2):
                here = modes[h * lines : (h + 1) * lines, s * half : (s + 1) * half]
                out[s, :, h * half : (h + 1) * half] = here.astype(jnp.bfloat16)


def mix(planar, weight, scale_in, scale_out, partner=None, copies=0):
    slabs, lines, width = planar.shape
    adjoint = partner is not None
    depth = KX // slabs
    channels = lines // depth
    rows = KY * KZ
    steps = 2
    z_in = constant(forward_z_table())
    z_out = constant(inverse_z_table())
    first = first_table(channels, depth)
    second = second_table(channels, depth)
    spread_table = constant(second[:, :128] if adjoint else first)
    sum_table = constant(first.T if adjoint else second[:, :128].T)
    shape = (2 * rows, lines)
    in_specs = [
        whole(planar.shape),
        pl.BlockSpec((depth // steps * rows, weight.shape[1]), lambda j: (j, 0)),
        whole(z_in.shape),
        whole(z_out.shape),
        whole(spread_table.shape),
        whole(sum_table.shape),
    ]
    operands = [planar, weight, z_in, z_out, spread_table, sum_table]
    scratch = [
        pltpu.VMEM(shape, jnp.float32),
        pltpu.VMEM((2 * rows, spread_table.shape[1]), jnp.float32),
        pltpu.VMEM((2 * rows, sum_table.shape[0]), jnp.bfloat16),
    ]
    if adjoint:
        in_specs.append(whole(shape))
        operands.append(partner)
        scratch = [pltpu.VMEM(shape, jnp.bfloat16)] + scratch
        outs = [planar.shape, (copies, 2 * shape[0], lines)]
    else:
        outs = [shape, planar.shape]
    return pl.pallas_call(
        functools.partial(mixing_kernel, scale_in, scale_out, adjoint),
        grid=(steps,),
        in_specs=in_specs,
        out_specs=[whole(out) for out in outs],
        out_shape=[jax.ShapeDtypeStruct(out, jnp.bfloat16) for out in outs],
        scratch_shapes=scratch,
        compiler_params=params(),
        cost_estimate=HEAVY,
        name="mix_back" if adjoint else "mix",
    )(*operands)


def plane_mobility(grains):
    same = [
        jnp.concatenate([grains[:1], grains[:-1]], axis=0),
        jnp.concatenate([grains[1:], grains[-1:]], axis=0),
        jnp.concatenate([grains[:, :1], grains[:, :-1]], axis=1),
        jnp.concatenate([grains[:, 1:], grains[:, -1:]], axis=1),
    ]
    total = jnp.full(grains.shape, 0.25, jnp.float32)
    for other in same:
        total = total + jnp.where(grains != other, 0.25, 0.0)
    return total


def layer_kernel(bias, planar, smooth, cotangent, grains, point_weight, repeat, ix_table, iy_table,
                 x_table, y_table, spread, out, first, last, *rest):
    pair = pl.program_id(0)
    waves, spectral, moving, delta, rows, bias_wide, mix_out, mix_in = rest
    pairs = rows.shape[0]
    channels = cotangent.shape[0]
    slabs = planar.shape[0]

    @pl.when(pair == 0)
    def _():
        for c in range(channels):
            bias_wide[c] = jnp.full(bias_wide.shape[1:], 0.5 * bias[c], jnp.float32)
        tall = dot(repeat[...], point_weight[...]).astype(jnp.bfloat16)
        square = lax.dot_general(
            tall, repeat[...], (((1,), (1,)), ((), ())), preferred_element_type=jnp.float32
        )
        row = lax.broadcasted_iota(jnp.int32, square.shape, 0) % 8
        column = lax.broadcasted_iota(jnp.int32, square.shape, 1) % 8
        square = jnp.where(row == column, square, 0.0)
        mix_in[...] = square.astype(jnp.bfloat16)
        mix_out[...] = square.T.astype(jnp.bfloat16)

    lines = planar.shape[1]
    step = jnp.concatenate([planar[s] for s in range(slabs)], axis=0)
    step = dot(step, iy_table[0]).astype(jnp.bfloat16)
    for s in range(slabs):
        for t in range(2):
            waves[s, t] = step[s * lines : (s + 1) * lines, 2 * NY * t : 2 * NY * (t + 1)]
    group = 8 * (KX // slabs)
    for g in range(channels // 8):
        here = slice(g * group, (g + 1) * group)
        wave = [waves[s, t, here, :] for s in range(slabs) for t in range(2)]
        step = dot(ix_table[...], jnp.concatenate(wave, axis=0))
        spectral[8 * g : 8 * g + 8] = step.reshape(8, NX, 2 * NY)
    for q in range(2):
        moving[:, q * NY : (q + 1) * NY] = 0.5 * plane_mobility(grains[q])

    def body(i, _):
        x = pl.multiple_of(16 * i, 16)
        halves = [cotangent[:, q, pl.ds(x, 16), :] for q in range(2)]
        cotangent_here = jnp.concatenate(halves, axis=2).astype(jnp.float32)
        spreads = []
        for h in range(2):
            at = pl.ds(pl.multiple_of(x + 8 * h, 8), 8)
            mobile = moving[at, :][None]
            local = dot(mix_out[...], smooth[0, 2 * i + h]).reshape(channels, 8, 2 * NY)
            half = spectral[:, at, :] + mobile * local + bias_wide[...]
            wave = jnp.tanh(half)
            slope = (1.0 + wave) * (1.0 + (half - half * wave))
            change = cotangent_here[:, 8 * h : 8 * h + 8, :] * slope
            right = change.reshape(8 * channels, 2 * NY).astype(jnp.bfloat16)
            delta[2 * i + h] = right
            back = dot(mix_in[...], right).reshape(channels, 8, 2 * NY)
            spreads.append(mobile * back)
        both = jnp.concatenate(spreads, axis=1).astype(jnp.bfloat16)
        for q in range(2):
            spread[:, q, pl.ds(x, 16), :] = both[:, :, q * NY : (q + 1) * NY]
        return 0

    lax.fori_loop(0, NX // 16, body, 0, unroll=8)


    @pl.when(pair == 0)
    def _():
        first[:, 0] = spread[:, 0]

    @pl.when(pair == pairs - 1)
    def _():
        last[:, 0] = spread[:, 1]

    def load(i):
        return delta[:, 16 * i : 16 * i + 16, :].reshape(2 * NX, 2 * NY)

    store_rows(rows, pair, x_table, load)

    @pl.when(pair == pairs - 1)
    def _():
        store_modes(rows, y_table, out)


def layer(planar, smooth, cotangent, grains, bias, point_weight):
    slabs, lines, width = planar.shape
    channels, planes = cotangent.shape[:2]
    pairs = planes // 2
    repeat = constant(np.repeat(np.eye(channels), 8, axis=0))
    ix_table = constant(inverse_x_table(slabs, 8))
    iy_table = constant(inverse_y_table(planes, 2))
    x_table = constant(forward_x_table(slabs, True))
    y_table = constant(forward_y_table(planes))
    field = pl.BlockSpec((channels, 2, NX, NY), lambda p: (0, p, 0, 0))
    outs = [cotangent.shape, planar.shape] + [(channels, 1, NX, NY)] * 2
    return pl.pallas_call(
        layer_kernel,
        grid=(pairs,),
        in_specs=[
            pl.BlockSpec(memory_space=pltpu.SMEM),
            whole(planar.shape),
            pl.BlockSpec((1,) + smooth.shape[1:], lambda p: (p, 0, 0, 0)),
            field,
            pl.BlockSpec((2, NX, NY), lambda p: (p, 0, 0)),
            whole(point_weight.shape),
            whole(repeat.shape),
            whole(ix_table.shape),
            pl.BlockSpec((1,) + iy_table.shape[1:], lambda p: (p, 0, 0)),
            whole(x_table.shape),
            whole(y_table.shape),
        ],
        out_specs=[field] + [whole(out) for out in outs[1:]],
        out_shape=[jax.ShapeDtypeStruct(out, jnp.bfloat16) for out in outs],
        scratch_shapes=[
            pltpu.VMEM((slabs, 2, lines, 2 * NY), jnp.bfloat16),
            pltpu.VMEM((channels, NX, 2 * NY), jnp.float32),
            pltpu.VMEM((NX, 2 * NY), jnp.float32),
            pltpu.VMEM((NX // 8, 8 * channels, 2 * NY), jnp.bfloat16),
            pltpu.VMEM((pairs, 2, slabs, lines, 2 * NY), jnp.bfloat16),
            pltpu.VMEM((channels, 8, 2 * NY), jnp.float32),
            pltpu.VMEM((8 * channels, 8 * channels), jnp.bfloat16),
            pltpu.VMEM((8 * channels, 8 * channels), jnp.bfloat16),
        ],
        compiler_params=params(),
        cost_estimate=LIGHT,
        name="layer",
    )(bias, planar, smooth, cotangent, grains, point_weight, repeat, ix_table, iy_table, x_table,
      y_table)


def build_band(adjoint, taps, channel, band):
    row = lax.broadcasted_iota(jnp.int32, (8, 128), 0)
    lane = lax.broadcasted_iota(jnp.int32, (8, 128), 1)
    for dy in range(3):
        for q in range(2):
            halves = []
            for side in range(2):
                tile = jnp.zeros((8, 128), jnp.float32)
                for k in range(2):
                    dz = 2 * side + k - q
                    if not 0 <= dz <= 2:
                        continue
                    for dx in range(3):
                        number = 9 * dz + 3 * dx + dy
                        tap = taps[26 - number if adjoint else number, channel]
                        hit = lane == (64 * k + row + (dx - 1)) % 128
                        tile = jnp.where(hit, tap, tile)
                tiles = [pltpu.roll(tile, 8 * k, axis=1) if k > 0 else tile for k in range(8)]
                low = (row == 0) & (lane % 64 == 63)
                high = (row == 7) & (lane % 64 == 0)
                tiles[0] = jnp.where(low, 0.0, tiles[0])
                tiles[7] = jnp.where(high, 0.0, tiles[7])
                halves.append(jnp.concatenate(tiles[1:7] + [tiles[0], tiles[7]], axis=0))
            at = 64 * (2 * dy + q)
            band[at : at + 64, :] = jnp.concatenate(halves, axis=1).astype(jnp.bfloat16)


def apply_band(quads, band):
    blocks = range(6)
    lefts = [
        band[...],
        jnp.concatenate([band[64 * b : 64 * b + 48, :] for b in blocks], axis=0),
        jnp.concatenate([band[64 * b + 32 : 64 * b + 64, :] for b in blocks], axis=0),
    ]
    lane = lax.broadcasted_iota(jnp.int32, (NX, NY), 1)
    totals = []
    for group in range(0, len(quads), 2):
        products = []
        for left, x in zip(lefts, (0, 48, 64)):
            right = [
                jnp.concatenate([sheet[x : x + 64] for sheet in quads[group + p]], axis=0)
                for p in range(2)
            ]
            products.append(dot(left, jnp.concatenate(right, axis=1)))
        for p in range(2):
            wide = slice(NY * p, NY * (p + 1))
            pair = []
            for q in range(2):
                shifted = []
                for dy in range(3):
                    b = 2 * dy + q
                    pieces = [
                        products[0][64 * b + 48 : 64 * b + 56, wide],
                        products[0][64 * b : 64 * b + 48, wide],
                        products[1][48 * b : 48 * b + 48, wide],
                        products[2][32 * b : 32 * b + 16, wide],
                        products[2][32 * b + 24 : 32 * b + 32, wide],
                    ]
                    shifted.append(jnp.concatenate(pieces, axis=0))
                before = jnp.where(lane == 0, 0.0, pltpu.roll(shifted[0], 1, axis=1))
                after = jnp.where(lane == NY - 1, 0.0, pltpu.roll(shifted[2], NY - 1, axis=1))
                pair.append(shifted[1] + before + after)
            totals.append(jnp.concatenate(pair, axis=1))
    return totals


def banded(adjoint, taps, start, even, odd, channels):
    step = pl.program_id(0)
    final = start + channels * pl.num_programs(0) - 1
    bands = (even, odd)

    @pl.when(step == 0)
    def _():
        even[...] = jnp.zeros_like(even)
        odd[...] = jnp.zeros_like(odd)
        build_band(adjoint, taps, start, even)

    def run(visit):
        for c in range(channels):
            following = jnp.minimum(start + channels * step + c + 1, final)
            build_band(adjoint, taps, following, bands[(c + 1) % 2])
            visit(c, bands[c % 2])

    return run


def smooth_kernel(start, taps, before, field, after, *rest):
    out, even, odd = rest[-3:]
    planes = field.shape[1]
    totals = []

    def visit(c, band):
        sheets = [before[c, 0]] + [field[c, z] for z in range(planes)] + [after[c, 0]]
        totals.append(apply_band([sheets[z : z + 4] for z in range(0, planes, 2)], band))

        if c % 2 == 1:
            for p in range(planes // 2):
                both = [total[p].reshape(NX // 8, 8, 2 * NY) for total in totals[c - 1 : c + 1]]
                both = jnp.concatenate(both, axis=1).astype(jnp.bfloat16)
                out[p, :, 8 * (c - 1) : 8 * (c + 1), :] = both

    banded(False, taps, start, even, odd, field.shape[0])(visit)


def smooth_planes(field, rims, taps, done=None):
    channels, planes = field.shape[:2]
    pairs = planes // 2
    start = 0 if done is None else channels // 2
    step = 8
    skip = start // step
    rim = pl.BlockSpec((step, 1, NX, NY), lambda c: (c, 0, 0, 0))
    sheets = pl.BlockSpec((step, planes, NX, NY), lambda c: (c + skip, 0, 0, 0))
    in_specs = [pl.BlockSpec(memory_space=pltpu.SMEM), rim, sheets, rim]
    operands = [taps, rims[0], field, rims[1]]
    if done is not None:
        in_specs.append(pl.BlockSpec(memory_space=pl.ANY))
        operands.append(done)
    return pl.pallas_call(
        functools.partial(smooth_kernel, start),
        grid=(channels // 2 // step,),
        in_specs=in_specs,
        out_specs=pl.BlockSpec((pairs, NX // 8, 8 * step, 2 * NY), lambda c: (0, 0, c + skip, 0)),
        out_shape=jax.ShapeDtypeStruct((pairs, NX // 8, 8 * channels, 2 * NY), jnp.bfloat16),
        input_output_aliases={} if done is None else {4: 0},
        scratch_shapes=[pltpu.VMEM((6 * 64, 4 * 64), jnp.bfloat16) for _ in range(2)],
        compiler_params=params(),
        cost_estimate=LIGHT,
        name="smooth_low" if done is None else "smooth_high",
    )(*operands)


def inner_kernel(taps, field, out, even, odd):
    planes = field.shape[1]

    def visit(c, band):
        quads = [[field[c, z + k] for k in range(4)] for z in range(1, planes - 3, 2)]
        for p, near in enumerate(apply_band(quads, band)):
            total = near.astype(jnp.bfloat16)
            out[c, 2 * p] = total[:, :NY]
            out[c, 2 * p + 1] = total[:, NY:]

    banded(True, taps, 0, even, odd, field.shape[0])(visit)


def near_inner(field, taps):
    channels, planes = field.shape[:2]
    step = 8
    shape = (channels, planes - 4, NX, NY)
    return pl.pallas_call(
        inner_kernel,
        grid=(channels // step,),
        in_specs=[
            pl.BlockSpec(memory_space=pltpu.SMEM),
            pl.BlockSpec((step, planes, NX, NY), lambda c: (c, 0, 0, 0)),
        ],
        out_specs=pl.BlockSpec((step,) + shape[1:], lambda c: (c, 0, 0, 0)),
        out_shape=jax.ShapeDtypeStruct(shape, jnp.bfloat16),
        scratch_shapes=[pltpu.VMEM((6 * 64, 4 * 64), jnp.bfloat16) for _ in range(2)],
        compiler_params=params(),
        cost_estimate=LIGHT,
        name="near_inner",
    )(taps, field)


def finish_kernel(taps, before, field, after, inner, planar, ix_table, iy_table, out, waves, even,
                  odd):
    step = pl.program_id(0)
    slabs, lines = planar.shape[:2]
    planes = field.shape[1]
    span = planes * NY

    @pl.when(step == 0)
    def _():
        left = jnp.concatenate([planar[s] for s in range(slabs)], axis=0)
        for t in range(2):
            wave = dot(left, iy_table[0, :, t * span : (t + 1) * span]).astype(jnp.bfloat16)
            for s in range(slabs):
                waves[s, t] = wave[s * lines : (s + 1) * lines]

    rows = field.shape[0] * (KX // slabs)
    here = pl.ds(pl.multiple_of(rows * step, rows), rows)
    right = [waves[s, t, here, :] for s in range(slabs) for t in range(2)]
    right = jnp.concatenate(right, axis=0)
    far = [
        dot(ix_table[...], right[:, 2 * p * NY : 2 * (p + 1) * NY]) for p in range(planes // 2)
    ]

    def store(c, p, near):
        for q in range(2):
            total = near[q] + far[p][c * NX : (c + 1) * NX, q * NY : (q + 1) * NY]
            out[c, 2 * p + q] = total.astype(jnp.bfloat16)

    def visit(c, band):
        low = [before[c, 0]] + [field[c, z] for z in range(3)]
        high = [field[c, z] for z in range(planes - 3, planes)] + [after[c, 0]]
        for p, near in zip((0, planes // 2 - 1), apply_band([low, high], band)):
            store(c, p, [near[:, :NY], near[:, NY:]])
        for p in range(1, planes // 2 - 1):
            store(c, p, [inner[c, 2 * p - 2 + q].astype(jnp.float32) for q in range(2)])

    banded(True, taps, 0, even, odd, field.shape[0])(visit)


def finish(planar, spread, rims, inner, taps):
    slabs, lines, width = planar.shape
    channels, planes = spread.shape[:2]
    step = 8
    ix_table = constant(inverse_x_table(slabs, step))
    iy_table = constant(inverse_y_table(planes, planes))
    rim = pl.BlockSpec((step, 1, NX, NY), lambda c: (c, 0, 0, 0))
    sheets = pl.BlockSpec((step, planes, NX, NY), lambda c: (c, 0, 0, 0))
    return pl.pallas_call(
        finish_kernel,
        grid=(channels // step,),
        in_specs=[
            pl.BlockSpec(memory_space=pltpu.SMEM),
            rim,
            sheets,
            rim,
            pl.BlockSpec((step,) + inner.shape[1:], lambda c: (c, 0, 0, 0)),
            whole(planar.shape),
            whole(ix_table.shape),
            whole(iy_table.shape),
        ],
        out_specs=sheets,
        out_shape=jax.ShapeDtypeStruct(spread.shape, jnp.bfloat16),
        scratch_shapes=[
            pltpu.VMEM((slabs, 2, lines, planes * NY), jnp.bfloat16),
            pltpu.VMEM((6 * 64, 4 * 64), jnp.bfloat16),
            pltpu.VMEM((6 * 64, 4 * 64), jnp.bfloat16),
        ],
        compiler_params=params(),
        cost_estimate=HEAVY,
        name="finish",
    )(taps, rims[0], spread, rims[1], inner, planar, ix_table, iy_table)


def gradient_kernel(depth, where, gathered, first, second, out):
    step = pl.program_id(0)
    samples, rows, lines = gathered.shape
    quarter = rows // 8
    lane = lax.broadcasted_iota(jnp.int32, (1, lines), 1)
    mine = lane % depth == step
    spectra = [gathered[s, : 4 * quarter] for s in range(samples)]
    duals = []
    for s in range(samples):
        for h in range(2):
            at = (2 * h + 4) * quarter
            real = gathered[s, at : at + quarter]
            imag = gathered[s, at + quarter : at + 2 * quarter]
            duals.append(jnp.where(where[0] == 0, real, imag))
            duals.append(jnp.where(where[0] == 0, imag, -real))
    spectra = jnp.where(mine, jnp.concatenate(spectra, axis=0), 0)
    duals = jnp.where(mine, jnp.concatenate(duals, axis=0), 0)
    wide = dot(duals, second[...])
    for column in range(0, out.shape[1], 256):
        product = dot(spectra, first[0, :, column : column + 256])
        for at in range(0, 256, 128):
            for h in range(2):
                total = 0.0
                for s in range(samples):
                    for part in range(2):
                        row = (4 * s + 2 * h + part) * quarter
                        here = slice(row, row + quarter)
                        total = total + product[here, at : at + 128] * wide[here]
                there = slice(column + at, column + at + 128)
                out[h * quarter : (h + 1) * quarter, there] = total * (1.0 / samples)


def weight_gradient(gathered, depth, width, index):
    samples, rows, lines = gathered.shape
    channels = lines // depth
    square = channels * channels
    cuts = square // width
    first = first_table(channels, depth).reshape(lines, cuts, width).transpose(1, 0, 2)
    first = constant(first)
    second = constant(second_table(channels, depth)[:, :128])
    where = jnp.stack([index // cuts, index % cuts]).astype(jnp.int32)
    half = rows // 4
    return pl.pallas_call(
        functools.partial(gradient_kernel, depth),
        grid_spec=pltpu.PrefetchScalarGridSpec(
            num_scalar_prefetch=1,
            grid=(depth,),
            in_specs=[
                pl.BlockSpec(gathered.shape, lambda j, w: (0, 0, 0)),
                pl.BlockSpec((1, lines, width), lambda j, w: (w[1], 0, 0)),
                pl.BlockSpec(second.shape, lambda j, w: (0, 0)),
            ],
            out_specs=pl.BlockSpec((half, width), lambda j, w: (j, 0)),
        ),
        out_shape=jax.ShapeDtypeStruct((depth * half, width), jnp.float32),
        compiler_params=params(),
        cost_estimate=LIGHT,
        name="weight_gradient",
    )(where, gathered, first, second)


def exchange(first, last):
    size = lax.axis_size("slab")
    up = [(i, i + 1) for i in range(size - 1)]
    down = [(j, i) for i, j in up]
    return lax.ppermute(last, "slab", up), lax.ppermute(first, "slab", down)


def swap(planar):
    return lax.all_to_all(planar, "slab", split_axis=0, concat_axis=0)


def local_fast(feats, grains, spec_weight, taps, point_weight, bias, cotangent):
    slabs = lax.axis_size("slab")
    copies = lax.axis_size("dp")
    barrier = lax.optimization_barrier
    field = feats[0]
    channels = field.shape[0]
    cell_scale = 1.0 / math.sqrt(NX * NY * NZ)
    mode_scale = 1.0 / math.sqrt(KX * KY * KZ)
    mode_rows = spec_weight.shape[0]
    weight = spec_weight.reshape(mode_rows * KZ, 2 * channels * channels)
    width = weight.shape[1] // copies

    first, first_high, last, last_high = cut_rims(field)
    rims = exchange(first, last)
    planar = swap(forward_modes(field, slabs))
    rims, first, last = barrier((rims, first_high, last_high))
    rims_high = exchange(first, last)
    planar, smooth = barrier((planar, smooth_planes(field, rims, taps)))
    spectrum, planar = mix(planar, weight, cell_scale, 0.5 * mode_scale)
    smooth, spectrum = barrier((smooth, spectrum))
    planar = swap(planar)
    smooth = smooth_planes(field, rims_high, taps, smooth)
    spread, planar, first, last = layer(planar, smooth, cotangent[0], grains[0], bias, point_weight)
    rims = exchange(first, last)
    planar, send = mix(swap(planar), weight, 0.5 * mode_scale, cell_scale, spectrum, copies)
    send, spread = barrier((send, spread))
    inner = near_inner(spread, taps)
    gathered = lax.all_to_all(send, "dp", split_axis=0, concat_axis=0)
    planar, gathered, inner, rims = barrier((planar, gathered, inner, rims))
    planar = swap(planar)
    grad_spec = weight_gradient(gathered, KX // slabs, width, lax.axis_index("dp"))
    planar, grad_spec = barrier((planar, grad_spec))
    grad_feats = finish(planar, spread, rims, inner, taps)[None]
    return (grad_feats, grad_spec.reshape(mode_rows, KZ, width))


def local(feats, grains, spec_weight, taps, point_weight, bias, cotangent):
    samples, channels, planes = feats.shape[:3]
    width = spec_weight.shape[2] // lax.axis_size("dp")
    fits = (
        lax.axis_size("slab") * 4 == KX
        and samples == 1
        and channels == 32
        and planes == 8
        and channels * channels % width == 0
        and width % 128 == 0
    )
    form = local_fast if fits else local_any
    return form(feats, grains, spec_weight, taps, point_weight, bias, cotangent)


def solution(mesh):
    in_specs = (
        P(("grp", "dp"), None, "slab", None, None),
        P(("grp", "dp"), "slab", None, None),
        P("slab", None, None),
        P(),
        P(),
        P(),
        P(("grp", "dp"), None, "slab", None, None),
    )
    out_specs = (P(("grp", "dp"), None, "slab", None, None), P("slab", "grp", "dp"))
    return jax.shard_map(local, mesh=mesh, in_specs=in_specs, out_specs=out_specs, check_vma=False)
```

```python
import functools
import math

import jax
import jax.numpy as jnp
import ml_dtypes
import numpy as np
from jax import lax
from jax.experimental import pallas as pl
from jax.experimental.pallas import tpu as pltpu
from jax.sharding import PartitionSpec as P

NX = 128
NY = 128
NZ = 32
KX = 16
KY = 16
KZ = 16


HIGHEST = lax.Precision.HIGHEST


def extended(shard, sides, width):
    for axis, dim in sides:
        size, length = (lax.axis_size(axis), shard.shape[dim])
        up = [(i, (i + 1) % size) for i in range(size - 1)]
        down = [(j, i) for i, j in up]
        last = lax.slice_in_dim(shard, length - width, length, axis=dim)
        first = lax.slice_in_dim(shard, 0, width, axis=dim)
        before = lax.ppermute(last, axis, up)
        after = lax.ppermute(first, axis, down)
        shard = jnp.concatenate([before, shard, after], axis=dim)
    return shard


def tables(count, length, span):
    indices = jnp.arange(count, dtype=jnp.int32)
    frequency = jnp.where(indices < count // 2, indices, length - count + indices)
    position = jnp.arange(span, dtype=jnp.int32)
    phases = frequency[:, None] * position[None, :] % length
    angles = phases.astype(jnp.float32) * (2.0 * math.pi / length)
    return (jnp.cos(angles), jnp.sin(angles))


def mobility(grains):
    leading = [(0, 0)] * (grains.ndim - 2)
    along_x = (grains[..., 1:, :] != grains[..., :-1, :]).astype(jnp.float32)
    along_y = (grains[..., :, 1:] != grains[..., :, :-1]).astype(jnp.float32)
    differ = jnp.pad(along_x, leading + [(1, 0), (0, 0)]) + jnp.pad(
        along_x, leading + [(0, 1), (0, 0)]
    )
    differ = (
        differ
        + jnp.pad(along_y, leading + [(0, 0), (1, 0)])
        + jnp.pad(along_y, leading + [(0, 0), (0, 1)])
    )
    return 0.25 * (1.0 + differ)


def stencil(padded, taps, adjoint):
    planes = padded.shape[-3] - 2
    rows_x = padded.shape[-2] - 2
    rows_y = padded.shape[-1] - 2
    total = jnp.zeros(padded.shape[:-3] + (planes, rows_x, rows_y), jnp.float32)
    for offset in range(27):
        shift_z, shift_x, shift_y = (offset // 9, offset // 3 % 3, offset % 3)
        if adjoint:
            shift_z, shift_x, shift_y = (2 - shift_z, 2 - shift_x, 2 - shift_y)
        window = padded[
            ..., shift_z : shift_z + planes, shift_x : shift_x + rows_x, shift_y : shift_y + rows_y
        ]
        total = total + taps[offset][:, None, None, None] * window.astype(jnp.float32)
    return total


def plane_forward(field, cos_x, sin_x, cos_y, sin_y):
    real_y = jnp.einsum("...xy,ky->...xk", field, cos_y, precision=HIGHEST)
    imag_y = -jnp.einsum("...xy,ky->...xk", field, sin_y, precision=HIGHEST)
    real_part = jnp.einsum("...xk,jx->...jk", real_y, cos_x, precision=HIGHEST) + jnp.einsum(
        "...xk,jx->...jk", imag_y, sin_x, precision=HIGHEST
    )
    imag_part = jnp.einsum("...xk,jx->...jk", imag_y, cos_x, precision=HIGHEST) - jnp.einsum(
        "...xk,jx->...jk", real_y, sin_x, precision=HIGHEST
    )
    return (real_part, imag_part)


def plane_inverse(real_part, imag_part, cos_x, sin_x, cos_y, sin_y):
    real_x = jnp.einsum("...jk,jx->...xk", real_part, cos_x, precision=HIGHEST) - jnp.einsum(
        "...jk,jx->...xk", imag_part, sin_x, precision=HIGHEST
    )
    imag_x = jnp.einsum("...jk,jx->...xk", imag_part, cos_x, precision=HIGHEST) + jnp.einsum(
        "...jk,jx->...xk", real_part, sin_x, precision=HIGHEST
    )
    return jnp.einsum("...xk,ky->...xy", real_x, cos_y, precision=HIGHEST) - jnp.einsum(
        "...xk,ky->...xy", imag_x, sin_y, precision=HIGHEST
    )


def depth_forward(packed, cos_table, sin_table):
    width = packed.shape[-1] // 2
    real_in = packed[..., :width]
    imag_in = packed[..., width:]
    real_out = jnp.einsum("pszc,kz->pskc", real_in, cos_table, precision=HIGHEST) + jnp.einsum(
        "pszc,kz->pskc", imag_in, sin_table, precision=HIGHEST
    )
    imag_out = jnp.einsum("pszc,kz->pskc", imag_in, cos_table, precision=HIGHEST) - jnp.einsum(
        "pszc,kz->pskc", real_in, sin_table, precision=HIGHEST
    )
    return jnp.concatenate([real_out, imag_out], axis=-1)


def depth_inverse(real_modes, imag_modes, cos_table, sin_table):
    real_out = jnp.einsum("pskc,kz->pszc", real_modes, cos_table, precision=HIGHEST) - jnp.einsum(
        "pskc,kz->pszc", imag_modes, sin_table, precision=HIGHEST
    )
    imag_out = jnp.einsum("pskc,kz->pszc", imag_modes, cos_table, precision=HIGHEST) + jnp.einsum(
        "pskc,kz->pszc", real_modes, sin_table, precision=HIGHEST
    )
    return jnp.concatenate([real_out, imag_out], axis=-1)


def rim_planes(field):
    return extended(field, (("slab", 2),), 1)


def local_any(feats, grains, spec_weight, taps, point_weight, bias, cotangent):
    samples_here = feats.shape[0]
    channels = feats.shape[1]
    planes = feats.shape[2]
    cos_x, sin_x = tables(KX, NX, NX)
    cos_y, sin_y = tables(KY, NY, NY)
    cos_full, sin_full = tables(KZ, NZ, NZ)
    cell_scale = math.sqrt(NX * NY * NZ)
    mode_scale = math.sqrt(KX * KY * KZ)
    mode_rows = spec_weight.shape[0]
    weights = spec_weight.astype(jnp.float32).reshape(mode_rows, KZ, 2, channels, channels)
    w_real = weights[:, :, 0]
    w_imag = weights[:, :, 1]
    moving = mobility(grains)[:, None]

    def to_modes(field):
        real_plane, imag_plane = plane_forward(field, cos_x, sin_x, cos_y, sin_y)
        packed = jnp.stack([real_plane, imag_plane], axis=1)
        packed = packed.transpose(4, 5, 0, 3, 1, 2).reshape(
            KX * KY, samples_here, planes, 2 * channels
        )
        moved = lax.all_to_all(packed, "slab", split_axis=0, concat_axis=2, tiled=True)
        summed = depth_forward(moved, cos_full, sin_full)
        return (summed[..., :channels], summed[..., channels:])

    def from_modes(real_modes, imag_modes):
        planar = depth_inverse(real_modes, imag_modes, cos_full, sin_full)
        packed = lax.all_to_all(planar, "slab", split_axis=2, concat_axis=0, tiled=True)
        grouped = packed.reshape(KX, KY, samples_here, planes, 2, channels).transpose(
            2, 4, 5, 3, 0, 1
        )
        return plane_inverse(grouped[:, 0], grouped[:, 1], cos_x, sin_x, cos_y, sin_y)

    zero_rim = ((0, 0), (0, 0), (0, 0), (1, 1), (1, 1))
    padded = jnp.pad(rim_planes(feats), zero_rim)
    smooth = stencil(padded, taps, False).astype(jnp.bfloat16)
    local_part = moving * jnp.einsum(
        "sczxy,co->sozxy", smooth, point_weight, preferred_element_type=jnp.float32
    )
    spec_real, spec_imag = to_modes(feats.astype(jnp.float32))
    spec_real = spec_real / cell_scale
    spec_imag = spec_imag / cell_scale
    mixed_real = jnp.einsum("pskc,pkco->psko", spec_real, w_real, precision=HIGHEST) - jnp.einsum(
        "pskc,pkco->psko", spec_imag, w_imag, precision=HIGHEST
    )
    mixed_imag = jnp.einsum("pskc,pkco->psko", spec_real, w_imag, precision=HIGHEST) + jnp.einsum(
        "pskc,pkco->psko", spec_imag, w_real, precision=HIGHEST
    )
    spectral = from_modes(mixed_real, mixed_imag) / mode_scale
    pre = spectral + local_part + bias[None, :, None, None, None]
    gate = jax.nn.sigmoid(pre)
    delta = (cotangent.astype(jnp.float32) * gate * (1.0 + pre * (1.0 - gate))).astype(jnp.bfloat16)
    dual_real, dual_imag = to_modes(delta.astype(jnp.float32))
    dual_real = dual_real / mode_scale
    dual_imag = dual_imag / mode_scale
    batch_total = samples_here * lax.axis_size("dp")
    grad_real = jnp.einsum("pskc,psko->pkco", spec_real, dual_real, precision=HIGHEST) + jnp.einsum(
        "pskc,psko->pkco", spec_imag, dual_imag, precision=HIGHEST
    )
    grad_imag = jnp.einsum("pskc,psko->pkco", spec_real, dual_imag, precision=HIGHEST) - jnp.einsum(
        "pskc,psko->pkco", spec_imag, dual_real, precision=HIGHEST
    )
    grad_terms = (jnp.stack([grad_real, grad_imag], axis=2) / batch_total).reshape(
        mode_rows, KZ, 2 * channels * channels
    )
    grad_spec = lax.psum_scatter(
        grad_terms.astype(jnp.bfloat16), "dp", scatter_dimension=2, tiled=True
    ).astype(jnp.float32)
    back_real = jnp.einsum("psko,pkco->pskc", dual_real, w_real, precision=HIGHEST) + jnp.einsum(
        "psko,pkco->pskc", dual_imag, w_imag, precision=HIGHEST
    )
    back_imag = jnp.einsum("psko,pkco->pskc", dual_imag, w_real, precision=HIGHEST) - jnp.einsum(
        "psko,pkco->pskc", dual_real, w_imag, precision=HIGHEST
    )
    spectral_back = from_modes(back_real, back_imag) / cell_scale
    spread = (
        moving
        * jnp.einsum("sozxy,co->sczxy", delta, point_weight, preferred_element_type=jnp.float32)
    ).astype(jnp.bfloat16)
    spread_padded = jnp.pad(rim_planes(spread), zero_rim)
    local_back = stencil(spread_padded, taps, True)
    grad_feats = (spectral_back + local_back).astype(jnp.bfloat16)
    return (grad_feats, grad_spec)


def frequencies(count, length):
    index = np.arange(count)
    return np.where(index < count // 2, index, length - count + index)


def angles(count, length):
    phases = np.outer(frequencies(count, length), np.arange(length)) % length
    return phases * (2.0 * np.pi / length)


def constant(array):
    return jnp.asarray(np.asarray(array, np.float32).astype(ml_dtypes.bfloat16))


def forward_x_table(slabs, split):
    a = angles(KX, NX).reshape(slabs, KX // slabs, NX)
    trig = np.stack([np.cos(a), np.sin(a)])
    table = np.einsum("tsjx,cd->tscjdx", trig, np.eye(2)).reshape(-1, 2, NX // 8, 8)
    if split:
        table = table.transpose(0, 2, 1, 3)
    return table.reshape(4 * KX, 2 * NX)


def halved(table, planes):
    table = table.reshape(-1, planes * 2, 2, KY // 2).transpose(0, 2, 1, 3)
    return table.reshape(-1, planes * 2 * KY)


def forward_y_table(planes):
    a = angles(KY, NY)
    cos, sin = np.cos(a).T, np.sin(a).T
    block = np.stack([np.stack([cos, -sin], 1), np.stack([-sin, -cos], 1)])
    pick = np.eye(planes).reshape(planes // 2, 2, planes)
    table = np.einsum("pqz,tyrk->ptqyzrk", pick, block)
    return halved(table.reshape(planes * 2 * NY, planes * 2 * KY), planes)


def forward_z_table():
    a = angles(KZ, NZ)
    cos, sin = np.cos(a).T, np.sin(a).T
    block = np.stack([np.stack([cos, -sin], 1), np.stack([sin, cos], 1)], 1)
    table = np.einsum("zrqm,kl->zrkqlm", block, np.eye(KY // 2))
    return table.reshape(NZ * KY, KY * KZ)


def inverse_z_table():
    a = angles(KZ, NZ)
    cos, sin = np.cos(a), np.sin(a)
    block = np.stack([np.stack([cos, sin], 2), np.stack([-sin, cos], 2)])
    table = np.einsum("rmzq,kl->rkmzql", block, np.eye(KY // 2))
    return table.reshape(KY * KZ, NZ * KY)


def inverse_y_table(planes, group):
    a = angles(KY, NY)
    cos, sin = np.cos(a), np.sin(a)
    block = np.stack([np.stack([cos, -sin], 1), np.stack([-sin, -cos], 1)])
    pick = np.eye(planes).reshape(planes // group, group, planes)
    table = np.einsum("pqz,rkty->ptqyzrk", pick, block)
    table = halved(table.reshape(-1, planes * 2 * KY), planes)
    return table.reshape(planes // group, 2 * group * NY, planes * 2 * KY).transpose(0, 2, 1)


def inverse_x_table(slabs, group):
    a = angles(KX, NX).reshape(slabs, KX // slabs, NX)
    trig = np.stack([np.cos(a), np.sin(a)])
    table = np.einsum("tsjx,cd->cxstdj", trig, np.eye(group))
    return table.reshape(group * NX, 2 * KX * group)


def first_table(channels, depth):
    table = np.einsum("ac,j,b->ajcb", np.eye(channels), np.ones(depth), np.ones(channels))
    return table.reshape(channels * depth, channels * channels)


def second_table(channels, depth):
    table = np.einsum("ac,j,b->ajbc", np.eye(channels), np.ones(depth), np.ones(channels))
    return table.reshape(channels * depth, channels * channels)


LIGHT = pl.CostEstimate(flops=10**7, bytes_accessed=10**5, transcendentals=0)
HEAVY = pl.CostEstimate(flops=10**11, bytes_accessed=10**8, transcendentals=0)


def dot(a, b):
    return jnp.dot(a, b, preferred_element_type=jnp.float32)


def whole(shape):
    return pl.BlockSpec(shape, lambda *_: (0,) * len(shape))


def params(**kw):
    return pltpu.CompilerParams(vmem_limit_bytes=63438848, **kw)


def store_rows(rows, pair, x_table, load):
    slabs, lines = rows.shape[2:4]
    for i in range(lines // 16):
        parts = [dot(x_table[...], load(2 * i + k)) for k in range(2)]
        for t in range(2):
            for s in range(slabs):
                here = slice(8 * (t * slabs + s), 8 * (t * slabs + s) + 8)
                both = jnp.concatenate([part[here] for part in parts], axis=0)
                rows[pair, t, s, 16 * i : 16 * i + 16, :] = both.astype(jnp.bfloat16)


def store_modes(rows, y_table, out):
    pairs, _, slabs, lines, _ = rows.shape
    left = [
        jnp.concatenate([rows[p, t, s] for p in range(pairs) for t in range(2)], axis=1)
        for s in range(slabs)
    ]
    modes = dot(jnp.concatenate(left, axis=0), y_table[...])
    for s in range(slabs):
        out[s] = modes[s * lines : (s + 1) * lines].astype(jnp.bfloat16)


def rims_kernel(field, *refs):
    rims, held, got, put = refs[:4], refs[4], refs[5], refs[6]
    half = field.shape[0] // 2
    last = field.shape[1] - 1
    loads, stores = [], []
    for k in range(4):
        source = field.at[pl.ds(half * (k % 2), half), pl.ds(last * (k // 2), 1)]
        loads.append(pltpu.make_async_copy(source, held.at[k], got.at[k]))
        stores.append(pltpu.make_async_copy(held.at[k], rims[k], put.at[k]))
    for load in loads:
        load.start()
    for load, store in zip(loads, stores):
        load.wait()
        store.start()
    for store in stores:
        store.wait()


def cut_rims(field):
    channels = field.shape[0]
    rim = jax.ShapeDtypeStruct((channels // 2, 1, NX, NY), jnp.bfloat16)
    return pl.pallas_call(
        rims_kernel,
        in_specs=[pl.BlockSpec(memory_space=pl.ANY)],
        out_specs=[pl.BlockSpec(memory_space=pl.ANY)] * 4,
        out_shape=[rim] * 4,
        scratch_shapes=[
            pltpu.VMEM((4,) + rim.shape, jnp.bfloat16),
            pltpu.SemaphoreType.DMA((4,)),
            pltpu.SemaphoreType.DMA((4,)),
        ],
        compiler_params=params(),
        cost_estimate=LIGHT,
        name="rims",
    )(field)


def forward_kernel(field, x_table, y_table, out, rows):
    pair = pl.program_id(0)
    pairs = rows.shape[0]

    def load(i):
        halves = [field[2 * i : 2 * i + 2, q].reshape(2 * NX, NY) for q in range(2)]
        return jnp.concatenate(halves, axis=1)

    store_rows(rows, pair, x_table, load)

    @pl.when(pair == pairs - 1)
    def _():
        store_modes(rows, y_table, out)


def forward_modes(field, slabs):
    channels, planes = field.shape[:2]
    lines = channels * (KX // slabs)
    x_table = constant(forward_x_table(slabs, False))
    y_table = constant(forward_y_table(planes))
    shape = (slabs, lines, planes * 2 * KY)
    return pl.pallas_call(
        forward_kernel,
        grid=(planes // 2,),
        in_specs=[
            pl.BlockSpec((channels, 2, NX, NY), lambda p: (0, p, 0, 0)),
            whole(x_table.shape),
            whole(y_table.shape),
        ],
        out_specs=whole(shape),
        out_shape=jax.ShapeDtypeStruct(shape, jnp.bfloat16),
        scratch_shapes=[pltpu.VMEM((planes // 2, 2, slabs, lines, 2 * NY), jnp.bfloat16)],
        compiler_params=params(),
        cost_estimate=LIGHT,
        name="forward_modes",
    )(field, x_table, y_table)


def mixing_kernel(scale_in, scale_out, adjoint, planar, weight, z_in, z_out, spread_table,
                  sum_table, *rest):
    if adjoint:
        partner, out, send, spectrum, total, wide, product = rest
    else:
        spectrum, out, total, wide, product = rest
    step = pl.program_id(0)
    steps = pl.num_programs(0)
    slabs, lines, width = planar.shape
    half = width // 2
    quarter = spectrum.shape[0] // 4
    lanes = weight.shape[1] // 2
    depth = weight.shape[0] // (2 * quarter)

    @pl.when(step == 0)
    def _():
        left = [
            jnp.concatenate([planar[s, :, h : h + half] for s in range(slabs)], axis=1)
            for h in (0, half)
        ]
        modes = dot(jnp.concatenate(left, axis=0), z_in[...]) * scale_in
        for h in range(2):
            here = modes[h * lines : (h + 1) * lines].T.astype(jnp.bfloat16)
            spectrum[2 * h * quarter : 2 * (h + 1) * quarter] = here
            if adjoint:
                for d in range(send.shape[0]):
                    send[d, 2 * (h + 1) * quarter : 2 * (h + 2) * quarter] = here
        if adjoint:
            rows = [partner[2 * h * quarter : 2 * (h + 1) * quarter] for h in range(2)]
            rows = [row.astype(jnp.float32) for row in rows]
            left = lax.broadcasted_iota(jnp.int32, (1, lines), 1) < lines // 2
            turned = [pltpu.roll(row, lines // 2, axis=1) for row in rows]
            packed = [jnp.where(left, rows[0], turned[1]), jnp.where(left, turned[0], rows[1])]
            for d in range(send.shape[0]):
                send[d, : 2 * quarter] = packed[d % 2].astype(jnp.bfloat16)
        total[...] = jnp.zeros_like(total)

    lane = lax.broadcasted_iota(jnp.int32, (1, lines), 1) % (depth * steps)
    block = 32
    tile = wide.shape[1]
    for j in range(depth):
        mine = lane == depth * step + j
        wide[...] = dot(jnp.where(mine, spectrum[...], 0), spread_table[...])
        for at in range(0, 2 * quarter, block):
            row = 2 * j * quarter + at
            real_at = at + (at // quarter) * quarter
            imag_at = real_at + quarter
            sums = [0.0, 0.0]
            for column in range(0, lanes, 128):
                here = slice(column, column + 128) if tile == lanes else slice(None)
                real_wide = wide[real_at : real_at + block, here]
                imag_wide = wide[imag_at : imag_at + block, here]
                w_real = weight[row : row + block, column : column + 128]
                w_imag = weight[row : row + block, lanes + column : lanes + column + 128]
                w_real = w_real.astype(jnp.float32)
                w_imag = w_imag.astype(jnp.float32)
                if adjoint:
                    real = real_wide * w_real + imag_wide * w_imag
                    imag = imag_wide * w_real - real_wide * w_imag
                    there = slice(column, column + 128)
                    product[real_at : real_at + block, there] = real.astype(jnp.bfloat16)
                    product[imag_at : imag_at + block, there] = imag.astype(jnp.bfloat16)
                else:
                    sums[0] = sums[0] + (real_wide * w_real - imag_wide * w_imag)
                    sums[1] = sums[1] + (real_wide * w_imag + imag_wide * w_real)
            if not adjoint:
                product[real_at : real_at + block] = sums[0].astype(jnp.bfloat16)
                product[imag_at : imag_at + block] = sums[1].astype(jnp.bfloat16)
        total[...] += jnp.where(mine, dot(product[...], sum_table[...]), 0.0)

    @pl.when(step == steps - 1)
    def _():
        modes = total[...] * scale_out
        left = [modes[2 * h * quarter : 2 * (h + 1) * quarter].T for h in range(2)]
        modes = dot(jnp.concatenate(left, axis=0).astype(jnp.bfloat16), z_out[...])
        for s in range(slabs):
            for h in range(2):
                here = modes[h * lines : (h + 1) * lines, s * half : (s + 1) * half]
                out[s, :, h * half : (h + 1) * half] = here.astype(jnp.bfloat16)


def mix(planar, weight, scale_in, scale_out, partner=None, copies=0):
    slabs, lines, width = planar.shape
    adjoint = partner is not None
    depth = KX // slabs
    channels = lines // depth
    rows = KY * KZ
    steps = 2
    z_in = constant(forward_z_table())
    z_out = constant(inverse_z_table())
    first = first_table(channels, depth)
    second = second_table(channels, depth)
    spread_table = constant(second[:, :128] if adjoint else first)
    sum_table = constant(first.T if adjoint else second[:, :128].T)
    shape = (2 * rows, lines)
    in_specs = [
        whole(planar.shape),
        pl.BlockSpec((depth // steps * rows, weight.shape[1]), lambda j: (j, 0)),
        whole(z_in.shape),
        whole(z_out.shape),
        whole(spread_table.shape),
        whole(sum_table.shape),
    ]
    operands = [planar, weight, z_in, z_out, spread_table, sum_table]
    scratch = [
        pltpu.VMEM(shape, jnp.float32),
        pltpu.VMEM((2 * rows, spread_table.shape[1]), jnp.float32),
        pltpu.VMEM((2 * rows, sum_table.shape[0]), jnp.bfloat16),
    ]
    if adjoint:
        in_specs.append(whole(shape))
        operands.append(partner)
        scratch = [pltpu.VMEM(shape, jnp.bfloat16)] + scratch
        outs = [planar.shape, (copies, 3 * rows, lines)]
    else:
        outs = [shape, planar.shape]
    return pl.pallas_call(
        functools.partial(mixing_kernel, scale_in, scale_out, adjoint),
        grid=(steps,),
        in_specs=in_specs,
        out_specs=[whole(out) for out in outs],
        out_shape=[jax.ShapeDtypeStruct(out, jnp.bfloat16) for out in outs],
        scratch_shapes=scratch,
        compiler_params=params(),
        cost_estimate=HEAVY,
        name="mix_back" if adjoint else "mix",
    )(*operands)


def plane_mobility(grains):
    same = [
        jnp.concatenate([grains[:1], grains[:-1]], axis=0),
        jnp.concatenate([grains[1:], grains[-1:]], axis=0),
        jnp.concatenate([grains[:, :1], grains[:, :-1]], axis=1),
        jnp.concatenate([grains[:, 1:], grains[:, -1:]], axis=1),
    ]
    total = jnp.full(grains.shape, 0.25, jnp.float32)
    for other in same:
        total = total + jnp.where(grains != other, 0.25, 0.0)
    return total


def layer_kernel(bias, planar, smooth, cotangent, grains, point_weight, repeat, ix_table, iy_table,
                 x_table, y_table, spread, out, first, last, *rest):
    pair = pl.program_id(0)
    waves, spectral, moving, delta, rows, bias_wide, mix_out, mix_in = rest
    pairs = rows.shape[0]
    channels = cotangent.shape[0]
    slabs = planar.shape[0]

    @pl.when(pair == 0)
    def _():
        for c in range(channels):
            bias_wide[c] = jnp.full(bias_wide.shape[1:], 0.5 * bias[c], jnp.float32)
        tall = dot(repeat[...], point_weight[...]).astype(jnp.bfloat16)
        square = lax.dot_general(
            tall, repeat[...], (((1,), (1,)), ((), ())), preferred_element_type=jnp.float32
        )
        row = lax.broadcasted_iota(jnp.int32, square.shape, 0) % 8
        column = lax.broadcasted_iota(jnp.int32, square.shape, 1) % 8
        square = jnp.where(row == column, square, 0.0)
        mix_in[...] = square.astype(jnp.bfloat16)
        mix_out[...] = square.T.astype(jnp.bfloat16)

    lines = planar.shape[1]
    step = jnp.concatenate([planar[s] for s in range(slabs)], axis=0)
    step = dot(step, iy_table[0]).astype(jnp.bfloat16)
    for s in range(slabs):
        for t in range(2):
            waves[s, t] = step[s * lines : (s + 1) * lines, 2 * NY * t : 2 * NY * (t + 1)]
    group = 8 * (KX // slabs)
    for g in range(channels // 8):
        here = slice(g * group, (g + 1) * group)
        wave = [waves[s, t, here, :] for s in range(slabs) for t in range(2)]
        step = dot(ix_table[...], jnp.concatenate(wave, axis=0))
        spectral[8 * g : 8 * g + 8] = step.reshape(8, NX, 2 * NY)
    for q in range(2):
        moving[:, q * NY : (q + 1) * NY] = 0.5 * plane_mobility(grains[q])

    def body(i, _):
        x = pl.multiple_of(16 * i, 16)
        halves = [cotangent[:, q, pl.ds(x, 16), :] for q in range(2)]
        cotangent_here = jnp.concatenate(halves, axis=2).astype(jnp.float32)
        spreads = []
        for h in range(2):
            at = pl.ds(pl.multiple_of(x + 8 * h, 8), 8)
            mobile = moving[at, :][None]
            local = dot(mix_out[...], smooth[0, 2 * i + h]).reshape(channels, 8, 2 * NY)
            half = spectral[:, at, :] + mobile * local + bias_wide[...]
            wave = jnp.tanh(half)
            slope = (1.0 + wave) * (1.0 + (half - half * wave))
            change = cotangent_here[:, 8 * h : 8 * h + 8, :] * slope
            right = change.reshape(8 * channels, 2 * NY).astype(jnp.bfloat16)
            delta[2 * i + h] = right
            back = dot(mix_in[...], right).reshape(channels, 8, 2 * NY)
            spreads.append(mobile * back)
        both = jnp.concatenate(spreads, axis=1).astype(jnp.bfloat16)
        for q in range(2):
            spread[:, q, pl.ds(x, 16), :] = both[:, :, q * NY : (q + 1) * NY]
        return 0

    lax.fori_loop(0, NX // 16, body, 0, unroll=8)


    @pl.when(pair == 0)
    def _():
        first[:, 0] = spread[:, 0]

    @pl.when(pair == pairs - 1)
    def _():
        last[:, 0] = spread[:, 1]

    def load(i):
        return delta[:, 16 * i : 16 * i + 16, :].reshape(2 * NX, 2 * NY)

    store_rows(rows, pair, x_table, load)

    @pl.when(pair == pairs - 1)
    def _():
        store_modes(rows, y_table, out)


def layer(planar, smooth, cotangent, grains, bias, point_weight):
    slabs, lines, width = planar.shape
    channels, planes = cotangent.shape[:2]
    pairs = planes // 2
    repeat = constant(np.repeat(np.eye(channels), 8, axis=0))
    ix_table = constant(inverse_x_table(slabs, 8))
    iy_table = constant(inverse_y_table(planes, 2))
    x_table = constant(forward_x_table(slabs, True))
    y_table = constant(forward_y_table(planes))
    field = pl.BlockSpec((channels, 2, NX, NY), lambda p: (0, p, 0, 0))
    outs = [cotangent.shape, planar.shape] + [(channels, 1, NX, NY)] * 2
    return pl.pallas_call(
        layer_kernel,
        grid=(pairs,),
        in_specs=[
            pl.BlockSpec(memory_space=pltpu.SMEM),
            whole(planar.shape),
            pl.BlockSpec((1,) + smooth.shape[1:], lambda p: (p, 0, 0, 0)),
            field,
            pl.BlockSpec((2, NX, NY), lambda p: (p, 0, 0)),
            whole(point_weight.shape),
            whole(repeat.shape),
            whole(ix_table.shape),
            pl.BlockSpec((1,) + iy_table.shape[1:], lambda p: (p, 0, 0)),
            whole(x_table.shape),
            whole(y_table.shape),
        ],
        out_specs=[field] + [whole(out) for out in outs[1:]],
        out_shape=[jax.ShapeDtypeStruct(out, jnp.bfloat16) for out in outs],
        scratch_shapes=[
            pltpu.VMEM((slabs, 2, lines, 2 * NY), jnp.bfloat16),
            pltpu.VMEM((channels, NX, 2 * NY), jnp.float32),
            pltpu.VMEM((NX, 2 * NY), jnp.float32),
            pltpu.VMEM((NX // 8, 8 * channels, 2 * NY), jnp.bfloat16),
            pltpu.VMEM((pairs, 2, slabs, lines, 2 * NY), jnp.bfloat16),
            pltpu.VMEM((channels, 8, 2 * NY), jnp.float32),
            pltpu.VMEM((8 * channels, 8 * channels), jnp.bfloat16),
            pltpu.VMEM((8 * channels, 8 * channels), jnp.bfloat16),
        ],
        compiler_params=params(),
        cost_estimate=LIGHT,
        name="layer",
    )(bias, planar, smooth, cotangent, grains, point_weight, repeat, ix_table, iy_table, x_table,
      y_table)


def build_band(adjoint, taps, channel, band):
    row = lax.broadcasted_iota(jnp.int32, (8, 128), 0)
    lane = lax.broadcasted_iota(jnp.int32, (8, 128), 1)
    for dy in range(3):
        for q in range(2):
            halves = []
            for side in range(2):
                tile = jnp.zeros((8, 128), jnp.float32)
                for k in range(2):
                    dz = 2 * side + k - q
                    if not 0 <= dz <= 2:
                        continue
                    for dx in range(3):
                        number = 9 * dz + 3 * dx + dy
                        tap = taps[26 - number if adjoint else number, channel]
                        hit = lane == (64 * k + row + (dx - 1)) % 128
                        tile = jnp.where(hit, tap, tile)
                tiles = [pltpu.roll(tile, 8 * k, axis=1) if k > 0 else tile for k in range(8)]
                low = (row == 0) & (lane % 64 == 63)
                high = (row == 7) & (lane % 64 == 0)
                tiles[0] = jnp.where(low, 0.0, tiles[0])
                tiles[7] = jnp.where(high, 0.0, tiles[7])
                halves.append(jnp.concatenate(tiles[1:7] + [tiles[0], tiles[7]], axis=0))
            at = 64 * (2 * dy + q)
            band[at : at + 64, :] = jnp.concatenate(halves, axis=1).astype(jnp.bfloat16)


def apply_band(quads, band):
    blocks = range(6)
    lefts = [
        band[...],
        jnp.concatenate([band[64 * b : 64 * b + 48, :] for b in blocks], axis=0),
        jnp.concatenate([band[64 * b + 32 : 64 * b + 64, :] for b in blocks], axis=0),
    ]
    lane = lax.broadcasted_iota(jnp.int32, (NX, NY), 1)
    totals = []
    for group in range(0, len(quads), 2):
        products = []
        for left, x in zip(lefts, (0, 48, 64)):
            right = [
                jnp.concatenate([sheet[x : x + 64] for sheet in quads[group + p]], axis=0)
                for p in range(2)
            ]
            products.append(dot(left, jnp.concatenate(right, axis=1)))
        for p in range(2):
            wide = slice(NY * p, NY * (p + 1))
            pair = []
            for q in range(2):
                shifted = []
                for dy in range(3):
                    b = 2 * dy + q
                    pieces = [
                        products[0][64 * b + 48 : 64 * b + 56, wide],
                        products[0][64 * b : 64 * b + 48, wide],
                        products[1][48 * b : 48 * b + 48, wide],
                        products[2][32 * b : 32 * b + 16, wide],
                        products[2][32 * b + 24 : 32 * b + 32, wide],
                    ]
                    shifted.append(jnp.concatenate(pieces, axis=0))
                before = jnp.where(lane == 0, 0.0, pltpu.roll(shifted[0], 1, axis=1))
                after = jnp.where(lane == NY - 1, 0.0, pltpu.roll(shifted[2], NY - 1, axis=1))
                pair.append(shifted[1] + before + after)
            totals.append(jnp.concatenate(pair, axis=1))
    return totals


def banded(adjoint, taps, start, even, odd, channels):
    step = pl.program_id(0)
    final = start + channels * pl.num_programs(0) - 1
    bands = (even, odd)

    @pl.when(step == 0)
    def _():
        even[...] = jnp.zeros_like(even)
        odd[...] = jnp.zeros_like(odd)
        build_band(adjoint, taps, start, even)

    def run(visit):
        for c in range(channels):
            following = jnp.minimum(start + channels * step + c + 1, final)
            build_band(adjoint, taps, following, bands[(c + 1) % 2])
            visit(c, bands[c % 2])

    return run


def smooth_kernel(start, taps, before, field, after, *rest):
    out, even, odd = rest[-3:]
    planes = field.shape[1]
    totals = []

    def visit(c, band):
        sheets = [before[c, 0]] + [field[c, z] for z in range(planes)] + [after[c, 0]]
        totals.append(apply_band([sheets[z : z + 4] for z in range(0, planes, 2)], band))

        if c % 2 == 1:
            for p in range(planes // 2):
                both = [total[p].reshape(NX // 8, 8, 2 * NY) for total in totals[c - 1 : c + 1]]
                both = jnp.concatenate(both, axis=1).astype(jnp.bfloat16)
                out[p, :, 8 * (c - 1) : 8 * (c + 1), :] = both

    banded(False, taps, start, even, odd, field.shape[0])(visit)


def smooth_planes(field, rims, taps, done=None):
    channels, planes = field.shape[:2]
    pairs = planes // 2
    start = 0 if done is None else channels // 2
    step = 4
    skip = start // step
    rim = pl.BlockSpec((step, 1, NX, NY), lambda c: (c, 0, 0, 0))
    sheets = pl.BlockSpec((step, planes, NX, NY), lambda c: (c + skip, 0, 0, 0))
    in_specs = [pl.BlockSpec(memory_space=pltpu.SMEM), rim, sheets, rim]
    operands = [taps, rims[0], field, rims[1]]
    if done is not None:
        in_specs.append(pl.BlockSpec(memory_space=pl.ANY))
        operands.append(done)
    return pl.pallas_call(
        functools.partial(smooth_kernel, start),
        grid=(channels // 2 // step,),
        in_specs=in_specs,
        out_specs=pl.BlockSpec((pairs, NX // 8, 8 * step, 2 * NY), lambda c: (0, 0, c + skip, 0)),
        out_shape=jax.ShapeDtypeStruct((pairs, NX // 8, 8 * channels, 2 * NY), jnp.bfloat16),
        input_output_aliases={} if done is None else {4: 0},
        scratch_shapes=[pltpu.VMEM((6 * 64, 4 * 64), jnp.bfloat16) for _ in range(2)],
        compiler_params=params(),
        cost_estimate=LIGHT,
        name="smooth_low" if done is None else "smooth_high",
    )(*operands)


def inner_kernel(taps, field, out, even, odd):
    planes = field.shape[1]

    def visit(c, band):
        quads = [[field[c, z + k] for k in range(4)] for z in range(1, planes - 3, 2)]
        for p, near in enumerate(apply_band(quads, band)):
            total = near.astype(jnp.bfloat16)
            out[c, 2 * p] = total[:, :NY]
            out[c, 2 * p + 1] = total[:, NY:]

    banded(True, taps, 0, even, odd, field.shape[0])(visit)


def near_inner(field, taps):
    channels, planes = field.shape[:2]
    step = 8
    shape = (channels, planes - 4, NX, NY)
    return pl.pallas_call(
        inner_kernel,
        grid=(channels // step,),
        in_specs=[
            pl.BlockSpec(memory_space=pltpu.SMEM),
            pl.BlockSpec((step, planes, NX, NY), lambda c: (c, 0, 0, 0)),
        ],
        out_specs=pl.BlockSpec((step,) + shape[1:], lambda c: (c, 0, 0, 0)),
        out_shape=jax.ShapeDtypeStruct(shape, jnp.bfloat16),
        scratch_shapes=[pltpu.VMEM((6 * 64, 4 * 64), jnp.bfloat16) for _ in range(2)],
        compiler_params=params(),
        cost_estimate=LIGHT,
        name="near_inner",
    )(taps, field)


def finish_kernel(taps, before, field, after, inner, planar, ix_table, iy_table, out, waves, even,
                  odd):
    step = pl.program_id(0)
    slabs, lines = planar.shape[:2]
    planes = field.shape[1]
    span = planes * NY

    @pl.when(step == 0)
    def _():
        left = jnp.concatenate([planar[s] for s in range(slabs)], axis=0)
        for t in range(2):
            wave = dot(left, iy_table[0, :, t * span : (t + 1) * span]).astype(jnp.bfloat16)
            for s in range(slabs):
                waves[s, t] = wave[s * lines : (s + 1) * lines]

    rows = field.shape[0] * (KX // slabs)
    here = pl.ds(pl.multiple_of(rows * step, rows), rows)
    right = [waves[s, t, here, :] for s in range(slabs) for t in range(2)]
    right = jnp.concatenate(right, axis=0)
    far = [
        dot(ix_table[...], right[:, 2 * p * NY : 2 * (p + 1) * NY]) for p in range(planes // 2)
    ]

    def store(c, p, near):
        for q in range(2):
            total = near[q] + far[p][c * NX : (c + 1) * NX, q * NY : (q + 1) * NY]
            out[c, 2 * p + q] = total.astype(jnp.bfloat16)

    def visit(c, band):
        low = [before[c, 0]] + [field[c, z] for z in range(3)]
        high = [field[c, z] for z in range(planes - 3, planes)] + [after[c, 0]]
        for p, near in zip((0, planes // 2 - 1), apply_band([low, high], band)):
            store(c, p, [near[:, :NY], near[:, NY:]])
        for p in range(1, planes // 2 - 1):
            store(c, p, [inner[c, 2 * p - 2 + q].astype(jnp.float32) for q in range(2)])

    banded(True, taps, 0, even, odd, field.shape[0])(visit)


def finish(planar, spread, rims, inner, taps):
    slabs, lines, width = planar.shape
    channels, planes = spread.shape[:2]
    step = 8
    ix_table = constant(inverse_x_table(slabs, step))
    iy_table = constant(inverse_y_table(planes, planes))
    rim = pl.BlockSpec((step, 1, NX, NY), lambda c: (c, 0, 0, 0))
    sheets = pl.BlockSpec((step, planes, NX, NY), lambda c: (c, 0, 0, 0))
    return pl.pallas_call(
        finish_kernel,
        grid=(channels // step,),
        in_specs=[
            pl.BlockSpec(memory_space=pltpu.SMEM),
            rim,
            sheets,
            rim,
            pl.BlockSpec((step,) + inner.shape[1:], lambda c: (c, 0, 0, 0)),
            whole(planar.shape),
            whole(ix_table.shape),
            whole(iy_table.shape),
        ],
        out_specs=sheets,
        out_shape=jax.ShapeDtypeStruct(spread.shape, jnp.bfloat16),
        scratch_shapes=[
            pltpu.VMEM((slabs, 2, lines, planes * NY), jnp.bfloat16),
            pltpu.VMEM((6 * 64, 4 * 64), jnp.bfloat16),
            pltpu.VMEM((6 * 64, 4 * 64), jnp.bfloat16),
        ],
        compiler_params=params(),
        cost_estimate=HEAVY,
        name="finish",
    )(taps, rims[0], spread, rims[1], inner, planar, ix_table, iy_table)


def gradient_kernel(gathered, first, second, out):
    step = pl.program_id(0)
    samples, rows, lines = gathered.shape
    quarter = rows // 6
    depth = out.shape[0] // (2 * quarter)
    real_part = lax.axis_index("dp") < lax.axis_size("dp") // 2
    lane = lax.broadcasted_iota(jnp.int32, (1, lines), 1)
    duals = []
    for s in range(samples):
        for h in range(2):
            at = (2 * h + 2) * quarter
            real = gathered[s, at : at + quarter]
            imag = gathered[s, at + quarter : at + 2 * quarter]
            duals.append(jnp.where(real_part, real, imag))
            duals.append(jnp.where(real_part, imag, -real))
    duals = jnp.concatenate(duals, axis=0)
    for j in range(depth):
        mine = lane % (depth * pl.num_programs(0)) == depth * step + j
        spectra = []
        for s in range(samples):
            for h in range(2):
                here = mine & (lane // (lines // 2) == h)
                spectra.append(jnp.where(here, gathered[s, : 2 * quarter], 0))
        spectra = jnp.concatenate(spectra, axis=0)
        wide = dot(jnp.where(mine, duals, 0), second[...])
        for column in range(0, out.shape[1], 256):
            product = dot(spectra, first[:, column : column + 256])
            for at in range(0, 256, 128):
                for h in range(2):
                    total = 0.0
                    for s in range(samples):
                        for part in range(2):
                            row = (4 * s + 2 * h + part) * quarter
                            here = slice(row, row + quarter)
                            total = total + product[here, at : at + 128] * wide[here]
                    row = (2 * j + h) * quarter
                    there = slice(column + at, column + at + 128)
                    out[row : row + quarter, there] = total * (1.0 / samples)


def weight_gradient(gathered, depth, width):
    samples, rows, lines = gathered.shape
    channels = lines // depth
    first = np.repeat(np.eye(channels // 2), channels, axis=1)
    first = constant(np.tile(np.repeat(first, depth, axis=0), (2, 1)))
    second = constant(second_table(channels, depth)[:, :128])
    steps = 2
    half = rows // 3
    return pl.pallas_call(
        gradient_kernel,
        grid=(steps,),
        in_specs=[whole(gathered.shape), whole(first.shape), whole(second.shape)],
        out_specs=pl.BlockSpec((depth // steps * half, width), lambda j: (j, 0)),
        out_shape=jax.ShapeDtypeStruct((depth * half, width), jnp.float32),
        compiler_params=params(),
        cost_estimate=LIGHT,
        name="weight_gradient",
    )(gathered, first, second)


def exchange(first, last):
    size = lax.axis_size("slab")
    up = [(i, i + 1) for i in range(size - 1)]
    down = [(j, i) for i, j in up]
    return lax.ppermute(last, "slab", up), lax.ppermute(first, "slab", down)


def swap(planar):
    return lax.all_to_all(planar, "slab", split_axis=0, concat_axis=0)


def local_fast(feats, grains, spec_weight, taps, point_weight, bias, cotangent):
    slabs = lax.axis_size("slab")
    copies = lax.axis_size("dp")
    barrier = lax.optimization_barrier
    field = feats[0]
    channels = field.shape[0]
    cell_scale = 1.0 / math.sqrt(NX * NY * NZ)
    mode_scale = 1.0 / math.sqrt(KX * KY * KZ)
    mode_rows = spec_weight.shape[0]
    weight = spec_weight.reshape(mode_rows * KZ, 2 * channels * channels)
    width = weight.shape[1] // copies

    first, first_high, last, last_high = cut_rims(field)
    rims = exchange(first, last)
    planar = swap(forward_modes(field, slabs))
    rims, first, last = barrier((rims, first_high, last_high))
    rims_high = exchange(first, last)
    planar, smooth = barrier((planar, smooth_planes(field, rims, taps)))
    spectrum, planar = mix(planar, weight, cell_scale, 0.5 * mode_scale)
    smooth, spectrum = barrier((smooth, spectrum))
    planar = swap(planar)
    smooth = smooth_planes(field, rims_high, taps, smooth)
    spread, planar, first, last = layer(planar, smooth, cotangent[0], grains[0], bias, point_weight)
    rims = exchange(first, last)
    planar, send = mix(swap(planar), weight, 0.5 * mode_scale, cell_scale, spectrum, copies)
    send, spread = barrier((send, spread))
    inner = near_inner(spread, taps)
    gathered = lax.all_to_all(send, "dp", split_axis=0, concat_axis=0)
    planar, gathered, inner, rims = barrier((planar, gathered, inner, rims))
    planar = swap(planar)
    grad_spec = weight_gradient(gathered, KX // slabs, width)
    planar, grad_spec = barrier((planar, grad_spec))
    grad_feats = finish(planar, spread, rims, inner, taps)[None]
    return (grad_feats, grad_spec.reshape(mode_rows, KZ, width))


def local(feats, grains, spec_weight, taps, point_weight, bias, cotangent):
    samples, channels, planes = feats.shape[:3]
    width = spec_weight.shape[2] // lax.axis_size("dp")
    fits = (
        lax.axis_size("slab") * 4 == KX
        and samples == 1
        and channels == 32
        and planes == 8
        and channels * channels == 2 * width
    )
    form = local_fast if fits else local_any
    return form(feats, grains, spec_weight, taps, point_weight, bias, cotangent)


def solution(mesh):
    in_specs = (
        P(("grp", "dp"), None, "slab", None, None),
        P(("grp", "dp"), "slab", None, None),
        P("slab", None, None),
        P(),
        P(),
        P(),
        P(("grp", "dp"), None, "slab", None, None),
    )
    out_specs = (P(("grp", "dp"), None, "slab", None, None), P("slab", "grp", "dp"))
    return jax.shard_map(local, mesh=mesh, in_specs=in_specs, out_specs=out_specs, check_vma=False)
```

```python
import functools
import math

import jax
import jax.numpy as jnp
import ml_dtypes
import numpy as np
from jax import lax
from jax.experimental import pallas as pl
from jax.experimental.pallas import tpu as pltpu
from jax.sharding import PartitionSpec as P

NX = 128
NY = 128
NZ = 32
KX = 16
KY = 16
KZ = 16


HIGHEST = lax.Precision.HIGHEST


def extended(shard, sides, width):
    for axis, dim in sides:
        size, length = (lax.axis_size(axis), shard.shape[dim])
        up = [(i, (i + 1) % size) for i in range(size - 1)]
        down = [(j, i) for i, j in up]
        last = lax.slice_in_dim(shard, length - width, length, axis=dim)
        first = lax.slice_in_dim(shard, 0, width, axis=dim)
        before = lax.ppermute(last, axis, up)
        after = lax.ppermute(first, axis, down)
        shard = jnp.concatenate([before, shard, after], axis=dim)
    return shard


def tables(count, length, span):
    indices = jnp.arange(count, dtype=jnp.int32)
    frequency = jnp.where(indices < count // 2, indices, length - count + indices)
    position = jnp.arange(span, dtype=jnp.int32)
    phases = frequency[:, None] * position[None, :] % length
    angles = phases.astype(jnp.float32) * (2.0 * math.pi / length)
    return (jnp.cos(angles), jnp.sin(angles))


def mobility(grains):
    leading = [(0, 0)] * (grains.ndim - 2)
    along_x = (grains[..., 1:, :] != grains[..., :-1, :]).astype(jnp.float32)
    along_y = (grains[..., :, 1:] != grains[..., :, :-1]).astype(jnp.float32)
    differ = jnp.pad(along_x, leading + [(1, 0), (0, 0)]) + jnp.pad(
        along_x, leading + [(0, 1), (0, 0)]
    )
    differ = (
        differ
        + jnp.pad(along_y, leading + [(0, 0), (1, 0)])
        + jnp.pad(along_y, leading + [(0, 0), (0, 1)])
    )
    return 0.25 * (1.0 + differ)


def stencil(padded, taps, adjoint):
    planes = padded.shape[-3] - 2
    rows_x = padded.shape[-2] - 2
    rows_y = padded.shape[-1] - 2
    total = jnp.zeros(padded.shape[:-3] + (planes, rows_x, rows_y), jnp.float32)
    for offset in range(27):
        shift_z, shift_x, shift_y = (offset // 9, offset // 3 % 3, offset % 3)
        if adjoint:
            shift_z, shift_x, shift_y = (2 - shift_z, 2 - shift_x, 2 - shift_y)
        window = padded[
            ..., shift_z : shift_z + planes, shift_x : shift_x + rows_x, shift_y : shift_y + rows_y
        ]
        total = total + taps[offset][:, None, None, None] * window.astype(jnp.float32)
    return total


def plane_forward(field, cos_x, sin_x, cos_y, sin_y):
    real_y = jnp.einsum("...xy,ky->...xk", field, cos_y, precision=HIGHEST)
    imag_y = -jnp.einsum("...xy,ky->...xk", field, sin_y, precision=HIGHEST)
    real_part = jnp.einsum("...xk,jx->...jk", real_y, cos_x, precision=HIGHEST) + jnp.einsum(
        "...xk,jx->...jk", imag_y, sin_x, precision=HIGHEST
    )
    imag_part = jnp.einsum("...xk,jx->...jk", imag_y, cos_x, precision=HIGHEST) - jnp.einsum(
        "...xk,jx->...jk", real_y, sin_x, precision=HIGHEST
    )
    return (real_part, imag_part)


def plane_inverse(real_part, imag_part, cos_x, sin_x, cos_y, sin_y):
    real_x = jnp.einsum("...jk,jx->...xk", real_part, cos_x, precision=HIGHEST) - jnp.einsum(
        "...jk,jx->...xk", imag_part, sin_x, precision=HIGHEST
    )
    imag_x = jnp.einsum("...jk,jx->...xk", imag_part, cos_x, precision=HIGHEST) + jnp.einsum(
        "...jk,jx->...xk", real_part, sin_x, precision=HIGHEST
    )
    return jnp.einsum("...xk,ky->...xy", real_x, cos_y, precision=HIGHEST) - jnp.einsum(
        "...xk,ky->...xy", imag_x, sin_y, precision=HIGHEST
    )


def depth_forward(packed, cos_table, sin_table):
    width = packed.shape[-1] // 2
    real_in = packed[..., :width]
    imag_in = packed[..., width:]
    real_out = jnp.einsum("pszc,kz->pskc", real_in, cos_table, precision=HIGHEST) + jnp.einsum(
        "pszc,kz->pskc", imag_in, sin_table, precision=HIGHEST
    )
    imag_out = jnp.einsum("pszc,kz->pskc", imag_in, cos_table, precision=HIGHEST) - jnp.einsum(
        "pszc,kz->pskc", real_in, sin_table, precision=HIGHEST
    )
    return jnp.concatenate([real_out, imag_out], axis=-1)


def depth_inverse(real_modes, imag_modes, cos_table, sin_table):
    real_out = jnp.einsum("pskc,kz->pszc", real_modes, cos_table, precision=HIGHEST) - jnp.einsum(
        "pskc,kz->pszc", imag_modes, sin_table, precision=HIGHEST
    )
    imag_out = jnp.einsum("pskc,kz->pszc", imag_modes, cos_table, precision=HIGHEST) + jnp.einsum(
        "pskc,kz->pszc", real_modes, sin_table, precision=HIGHEST
    )
    return jnp.concatenate([real_out, imag_out], axis=-1)


def rim_planes(field):
    return extended(field, (("slab", 2),), 1)


def local_any(feats, grains, spec_weight, taps, point_weight, bias, cotangent):
    samples_here = feats.shape[0]
    channels = feats.shape[1]
    planes = feats.shape[2]
    cos_x, sin_x = tables(KX, NX, NX)
    cos_y, sin_y = tables(KY, NY, NY)
    cos_full, sin_full = tables(KZ, NZ, NZ)
    cell_scale = math.sqrt(NX * NY * NZ)
    mode_scale = math.sqrt(KX * KY * KZ)
    mode_rows = spec_weight.shape[0]
    weights = spec_weight.astype(jnp.float32).reshape(mode_rows, KZ, 2, channels, channels)
    w_real = weights[:, :, 0]
    w_imag = weights[:, :, 1]
    moving = mobility(grains)[:, None]

    def to_modes(field):
        real_plane, imag_plane = plane_forward(field, cos_x, sin_x, cos_y, sin_y)
        packed = jnp.stack([real_plane, imag_plane], axis=1)
        packed = packed.transpose(4, 5, 0, 3, 1, 2).reshape(
            KX * KY, samples_here, planes, 2 * channels
        )
        moved = lax.all_to_all(packed, "slab", split_axis=0, concat_axis=2, tiled=True)
        summed = depth_forward(moved, cos_full, sin_full)
        return (summed[..., :channels], summed[..., channels:])

    def from_modes(real_modes, imag_modes):
        planar = depth_inverse(real_modes, imag_modes, cos_full, sin_full)
        packed = lax.all_to_all(planar, "slab", split_axis=2, concat_axis=0, tiled=True)
        grouped = packed.reshape(KX, KY, samples_here, planes, 2, channels).transpose(
            2, 4, 5, 3, 0, 1
        )
        return plane_inverse(grouped[:, 0], grouped[:, 1], cos_x, sin_x, cos_y, sin_y)

    zero_rim = ((0, 0), (0, 0), (0, 0), (1, 1), (1, 1))
    padded = jnp.pad(rim_planes(feats), zero_rim)
    smooth = stencil(padded, taps, False).astype(jnp.bfloat16)
    local_part = moving * jnp.einsum(
        "sczxy,co->sozxy", smooth, point_weight, preferred_element_type=jnp.float32
    )
    spec_real, spec_imag = to_modes(feats.astype(jnp.float32))
    spec_real = spec_real / cell_scale
    spec_imag = spec_imag / cell_scale
    mixed_real = jnp.einsum("pskc,pkco->psko", spec_real, w_real, precision=HIGHEST) - jnp.einsum(
        "pskc,pkco->psko", spec_imag, w_imag, precision=HIGHEST
    )
    mixed_imag = jnp.einsum("pskc,pkco->psko", spec_real, w_imag, precision=HIGHEST) + jnp.einsum(
        "pskc,pkco->psko", spec_imag, w_real, precision=HIGHEST
    )
    spectral = from_modes(mixed_real, mixed_imag) / mode_scale
    pre = spectral + local_part + bias[None, :, None, None, None]
    gate = jax.nn.sigmoid(pre)
    delta = (cotangent.astype(jnp.float32) * gate * (1.0 + pre * (1.0 - gate))).astype(jnp.bfloat16)
    dual_real, dual_imag = to_modes(delta.astype(jnp.float32))
    dual_real = dual_real / mode_scale
    dual_imag = dual_imag / mode_scale
    batch_total = samples_here * lax.axis_size("dp")
    grad_real = jnp.einsum("pskc,psko->pkco", spec_real, dual_real, precision=HIGHEST) + jnp.einsum(
        "pskc,psko->pkco", spec_imag, dual_imag, precision=HIGHEST
    )
    grad_imag = jnp.einsum("pskc,psko->pkco", spec_real, dual_imag, precision=HIGHEST) - jnp.einsum(
        "pskc,psko->pkco", spec_imag, dual_real, precision=HIGHEST
    )
    grad_terms = (jnp.stack([grad_real, grad_imag], axis=2) / batch_total).reshape(
        mode_rows, KZ, 2 * channels * channels
    )
    grad_spec = lax.psum_scatter(
        grad_terms.astype(jnp.bfloat16), "dp", scatter_dimension=2, tiled=True
    ).astype(jnp.float32)
    back_real = jnp.einsum("psko,pkco->pskc", dual_real, w_real, precision=HIGHEST) + jnp.einsum(
        "psko,pkco->pskc", dual_imag, w_imag, precision=HIGHEST
    )
    back_imag = jnp.einsum("psko,pkco->pskc", dual_imag, w_real, precision=HIGHEST) - jnp.einsum(
        "psko,pkco->pskc", dual_real, w_imag, precision=HIGHEST
    )
    spectral_back = from_modes(back_real, back_imag) / cell_scale
    spread = (
        moving
        * jnp.einsum("sozxy,co->sczxy", delta, point_weight, preferred_element_type=jnp.float32)
    ).astype(jnp.bfloat16)
    spread_padded = jnp.pad(rim_planes(spread), zero_rim)
    local_back = stencil(spread_padded, taps, True)
    grad_feats = (spectral_back + local_back).astype(jnp.bfloat16)
    return (grad_feats, grad_spec)


def frequencies(count, length):
    index = np.arange(count)
    return np.where(index < count // 2, index, length - count + index)


def angles(count, length):
    phases = np.outer(frequencies(count, length), np.arange(length)) % length
    return phases * (2.0 * np.pi / length)


def constant(array):
    return jnp.asarray(np.asarray(array, np.float32).astype(ml_dtypes.bfloat16))


def forward_x_table(slabs, split):
    a = angles(KX, NX).reshape(slabs, KX // slabs, NX)
    trig = np.stack([np.cos(a), np.sin(a)])
    table = np.einsum("tsjx,cd->tscjdx", trig, np.eye(2)).reshape(-1, 2, NX // 8, 8)
    if split:
        table = table.transpose(0, 2, 1, 3)
    return table.reshape(4 * KX, 2 * NX)


def halved(table, planes):
    table = table.reshape(-1, planes * 2, 2, KY // 2).transpose(0, 2, 1, 3)
    return table.reshape(-1, planes * 2 * KY)


def forward_y_table(planes):
    a = angles(KY, NY)
    cos, sin = np.cos(a).T, np.sin(a).T
    block = np.stack([np.stack([cos, -sin], 1), np.stack([-sin, -cos], 1)])
    pick = np.eye(planes).reshape(planes // 2, 2, planes)
    table = np.einsum("pqz,tyrk->ptqyzrk", pick, block)
    return halved(table.reshape(planes * 2 * NY, planes * 2 * KY), planes)


def forward_z_table():
    a = angles(KZ, NZ)
    cos, sin = np.cos(a).T, np.sin(a).T
    block = np.stack([np.stack([cos, -sin], 1), np.stack([sin, cos], 1)], 1)
    table = np.einsum("zrqm,kl->zrkqlm", block, np.eye(KY // 2))
    return table.reshape(NZ * KY, KY * KZ)


def inverse_z_table():
    a = angles(KZ, NZ)
    cos, sin = np.cos(a), np.sin(a)
    block = np.stack([np.stack([cos, sin], 2), np.stack([-sin, cos], 2)])
    table = np.einsum("rmzq,kl->rkmzql", block, np.eye(KY // 2))
    return table.reshape(KY * KZ, NZ * KY)


def inverse_y_table(planes, group):
    a = angles(KY, NY)
    cos, sin = np.cos(a), np.sin(a)
    block = np.stack([np.stack([cos, -sin], 1), np.stack([-sin, -cos], 1)])
    pick = np.eye(planes).reshape(planes // group, group, planes)
    table = np.einsum("pqz,rkty->ptqyzrk", pick, block)
    table = halved(table.reshape(-1, planes * 2 * KY), planes)
    return table.reshape(planes // group, 2 * group * NY, planes * 2 * KY).transpose(0, 2, 1)


def inverse_x_table(slabs, group):
    a = angles(KX, NX).reshape(slabs, KX // slabs, NX)
    trig = np.stack([np.cos(a), np.sin(a)])
    table = np.einsum("tsjx,cd->cxstdj", trig, np.eye(group))
    return table.reshape(group * NX, 2 * KX * group)


def first_table(channels, depth):
    table = np.einsum("ac,j,b->ajcb", np.eye(channels), np.ones(depth), np.ones(channels))
    return table.reshape(channels * depth, channels * channels)


def second_table(channels, depth):
    table = np.einsum("ac,j,b->ajbc", np.eye(channels), np.ones(depth), np.ones(channels))
    return table.reshape(channels * depth, channels * channels)


LIGHT = pl.CostEstimate(flops=10**7, bytes_accessed=10**5, transcendentals=0)
HEAVY = pl.CostEstimate(flops=10**11, bytes_accessed=10**8, transcendentals=0)


def dot(a, b):
    return jnp.dot(a, b, preferred_element_type=jnp.float32)


def whole(shape):
    return pl.BlockSpec(shape, lambda *_: (0,) * len(shape))


def params(**kw):
    return pltpu.CompilerParams(vmem_limit_bytes=63438848, **kw)


def store_rows(rows, pair, x_table, load):
    slabs, lines = rows.shape[2:4]
    for i in range(lines // 16):
        parts = [dot(x_table[...], load(2 * i + k)) for k in range(2)]
        for t in range(2):
            for s in range(slabs):
                here = slice(8 * (t * slabs + s), 8 * (t * slabs + s) + 8)
                both = jnp.concatenate([part[here] for part in parts], axis=0)
                rows[pair, t, s, 16 * i : 16 * i + 16, :] = both.astype(jnp.bfloat16)


def store_modes(rows, y_table, out):
    pairs, _, slabs, lines, _ = rows.shape
    left = [
        jnp.concatenate([rows[p, t, s] for p in range(pairs) for t in range(2)], axis=1)
        for s in range(slabs)
    ]
    modes = dot(jnp.concatenate(left, axis=0), y_table[...])
    for s in range(slabs):
        out[s] = modes[s * lines : (s + 1) * lines].astype(jnp.bfloat16)


def low_channels(channels):
    return 3 * channels // 8


def rims_kernel(field, *refs):
    rims, held, got, put = refs[:4], refs[4:8], refs[8], refs[9]
    last = field.shape[1] - 1
    loads, stores = [], []
    for k in range(4):
        count = rims[k].shape[0]
        source = field.at[pl.ds((k % 2) * rims[0].shape[0], count), pl.ds(last * (k // 2), 1)]
        loads.append(pltpu.make_async_copy(source, held[k], got.at[k]))
        stores.append(pltpu.make_async_copy(held[k], rims[k], put.at[k]))
    for load in loads:
        load.start()
    for load, store in zip(loads, stores):
        load.wait()
        store.start()
    for store in stores:
        store.wait()


def cut_rims(field):
    channels = field.shape[0]
    low = low_channels(channels)
    rims = [
        jax.ShapeDtypeStruct((count, 1, NX, NY), jnp.bfloat16) for count in (low, channels - low) * 2
    ]
    return pl.pallas_call(
        rims_kernel,
        in_specs=[pl.BlockSpec(memory_space=pl.ANY)],
        out_specs=[pl.BlockSpec(memory_space=pl.ANY)] * 4,
        out_shape=rims,
        scratch_shapes=[
            *(pltpu.VMEM(rim.shape, jnp.bfloat16) for rim in rims),
            pltpu.SemaphoreType.DMA((4,)),
            pltpu.SemaphoreType.DMA((4,)),
        ],
        compiler_params=params(),
        cost_estimate=LIGHT,
        name="rims",
    )(field)


def forward_kernel(field, x_table, y_table, out, rows):
    pair = pl.program_id(0)
    pairs = rows.shape[0]

    def load(i):
        halves = [field[2 * i : 2 * i + 2, q].reshape(2 * NX, NY) for q in range(2)]
        return jnp.concatenate(halves, axis=1)

    store_rows(rows, pair, x_table, load)

    @pl.when(pair == pairs - 1)
    def _():
        store_modes(rows, y_table, out)


def forward_modes(field, slabs):
    channels, planes = field.shape[:2]
    lines = channels * (KX // slabs)
    x_table = constant(forward_x_table(slabs, False))
    y_table = constant(forward_y_table(planes))
    shape = (slabs, lines, planes * 2 * KY)
    return pl.pallas_call(
        forward_kernel,
        grid=(planes // 2,),
        in_specs=[
            pl.BlockSpec((channels, 2, NX, NY), lambda p: (0, p, 0, 0)),
            whole(x_table.shape),
            whole(y_table.shape),
        ],
        out_specs=whole(shape),
        out_shape=jax.ShapeDtypeStruct(shape, jnp.bfloat16),
        scratch_shapes=[pltpu.VMEM((planes // 2, 2, slabs, lines, 2 * NY), jnp.bfloat16)],
        compiler_params=params(),
        cost_estimate=LIGHT,
        name="forward_modes",
    )(field, x_table, y_table)


def mixing_kernel(scale_in, scale_out, adjoint, planar, weight, z_in, z_out, spread_table,
                  sum_table, *rest):
    if adjoint:
        partner, out, send, spectrum, total, wide, product = rest
    else:
        spectrum, out, total, wide, product = rest
    step = pl.program_id(0)
    steps = pl.num_programs(0)
    slabs, lines, width = planar.shape
    half = width // 2
    quarter = spectrum.shape[0] // 4
    lanes = weight.shape[1] // 2
    depth = weight.shape[0] // (2 * quarter)

    @pl.when(step == 0)
    def _():
        left = [
            jnp.concatenate([planar[s, :, h : h + half] for s in range(slabs)], axis=1)
            for h in (0, half)
        ]
        modes = dot(jnp.concatenate(left, axis=0), z_in[...]) * scale_in
        for h in range(2):
            here = modes[h * lines : (h + 1) * lines].T.astype(jnp.bfloat16)
            spectrum[2 * h * quarter : 2 * (h + 1) * quarter] = here
            if adjoint:
                for d in range(send.shape[0]):
                    send[d, 2 * (h + 1) * quarter : 2 * (h + 2) * quarter] = here
        if adjoint:
            rows = [partner[2 * h * quarter : 2 * (h + 1) * quarter] for h in range(2)]
            rows = [row.astype(jnp.float32) for row in rows]
            left = lax.broadcasted_iota(jnp.int32, (1, lines), 1) < lines // 2
            turned = [pltpu.roll(row, lines // 2, axis=1) for row in rows]
            packed = [jnp.where(left, rows[0], turned[1]), jnp.where(left, turned[0], rows[1])]
            for d in range(send.shape[0]):
                send[d, : 2 * quarter] = packed[d % 2].astype(jnp.bfloat16)
        total[...] = jnp.zeros_like(total)

    lane = lax.broadcasted_iota(jnp.int32, (1, lines), 1) % (depth * steps)
    block = 32
    tile = wide.shape[1]
    for j in range(depth):
        mine = lane == depth * step + j
        wide[...] = dot(jnp.where(mine, spectrum[...], 0), spread_table[...])
        for at in range(0, 2 * quarter, block):
            row = 2 * j * quarter + at
            real_at = at + (at // quarter) * quarter
            imag_at = real_at + quarter
            sums = [0.0, 0.0]
            for column in range(0, lanes, 128):
                here = slice(column, column + 128) if tile == lanes else slice(None)
                real_wide = wide[real_at : real_at + block, here]
                imag_wide = wide[imag_at : imag_at + block, here]
                w_real = weight[row : row + block, column : column + 128]
                w_imag = weight[row : row + block, lanes + column : lanes + column + 128]
                w_real = w_real.astype(jnp.float32)
                w_imag = w_imag.astype(jnp.float32)
                if adjoint:
                    real = real_wide * w_real + imag_wide * w_imag
                    imag = imag_wide * w_real - real_wide * w_imag
                    there = slice(column, column + 128)
                    product[real_at : real_at + block, there] = real.astype(jnp.bfloat16)
                    product[imag_at : imag_at + block, there] = imag.astype(jnp.bfloat16)
                else:
                    sums[0] = sums[0] + (real_wide * w_real - imag_wide * w_imag)
                    sums[1] = sums[1] + (real_wide * w_imag + imag_wide * w_real)
            if not adjoint:
                product[real_at : real_at + block] = sums[0].astype(jnp.bfloat16)
                product[imag_at : imag_at + block] = sums[1].astype(jnp.bfloat16)
        total[...] += jnp.where(mine, dot(product[...], sum_table[...]), 0.0)

    @pl.when(step == steps - 1)
    def _():
        modes = total[...] * scale_out
        left = [modes[2 * h * quarter : 2 * (h + 1) * quarter].T for h in range(2)]
        modes = dot(jnp.concatenate(left, axis=0).astype(jnp.bfloat16), z_out[...])
        for s in range(slabs):
            for h in range(2):
                here = modes[h * lines : (h + 1) * lines, s * half : (s + 1) * half]
                out[s, :, h * half : (h + 1) * half] = here.astype(jnp.bfloat16)


def mix(planar, weight, scale_in, scale_out, partner=None, copies=0):
    slabs, lines, width = planar.shape
    adjoint = partner is not None
    depth = KX // slabs
    channels = lines // depth
    rows = KY * KZ
    steps = 2
    z_in = constant(forward_z_table())
    z_out = constant(inverse_z_table())
    first = first_table(channels, depth)
    second = second_table(channels, depth)
    spread_table = constant(second[:, :128] if adjoint else first)
    sum_table = constant(first.T if adjoint else second[:, :128].T)
    shape = (2 * rows, lines)
    in_specs = [
        whole(planar.shape),
        pl.BlockSpec((depth // steps * rows, weight.shape[1]), lambda j: (j, 0)),
        whole(z_in.shape),
        whole(z_out.shape),
        whole(spread_table.shape),
        whole(sum_table.shape),
    ]
    operands = [planar, weight, z_in, z_out, spread_table, sum_table]
    scratch = [
        pltpu.VMEM(shape, jnp.float32),
        pltpu.VMEM((2 * rows, spread_table.shape[1]), jnp.float32),
        pltpu.VMEM((2 * rows, sum_table.shape[0]), jnp.bfloat16),
    ]
    if adjoint:
        in_specs.append(whole(shape))
        operands.append(partner)
        scratch = [pltpu.VMEM(shape, jnp.bfloat16)] + scratch
        outs = [planar.shape, (copies, 3 * rows, lines)]
    else:
        outs = [shape, planar.shape]
    return pl.pallas_call(
        functools.partial(mixing_kernel, scale_in, scale_out, adjoint),
        grid=(steps,),
        in_specs=in_specs,
        out_specs=[whole(out) for out in outs],
        out_shape=[jax.ShapeDtypeStruct(out, jnp.bfloat16) for out in outs],
        scratch_shapes=scratch,
        compiler_params=params(),
        cost_estimate=HEAVY,
        name="mix_back" if adjoint else "mix",
    )(*operands)


def plane_mobility(grains):
    same = [
        jnp.concatenate([grains[:1], grains[:-1]], axis=0),
        jnp.concatenate([grains[1:], grains[-1:]], axis=0),
        jnp.concatenate([grains[:, :1], grains[:, :-1]], axis=1),
        jnp.concatenate([grains[:, 1:], grains[:, -1:]], axis=1),
    ]
    total = jnp.full(grains.shape, 0.25, jnp.float32)
    for other in same:
        total = total + jnp.where(grains != other, 0.25, 0.0)
    return total


def layer_kernel(bias, planar, smooth, cotangent, grains, point_weight, repeat, ix_table, iy_table,
                 x_table, y_table, spread, out, first, last, *rest):
    pair = pl.program_id(0)
    waves, spectral, moving, delta, rows, bias_wide, mix_out, mix_in = rest
    pairs = rows.shape[0]
    channels = cotangent.shape[0]
    slabs = planar.shape[0]

    @pl.when(pair == 0)
    def _():
        for c in range(channels):
            bias_wide[c] = jnp.full(bias_wide.shape[1:], 0.5 * bias[c], jnp.float32)
        tall = dot(repeat[...], point_weight[...]).astype(jnp.bfloat16)
        square = lax.dot_general(
            tall, repeat[...], (((1,), (1,)), ((), ())), preferred_element_type=jnp.float32
        )
        row = lax.broadcasted_iota(jnp.int32, square.shape, 0) % 8
        column = lax.broadcasted_iota(jnp.int32, square.shape, 1) % 8
        square = jnp.where(row == column, square, 0.0)
        mix_in[...] = square.astype(jnp.bfloat16)
        mix_out[...] = square.T.astype(jnp.bfloat16)

    lines = planar.shape[1]
    step = jnp.concatenate([planar[s] for s in range(slabs)], axis=0)
    step = dot(step, iy_table[0]).astype(jnp.bfloat16)
    for s in range(slabs):
        for t in range(2):
            waves[s, t] = step[s * lines : (s + 1) * lines, 2 * NY * t : 2 * NY * (t + 1)]
    group = 8 * (KX // slabs)
    for g in range(channels // 8):
        here = slice(g * group, (g + 1) * group)
        wave = [waves[s, t, here, :] for s in range(slabs) for t in range(2)]
        step = dot(ix_table[...], jnp.concatenate(wave, axis=0))
        spectral[8 * g : 8 * g + 8] = step.reshape(8, NX, 2 * NY)
    for q in range(2):
        moving[:, q * NY : (q + 1) * NY] = 0.5 * plane_mobility(grains[q])

    def body(i, _):
        x = pl.multiple_of(16 * i, 16)
        halves = [cotangent[:, q, pl.ds(x, 16), :] for q in range(2)]
        cotangent_here = jnp.concatenate(halves, axis=2).astype(jnp.float32)
        spreads = []
        for h in range(2):
            at = pl.ds(pl.multiple_of(x + 8 * h, 8), 8)
            mobile = moving[at, :][None]
            local = dot(mix_out[...], smooth[0, 2 * i + h]).reshape(channels, 8, 2 * NY)
            half = spectral[:, at, :] + mobile * local + bias_wide[...]
            wave = jnp.tanh(half)
            slope = (1.0 + wave) * (1.0 + (half - half * wave))
            change = cotangent_here[:, 8 * h : 8 * h + 8, :] * slope
            right = change.reshape(8 * channels, 2 * NY).astype(jnp.bfloat16)
            delta[2 * i + h] = right
            back = dot(mix_in[...], right).reshape(channels, 8, 2 * NY)
            spreads.append(mobile * back)
        both = jnp.concatenate(spreads, axis=1).astype(jnp.bfloat16)
        for q in range(2):
            spread[:, q, pl.ds(x, 16), :] = both[:, :, q * NY : (q + 1) * NY]
        return 0

    lax.fori_loop(0, NX // 16, body, 0, unroll=8)


    @pl.when(pair == 0)
    def _():
        first[:, 0] = spread[:, 0]

    @pl.when(pair == pairs - 1)
    def _():
        last[:, 0] = spread[:, 1]

    def load(i):
        return delta[:, 16 * i : 16 * i + 16, :].reshape(2 * NX, 2 * NY)

    store_rows(rows, pair, x_table, load)

    @pl.when(pair == pairs - 1)
    def _():
        store_modes(rows, y_table, out)


def layer(planar, smooth, cotangent, grains, bias, point_weight):
    slabs, lines, width = planar.shape
    channels, planes = cotangent.shape[:2]
    pairs = planes // 2
    repeat = constant(np.repeat(np.eye(channels), 8, axis=0))
    ix_table = constant(inverse_x_table(slabs, 8))
    iy_table = constant(inverse_y_table(planes, 2))
    x_table = constant(forward_x_table(slabs, True))
    y_table = constant(forward_y_table(planes))
    field = pl.BlockSpec((channels, 2, NX, NY), lambda p: (0, p, 0, 0))
    outs = [cotangent.shape, planar.shape] + [(channels, 1, NX, NY)] * 2
    return pl.pallas_call(
        layer_kernel,
        grid=(pairs,),
        in_specs=[
            pl.BlockSpec(memory_space=pltpu.SMEM),
            whole(planar.shape),
            pl.BlockSpec((1,) + smooth.shape[1:], lambda p: (p, 0, 0, 0)),
            field,
            pl.BlockSpec((2, NX, NY), lambda p: (p, 0, 0)),
            whole(point_weight.shape),
            whole(repeat.shape),
            whole(ix_table.shape),
            pl.BlockSpec((1,) + iy_table.shape[1:], lambda p: (p, 0, 0)),
            whole(x_table.shape),
            whole(y_table.shape),
        ],
        out_specs=[field] + [whole(out) for out in outs[1:]],
        out_shape=[jax.ShapeDtypeStruct(out, jnp.bfloat16) for out in outs],
        scratch_shapes=[
            pltpu.VMEM((slabs, 2, lines, 2 * NY), jnp.bfloat16),
            pltpu.VMEM((channels, NX, 2 * NY), jnp.float32),
            pltpu.VMEM((NX, 2 * NY), jnp.float32),
            pltpu.VMEM((NX // 8, 8 * channels, 2 * NY), jnp.bfloat16),
            pltpu.VMEM((pairs, 2, slabs, lines, 2 * NY), jnp.bfloat16),
            pltpu.VMEM((channels, 8, 2 * NY), jnp.float32),
            pltpu.VMEM((8 * channels, 8 * channels), jnp.bfloat16),
            pltpu.VMEM((8 * channels, 8 * channels), jnp.bfloat16),
        ],
        compiler_params=params(),
        cost_estimate=LIGHT,
        name="layer",
    )(bias, planar, smooth, cotangent, grains, point_weight, repeat, ix_table, iy_table, x_table,
      y_table)


def build_tile(adjoint, taps, channel, dy, q, planes, span):
    row = lax.broadcasted_iota(jnp.int32, (8, 128), 0)
    lane = lax.broadcasted_iota(jnp.int32, (8, 128), 1)
    tile = jnp.zeros((8, 128), jnp.float32)
    for k, plane in enumerate(planes):
        dz = plane - q
        if not 0 <= dz <= 2:
            continue
        for dx in range(3):
            number = 9 * dz + 3 * dx + dy
            tap = taps[26 - number if adjoint else number, channel]
            tile = jnp.where(lane == (span * k + row + (dx - 1)) % 128, tap, tile)
    return tile


def build_band(adjoint, taps, channel, band, tail):
    row = lax.broadcasted_iota(jnp.int32, (8, 128), 0)
    lane = lax.broadcasted_iota(jnp.int32, (8, 128), 1)
    heads, middles, tails = [], [], []
    for dy in range(3):
        for q in range(2):
            sides = []
            for planes in ((0, 1), (2, 3)):
                tile = build_tile(adjoint, taps, channel, dy, q, planes, 64)
                tiles = [pltpu.roll(tile, 8 * k, axis=1) for k in range(1, 7)]
                first = jnp.where((row == 0) & (lane % 64 == 63), 0.0, tile)
                sides.append([first] + tiles)
            blocks = [jnp.concatenate(pair, axis=1) for pair in zip(*sides)]
            heads += blocks
            middles += blocks[1:]
            tile = build_tile(adjoint, taps, channel, dy, q, range(4), 32)
            tiles = [pltpu.roll(tile, 8 * k, axis=1) for k in range(1, 4)]
            tiles[2] = jnp.where((row == 7) & (lane % 32 == 0), 0.0, tiles[2])
            tails += tiles
    band[...] = jnp.concatenate(heads + middles, axis=0).astype(jnp.bfloat16)
    tail[...] = jnp.concatenate(tails, axis=0).astype(jnp.bfloat16)


def apply_band(quads, band):
    band, tail = band
    counts = (56, 48, 24)
    ends = (6 * counts[0], 6 * (counts[0] + counts[1]))
    lefts = (band[: ends[0], :], band[ends[0] : ends[1], :], tail[...])
    lane = lax.broadcasted_iota(jnp.int32, (NX, NY), 1)
    totals = []
    for group in range(0, len(quads), 2):
        products = []
        for left, x, span in zip(lefts, (0, 48, 96), (64, 64, 32)):
            right = [
                jnp.concatenate([sheet[x : x + span] for sheet in quads[group + p]], axis=0)
                for p in range(2)
            ]
            products.append(dot(left, jnp.concatenate(right, axis=1)))
        for p in range(2):
            wide = slice(NY * p, NY * (p + 1))
            pair = []
            for q in range(2):
                shifted = []
                for dy in range(3):
                    b = 2 * dy + q
                    pieces = [
                        product[count * b : count * (b + 1), wide]
                        for product, count in zip(products, counts)
                    ]
                    shifted.append(jnp.concatenate(pieces, axis=0))
                before = jnp.where(lane == 0, 0.0, pltpu.roll(shifted[0], 1, axis=1))
                after = jnp.where(lane == NY - 1, 0.0, pltpu.roll(shifted[2], NY - 1, axis=1))
                pair.append(shifted[1] + before + after)
            totals.append(jnp.concatenate(pair, axis=1))
    return totals


def banded(adjoint, taps, start, bands, channels):
    step = pl.program_id(0)
    final = start + channels * pl.num_programs(0) - 1

    @pl.when(step == 0)
    def _():
        build_band(adjoint, taps, start, *bands[0])

    def run(visit):
        for c in range(channels):
            following = jnp.minimum(start + channels * step + c + 1, final)
            build_band(adjoint, taps, following, *bands[(c + 1) % 2])
            visit(c, bands[c % 2])

    return run


def band_scratch():
    shapes = [(6 * (56 + 48), 256), (6 * 24, 128)]
    return [pltpu.VMEM(shape, jnp.bfloat16) for shape in shapes * 2]


def smooth_kernel(start, taps, before, field, after, *rest):
    out, *bands = rest[-5:]
    bands = bands[:2], bands[2:]
    planes = field.shape[1]
    totals = []

    def visit(c, band):
        sheets = [before[c, 0]] + [field[c, z] for z in range(planes)] + [after[c, 0]]
        totals.append(apply_band([sheets[z : z + 4] for z in range(0, planes, 2)], band))

        if c % 2 == 1:
            for p in range(planes // 2):
                both = [total[p].reshape(NX // 8, 8, 2 * NY) for total in totals[c - 1 : c + 1]]
                both = jnp.concatenate(both, axis=1).astype(jnp.bfloat16)
                out[p, :, 8 * (c - 1) : 8 * (c + 1), :] = both

    banded(False, taps, start, bands, field.shape[0])(visit)


def smooth_planes(field, rims, taps, done=None):
    channels, planes = field.shape[:2]
    pairs = planes // 2
    low = low_channels(channels)
    start = 0 if done is None else low
    count = low if done is None else channels - low
    step = 4
    skip = start // step
    rim = pl.BlockSpec((step, 1, NX, NY), lambda c: (c, 0, 0, 0))
    sheets = pl.BlockSpec((step, planes, NX, NY), lambda c: (c + skip, 0, 0, 0))
    in_specs = [pl.BlockSpec(memory_space=pltpu.SMEM), rim, sheets, rim]
    operands = [taps, rims[0], field, rims[1]]
    if done is not None:
        in_specs.append(pl.BlockSpec(memory_space=pl.ANY))
        operands.append(done)
    return pl.pallas_call(
        functools.partial(smooth_kernel, start),
        grid=(count // step,),
        in_specs=in_specs,
        out_specs=pl.BlockSpec((pairs, NX // 8, 8 * step, 2 * NY), lambda c: (0, 0, c + skip, 0)),
        out_shape=jax.ShapeDtypeStruct((pairs, NX // 8, 8 * channels, 2 * NY), jnp.bfloat16),
        input_output_aliases={} if done is None else {4: 0},
        scratch_shapes=band_scratch(),
        compiler_params=params(),
        cost_estimate=LIGHT,
        name="smooth_low" if done is None else "smooth_high",
    )(*operands)


def inner_kernel(taps, field, out, *bands):
    bands = bands[:2], bands[2:]
    planes = field.shape[1]

    def visit(c, band):
        quads = [[field[c, z + k] for k in range(4)] for z in range(1, planes - 3, 2)]
        for p, near in enumerate(apply_band(quads, band)):
            total = near.astype(jnp.bfloat16)
            out[c, 2 * p] = total[:, :NY]
            out[c, 2 * p + 1] = total[:, NY:]

    banded(True, taps, 0, bands, field.shape[0])(visit)


def near_inner(field, taps):
    channels, planes = field.shape[:2]
    step = 8
    shape = (channels, planes - 4, NX, NY)
    return pl.pallas_call(
        inner_kernel,
        grid=(channels // step,),
        in_specs=[
            pl.BlockSpec(memory_space=pltpu.SMEM),
            pl.BlockSpec((step, planes, NX, NY), lambda c: (c, 0, 0, 0)),
        ],
        out_specs=pl.BlockSpec((step,) + shape[1:], lambda c: (c, 0, 0, 0)),
        out_shape=jax.ShapeDtypeStruct(shape, jnp.bfloat16),
        scratch_shapes=band_scratch(),
        compiler_params=params(),
        cost_estimate=LIGHT,
        name="near_inner",
    )(taps, field)


def finish_kernel(taps, before, field, after, inner, planar, ix_table, iy_table, out, waves,
                  *bands):
    bands = bands[:2], bands[2:]
    step = pl.program_id(0)
    slabs, lines = planar.shape[:2]
    planes = field.shape[1]
    span = planes * NY

    @pl.when(step == 0)
    def _():
        left = jnp.concatenate([planar[s] for s in range(slabs)], axis=0)
        for t in range(2):
            wave = dot(left, iy_table[0, :, t * span : (t + 1) * span]).astype(jnp.bfloat16)
            for s in range(slabs):
                waves[s, t] = wave[s * lines : (s + 1) * lines]

    rows = field.shape[0] * (KX // slabs)
    here = pl.ds(pl.multiple_of(rows * step, rows), rows)
    right = [waves[s, t, here, :] for s in range(slabs) for t in range(2)]
    right = jnp.concatenate(right, axis=0)
    far = [
        dot(ix_table[...], right[:, 2 * p * NY : 2 * (p + 1) * NY]) for p in range(planes // 2)
    ]

    def store(c, p, near):
        for q in range(2):
            total = near[q] + far[p][c * NX : (c + 1) * NX, q * NY : (q + 1) * NY]
            out[c, 2 * p + q] = total.astype(jnp.bfloat16)

    def visit(c, band):
        low = [before[c, 0]] + [field[c, z] for z in range(3)]
        high = [field[c, z] for z in range(planes - 3, planes)] + [after[c, 0]]
        for p, near in zip((0, planes // 2 - 1), apply_band([low, high], band)):
            store(c, p, [near[:, :NY], near[:, NY:]])
        for p in range(1, planes // 2 - 1):
            store(c, p, [inner[c, 2 * p - 2 + q].astype(jnp.float32) for q in range(2)])

    banded(True, taps, 0, bands, field.shape[0])(visit)


def finish(planar, spread, rims, inner, taps):
    slabs, lines, width = planar.shape
    channels, planes = spread.shape[:2]
    step = 8
    ix_table = constant(inverse_x_table(slabs, step))
    iy_table = constant(inverse_y_table(planes, planes))
    rim = pl.BlockSpec((step, 1, NX, NY), lambda c: (c, 0, 0, 0))
    sheets = pl.BlockSpec((step, planes, NX, NY), lambda c: (c, 0, 0, 0))
    return pl.pallas_call(
        finish_kernel,
        grid=(channels // step,),
        in_specs=[
            pl.BlockSpec(memory_space=pltpu.SMEM),
            rim,
            sheets,
            rim,
            pl.BlockSpec((step,) + inner.shape[1:], lambda c: (c, 0, 0, 0)),
            whole(planar.shape),
            whole(ix_table.shape),
            whole(iy_table.shape),
        ],
        out_specs=sheets,
        out_shape=jax.ShapeDtypeStruct(spread.shape, jnp.bfloat16),
        scratch_shapes=[
            pltpu.VMEM((slabs, 2, lines, planes * NY), jnp.bfloat16),
            *band_scratch(),
        ],
        compiler_params=params(),
        cost_estimate=HEAVY,
        name="finish",
    )(taps, rims[0], spread, rims[1], inner, planar, ix_table, iy_table)


def gradient_kernel(gathered, first, second, out):
    step = pl.program_id(0)
    samples, rows, lines = gathered.shape
    quarter = rows // 6
    depth = out.shape[0] // (2 * quarter)
    real_part = lax.axis_index("dp") < lax.axis_size("dp") // 2
    lane = lax.broadcasted_iota(jnp.int32, (1, lines), 1)
    duals = []
    for s in range(samples):
        for h in range(2):
            at = (2 * h + 2) * quarter
            real = gathered[s, at : at + quarter]
            imag = gathered[s, at + quarter : at + 2 * quarter]
            duals.append(jnp.where(real_part, real, imag))
            duals.append(jnp.where(real_part, imag, -real))
    duals = jnp.concatenate(duals, axis=0)
    for j in range(depth):
        mine = lane % (depth * pl.num_programs(0)) == depth * step + j
        spectra = []
        for s in range(samples):
            for h in range(2):
                here = mine & (lane // (lines // 2) == h)
                spectra.append(jnp.where(here, gathered[s, : 2 * quarter], 0))
        spectra = jnp.concatenate(spectra, axis=0)
        wide = dot(jnp.where(mine, duals, 0), second[...])
        for column in range(0, out.shape[1], 256):
            product = dot(spectra, first[:, column : column + 256])
            for at in range(0, 256, 128):
                for h in range(2):
                    total = 0.0
                    for s in range(samples):
                        for part in range(2):
                            row = (4 * s + 2 * h + part) * quarter
                            here = slice(row, row + quarter)
                            total = total + product[here, at : at + 128] * wide[here]
                    row = (2 * j + h) * quarter
                    there = slice(column + at, column + at + 128)
                    out[row : row + quarter, there] = total * (1.0 / samples)


def weight_gradient(gathered, depth, width):
    samples, rows, lines = gathered.shape
    channels = lines // depth
    first = np.repeat(np.eye(channels // 2), channels, axis=1)
    first = constant(np.tile(np.repeat(first, depth, axis=0), (2, 1)))
    second = constant(second_table(channels, depth)[:, :128])
    steps = 2
    half = rows // 3
    return pl.pallas_call(
        gradient_kernel,
        grid=(steps,),
        in_specs=[whole(gathered.shape), whole(first.shape), whole(second.shape)],
        out_specs=pl.BlockSpec((depth // steps * half, width), lambda j: (j, 0)),
        out_shape=jax.ShapeDtypeStruct((depth * half, width), jnp.float32),
        compiler_params=params(),
        cost_estimate=LIGHT,
        name="weight_gradient",
    )(gathered, first, second)


def exchange(first, last):
    size = lax.axis_size("slab")
    up = [(i, i + 1) for i in range(size - 1)]
    down = [(j, i) for i, j in up]
    return lax.ppermute(last, "slab", up), lax.ppermute(first, "slab", down)


def swap(planar):
    return lax.all_to_all(planar, "slab", split_axis=0, concat_axis=0)


def local_fast(feats, grains, spec_weight, taps, point_weight, bias, cotangent):
    slabs = lax.axis_size("slab")
    copies = lax.axis_size("dp")
    barrier = lax.optimization_barrier
    field = feats[0]
    channels = field.shape[0]
    cell_scale = 1.0 / math.sqrt(NX * NY * NZ)
    mode_scale = 1.0 / math.sqrt(KX * KY * KZ)
    mode_rows = spec_weight.shape[0]
    weight = spec_weight.reshape(mode_rows * KZ, 2 * channels * channels)
    width = weight.shape[1] // copies

    first, first_high, last, last_high = cut_rims(field)
    rims = exchange(first, last)
    planar = swap(forward_modes(field, slabs))
    rims, first, last = barrier((rims, first_high, last_high))
    rims_high = exchange(first, last)
    planar, smooth = barrier((planar, smooth_planes(field, rims, taps)))
    spectrum, planar = mix(planar, weight, cell_scale, 0.5 * mode_scale)
    smooth, spectrum = barrier((smooth, spectrum))
    planar = swap(planar)
    smooth = smooth_planes(field, rims_high, taps, smooth)
    spread, planar, first, last = layer(planar, smooth, cotangent[0], grains[0], bias, point_weight)
    rims = exchange(first, last)
    planar, send = mix(swap(planar), weight, 0.5 * mode_scale, cell_scale, spectrum, copies)
    send, spread = barrier((send, spread))
    inner = near_inner(spread, taps)
    gathered = lax.all_to_all(send, "dp", split_axis=0, concat_axis=0)
    planar, gathered, inner, rims = barrier((planar, gathered, inner, rims))
    planar = swap(planar)
    grad_spec = weight_gradient(gathered, KX // slabs, width)
    planar, grad_spec = barrier((planar, grad_spec))
    grad_feats = finish(planar, spread, rims, inner, taps)[None]
    return (grad_feats, grad_spec.reshape(mode_rows, KZ, width))


def local(feats, grains, spec_weight, taps, point_weight, bias, cotangent):
    samples, channels, planes = feats.shape[:3]
    width = spec_weight.shape[2] // lax.axis_size("dp")
    fits = (
        lax.axis_size("slab") * 4 == KX
        and samples == 1
        and channels == 32
        and planes == 8
        and channels * channels == 2 * width
    )
    form = local_fast if fits else local_any
    return form(feats, grains, spec_weight, taps, point_weight, bias, cotangent)


def solution(mesh):
    in_specs = (
        P(("grp", "dp"), None, "slab", None, None),
        P(("grp", "dp"), "slab", None, None),
        P("slab", None, None),
        P(),
        P(),
        P(),
        P(("grp", "dp"), None, "slab", None, None),
    )
    out_specs = (P(("grp", "dp"), None, "slab", None, None), P("slab", "grp", "dp"))
    return jax.shard_map(local, mesh=mesh, in_specs=in_specs, out_specs=out_specs, check_vma=False)
```

```python
import functools
import math

import jax
import jax.numpy as jnp
import ml_dtypes
import numpy as np
from jax import lax
from jax.experimental import pallas as pl
from jax.experimental.pallas import tpu as pltpu
from jax.sharding import PartitionSpec as P

NX = 128
NY = 128
NZ = 32
KX = 16
KY = 16
KZ = 16


HIGHEST = lax.Precision.HIGHEST


def extended(shard, sides, width):
    for axis, dim in sides:
        size, length = (lax.axis_size(axis), shard.shape[dim])
        up = [(i, (i + 1) % size) for i in range(size - 1)]
        down = [(j, i) for i, j in up]
        last = lax.slice_in_dim(shard, length - width, length, axis=dim)
        first = lax.slice_in_dim(shard, 0, width, axis=dim)
        before = lax.ppermute(last, axis, up)
        after = lax.ppermute(first, axis, down)
        shard = jnp.concatenate([before, shard, after], axis=dim)
    return shard


def tables(count, length, span):
    indices = jnp.arange(count, dtype=jnp.int32)
    frequency = jnp.where(indices < count // 2, indices, length - count + indices)
    position = jnp.arange(span, dtype=jnp.int32)
    phases = frequency[:, None] * position[None, :] % length
    angles = phases.astype(jnp.float32) * (2.0 * math.pi / length)
    return (jnp.cos(angles), jnp.sin(angles))


def mobility(grains):
    leading = [(0, 0)] * (grains.ndim - 2)
    along_x = (grains[..., 1:, :] != grains[..., :-1, :]).astype(jnp.float32)
    along_y = (grains[..., :, 1:] != grains[..., :, :-1]).astype(jnp.float32)
    differ = jnp.pad(along_x, leading + [(1, 0), (0, 0)]) + jnp.pad(
        along_x, leading + [(0, 1), (0, 0)]
    )
    differ = (
        differ
        + jnp.pad(along_y, leading + [(0, 0), (1, 0)])
        + jnp.pad(along_y, leading + [(0, 0), (0, 1)])
    )
    return 0.25 * (1.0 + differ)


def stencil(padded, taps, adjoint):
    planes = padded.shape[-3] - 2
    rows_x = padded.shape[-2] - 2
    rows_y = padded.shape[-1] - 2
    total = jnp.zeros(padded.shape[:-3] + (planes, rows_x, rows_y), jnp.float32)
    for offset in range(27):
        shift_z, shift_x, shift_y = (offset // 9, offset // 3 % 3, offset % 3)
        if adjoint:
            shift_z, shift_x, shift_y = (2 - shift_z, 2 - shift_x, 2 - shift_y)
        window = padded[
            ..., shift_z : shift_z + planes, shift_x : shift_x + rows_x, shift_y : shift_y + rows_y
        ]
        total = total + taps[offset][:, None, None, None] * window.astype(jnp.float32)
    return total


def plane_forward(field, cos_x, sin_x, cos_y, sin_y):
    real_y = jnp.einsum("...xy,ky->...xk", field, cos_y, precision=HIGHEST)
    imag_y = -jnp.einsum("...xy,ky->...xk", field, sin_y, precision=HIGHEST)
    real_part = jnp.einsum("...xk,jx->...jk", real_y, cos_x, precision=HIGHEST) + jnp.einsum(
        "...xk,jx->...jk", imag_y, sin_x, precision=HIGHEST
    )
    imag_part = jnp.einsum("...xk,jx->...jk", imag_y, cos_x, precision=HIGHEST) - jnp.einsum(
        "...xk,jx->...jk", real_y, sin_x, precision=HIGHEST
    )
    return (real_part, imag_part)


def plane_inverse(real_part, imag_part, cos_x, sin_x, cos_y, sin_y):
    real_x = jnp.einsum("...jk,jx->...xk", real_part, cos_x, precision=HIGHEST) - jnp.einsum(
        "...jk,jx->...xk", imag_part, sin_x, precision=HIGHEST
    )
    imag_x = jnp.einsum("...jk,jx->...xk", imag_part, cos_x, precision=HIGHEST) + jnp.einsum(
        "...jk,jx->...xk", real_part, sin_x, precision=HIGHEST
    )
    return jnp.einsum("...xk,ky->...xy", real_x, cos_y, precision=HIGHEST) - jnp.einsum(
        "...xk,ky->...xy", imag_x, sin_y, precision=HIGHEST
    )


def depth_forward(packed, cos_table, sin_table):
    width = packed.shape[-1] // 2
    real_in = packed[..., :width]
    imag_in = packed[..., width:]
    real_out = jnp.einsum("pszc,kz->pskc", real_in, cos_table, precision=HIGHEST) + jnp.einsum(
        "pszc,kz->pskc", imag_in, sin_table, precision=HIGHEST
    )
    imag_out = jnp.einsum("pszc,kz->pskc", imag_in, cos_table, precision=HIGHEST) - jnp.einsum(
        "pszc,kz->pskc", real_in, sin_table, precision=HIGHEST
    )
    return jnp.concatenate([real_out, imag_out], axis=-1)


def depth_inverse(real_modes, imag_modes, cos_table, sin_table):
    real_out = jnp.einsum("pskc,kz->pszc", real_modes, cos_table, precision=HIGHEST) - jnp.einsum(
        "pskc,kz->pszc", imag_modes, sin_table, precision=HIGHEST
    )
    imag_out = jnp.einsum("pskc,kz->pszc", imag_modes, cos_table, precision=HIGHEST) + jnp.einsum(
        "pskc,kz->pszc", real_modes, sin_table, precision=HIGHEST
    )
    return jnp.concatenate([real_out, imag_out], axis=-1)


def rim_planes(field):
    return extended(field, (("slab", 2),), 1)


def local_any(feats, grains, spec_weight, taps, point_weight, bias, cotangent):
    samples_here = feats.shape[0]
    channels = feats.shape[1]
    planes = feats.shape[2]
    cos_x, sin_x = tables(KX, NX, NX)
    cos_y, sin_y = tables(KY, NY, NY)
    cos_full, sin_full = tables(KZ, NZ, NZ)
    cell_scale = math.sqrt(NX * NY * NZ)
    mode_scale = math.sqrt(KX * KY * KZ)
    mode_rows = spec_weight.shape[0]
    weights = spec_weight.astype(jnp.float32).reshape(mode_rows, KZ, 2, channels, channels)
    w_real = weights[:, :, 0]
    w_imag = weights[:, :, 1]
    moving = mobility(grains)[:, None]

    def to_modes(field):
        real_plane, imag_plane = plane_forward(field, cos_x, sin_x, cos_y, sin_y)
        packed = jnp.stack([real_plane, imag_plane], axis=1)
        packed = packed.transpose(4, 5, 0, 3, 1, 2).reshape(
            KX * KY, samples_here, planes, 2 * channels
        )
        moved = lax.all_to_all(packed, "slab", split_axis=0, concat_axis=2, tiled=True)
        summed = depth_forward(moved, cos_full, sin_full)
        return (summed[..., :channels], summed[..., channels:])

    def from_modes(real_modes, imag_modes):
        planar = depth_inverse(real_modes, imag_modes, cos_full, sin_full)
        packed = lax.all_to_all(planar, "slab", split_axis=2, concat_axis=0, tiled=True)
        grouped = packed.reshape(KX, KY, samples_here, planes, 2, channels).transpose(
            2, 4, 5, 3, 0, 1
        )
        return plane_inverse(grouped[:, 0], grouped[:, 1], cos_x, sin_x, cos_y, sin_y)

    zero_rim = ((0, 0), (0, 0), (0, 0), (1, 1), (1, 1))
    padded = jnp.pad(rim_planes(feats), zero_rim)
    smooth = stencil(padded, taps, False).astype(jnp.bfloat16)
    local_part = moving * jnp.einsum(
        "sczxy,co->sozxy", smooth, point_weight, preferred_element_type=jnp.float32
    )
    spec_real, spec_imag = to_modes(feats.astype(jnp.float32))
    spec_real = spec_real / cell_scale
    spec_imag = spec_imag / cell_scale
    mixed_real = jnp.einsum("pskc,pkco->psko", spec_real, w_real, precision=HIGHEST) - jnp.einsum(
        "pskc,pkco->psko", spec_imag, w_imag, precision=HIGHEST
    )
    mixed_imag = jnp.einsum("pskc,pkco->psko", spec_real, w_imag, precision=HIGHEST) + jnp.einsum(
        "pskc,pkco->psko", spec_imag, w_real, precision=HIGHEST
    )
    spectral = from_modes(mixed_real, mixed_imag) / mode_scale
    pre = spectral + local_part + bias[None, :, None, None, None]
    gate = jax.nn.sigmoid(pre)
    delta = (cotangent.astype(jnp.float32) * gate * (1.0 + pre * (1.0 - gate))).astype(jnp.bfloat16)
    dual_real, dual_imag = to_modes(delta.astype(jnp.float32))
    dual_real = dual_real / mode_scale
    dual_imag = dual_imag / mode_scale
    batch_total = samples_here * lax.axis_size("dp")
    grad_real = jnp.einsum("pskc,psko->pkco", spec_real, dual_real, precision=HIGHEST) + jnp.einsum(
        "pskc,psko->pkco", spec_imag, dual_imag, precision=HIGHEST
    )
    grad_imag = jnp.einsum("pskc,psko->pkco", spec_real, dual_imag, precision=HIGHEST) - jnp.einsum(
        "pskc,psko->pkco", spec_imag, dual_real, precision=HIGHEST
    )
    grad_terms = (jnp.stack([grad_real, grad_imag], axis=2) / batch_total).reshape(
        mode_rows, KZ, 2 * channels * channels
    )
    grad_spec = lax.psum_scatter(
        grad_terms.astype(jnp.bfloat16), "dp", scatter_dimension=2, tiled=True
    ).astype(jnp.float32)
    back_real = jnp.einsum("psko,pkco->pskc", dual_real, w_real, precision=HIGHEST) + jnp.einsum(
        "psko,pkco->pskc", dual_imag, w_imag, precision=HIGHEST
    )
    back_imag = jnp.einsum("psko,pkco->pskc", dual_imag, w_real, precision=HIGHEST) - jnp.einsum(
        "psko,pkco->pskc", dual_real, w_imag, precision=HIGHEST
    )
    spectral_back = from_modes(back_real, back_imag) / cell_scale
    spread = (
        moving
        * jnp.einsum("sozxy,co->sczxy", delta, point_weight, preferred_element_type=jnp.float32)
    ).astype(jnp.bfloat16)
    spread_padded = jnp.pad(rim_planes(spread), zero_rim)
    local_back = stencil(spread_padded, taps, True)
    grad_feats = (spectral_back + local_back).astype(jnp.bfloat16)
    return (grad_feats, grad_spec)


def frequencies(count, length):
    index = np.arange(count)
    return np.where(index < count // 2, index, length - count + index)


def angles(count, length):
    phases = np.outer(frequencies(count, length), np.arange(length)) % length
    return phases * (2.0 * np.pi / length)


def constant(array):
    return jnp.asarray(np.asarray(array, np.float32).astype(ml_dtypes.bfloat16))


def forward_x_table(slabs, split):
    a = angles(KX, NX).reshape(slabs, KX // slabs, NX)
    trig = np.stack([np.cos(a), np.sin(a)])
    table = np.einsum("tsjx,cd->tscjdx", trig, np.eye(2)).reshape(-1, 2, NX // 8, 8)
    if split:
        table = table.transpose(0, 2, 1, 3)
    return table.reshape(4 * KX, 2 * NX)


def halved(table, planes):
    table = table.reshape(-1, planes * 2, 2, KY // 2).transpose(0, 2, 1, 3)
    return table.reshape(-1, planes * 2 * KY)


def forward_y_table(planes):
    a = angles(KY, NY)
    cos, sin = np.cos(a).T, np.sin(a).T
    block = np.stack([np.stack([cos, -sin], 1), np.stack([-sin, -cos], 1)])
    pick = np.eye(planes).reshape(planes // 2, 2, planes)
    table = np.einsum("pqz,tyrk->ptqyzrk", pick, block)
    return halved(table.reshape(planes * 2 * NY, planes * 2 * KY), planes)


def forward_z_table():
    a = angles(KZ, NZ)
    cos, sin = np.cos(a).T, np.sin(a).T
    block = np.stack([np.stack([cos, -sin], 1), np.stack([sin, cos], 1)], 1)
    table = np.einsum("zrqm,kl->zrkqlm", block, np.eye(KY // 2))
    return table.reshape(NZ * KY, KY * KZ)


def inverse_z_table():
    a = angles(KZ, NZ)
    cos, sin = np.cos(a), np.sin(a)
    block = np.stack([np.stack([cos, sin], 2), np.stack([-sin, cos], 2)])
    table = np.einsum("rmzq,kl->rkmzql", block, np.eye(KY // 2))
    return table.reshape(KY * KZ, NZ * KY)


def inverse_y_table(planes, group):
    a = angles(KY, NY)
    cos, sin = np.cos(a), np.sin(a)
    block = np.stack([np.stack([cos, -sin], 1), np.stack([-sin, -cos], 1)])
    pick = np.eye(planes).reshape(planes // group, group, planes)
    table = np.einsum("pqz,rkty->ptqyzrk", pick, block)
    table = halved(table.reshape(-1, planes * 2 * KY), planes)
    return table.reshape(planes // group, 2 * group * NY, planes * 2 * KY).transpose(0, 2, 1)


def inverse_x_table(slabs, group):
    a = angles(KX, NX).reshape(slabs, KX // slabs, NX)
    trig = np.stack([np.cos(a), np.sin(a)])
    table = np.einsum("tsjx,cd->cxstdj", trig, np.eye(group))
    return table.reshape(group * NX, 2 * KX * group)


def first_table(channels, depth):
    table = np.einsum("ac,j,b->ajcb", np.eye(channels), np.ones(depth), np.ones(channels))
    return table.reshape(channels * depth, channels * channels)


def second_table(channels, depth):
    table = np.einsum("ac,j,b->ajbc", np.eye(channels), np.ones(depth), np.ones(channels))
    return table.reshape(channels * depth, channels * channels)


LIGHT = pl.CostEstimate(flops=10**7, bytes_accessed=10**5, transcendentals=0)
HEAVY = pl.CostEstimate(flops=10**11, bytes_accessed=10**8, transcendentals=0)


def dot(a, b):
    return jnp.dot(a, b, preferred_element_type=jnp.float32)


def whole(shape):
    return pl.BlockSpec(shape, lambda *_: (0,) * len(shape))


def params(limit=63438848):
    return pltpu.CompilerParams(vmem_limit_bytes=limit)


ROOMY = 48 * 2**20


def store_rows(rows, pair, x_table, load):
    slabs, lines = rows.shape[2:4]
    for i in range(lines // 16):
        parts = [dot(x_table[...], load(2 * i + k)) for k in range(2)]
        for t in range(2):
            for s in range(slabs):
                here = slice(8 * (t * slabs + s), 8 * (t * slabs + s) + 8)
                both = jnp.concatenate([part[here] for part in parts], axis=0)
                rows[pair, t, s, 16 * i : 16 * i + 16, :] = both.astype(jnp.bfloat16)


def store_modes(rows, y_table, out):
    pairs, _, slabs, lines, _ = rows.shape
    left = [
        jnp.concatenate([rows[p, t, s] for p in range(pairs) for t in range(2)], axis=1)
        for s in range(slabs)
    ]
    modes = dot(jnp.concatenate(left, axis=0), y_table[...])
    for s in range(slabs):
        out[s] = modes[s * lines : (s + 1) * lines].astype(jnp.bfloat16)


def low_channels(channels):
    return 3 * channels // 8


def rims_kernel(field, *refs):
    rims, held, got, put = refs[:4], refs[4:8], refs[8], refs[9]
    last = field.shape[1] - 1
    loads, stores = [], []
    for k in range(4):
        count = rims[k].shape[0]
        source = field.at[pl.ds((k % 2) * rims[0].shape[0], count), pl.ds(last * (k // 2), 1)]
        loads.append(pltpu.make_async_copy(source, held[k], got.at[k]))
        stores.append(pltpu.make_async_copy(held[k], rims[k], put.at[k]))
    for load in loads:
        load.start()
    for load, store in zip(loads, stores):
        load.wait()
        store.start()
    for store in stores:
        store.wait()


def cut_rims(field):
    channels = field.shape[0]
    low = low_channels(channels)
    rims = [
        jax.ShapeDtypeStruct((count, 1, NX, NY), jnp.bfloat16) for count in (low, channels - low) * 2
    ]
    return pl.pallas_call(
        rims_kernel,
        in_specs=[pl.BlockSpec(memory_space=pl.ANY)],
        out_specs=[pl.BlockSpec(memory_space=pl.ANY)] * 4,
        out_shape=rims,
        scratch_shapes=[
            *(pltpu.VMEM(rim.shape, jnp.bfloat16) for rim in rims),
            pltpu.SemaphoreType.DMA((4,)),
            pltpu.SemaphoreType.DMA((4,)),
        ],
        compiler_params=params(),
        cost_estimate=LIGHT,
        name="rims",
    )(field)


def forward_kernel(field, x_table, y_table, out, rows):
    pair = pl.program_id(0)
    pairs = rows.shape[0]

    def load(i):
        halves = [field[2 * i : 2 * i + 2, q].reshape(2 * NX, NY) for q in range(2)]
        return jnp.concatenate(halves, axis=1)

    store_rows(rows, pair, x_table, load)

    @pl.when(pair == pairs - 1)
    def _():
        store_modes(rows, y_table, out)


def forward_modes(field, slabs):
    channels, planes = field.shape[:2]
    lines = channels * (KX // slabs)
    x_table = constant(forward_x_table(slabs, False))
    y_table = constant(forward_y_table(planes))
    shape = (slabs, lines, planes * 2 * KY)
    return pl.pallas_call(
        forward_kernel,
        grid=(planes // 2,),
        in_specs=[
            pl.BlockSpec((channels, 2, NX, NY), lambda p: (0, p, 0, 0)),
            whole(x_table.shape),
            whole(y_table.shape),
        ],
        out_specs=whole(shape),
        out_shape=jax.ShapeDtypeStruct(shape, jnp.bfloat16),
        scratch_shapes=[pltpu.VMEM((planes // 2, 2, slabs, lines, 2 * NY), jnp.bfloat16)],
        compiler_params=params(),
        cost_estimate=LIGHT,
        name="forward_modes",
    )(field, x_table, y_table)


def mixing_kernel(scale_in, scale_out, adjoint, planar, weight, z_in, z_out, spread_table,
                  sum_table, *rest):
    if adjoint:
        partner, out, send, spectrum, total, wide, product = rest
    else:
        spectrum, out, total, wide, product = rest
    step = pl.program_id(0)
    steps = pl.num_programs(0)
    slabs, lines, width = planar.shape
    half = width // 2
    quarter = spectrum.shape[0] // 4
    lanes = weight.shape[1] // 2
    depth = weight.shape[0] // (2 * quarter)

    @pl.when(step == 0)
    def _():
        left = [
            jnp.concatenate([planar[s, :, h : h + half] for s in range(slabs)], axis=1)
            for h in (0, half)
        ]
        modes = dot(jnp.concatenate(left, axis=0), z_in[...]) * scale_in
        for h in range(2):
            here = modes[h * lines : (h + 1) * lines].T.astype(jnp.bfloat16)
            spectrum[2 * h * quarter : 2 * (h + 1) * quarter] = here
            if adjoint:
                for d in range(send.shape[0]):
                    send[d, 2 * (h + 1) * quarter : 2 * (h + 2) * quarter] = here
        if adjoint:
            rows = [partner[2 * h * quarter : 2 * (h + 1) * quarter] for h in range(2)]
            rows = [row.astype(jnp.float32) for row in rows]
            left = lax.broadcasted_iota(jnp.int32, (1, lines), 1) < lines // 2
            turned = [pltpu.roll(row, lines // 2, axis=1) for row in rows]
            packed = [jnp.where(left, rows[0], turned[1]), jnp.where(left, turned[0], rows[1])]
            for d in range(send.shape[0]):
                send[d, : 2 * quarter] = packed[d % 2].astype(jnp.bfloat16)
        total[...] = jnp.zeros_like(total)

    lane = lax.broadcasted_iota(jnp.int32, (1, lines), 1) % (depth * steps)
    block = 32
    tile = wide.shape[1]
    for j in range(depth):
        mine = lane == depth * step + j
        wide[...] = dot(jnp.where(mine, spectrum[...], 0), spread_table[...])
        for at in range(0, 2 * quarter, block):
            row = 2 * j * quarter + at
            real_at = at + (at // quarter) * quarter
            imag_at = real_at + quarter
            sums = [0.0, 0.0]
            for column in range(0, lanes, 128):
                here = slice(column, column + 128) if tile == lanes else slice(None)
                real_wide = wide[real_at : real_at + block, here]
                imag_wide = wide[imag_at : imag_at + block, here]
                w_real = weight[row : row + block, column : column + 128]
                w_imag = weight[row : row + block, lanes + column : lanes + column + 128]
                w_real = w_real.astype(jnp.float32)
                w_imag = w_imag.astype(jnp.float32)
                if adjoint:
                    real = real_wide * w_real + imag_wide * w_imag
                    imag = imag_wide * w_real - real_wide * w_imag
                    there = slice(column, column + 128)
                    product[real_at : real_at + block, there] = real.astype(jnp.bfloat16)
                    product[imag_at : imag_at + block, there] = imag.astype(jnp.bfloat16)
                else:
                    sums[0] = sums[0] + (real_wide * w_real - imag_wide * w_imag)
                    sums[1] = sums[1] + (real_wide * w_imag + imag_wide * w_real)
            if not adjoint:
                product[real_at : real_at + block] = sums[0].astype(jnp.bfloat16)
                product[imag_at : imag_at + block] = sums[1].astype(jnp.bfloat16)
        total[...] += jnp.where(mine, dot(product[...], sum_table[...]), 0.0)

    @pl.when(step == steps - 1)
    def _():
        modes = total[...] * scale_out
        left = [modes[2 * h * quarter : 2 * (h + 1) * quarter].T for h in range(2)]
        modes = dot(jnp.concatenate(left, axis=0).astype(jnp.bfloat16), z_out[...])
        for s in range(slabs):
            for h in range(2):
                here = modes[h * lines : (h + 1) * lines, s * half : (s + 1) * half]
                out[s, :, h * half : (h + 1) * half] = here.astype(jnp.bfloat16)


def mix(planar, weight, scale_in, scale_out, partner=None, copies=0):
    slabs, lines, width = planar.shape
    adjoint = partner is not None
    depth = KX // slabs
    channels = lines // depth
    rows = KY * KZ
    steps = 2
    z_in = constant(forward_z_table())
    z_out = constant(inverse_z_table())
    first = first_table(channels, depth)
    second = second_table(channels, depth)
    spread_table = constant(second[:, :128] if adjoint else first)
    sum_table = constant(first.T if adjoint else second[:, :128].T)
    shape = (2 * rows, lines)
    in_specs = [
        whole(planar.shape),
        pl.BlockSpec((depth // steps * rows, weight.shape[1]), lambda j: (j, 0)),
        whole(z_in.shape),
        whole(z_out.shape),
        whole(spread_table.shape),
        whole(sum_table.shape),
    ]
    operands = [planar, weight, z_in, z_out, spread_table, sum_table]
    scratch = [
        pltpu.VMEM(shape, jnp.float32),
        pltpu.VMEM((2 * rows, spread_table.shape[1]), jnp.float32),
        pltpu.VMEM((2 * rows, sum_table.shape[0]), jnp.bfloat16),
    ]
    if adjoint:
        in_specs.append(whole(shape))
        operands.append(partner)
        scratch = [pltpu.VMEM(shape, jnp.bfloat16)] + scratch
        outs = [planar.shape, (copies, 3 * rows, lines)]
    else:
        outs = [shape, planar.shape]
    return pl.pallas_call(
        functools.partial(mixing_kernel, scale_in, scale_out, adjoint),
        grid=(steps,),
        in_specs=in_specs,
        out_specs=[whole(out) for out in outs],
        out_shape=[jax.ShapeDtypeStruct(out, jnp.bfloat16) for out in outs],
        scratch_shapes=scratch,
        compiler_params=params(ROOMY),
        cost_estimate=HEAVY,
        name="mix_back" if adjoint else "mix",
    )(*operands)


def plane_mobility(grains):
    same = [
        jnp.concatenate([grains[:1], grains[:-1]], axis=0),
        jnp.concatenate([grains[1:], grains[-1:]], axis=0),
        jnp.concatenate([grains[:, :1], grains[:, :-1]], axis=1),
        jnp.concatenate([grains[:, 1:], grains[:, -1:]], axis=1),
    ]
    total = jnp.full(grains.shape, 0.25, jnp.float32)
    for other in same:
        total = total + jnp.where(grains != other, 0.25, 0.0)
    return total


def layer_kernel(bias, planar, smooth, cotangent, grains, point_weight, repeat, ix_table, iy_table,
                 x_table, y_table, spread, out, first, last, *rest):
    pair = pl.program_id(0)
    waves, spectral, moving, delta, rows, bias_wide, mix_out, mix_in = rest
    pairs = rows.shape[0]
    channels = cotangent.shape[0]
    slabs = planar.shape[0]

    @pl.when(pair == 0)
    def _():
        for c in range(channels):
            bias_wide[c] = jnp.full(bias_wide.shape[1:], 0.5 * bias[c], jnp.float32)
        tall = dot(repeat[...], point_weight[...]).astype(jnp.bfloat16)
        square = lax.dot_general(
            tall, repeat[...], (((1,), (1,)), ((), ())), preferred_element_type=jnp.float32
        )
        row = lax.broadcasted_iota(jnp.int32, square.shape, 0) % 8
        column = lax.broadcasted_iota(jnp.int32, square.shape, 1) % 8
        square = jnp.where(row == column, square, 0.0)
        mix_in[...] = square.astype(jnp.bfloat16)
        mix_out[...] = square.T.astype(jnp.bfloat16)

    lines = planar.shape[1]
    step = jnp.concatenate([planar[s] for s in range(slabs)], axis=0)
    step = dot(step, iy_table[0]).astype(jnp.bfloat16)
    for s in range(slabs):
        for t in range(2):
            waves[s, t] = step[s * lines : (s + 1) * lines, 2 * NY * t : 2 * NY * (t + 1)]
    group = 8 * (KX // slabs)
    for g in range(channels // 8):
        here = slice(g * group, (g + 1) * group)
        wave = [waves[s, t, here, :] for s in range(slabs) for t in range(2)]
        step = dot(ix_table[...], jnp.concatenate(wave, axis=0))
        spectral[8 * g : 8 * g + 8] = step.reshape(8, NX, 2 * NY)
    for q in range(2):
        moving[:, q * NY : (q + 1) * NY] = 0.5 * plane_mobility(grains[q])

    def body(i, _):
        x = pl.multiple_of(16 * i, 16)
        halves = [cotangent[:, q, pl.ds(x, 16), :] for q in range(2)]
        cotangent_here = jnp.concatenate(halves, axis=2).astype(jnp.float32)
        spreads = []
        for h in range(2):
            at = pl.ds(pl.multiple_of(x + 8 * h, 8), 8)
            mobile = moving[at, :][None]
            local = dot(mix_out[...], smooth[0, 2 * i + h]).reshape(channels, 8, 2 * NY)
            half = spectral[:, at, :] + mobile * local + bias_wide[...]
            wave = jnp.tanh(half)
            slope = (1.0 + wave) * (1.0 + (half - half * wave))
            change = cotangent_here[:, 8 * h : 8 * h + 8, :] * slope
            right = change.reshape(8 * channels, 2 * NY).astype(jnp.bfloat16)
            delta[2 * i + h] = right
            back = dot(mix_in[...], right).reshape(channels, 8, 2 * NY)
            spreads.append(mobile * back)
        both = jnp.concatenate(spreads, axis=1).astype(jnp.bfloat16)
        for q in range(2):
            spread[:, q, pl.ds(x, 16), :] = both[:, :, q * NY : (q + 1) * NY]
        return 0

    lax.fori_loop(0, NX // 16, body, 0, unroll=8)


    @pl.when(pair == 0)
    def _():
        first[:, 0] = spread[:, 0]

    @pl.when(pair == pairs - 1)
    def _():
        last[:, 0] = spread[:, 1]

    def load(i):
        return delta[:, 16 * i : 16 * i + 16, :].reshape(2 * NX, 2 * NY)

    store_rows(rows, pair, x_table, load)

    @pl.when(pair == pairs - 1)
    def _():
        store_modes(rows, y_table, out)


def layer(planar, smooth, cotangent, grains, bias, point_weight):
    slabs, lines, width = planar.shape
    channels, planes = cotangent.shape[:2]
    pairs = planes // 2
    repeat = constant(np.repeat(np.eye(channels), 8, axis=0))
    ix_table = constant(inverse_x_table(slabs, 8))
    iy_table = constant(inverse_y_table(planes, 2))
    x_table = constant(forward_x_table(slabs, True))
    y_table = constant(forward_y_table(planes))
    field = pl.BlockSpec((channels, 2, NX, NY), lambda p: (0, p, 0, 0))
    outs = [cotangent.shape, planar.shape] + [(channels, 1, NX, NY)] * 2
    return pl.pallas_call(
        layer_kernel,
        grid=(pairs,),
        in_specs=[
            pl.BlockSpec(memory_space=pltpu.SMEM),
            whole(planar.shape),
            pl.BlockSpec((1,) + smooth.shape[1:], lambda p: (p, 0, 0, 0)),
            field,
            pl.BlockSpec((2, NX, NY), lambda p: (p, 0, 0)),
            whole(point_weight.shape),
            whole(repeat.shape),
            whole(ix_table.shape),
            pl.BlockSpec((1,) + iy_table.shape[1:], lambda p: (p, 0, 0)),
            whole(x_table.shape),
            whole(y_table.shape),
        ],
        out_specs=[field] + [whole(out) for out in outs[1:]],
        out_shape=[jax.ShapeDtypeStruct(out, jnp.bfloat16) for out in outs],
        scratch_shapes=[
            pltpu.VMEM((slabs, 2, lines, 2 * NY), jnp.bfloat16),
            pltpu.VMEM((channels, NX, 2 * NY), jnp.float32),
            pltpu.VMEM((NX, 2 * NY), jnp.float32),
            pltpu.VMEM((NX // 8, 8 * channels, 2 * NY), jnp.bfloat16),
            pltpu.VMEM((pairs, 2, slabs, lines, 2 * NY), jnp.bfloat16),
            pltpu.VMEM((channels, 8, 2 * NY), jnp.float32),
            pltpu.VMEM((8 * channels, 8 * channels), jnp.bfloat16),
            pltpu.VMEM((8 * channels, 8 * channels), jnp.bfloat16),
        ],
        compiler_params=params(),
        cost_estimate=LIGHT,
        name="layer",
    )(bias, planar, smooth, cotangent, grains, point_weight, repeat, ix_table, iy_table, x_table,
      y_table)


def build_tile(adjoint, taps, channel, dy, q, planes, span):
    row = lax.broadcasted_iota(jnp.int32, (8, 128), 0)
    lane = lax.broadcasted_iota(jnp.int32, (8, 128), 1)
    tile = jnp.zeros((8, 128), jnp.float32)
    for k, plane in enumerate(planes):
        dz = plane - q
        if not 0 <= dz <= 2:
            continue
        for dx in range(3):
            number = 9 * dz + 3 * dx + dy
            tap = taps[26 - number if adjoint else number, channel]
            tile = jnp.where(lane == (span * k + row + (dx - 1)) % 128, tap, tile)
    return tile


def build_band(adjoint, taps, channel, band, tail):
    row = lax.broadcasted_iota(jnp.int32, (8, 128), 0)
    lane = lax.broadcasted_iota(jnp.int32, (8, 128), 1)
    heads, middles, tails = [], [], []
    for dy in range(3):
        for q in range(2):
            sides = []
            for planes in ((0, 1), (2, 3)):
                tile = build_tile(adjoint, taps, channel, dy, q, planes, 64)
                tiles = [pltpu.roll(tile, 8 * k, axis=1) for k in range(1, 7)]
                first = jnp.where((row == 0) & (lane % 64 == 63), 0.0, tile)
                sides.append([first] + tiles)
            blocks = [jnp.concatenate(pair, axis=1) for pair in zip(*sides)]
            heads += blocks
            middles += blocks[1:]
            tile = build_tile(adjoint, taps, channel, dy, q, range(4), 32)
            tiles = [pltpu.roll(tile, 8 * k, axis=1) for k in range(1, 4)]
            tiles[2] = jnp.where((row == 7) & (lane % 32 == 0), 0.0, tiles[2])
            tails += tiles
    band[...] = jnp.concatenate(heads + middles, axis=0).astype(jnp.bfloat16)
    tail[...] = jnp.concatenate(tails, axis=0).astype(jnp.bfloat16)


def apply_band(quads, band):
    band, tail = band
    counts = (56, 48, 24)
    ends = (6 * counts[0], 6 * (counts[0] + counts[1]))
    lefts = (band[: ends[0], :], band[ends[0] : ends[1], :], tail[...])
    lane = lax.broadcasted_iota(jnp.int32, (NX, NY), 1)
    totals = []
    for group in range(0, len(quads), 2):
        products = []
        for left, x, span in zip(lefts, (0, 48, 96), (64, 64, 32)):
            right = [
                jnp.concatenate([sheet[x : x + span] for sheet in quads[group + p]], axis=0)
                for p in range(2)
            ]
            products.append(dot(left, jnp.concatenate(right, axis=1)))
        for p in range(2):
            wide = slice(NY * p, NY * (p + 1))
            pair = []
            for q in range(2):
                shifted = []
                for dy in range(3):
                    b = 2 * dy + q
                    pieces = [
                        product[count * b : count * (b + 1), wide]
                        for product, count in zip(products, counts)
                    ]
                    shifted.append(jnp.concatenate(pieces, axis=0))
                before = jnp.where(lane == 0, 0.0, pltpu.roll(shifted[0], 1, axis=1))
                after = jnp.where(lane == NY - 1, 0.0, pltpu.roll(shifted[2], NY - 1, axis=1))
                pair.append(shifted[1] + before + after)
            totals.append(jnp.concatenate(pair, axis=1))
    return totals


def banded(adjoint, taps, start, bands, channels):
    step = pl.program_id(0)
    final = start + channels * pl.num_programs(0) - 1

    @pl.when(step == 0)
    def _():
        build_band(adjoint, taps, start, *bands[0])

    def run(visit):
        for c in range(channels):
            following = jnp.minimum(start + channels * step + c + 1, final)
            build_band(adjoint, taps, following, *bands[(c + 1) % channels])
            visit(c, bands[c])

    return run


def band_scratch(channels):
    shapes = [(6 * (56 + 48), 256), (6 * 24, 128)]
    return [pltpu.VMEM(shape, jnp.bfloat16) for shape in shapes * channels]


def paired(refs):
    return list(zip(refs[0::2], refs[1::2]))


def smooth_kernel(start, taps, before, field, after, *rest):
    out, *bands = rest[-2 * field.shape[0] - 1 :]
    bands = paired(bands)
    planes = field.shape[1]
    totals = []

    def visit(c, band):
        sheets = [before[c, 0]] + [field[c, z] for z in range(planes)] + [after[c, 0]]
        totals.append(apply_band([sheets[z : z + 4] for z in range(0, planes, 2)], band))

        if c % 2 == 1:
            for p in range(planes // 2):
                both = [total[p].reshape(NX // 8, 8, 2 * NY) for total in totals[c - 1 : c + 1]]
                both = jnp.concatenate(both, axis=1).astype(jnp.bfloat16)
                out[p, :, 8 * (c - 1) : 8 * (c + 1), :] = both

    banded(False, taps, start, bands, field.shape[0])(visit)


def smooth_planes(field, rims, taps, done=None):
    channels, planes = field.shape[:2]
    pairs = planes // 2
    low = low_channels(channels)
    start = 0 if done is None else low
    count = low if done is None else channels - low
    step = 4
    skip = start // step
    rim = pl.BlockSpec((step, 1, NX, NY), lambda c: (c, 0, 0, 0))
    sheets = pl.BlockSpec((step, planes, NX, NY), lambda c: (c + skip, 0, 0, 0))
    in_specs = [pl.BlockSpec(memory_space=pltpu.SMEM), rim, sheets, rim]
    operands = [taps, rims[0], field, rims[1]]
    if done is not None:
        in_specs.append(pl.BlockSpec(memory_space=pl.ANY))
        operands.append(done)
    return pl.pallas_call(
        functools.partial(smooth_kernel, start),
        grid=(count // step,),
        in_specs=in_specs,
        out_specs=pl.BlockSpec((pairs, NX // 8, 8 * step, 2 * NY), lambda c: (0, 0, c + skip, 0)),
        out_shape=jax.ShapeDtypeStruct((pairs, NX // 8, 8 * channels, 2 * NY), jnp.bfloat16),
        input_output_aliases={} if done is None else {4: 0},
        scratch_shapes=band_scratch(step),
        compiler_params=params(ROOMY),
        cost_estimate=LIGHT,
        name="smooth_low" if done is None else "smooth_high",
    )(*operands)


def inner_kernel(taps, field, out, *bands):
    bands = paired(bands)
    planes = field.shape[1]

    def visit(c, band):
        quads = [[field[c, z + k] for k in range(4)] for z in range(1, planes - 3, 2)]
        for p, near in enumerate(apply_band(quads, band)):
            total = near.astype(jnp.bfloat16)
            out[c, 2 * p] = total[:, :NY]
            out[c, 2 * p + 1] = total[:, NY:]

    banded(True, taps, 0, bands, field.shape[0])(visit)


def near_inner(field, taps):
    channels, planes = field.shape[:2]
    step = 8
    shape = (channels, planes - 4, NX, NY)
    return pl.pallas_call(
        inner_kernel,
        grid=(channels // step,),
        in_specs=[
            pl.BlockSpec(memory_space=pltpu.SMEM),
            pl.BlockSpec((step, planes, NX, NY), lambda c: (c, 0, 0, 0)),
        ],
        out_specs=pl.BlockSpec((step,) + shape[1:], lambda c: (c, 0, 0, 0)),
        out_shape=jax.ShapeDtypeStruct(shape, jnp.bfloat16),
        scratch_shapes=band_scratch(step),
        compiler_params=params(ROOMY),
        cost_estimate=LIGHT,
        name="near_inner",
    )(taps, field)


def finish_kernel(taps, before, field, after, inner, planar, ix_table, iy_table, out, waves,
                  *bands):
    bands = paired(bands)
    step = pl.program_id(0)
    slabs, lines = planar.shape[:2]
    planes = field.shape[1]
    span = planes * NY

    @pl.when(step == 0)
    def _():
        left = jnp.concatenate([planar[s] for s in range(slabs)], axis=0)
        for t in range(2):
            wave = dot(left, iy_table[0, :, t * span : (t + 1) * span]).astype(jnp.bfloat16)
            for s in range(slabs):
                waves[s, t] = wave[s * lines : (s + 1) * lines]

    rows = field.shape[0] * (KX // slabs)
    here = pl.ds(pl.multiple_of(rows * step, rows), rows)
    right = [waves[s, t, here, :] for s in range(slabs) for t in range(2)]
    right = jnp.concatenate(right, axis=0)
    far = [
        dot(ix_table[...], right[:, 2 * p * NY : 2 * (p + 1) * NY]) for p in range(planes // 2)
    ]

    def store(c, p, near):
        for q in range(2):
            total = near[q] + far[p][c * NX : (c + 1) * NX, q * NY : (q + 1) * NY]
            out[c, 2 * p + q] = total.astype(jnp.bfloat16)

    def visit(c, band):
        low = [before[c, 0]] + [field[c, z] for z in range(3)]
        high = [field[c, z] for z in range(planes - 3, planes)] + [after[c, 0]]
        for p, near in zip((0, planes // 2 - 1), apply_band([low, high], band)):
            store(c, p, [near[:, :NY], near[:, NY:]])
        for p in range(1, planes // 2 - 1):
            store(c, p, [inner[c, 2 * p - 2 + q].astype(jnp.float32) for q in range(2)])

    banded(True, taps, 0, bands, field.shape[0])(visit)


def finish(planar, spread, rims, inner, taps):
    slabs, lines, width = planar.shape
    channels, planes = spread.shape[:2]
    step = 8
    ix_table = constant(inverse_x_table(slabs, step))
    iy_table = constant(inverse_y_table(planes, planes))
    rim = pl.BlockSpec((step, 1, NX, NY), lambda c: (c, 0, 0, 0))
    sheets = pl.BlockSpec((step, planes, NX, NY), lambda c: (c, 0, 0, 0))
    return pl.pallas_call(
        finish_kernel,
        grid=(channels // step,),
        in_specs=[
            pl.BlockSpec(memory_space=pltpu.SMEM),
            rim,
            sheets,
            rim,
            pl.BlockSpec((step,) + inner.shape[1:], lambda c: (c, 0, 0, 0)),
            whole(planar.shape),
            whole(ix_table.shape),
            whole(iy_table.shape),
        ],
        out_specs=sheets,
        out_shape=jax.ShapeDtypeStruct(spread.shape, jnp.bfloat16),
        scratch_shapes=[
            pltpu.VMEM((slabs, 2, lines, planes * NY), jnp.bfloat16),
            *band_scratch(step),
        ],
        compiler_params=params(),
        cost_estimate=HEAVY,
        name="finish",
    )(taps, rims[0], spread, rims[1], inner, planar, ix_table, iy_table)


def gradient_kernel(gathered, first, second, out):
    step = pl.program_id(0)
    samples, rows, lines = gathered.shape
    quarter = rows // 6
    depth = out.shape[0] // (2 * quarter)
    real_part = lax.axis_index("dp") < lax.axis_size("dp") // 2
    lane = lax.broadcasted_iota(jnp.int32, (1, lines), 1)
    duals = []
    for s in range(samples):
        for h in range(2):
            at = (2 * h + 2) * quarter
            real = gathered[s, at : at + quarter]
            imag = gathered[s, at + quarter : at + 2 * quarter]
            duals.append(jnp.where(real_part, real, imag))
            duals.append(jnp.where(real_part, imag, -real))
    duals = jnp.concatenate(duals, axis=0)
    for j in range(depth):
        mine = lane % (depth * pl.num_programs(0)) == depth * step + j
        spectra = []
        for s in range(samples):
            for h in range(2):
                here = mine & (lane // (lines // 2) == h)
                spectra.append(jnp.where(here, gathered[s, : 2 * quarter], 0))
        spectra = jnp.concatenate(spectra, axis=0)
        wide = dot(jnp.where(mine, duals, 0), second[...])
        for column in range(0, out.shape[1], 256):
            product = dot(spectra, first[:, column : column + 256])
            for at in range(0, 256, 128):
                for h in range(2):
                    total = 0.0
                    for s in range(samples):
                        for part in range(2):
                            row = (4 * s + 2 * h + part) * quarter
                            here = slice(row, row + quarter)
                            total = total + product[here, at : at + 128] * wide[here]
                    row = (2 * j + h) * quarter
                    there = slice(column + at, column + at + 128)
                    out[row : row + quarter, there] = total * (1.0 / samples)


def weight_gradient(gathered, depth, width):
    samples, rows, lines = gathered.shape
    channels = lines // depth
    first = np.repeat(np.eye(channels // 2), channels, axis=1)
    first = constant(np.tile(np.repeat(first, depth, axis=0), (2, 1)))
    second = constant(second_table(channels, depth)[:, :128])
    steps = 2
    half = rows // 3
    return pl.pallas_call(
        gradient_kernel,
        grid=(steps,),
        in_specs=[whole(gathered.shape), whole(first.shape), whole(second.shape)],
        out_specs=pl.BlockSpec((depth // steps * half, width), lambda j: (j, 0)),
        out_shape=jax.ShapeDtypeStruct((depth * half, width), jnp.float32),
        compiler_params=params(ROOMY),
        cost_estimate=LIGHT,
        name="weight_gradient",
    )(gathered, first, second)


def exchange(first, last):
    size = lax.axis_size("slab")
    up = [(i, i + 1) for i in range(size - 1)]
    down = [(j, i) for i, j in up]
    return lax.ppermute(last, "slab", up), lax.ppermute(first, "slab", down)


def swap(planar):
    return lax.all_to_all(planar, "slab", split_axis=0, concat_axis=0)


def local_fast(feats, grains, spec_weight, taps, point_weight, bias, cotangent):
    slabs = lax.axis_size("slab")
    copies = lax.axis_size("dp")
    barrier = lax.optimization_barrier
    field = feats[0]
    channels = field.shape[0]
    cell_scale = 1.0 / math.sqrt(NX * NY * NZ)
    mode_scale = 1.0 / math.sqrt(KX * KY * KZ)
    mode_rows = spec_weight.shape[0]
    weight = spec_weight.reshape(mode_rows * KZ, 2 * channels * channels)
    width = weight.shape[1] // copies

    first, first_high, last, last_high = cut_rims(field)
    rims = exchange(first, last)
    planar = swap(forward_modes(field, slabs))
    rims, first, last = barrier((rims, first_high, last_high))
    rims_high = exchange(first, last)
    planar, smooth = barrier((planar, smooth_planes(field, rims, taps)))
    spectrum, planar = mix(planar, weight, cell_scale, 0.5 * mode_scale)
    smooth, spectrum = barrier((smooth, spectrum))
    planar = swap(planar)
    smooth = smooth_planes(field, rims_high, taps, smooth)
    spread, planar, first, last = layer(planar, smooth, cotangent[0], grains[0], bias, point_weight)
    rims = exchange(first, last)
    planar, send = mix(swap(planar), weight, 0.5 * mode_scale, cell_scale, spectrum, copies)
    send, spread = barrier((send, spread))
    inner = near_inner(spread, taps)
    gathered = lax.all_to_all(send, "dp", split_axis=0, concat_axis=0)
    planar, gathered, inner, rims = barrier((planar, gathered, inner, rims))
    planar = swap(planar)
    grad_spec = weight_gradient(gathered, KX // slabs, width)
    planar, grad_spec = barrier((planar, grad_spec))
    grad_feats = finish(planar, spread, rims, inner, taps)[None]
    return (grad_feats, grad_spec.reshape(mode_rows, KZ, width))


def local(feats, grains, spec_weight, taps, point_weight, bias, cotangent):
    samples, channels, planes = feats.shape[:3]
    width = spec_weight.shape[2] // lax.axis_size("dp")
    fits = (
        lax.axis_size("slab") * 4 == KX
        and samples == 1
        and channels == 32
        and planes == 8
        and channels * channels == 2 * width
    )
    form = local_fast if fits else local_any
    return form(feats, grains, spec_weight, taps, point_weight, bias, cotangent)


def solution(mesh):
    in_specs = (
        P(("grp", "dp"), None, "slab", None, None),
        P(("grp", "dp"), "slab", None, None),
        P("slab", None, None),
        P(),
        P(),
        P(),
        P(("grp", "dp"), None, "slab", None, None),
    )
    out_specs = (P(("grp", "dp"), None, "slab", None, None), P("slab", "grp", "dp"))
    return jax.shard_map(local, mesh=mesh, in_specs=in_specs, out_specs=out_specs, check_vma=False)
```

```python
import functools
import math

import jax
import jax.numpy as jnp
import ml_dtypes
import numpy as np
from jax import lax
from jax.experimental import pallas as pl
from jax.experimental.pallas import tpu as pltpu
from jax.sharding import PartitionSpec as P

NX = 128
NY = 128
NZ = 32
KX = 16
KY = 16
KZ = 16


HIGHEST = lax.Precision.HIGHEST


def extended(shard, sides, width):
    for axis, dim in sides:
        size, length = (lax.axis_size(axis), shard.shape[dim])
        up = [(i, (i + 1) % size) for i in range(size - 1)]
        down = [(j, i) for i, j in up]
        last = lax.slice_in_dim(shard, length - width, length, axis=dim)
        first = lax.slice_in_dim(shard, 0, width, axis=dim)
        before = lax.ppermute(last, axis, up)
        after = lax.ppermute(first, axis, down)
        shard = jnp.concatenate([before, shard, after], axis=dim)
    return shard


def tables(count, length, span):
    indices = jnp.arange(count, dtype=jnp.int32)
    frequency = jnp.where(indices < count // 2, indices, length - count + indices)
    position = jnp.arange(span, dtype=jnp.int32)
    phases = frequency[:, None] * position[None, :] % length
    angles = phases.astype(jnp.float32) * (2.0 * math.pi / length)
    return (jnp.cos(angles), jnp.sin(angles))


def mobility(grains):
    leading = [(0, 0)] * (grains.ndim - 2)
    along_x = (grains[..., 1:, :] != grains[..., :-1, :]).astype(jnp.float32)
    along_y = (grains[..., :, 1:] != grains[..., :, :-1]).astype(jnp.float32)
    differ = jnp.pad(along_x, leading + [(1, 0), (0, 0)]) + jnp.pad(
        along_x, leading + [(0, 1), (0, 0)]
    )
    differ = (
        differ
        + jnp.pad(along_y, leading + [(0, 0), (1, 0)])
        + jnp.pad(along_y, leading + [(0, 0), (0, 1)])
    )
    return 0.25 * (1.0 + differ)


def stencil(padded, taps, adjoint):
    planes = padded.shape[-3] - 2
    rows_x = padded.shape[-2] - 2
    rows_y = padded.shape[-1] - 2
    total = jnp.zeros(padded.shape[:-3] + (planes, rows_x, rows_y), jnp.float32)
    for offset in range(27):
        shift_z, shift_x, shift_y = (offset // 9, offset // 3 % 3, offset % 3)
        if adjoint:
            shift_z, shift_x, shift_y = (2 - shift_z, 2 - shift_x, 2 - shift_y)
        window = padded[
            ..., shift_z : shift_z + planes, shift_x : shift_x + rows_x, shift_y : shift_y + rows_y
        ]
        total = total + taps[offset][:, None, None, None] * window.astype(jnp.float32)
    return total


def plane_forward(field, cos_x, sin_x, cos_y, sin_y):
    real_y = jnp.einsum("...xy,ky->...xk", field, cos_y, precision=HIGHEST)
    imag_y = -jnp.einsum("...xy,ky->...xk", field, sin_y, precision=HIGHEST)
    real_part = jnp.einsum("...xk,jx->...jk", real_y, cos_x, precision=HIGHEST) + jnp.einsum(
        "...xk,jx->...jk", imag_y, sin_x, precision=HIGHEST
    )
    imag_part = jnp.einsum("...xk,jx->...jk", imag_y, cos_x, precision=HIGHEST) - jnp.einsum(
        "...xk,jx->...jk", real_y, sin_x, precision=HIGHEST
    )
    return (real_part, imag_part)


def plane_inverse(real_part, imag_part, cos_x, sin_x, cos_y, sin_y):
    real_x = jnp.einsum("...jk,jx->...xk", real_part, cos_x, precision=HIGHEST) - jnp.einsum(
        "...jk,jx->...xk", imag_part, sin_x, precision=HIGHEST
    )
    imag_x = jnp.einsum("...jk,jx->...xk", imag_part, cos_x, precision=HIGHEST) + jnp.einsum(
        "...jk,jx->...xk", real_part, sin_x, precision=HIGHEST
    )
    return jnp.einsum("...xk,ky->...xy", real_x, cos_y, precision=HIGHEST) - jnp.einsum(
        "...xk,ky->...xy", imag_x, sin_y, precision=HIGHEST
    )


def depth_forward(packed, cos_table, sin_table):
    width = packed.shape[-1] // 2
    real_in = packed[..., :width]
    imag_in = packed[..., width:]
    real_out = jnp.einsum("pszc,kz->pskc", real_in, cos_table, precision=HIGHEST) + jnp.einsum(
        "pszc,kz->pskc", imag_in, sin_table, precision=HIGHEST
    )
    imag_out = jnp.einsum("pszc,kz->pskc", imag_in, cos_table, precision=HIGHEST) - jnp.einsum(
        "pszc,kz->pskc", real_in, sin_table, precision=HIGHEST
    )
    return jnp.concatenate([real_out, imag_out], axis=-1)


def depth_inverse(real_modes, imag_modes, cos_table, sin_table):
    real_out = jnp.einsum("pskc,kz->pszc", real_modes, cos_table, precision=HIGHEST) - jnp.einsum(
        "pskc,kz->pszc", imag_modes, sin_table, precision=HIGHEST
    )
    imag_out = jnp.einsum("pskc,kz->pszc", imag_modes, cos_table, precision=HIGHEST) + jnp.einsum(
        "pskc,kz->pszc", real_modes, sin_table, precision=HIGHEST
    )
    return jnp.concatenate([real_out, imag_out], axis=-1)


def rim_planes(field):
    return extended(field, (("slab", 2),), 1)


def local_any(feats, grains, spec_weight, taps, point_weight, bias, cotangent):
    samples_here = feats.shape[0]
    channels = feats.shape[1]
    planes = feats.shape[2]
    cos_x, sin_x = tables(KX, NX, NX)
    cos_y, sin_y = tables(KY, NY, NY)
    cos_full, sin_full = tables(KZ, NZ, NZ)
    cell_scale = math.sqrt(NX * NY * NZ)
    mode_scale = math.sqrt(KX * KY * KZ)
    mode_rows = spec_weight.shape[0]
    weights = spec_weight.astype(jnp.float32).reshape(mode_rows, KZ, 2, channels, channels)
    w_real = weights[:, :, 0]
    w_imag = weights[:, :, 1]
    moving = mobility(grains)[:, None]

    def to_modes(field):
        real_plane, imag_plane = plane_forward(field, cos_x, sin_x, cos_y, sin_y)
        packed = jnp.stack([real_plane, imag_plane], axis=1)
        packed = packed.transpose(4, 5, 0, 3, 1, 2).reshape(
            KX * KY, samples_here, planes, 2 * channels
        )
        moved = lax.all_to_all(packed, "slab", split_axis=0, concat_axis=2, tiled=True)
        summed = depth_forward(moved, cos_full, sin_full)
        return (summed[..., :channels], summed[..., channels:])

    def from_modes(real_modes, imag_modes):
        planar = depth_inverse(real_modes, imag_modes, cos_full, sin_full)
        packed = lax.all_to_all(planar, "slab", split_axis=2, concat_axis=0, tiled=True)
        grouped = packed.reshape(KX, KY, samples_here, planes, 2, channels).transpose(
            2, 4, 5, 3, 0, 1
        )
        return plane_inverse(grouped[:, 0], grouped[:, 1], cos_x, sin_x, cos_y, sin_y)

    zero_rim = ((0, 0), (0, 0), (0, 0), (1, 1), (1, 1))
    padded = jnp.pad(rim_planes(feats), zero_rim)
    smooth = stencil(padded, taps, False).astype(jnp.bfloat16)
    local_part = moving * jnp.einsum(
        "sczxy,co->sozxy", smooth, point_weight, preferred_element_type=jnp.float32
    )
    spec_real, spec_imag = to_modes(feats.astype(jnp.float32))
    spec_real = spec_real / cell_scale
    spec_imag = spec_imag / cell_scale
    mixed_real = jnp.einsum("pskc,pkco->psko", spec_real, w_real, precision=HIGHEST) - jnp.einsum(
        "pskc,pkco->psko", spec_imag, w_imag, precision=HIGHEST
    )
    mixed_imag = jnp.einsum("pskc,pkco->psko", spec_real, w_imag, precision=HIGHEST) + jnp.einsum(
        "pskc,pkco->psko", spec_imag, w_real, precision=HIGHEST
    )
    spectral = from_modes(mixed_real, mixed_imag) / mode_scale
    pre = spectral + local_part + bias[None, :, None, None, None]
    gate = jax.nn.sigmoid(pre)
    delta = (cotangent.astype(jnp.float32) * gate * (1.0 + pre * (1.0 - gate))).astype(jnp.bfloat16)
    dual_real, dual_imag = to_modes(delta.astype(jnp.float32))
    dual_real = dual_real / mode_scale
    dual_imag = dual_imag / mode_scale
    batch_total = samples_here * lax.axis_size("dp")
    grad_real = jnp.einsum("pskc,psko->pkco", spec_real, dual_real, precision=HIGHEST) + jnp.einsum(
        "pskc,psko->pkco", spec_imag, dual_imag, precision=HIGHEST
    )
    grad_imag = jnp.einsum("pskc,psko->pkco", spec_real, dual_imag, precision=HIGHEST) - jnp.einsum(
        "pskc,psko->pkco", spec_imag, dual_real, precision=HIGHEST
    )
    grad_terms = (jnp.stack([grad_real, grad_imag], axis=2) / batch_total).reshape(
        mode_rows, KZ, 2 * channels * channels
    )
    grad_spec = lax.psum_scatter(
        grad_terms.astype(jnp.bfloat16), "dp", scatter_dimension=2, tiled=True
    ).astype(jnp.float32)
    back_real = jnp.einsum("psko,pkco->pskc", dual_real, w_real, precision=HIGHEST) + jnp.einsum(
        "psko,pkco->pskc", dual_imag, w_imag, precision=HIGHEST
    )
    back_imag = jnp.einsum("psko,pkco->pskc", dual_imag, w_real, precision=HIGHEST) - jnp.einsum(
        "psko,pkco->pskc", dual_real, w_imag, precision=HIGHEST
    )
    spectral_back = from_modes(back_real, back_imag) / cell_scale
    spread = (
        moving
        * jnp.einsum("sozxy,co->sczxy", delta, point_weight, preferred_element_type=jnp.float32)
    ).astype(jnp.bfloat16)
    spread_padded = jnp.pad(rim_planes(spread), zero_rim)
    local_back = stencil(spread_padded, taps, True)
    grad_feats = (spectral_back + local_back).astype(jnp.bfloat16)
    return (grad_feats, grad_spec)


def frequencies(count, length):
    index = np.arange(count)
    return np.where(index < count // 2, index, length - count + index)


def angles(count, length):
    phases = np.outer(frequencies(count, length), np.arange(length)) % length
    return phases * (2.0 * np.pi / length)


def constant(array):
    return jnp.asarray(np.asarray(array, np.float32).astype(ml_dtypes.bfloat16))


def forward_x_table(slabs, split):
    a = angles(KX, NX).reshape(slabs, KX // slabs, NX)
    trig = np.stack([np.cos(a), np.sin(a)])
    table = np.einsum("tsjx,cd->tscjdx", trig, np.eye(2)).reshape(-1, 2, NX // 8, 8)
    if split:
        table = table.transpose(0, 2, 1, 3)
    return table.reshape(4 * KX, 2 * NX)


def halved(table, planes):
    table = table.reshape(-1, planes * 2, 2, KY // 2).transpose(0, 2, 1, 3)
    return table.reshape(-1, planes * 2 * KY)


def forward_y_table(planes):
    a = angles(KY, NY)
    cos, sin = np.cos(a).T, np.sin(a).T
    block = np.stack([np.stack([cos, -sin], 1), np.stack([-sin, -cos], 1)])
    pick = np.eye(planes).reshape(planes // 2, 2, planes)
    table = np.einsum("pqz,tyrk->ptqyzrk", pick, block)
    return halved(table.reshape(planes * 2 * NY, planes * 2 * KY), planes)


def forward_z_table():
    a = angles(KZ, NZ)
    cos, sin = np.cos(a).T, np.sin(a).T
    block = np.stack([np.stack([cos, -sin], 1), np.stack([sin, cos], 1)], 1)
    table = np.einsum("zrqm,kl->zrkqlm", block, np.eye(KY // 2))
    return table.reshape(NZ * KY, KY * KZ)


def inverse_z_table():
    a = angles(KZ, NZ)
    cos, sin = np.cos(a), np.sin(a)
    block = np.stack([np.stack([cos, sin], 2), np.stack([-sin, cos], 2)])
    table = np.einsum("rmzq,kl->rkmzql", block, np.eye(KY // 2))
    return table.reshape(KY * KZ, NZ * KY)


def inverse_y_table(planes, group):
    a = angles(KY, NY)
    cos, sin = np.cos(a), np.sin(a)
    block = np.stack([np.stack([cos, -sin], 1), np.stack([-sin, -cos], 1)])
    pick = np.eye(planes).reshape(planes // group, group, planes)
    table = np.einsum("pqz,rkty->ptqyzrk", pick, block)
    table = halved(table.reshape(-1, planes * 2 * KY), planes)
    return table.reshape(planes // group, 2 * group * NY, planes * 2 * KY).transpose(0, 2, 1)


def inverse_x_table(slabs, group):
    a = angles(KX, NX).reshape(slabs, KX // slabs, NX)
    trig = np.stack([np.cos(a), np.sin(a)])
    table = np.einsum("tsjx,cd->cxstdj", trig, np.eye(group))
    return table.reshape(group * NX, 2 * KX * group)


def first_table(channels, depth):
    table = np.einsum("ac,j,b->ajcb", np.eye(channels), np.ones(depth), np.ones(channels))
    return table.reshape(channels * depth, channels * channels)


def second_table(channels, depth):
    table = np.einsum("ac,j,b->ajbc", np.eye(channels), np.ones(depth), np.ones(channels))
    return table.reshape(channels * depth, channels * channels)


LIGHT = pl.CostEstimate(flops=10**7, bytes_accessed=10**5, transcendentals=0)
HEAVY = pl.CostEstimate(flops=10**11, bytes_accessed=10**8, transcendentals=0)
MIDDLE = pl.CostEstimate(flops=10**10, bytes_accessed=2 * 10**7, transcendentals=0)


def dot(a, b):
    return jnp.dot(a, b, preferred_element_type=jnp.float32)


def whole(shape):
    return pl.BlockSpec(shape, lambda *_: (0,) * len(shape))


def params(limit=63438848):
    return pltpu.CompilerParams(vmem_limit_bytes=limit)


ROOMY = 48 * 2**20


def store_rows(rows, pair, x_table, load):
    slabs, lines = rows.shape[2:4]
    for i in range(lines // 16):
        parts = [dot(x_table[...], load(2 * i + k)) for k in range(2)]
        for t in range(2):
            for s in range(slabs):
                here = slice(8 * (t * slabs + s), 8 * (t * slabs + s) + 8)
                both = jnp.concatenate([part[here] for part in parts], axis=0)
                rows[pair, t, s, 16 * i : 16 * i + 16, :] = both.astype(jnp.bfloat16)


def store_modes(rows, y_table, out):
    pairs, _, slabs, lines, _ = rows.shape
    left = [
        jnp.concatenate([rows[p, t, s] for p in range(pairs) for t in range(2)], axis=1)
        for s in range(slabs)
    ]
    modes = dot(jnp.concatenate(left, axis=0), y_table[...])
    for s in range(slabs):
        out[s] = modes[s * lines : (s + 1) * lines].astype(jnp.bfloat16)


def low_channels(channels):
    return 3 * channels // 8


def rims_kernel(field, *refs):
    rims, held, got, put = refs[:4], refs[4:8], refs[8], refs[9]
    last = field.shape[1] - 1
    loads, stores = [], []
    for k in range(4):
        count = rims[k].shape[0]
        source = field.at[pl.ds((k % 2) * rims[0].shape[0], count), pl.ds(last * (k // 2), 1)]
        loads.append(pltpu.make_async_copy(source, held[k], got.at[k]))
        stores.append(pltpu.make_async_copy(held[k], rims[k], put.at[k]))
    for load in loads:
        load.start()
    for load, store in zip(loads, stores):
        load.wait()
        store.start()
    for store in stores:
        store.wait()


def cut_rims(field):
    channels = field.shape[0]
    low = low_channels(channels)
    rims = [
        jax.ShapeDtypeStruct((count, 1, NX, NY), jnp.bfloat16) for count in (low, channels - low) * 2
    ]
    return pl.pallas_call(
        rims_kernel,
        in_specs=[pl.BlockSpec(memory_space=pl.ANY)],
        out_specs=[pl.BlockSpec(memory_space=pl.ANY)] * 4,
        out_shape=rims,
        scratch_shapes=[
            *(pltpu.VMEM(rim.shape, jnp.bfloat16) for rim in rims),
            pltpu.SemaphoreType.DMA((4,)),
            pltpu.SemaphoreType.DMA((4,)),
        ],
        compiler_params=params(),
        cost_estimate=LIGHT,
        name="rims",
    )(field)


def forward_kernel(field, x_table, y_table, out, rows):
    pair = pl.program_id(0)
    pairs = rows.shape[0]

    def load(i):
        halves = [field[2 * i : 2 * i + 2, q].reshape(2 * NX, NY) for q in range(2)]
        return jnp.concatenate(halves, axis=1)

    store_rows(rows, pair, x_table, load)

    @pl.when(pair == pairs - 1)
    def _():
        store_modes(rows, y_table, out)


def forward_modes(field, slabs):
    channels, planes = field.shape[:2]
    lines = channels * (KX // slabs)
    x_table = constant(forward_x_table(slabs, False))
    y_table = constant(forward_y_table(planes))
    shape = (slabs, lines, planes * 2 * KY)
    return pl.pallas_call(
        forward_kernel,
        grid=(planes // 2,),
        in_specs=[
            pl.BlockSpec((channels, 2, NX, NY), lambda p: (0, p, 0, 0)),
            whole(x_table.shape),
            whole(y_table.shape),
        ],
        out_specs=whole(shape),
        out_shape=jax.ShapeDtypeStruct(shape, jnp.bfloat16),
        scratch_shapes=[pltpu.VMEM((planes // 2, 2, slabs, lines, 2 * NY), jnp.bfloat16)],
        compiler_params=params(),
        cost_estimate=LIGHT,
        name="forward_modes",
    )(field, x_table, y_table)


def mixing_kernel(scale_in, scale_out, adjoint, planar, weight, z_in, z_out, spread_table,
                  sum_table, *rest):
    if adjoint:
        partner, out, send, spectrum, total, wide, product = rest
    else:
        spectrum, out, total, wide, product = rest
    step = pl.program_id(0)
    steps = pl.num_programs(0)
    slabs, lines, width = planar.shape
    half = width // 2
    quarter = spectrum.shape[0] // 4
    lanes = weight.shape[1] // 2
    depth = weight.shape[0] // (2 * quarter)

    @pl.when(step == 0)
    def _():
        left = [
            jnp.concatenate([planar[s, :, h : h + half] for s in range(slabs)], axis=1)
            for h in (0, half)
        ]
        modes = dot(jnp.concatenate(left, axis=0), z_in[...]) * scale_in
        for h in range(2):
            here = modes[h * lines : (h + 1) * lines].T.astype(jnp.bfloat16)
            spectrum[2 * h * quarter : 2 * (h + 1) * quarter] = here
            if adjoint:
                for d in range(send.shape[0]):
                    send[d, 2 * (h + 1) * quarter : 2 * (h + 2) * quarter] = here
        if adjoint:
            rows = [partner[2 * h * quarter : 2 * (h + 1) * quarter] for h in range(2)]
            rows = [row.astype(jnp.float32) for row in rows]
            left = lax.broadcasted_iota(jnp.int32, (1, lines), 1) < lines // 2
            turned = [pltpu.roll(row, lines // 2, axis=1) for row in rows]
            packed = [jnp.where(left, rows[0], turned[1]), jnp.where(left, turned[0], rows[1])]
            for d in range(send.shape[0]):
                send[d, : 2 * quarter] = packed[d % 2].astype(jnp.bfloat16)
        total[...] = jnp.zeros_like(total)

    lane = lax.broadcasted_iota(jnp.int32, (1, lines), 1) % (depth * steps)
    block = 32
    tile = wide.shape[1]
    for j in range(depth):
        mine = lane == depth * step + j
        wide[...] = dot(jnp.where(mine, spectrum[...], 0), spread_table[...])
        for at in range(0, 2 * quarter, block):
            row = 2 * j * quarter + at
            real_at = at + (at // quarter) * quarter
            imag_at = real_at + quarter
            sums = [0.0, 0.0]
            for column in range(0, lanes, 128):
                here = slice(column, column + 128) if tile == lanes else slice(None)
                real_wide = wide[real_at : real_at + block, here]
                imag_wide = wide[imag_at : imag_at + block, here]
                w_real = weight[row : row + block, column : column + 128]
                w_imag = weight[row : row + block, lanes + column : lanes + column + 128]
                w_real = w_real.astype(jnp.float32)
                w_imag = w_imag.astype(jnp.float32)
                if adjoint:
                    real = real_wide * w_real + imag_wide * w_imag
                    imag = imag_wide * w_real - real_wide * w_imag
                    there = slice(column, column + 128)
                    product[real_at : real_at + block, there] = real.astype(jnp.bfloat16)
                    product[imag_at : imag_at + block, there] = imag.astype(jnp.bfloat16)
                else:
                    sums[0] = sums[0] + (real_wide * w_real - imag_wide * w_imag)
                    sums[1] = sums[1] + (real_wide * w_imag + imag_wide * w_real)
            if not adjoint:
                product[real_at : real_at + block] = sums[0].astype(jnp.bfloat16)
                product[imag_at : imag_at + block] = sums[1].astype(jnp.bfloat16)
        total[...] += jnp.where(mine, dot(product[...], sum_table[...]), 0.0)

    @pl.when(step == steps - 1)
    def _():
        modes = total[...] * scale_out
        left = [modes[2 * h * quarter : 2 * (h + 1) * quarter].T for h in range(2)]
        modes = dot(jnp.concatenate(left, axis=0).astype(jnp.bfloat16), z_out[...])
        for s in range(slabs):
            for h in range(2):
                here = modes[h * lines : (h + 1) * lines, s * half : (s + 1) * half]
                out[s, :, h * half : (h + 1) * half] = here.astype(jnp.bfloat16)


def mix(planar, weight, scale_in, scale_out, partner=None, copies=0):
    slabs, lines, width = planar.shape
    adjoint = partner is not None
    depth = KX // slabs
    channels = lines // depth
    rows = KY * KZ
    steps = 2
    z_in = constant(forward_z_table())
    z_out = constant(inverse_z_table())
    first = first_table(channels, depth)
    second = second_table(channels, depth)
    spread_table = constant(second[:, :128] if adjoint else first)
    sum_table = constant(first.T if adjoint else second[:, :128].T)
    shape = (2 * rows, lines)
    in_specs = [
        whole(planar.shape),
        pl.BlockSpec((depth // steps * rows, weight.shape[1]), lambda j: (j, 0)),
        whole(z_in.shape),
        whole(z_out.shape),
        whole(spread_table.shape),
        whole(sum_table.shape),
    ]
    operands = [planar, weight, z_in, z_out, spread_table, sum_table]
    scratch = [
        pltpu.VMEM(shape, jnp.float32),
        pltpu.VMEM((2 * rows, spread_table.shape[1]), jnp.float32),
        pltpu.VMEM((2 * rows, sum_table.shape[0]), jnp.bfloat16),
    ]
    if adjoint:
        in_specs.append(whole(shape))
        operands.append(partner)
        scratch = [pltpu.VMEM(shape, jnp.bfloat16)] + scratch
        outs = [planar.shape, (copies, 3 * rows, lines)]
    else:
        outs = [shape, planar.shape]
    return pl.pallas_call(
        functools.partial(mixing_kernel, scale_in, scale_out, adjoint),
        grid=(steps,),
        in_specs=in_specs,
        out_specs=[whole(out) for out in outs],
        out_shape=[jax.ShapeDtypeStruct(out, jnp.bfloat16) for out in outs],
        scratch_shapes=scratch,
        compiler_params=params(ROOMY),
        cost_estimate=HEAVY,
        name="mix_back" if adjoint else "mix",
    )(*operands)


def plane_mobility(grains):
    same = [
        jnp.concatenate([grains[:1], grains[:-1]], axis=0),
        jnp.concatenate([grains[1:], grains[-1:]], axis=0),
        jnp.concatenate([grains[:, :1], grains[:, :-1]], axis=1),
        jnp.concatenate([grains[:, 1:], grains[:, -1:]], axis=1),
    ]
    total = jnp.full(grains.shape, 0.25, jnp.float32)
    for other in same:
        total = total + jnp.where(grains != other, 0.25, 0.0)
    return total


def layer_kernel(bias, planar, smooth, cotangent, grains, point_weight, repeat, ix_table, iy_table,
                 x_table, y_table, spread, out, first, last, *rest):
    pair = pl.program_id(0)
    waves, spectral, moving, delta, rows, bias_wide, mix_out, mix_in = rest
    pairs = rows.shape[0]
    channels = cotangent.shape[0]
    slabs = planar.shape[0]

    @pl.when(pair == 0)
    def _():
        for c in range(channels):
            bias_wide[c] = jnp.full(bias_wide.shape[1:], 0.5 * bias[c], jnp.float32)
        tall = dot(repeat[...], point_weight[...]).astype(jnp.bfloat16)
        square = lax.dot_general(
            tall, repeat[...], (((1,), (1,)), ((), ())), preferred_element_type=jnp.float32
        )
        row = lax.broadcasted_iota(jnp.int32, square.shape, 0) % 8
        column = lax.broadcasted_iota(jnp.int32, square.shape, 1) % 8
        square = jnp.where(row == column, square, 0.0)
        mix_in[...] = square.astype(jnp.bfloat16)
        mix_out[...] = square.T.astype(jnp.bfloat16)

    lines = planar.shape[1]
    step = jnp.concatenate([planar[s] for s in range(slabs)], axis=0)
    step = dot(step, iy_table[0]).astype(jnp.bfloat16)
    for s in range(slabs):
        for t in range(2):
            waves[s, t] = step[s * lines : (s + 1) * lines, 2 * NY * t : 2 * NY * (t + 1)]
    group = 8 * (KX // slabs)
    for g in range(channels // 8):
        here = slice(g * group, (g + 1) * group)
        wave = [waves[s, t, here, :] for s in range(slabs) for t in range(2)]
        step = dot(ix_table[...], jnp.concatenate(wave, axis=0))
        spectral[8 * g : 8 * g + 8] = step.reshape(8, NX, 2 * NY)
    for q in range(2):
        moving[:, q * NY : (q + 1) * NY] = 0.5 * plane_mobility(grains[q])

    def body(i, _):
        x = pl.multiple_of(16 * i, 16)
        halves = [cotangent[:, q, pl.ds(x, 16), :] for q in range(2)]
        cotangent_here = jnp.concatenate(halves, axis=2).astype(jnp.float32)
        spreads = []
        for h in range(2):
            at = pl.ds(pl.multiple_of(x + 8 * h, 8), 8)
            mobile = moving[at, :][None]
            local = dot(mix_out[...], smooth[0, 2 * i + h]).reshape(channels, 8, 2 * NY)
            half = spectral[:, at, :] + mobile * local + bias_wide[...]
            wave = jnp.tanh(half)
            slope = (1.0 + wave) * (1.0 + (half - half * wave))
            change = cotangent_here[:, 8 * h : 8 * h + 8, :] * slope
            right = change.reshape(8 * channels, 2 * NY).astype(jnp.bfloat16)
            delta[2 * i + h] = right
            back = dot(mix_in[...], right).reshape(channels, 8, 2 * NY)
            spreads.append(mobile * back)
        both = jnp.concatenate(spreads, axis=1).astype(jnp.bfloat16)
        for q in range(2):
            spread[:, q, pl.ds(x, 16), :] = both[:, :, q * NY : (q + 1) * NY]
        return 0

    lax.fori_loop(0, NX // 16, body, 0, unroll=8)


    @pl.when(pair == 0)
    def _():
        first[:, 0] = spread[:, 0]

    @pl.when(pair == pairs - 1)
    def _():
        last[:, 0] = spread[:, 1]

    def load(i):
        return delta[:, 16 * i : 16 * i + 16, :].reshape(2 * NX, 2 * NY)

    store_rows(rows, pair, x_table, load)

    @pl.when(pair == pairs - 1)
    def _():
        store_modes(rows, y_table, out)


def layer(planar, smooth, cotangent, grains, bias, point_weight):
    slabs, lines, width = planar.shape
    channels, planes = cotangent.shape[:2]
    pairs = planes // 2
    repeat = constant(np.repeat(np.eye(channels), 8, axis=0))
    ix_table = constant(inverse_x_table(slabs, 8))
    iy_table = constant(inverse_y_table(planes, 2))
    x_table = constant(forward_x_table(slabs, True))
    y_table = constant(forward_y_table(planes))
    field = pl.BlockSpec((channels, 2, NX, NY), lambda p: (0, p, 0, 0))
    outs = [cotangent.shape, planar.shape] + [(channels, 1, NX, NY)] * 2
    return pl.pallas_call(
        layer_kernel,
        grid=(pairs,),
        in_specs=[
            pl.BlockSpec(memory_space=pltpu.SMEM),
            whole(planar.shape),
            pl.BlockSpec((1,) + smooth.shape[1:], lambda p: (p, 0, 0, 0)),
            field,
            pl.BlockSpec((2, NX, NY), lambda p: (p, 0, 0)),
            whole(point_weight.shape),
            whole(repeat.shape),
            whole(ix_table.shape),
            pl.BlockSpec((1,) + iy_table.shape[1:], lambda p: (p, 0, 0)),
            whole(x_table.shape),
            whole(y_table.shape),
        ],
        out_specs=[field] + [whole(out) for out in outs[1:]],
        out_shape=[jax.ShapeDtypeStruct(out, jnp.bfloat16) for out in outs],
        scratch_shapes=[
            pltpu.VMEM((slabs, 2, lines, 2 * NY), jnp.bfloat16),
            pltpu.VMEM((channels, NX, 2 * NY), jnp.float32),
            pltpu.VMEM((NX, 2 * NY), jnp.float32),
            pltpu.VMEM((NX // 8, 8 * channels, 2 * NY), jnp.bfloat16),
            pltpu.VMEM((pairs, 2, slabs, lines, 2 * NY), jnp.bfloat16),
            pltpu.VMEM((channels, 8, 2 * NY), jnp.float32),
            pltpu.VMEM((8 * channels, 8 * channels), jnp.bfloat16),
            pltpu.VMEM((8 * channels, 8 * channels), jnp.bfloat16),
        ],
        compiler_params=params(ROOMY),
        cost_estimate=LIGHT,
        name="layer",
    )(bias, planar, smooth, cotangent, grains, point_weight, repeat, ix_table, iy_table, x_table,
      y_table)


def build_tile(adjoint, taps, channel, dy, q, planes, span):
    row = lax.broadcasted_iota(jnp.int32, (8, 128), 0)
    lane = lax.broadcasted_iota(jnp.int32, (8, 128), 1)
    tile = jnp.zeros((8, 128), jnp.float32)
    for k, plane in enumerate(planes):
        dz = plane - q
        if not 0 <= dz <= 2:
            continue
        for dx in range(3):
            number = 9 * dz + 3 * dx + dy
            tap = taps[26 - number if adjoint else number, channel]
            tile = jnp.where(lane == (span * k + row + (dx - 1)) % 128, tap, tile)
    return tile


def build_band(adjoint, taps, channel, band, tail):
    row = lax.broadcasted_iota(jnp.int32, (8, 128), 0)
    lane = lax.broadcasted_iota(jnp.int32, (8, 128), 1)
    heads, middles, tails = [], [], []
    for dy in range(3):
        for q in range(2):
            sides = []
            for planes in ((0, 1), (2, 3)):
                tile = build_tile(adjoint, taps, channel, dy, q, planes, 64)
                tiles = [pltpu.roll(tile, 8 * k, axis=1) for k in range(1, 7)]
                first = jnp.where((row == 0) & (lane % 64 == 63), 0.0, tile)
                sides.append([first] + tiles)
            blocks = [jnp.concatenate(pair, axis=1) for pair in zip(*sides)]
            heads += blocks
            middles += blocks[1:]
            tile = build_tile(adjoint, taps, channel, dy, q, range(4), 32)
            tiles = [pltpu.roll(tile, 8 * k, axis=1) for k in range(1, 4)]
            tiles[2] = jnp.where((row == 7) & (lane % 32 == 0), 0.0, tiles[2])
            tails += tiles
    band[...] = jnp.concatenate(heads + middles, axis=0).astype(jnp.bfloat16)
    tail[...] = jnp.concatenate(tails, axis=0).astype(jnp.bfloat16)


def apply_band(quads, band):
    band, tail = band
    counts = (56, 48, 24)
    ends = (6 * counts[0], 6 * (counts[0] + counts[1]))
    lefts = (band[: ends[0], :], band[ends[0] : ends[1], :], tail[...])
    lane = lax.broadcasted_iota(jnp.int32, (NX, NY), 1)
    totals = []
    for group in range(0, len(quads), 2):
        products = []
        for left, x, span in zip(lefts, (0, 48, 96), (64, 64, 32)):
            right = [
                jnp.concatenate([sheet[x : x + span] for sheet in quads[group + p]], axis=0)
                for p in range(2)
            ]
            products.append(dot(left, jnp.concatenate(right, axis=1)))
        for p in range(2):
            wide = slice(NY * p, NY * (p + 1))
            pair = []
            for q in range(2):
                shifted = []
                for dy in range(3):
                    b = 2 * dy + q
                    pieces = [
                        product[count * b : count * (b + 1), wide]
                        for product, count in zip(products, counts)
                    ]
                    shifted.append(jnp.concatenate(pieces, axis=0))
                before = jnp.where(lane == 0, 0.0, pltpu.roll(shifted[0], 1, axis=1))
                after = jnp.where(lane == NY - 1, 0.0, pltpu.roll(shifted[2], NY - 1, axis=1))
                pair.append(shifted[1] + before + after)
            totals.append(jnp.concatenate(pair, axis=1))
    return totals


def banded(adjoint, taps, start, bands, channels):
    step = pl.program_id(0)
    final = start + channels * pl.num_programs(0) - 1

    @pl.when(step == 0)
    def _():
        build_band(adjoint, taps, start, *bands[0])

    def run(visit):
        for c in range(channels):
            following = jnp.minimum(start + channels * step + c + 1, final)
            build_band(adjoint, taps, following, *bands[(c + 1) % channels])
            visit(c, bands[c])

    return run


def band_scratch(channels):
    shapes = [(6 * (56 + 48), 256), (6 * 24, 128)]
    return [pltpu.VMEM(shape, jnp.bfloat16) for shape in shapes * channels]


def paired(refs):
    return list(zip(refs[0::2], refs[1::2]))


def smooth_kernel(start, taps, before, field, after, *rest):
    out, *bands = rest[-2 * field.shape[0] - 1 :]
    bands = paired(bands)
    planes = field.shape[1]
    totals = []

    def visit(c, band):
        sheets = [before[c, 0]] + [field[c, z] for z in range(planes)] + [after[c, 0]]
        totals.append(apply_band([sheets[z : z + 4] for z in range(0, planes, 2)], band))

        if c % 2 == 1:
            for p in range(planes // 2):
                both = [total[p].reshape(NX // 8, 8, 2 * NY) for total in totals[c - 1 : c + 1]]
                both = jnp.concatenate(both, axis=1).astype(jnp.bfloat16)
                out[p, :, 8 * (c - 1) : 8 * (c + 1), :] = both

    banded(False, taps, start, bands, field.shape[0])(visit)


def smooth_planes(field, rims, taps, done=None):
    channels, planes = field.shape[:2]
    pairs = planes // 2
    low = low_channels(channels)
    start = 0 if done is None else low
    count = low if done is None else channels - low
    step = 4
    skip = start // step
    rim = pl.BlockSpec((step, 1, NX, NY), lambda c: (c, 0, 0, 0))
    sheets = pl.BlockSpec((step, planes, NX, NY), lambda c: (c + skip, 0, 0, 0))
    in_specs = [pl.BlockSpec(memory_space=pltpu.SMEM), rim, sheets, rim]
    operands = [taps, rims[0], field, rims[1]]
    if done is not None:
        in_specs.append(pl.BlockSpec(memory_space=pl.ANY))
        operands.append(done)
    return pl.pallas_call(
        functools.partial(smooth_kernel, start),
        grid=(count // step,),
        in_specs=in_specs,
        out_specs=pl.BlockSpec((pairs, NX // 8, 8 * step, 2 * NY), lambda c: (0, 0, c + skip, 0)),
        out_shape=jax.ShapeDtypeStruct((pairs, NX // 8, 8 * channels, 2 * NY), jnp.bfloat16),
        input_output_aliases={} if done is None else {4: 0},
        scratch_shapes=band_scratch(step),
        compiler_params=params(ROOMY),
        cost_estimate=MIDDLE,
        name="smooth_low" if done is None else "smooth_high",
    )(*operands)


def inner_kernel(taps, field, out, *bands):
    bands = paired(bands)
    planes = field.shape[1]

    def visit(c, band):
        quads = [[field[c, z + k] for k in range(4)] for z in range(1, planes - 3, 2)]
        for p, near in enumerate(apply_band(quads, band)):
            total = near.astype(jnp.bfloat16)
            out[c, 2 * p] = total[:, :NY]
            out[c, 2 * p + 1] = total[:, NY:]

    banded(True, taps, 0, bands, field.shape[0])(visit)


def near_inner(field, taps):
    channels, planes = field.shape[:2]
    step = 8
    shape = (channels, planes - 4, NX, NY)
    return pl.pallas_call(
        inner_kernel,
        grid=(channels // step,),
        in_specs=[
            pl.BlockSpec(memory_space=pltpu.SMEM),
            pl.BlockSpec((step, planes, NX, NY), lambda c: (c, 0, 0, 0)),
        ],
        out_specs=pl.BlockSpec((step,) + shape[1:], lambda c: (c, 0, 0, 0)),
        out_shape=jax.ShapeDtypeStruct(shape, jnp.bfloat16),
        scratch_shapes=band_scratch(step),
        compiler_params=params(),
        cost_estimate=LIGHT,
        name="near_inner",
    )(taps, field)


def finish_kernel(taps, before, field, after, inner, planar, ix_table, iy_table, out, waves,
                  *bands):
    bands = paired(bands)
    step = pl.program_id(0)
    slabs, lines = planar.shape[:2]
    planes = field.shape[1]
    span = planes * NY

    @pl.when(step == 0)
    def _():
        left = jnp.concatenate([planar[s] for s in range(slabs)], axis=0)
        for t in range(2):
            wave = dot(left, iy_table[0, :, t * span : (t + 1) * span]).astype(jnp.bfloat16)
            for s in range(slabs):
                waves[s, t] = wave[s * lines : (s + 1) * lines]

    rows = field.shape[0] * (KX // slabs)
    here = pl.ds(pl.multiple_of(rows * step, rows), rows)
    right = [waves[s, t, here, :] for s in range(slabs) for t in range(2)]
    right = jnp.concatenate(right, axis=0)
    far = [
        dot(ix_table[...], right[:, 2 * p * NY : 2 * (p + 1) * NY]) for p in range(planes // 2)
    ]

    def store(c, p, near):
        for q in range(2):
            total = near[q] + far[p][c * NX : (c + 1) * NX, q * NY : (q + 1) * NY]
            out[c, 2 * p + q] = total.astype(jnp.bfloat16)

    def visit(c, band):
        low = [before[c, 0]] + [field[c, z] for z in range(3)]
        high = [field[c, z] for z in range(planes - 3, planes)] + [after[c, 0]]
        for p, near in zip((0, planes // 2 - 1), apply_band([low, high], band)):
            store(c, p, [near[:, :NY], near[:, NY:]])
        for p in range(1, planes // 2 - 1):
            store(c, p, [inner[c, 2 * p - 2 + q].astype(jnp.float32) for q in range(2)])

    banded(True, taps, 0, bands, field.shape[0])(visit)


def finish(planar, spread, rims, inner, taps):
    slabs, lines, width = planar.shape
    channels, planes = spread.shape[:2]
    step = 8
    ix_table = constant(inverse_x_table(slabs, step))
    iy_table = constant(inverse_y_table(planes, planes))
    rim = pl.BlockSpec((step, 1, NX, NY), lambda c: (c, 0, 0, 0))
    sheets = pl.BlockSpec((step, planes, NX, NY), lambda c: (c, 0, 0, 0))
    return pl.pallas_call(
        finish_kernel,
        grid=(channels // step,),
        in_specs=[
            pl.BlockSpec(memory_space=pltpu.SMEM),
            rim,
            sheets,
            rim,
            pl.BlockSpec((step,) + inner.shape[1:], lambda c: (c, 0, 0, 0)),
            whole(planar.shape),
            whole(ix_table.shape),
            whole(iy_table.shape),
        ],
        out_specs=sheets,
        out_shape=jax.ShapeDtypeStruct(spread.shape, jnp.bfloat16),
        scratch_shapes=[
            pltpu.VMEM((slabs, 2, lines, planes * NY), jnp.bfloat16),
            *band_scratch(step),
        ],
        compiler_params=params(ROOMY),
        cost_estimate=HEAVY,
        name="finish",
    )(taps, rims[0], spread, rims[1], inner, planar, ix_table, iy_table)


def gradient_kernel(gathered, first, second, out):
    step = pl.program_id(0)
    samples, rows, lines = gathered.shape
    quarter = rows // 6
    depth = out.shape[0] // (2 * quarter)
    real_part = lax.axis_index("dp") < lax.axis_size("dp") // 2
    lane = lax.broadcasted_iota(jnp.int32, (1, lines), 1)
    duals = []
    for s in range(samples):
        for h in range(2):
            at = (2 * h + 2) * quarter
            real = gathered[s, at : at + quarter]
            imag = gathered[s, at + quarter : at + 2 * quarter]
            duals.append(jnp.where(real_part, real, imag))
            duals.append(jnp.where(real_part, imag, -real))
    duals = jnp.concatenate(duals, axis=0)
    for j in range(depth):
        mine = lane % (depth * pl.num_programs(0)) == depth * step + j
        spectra = []
        for s in range(samples):
            for h in range(2):
                here = mine & (lane // (lines // 2) == h)
                spectra.append(jnp.where(here, gathered[s, : 2 * quarter], 0))
        spectra = jnp.concatenate(spectra, axis=0)
        wide = dot(jnp.where(mine, duals, 0), second[...])
        for column in range(0, out.shape[1], 256):
            product = dot(spectra, first[:, column : column + 256])
            for at in range(0, 256, 128):
                for h in range(2):
                    total = 0.0
                    for s in range(samples):
                        for part in range(2):
                            row = (4 * s + 2 * h + part) * quarter
                            here = slice(row, row + quarter)
                            total = total + product[here, at : at + 128] * wide[here]
                    row = (2 * j + h) * quarter
                    there = slice(column + at, column + at + 128)
                    out[row : row + quarter, there] = total * (1.0 / samples)


def weight_gradient(gathered, depth, width):
    samples, rows, lines = gathered.shape
    channels = lines // depth
    first = np.repeat(np.eye(channels // 2), channels, axis=1)
    first = constant(np.tile(np.repeat(first, depth, axis=0), (2, 1)))
    second = constant(second_table(channels, depth)[:, :128])
    steps = 2
    half = rows // 3
    return pl.pallas_call(
        gradient_kernel,
        grid=(steps,),
        in_specs=[whole(gathered.shape), whole(first.shape), whole(second.shape)],
        out_specs=pl.BlockSpec((depth // steps * half, width), lambda j: (j, 0)),
        out_shape=jax.ShapeDtypeStruct((depth * half, width), jnp.float32),
        compiler_params=params(ROOMY),
        cost_estimate=MIDDLE,
        name="weight_gradient",
    )(gathered, first, second)


def exchange(first, last):
    size = lax.axis_size("slab")
    up = [(i, i + 1) for i in range(size - 1)]
    down = [(j, i) for i, j in up]
    return lax.ppermute(last, "slab", up), lax.ppermute(first, "slab", down)


def swap(planar):
    return lax.all_to_all(planar, "slab", split_axis=0, concat_axis=0)


def local_fast(feats, grains, spec_weight, taps, point_weight, bias, cotangent):
    slabs = lax.axis_size("slab")
    copies = lax.axis_size("dp")
    barrier = lax.optimization_barrier
    field = feats[0]
    channels = field.shape[0]
    cell_scale = 1.0 / math.sqrt(NX * NY * NZ)
    mode_scale = 1.0 / math.sqrt(KX * KY * KZ)
    mode_rows = spec_weight.shape[0]
    weight = spec_weight.reshape(mode_rows * KZ, 2 * channels * channels)
    width = weight.shape[1] // copies

    first, first_high, last, last_high = cut_rims(field)
    rims = exchange(first, last)
    planar = swap(forward_modes(field, slabs))
    rims, first, last = barrier((rims, first_high, last_high))
    rims_high = exchange(first, last)
    planar, smooth = barrier((planar, smooth_planes(field, rims, taps)))
    spectrum, planar = mix(planar, weight, cell_scale, 0.5 * mode_scale)
    smooth, spectrum = barrier((smooth, spectrum))
    planar = swap(planar)
    smooth = smooth_planes(field, rims_high, taps, smooth)
    spread, planar, first, last = layer(planar, smooth, cotangent[0], grains[0], bias, point_weight)
    rims = exchange(first, last)
    planar, send = mix(swap(planar), weight, 0.5 * mode_scale, cell_scale, spectrum, copies)
    send, spread = barrier((send, spread))
    inner = near_inner(spread, taps)
    gathered = lax.all_to_all(send, "dp", split_axis=0, concat_axis=0)
    planar, gathered, inner, rims = barrier((planar, gathered, inner, rims))
    planar = swap(planar)
    grad_spec = weight_gradient(gathered, KX // slabs, width)
    planar, grad_spec = barrier((planar, grad_spec))
    grad_feats = finish(planar, spread, rims, inner, taps)[None]
    return (grad_feats, grad_spec.reshape(mode_rows, KZ, width))


def local(feats, grains, spec_weight, taps, point_weight, bias, cotangent):
    samples, channels, planes = feats.shape[:3]
    width = spec_weight.shape[2] // lax.axis_size("dp")
    fits = (
        lax.axis_size("slab") * 4 == KX
        and samples == 1
        and channels == 32
        and planes == 8
        and channels * channels == 2 * width
    )
    form = local_fast if fits else local_any
    return form(feats, grains, spec_weight, taps, point_weight, bias, cotangent)


def solution(mesh):
    in_specs = (
        P(("grp", "dp"), None, "slab", None, None),
        P(("grp", "dp"), "slab", None, None),
        P("slab", None, None),
        P(),
        P(),
        P(),
        P(("grp", "dp"), None, "slab", None, None),
    )
    out_specs = (P(("grp", "dp"), None, "slab", None, None), P("slab", "grp", "dp"))
    return jax.shard_map(local, mesh=mesh, in_specs=in_specs, out_specs=out_specs, check_vma=False)
```

```python
import functools
import math

import jax
import jax.numpy as jnp
import ml_dtypes
import numpy as np
from jax import lax
from jax.experimental import pallas as pl
from jax.experimental.pallas import tpu as pltpu
from jax.sharding import PartitionSpec as P

NX = 128
NY = 128
NZ = 32
KX = 16
KY = 16
KZ = 16


HIGHEST = lax.Precision.HIGHEST


def extended(shard, sides, width):
    for axis, dim in sides:
        size, length = (lax.axis_size(axis), shard.shape[dim])
        up = [(i, (i + 1) % size) for i in range(size - 1)]
        down = [(j, i) for i, j in up]
        last = lax.slice_in_dim(shard, length - width, length, axis=dim)
        first = lax.slice_in_dim(shard, 0, width, axis=dim)
        before = lax.ppermute(last, axis, up)
        after = lax.ppermute(first, axis, down)
        shard = jnp.concatenate([before, shard, after], axis=dim)
    return shard


def tables(count, length, span):
    indices = jnp.arange(count, dtype=jnp.int32)
    frequency = jnp.where(indices < count // 2, indices, length - count + indices)
    position = jnp.arange(span, dtype=jnp.int32)
    phases = frequency[:, None] * position[None, :] % length
    angles = phases.astype(jnp.float32) * (2.0 * math.pi / length)
    return (jnp.cos(angles), jnp.sin(angles))


def mobility(grains):
    leading = [(0, 0)] * (grains.ndim - 2)
    along_x = (grains[..., 1:, :] != grains[..., :-1, :]).astype(jnp.float32)
    along_y = (grains[..., :, 1:] != grains[..., :, :-1]).astype(jnp.float32)
    differ = jnp.pad(along_x, leading + [(1, 0), (0, 0)]) + jnp.pad(
        along_x, leading + [(0, 1), (0, 0)]
    )
    differ = (
        differ
        + jnp.pad(along_y, leading + [(0, 0), (1, 0)])
        + jnp.pad(along_y, leading + [(0, 0), (0, 1)])
    )
    return 0.25 * (1.0 + differ)


def stencil(padded, taps, adjoint):
    planes = padded.shape[-3] - 2
    rows_x = padded.shape[-2] - 2
    rows_y = padded.shape[-1] - 2
    total = jnp.zeros(padded.shape[:-3] + (planes, rows_x, rows_y), jnp.float32)
    for offset in range(27):
        shift_z, shift_x, shift_y = (offset // 9, offset // 3 % 3, offset % 3)
        if adjoint:
            shift_z, shift_x, shift_y = (2 - shift_z, 2 - shift_x, 2 - shift_y)
        window = padded[
            ..., shift_z : shift_z + planes, shift_x : shift_x + rows_x, shift_y : shift_y + rows_y
        ]
        total = total + taps[offset][:, None, None, None] * window.astype(jnp.float32)
    return total


def plane_forward(field, cos_x, sin_x, cos_y, sin_y):
    real_y = jnp.einsum("...xy,ky->...xk", field, cos_y, precision=HIGHEST)
    imag_y = -jnp.einsum("...xy,ky->...xk", field, sin_y, precision=HIGHEST)
    real_part = jnp.einsum("...xk,jx->...jk", real_y, cos_x, precision=HIGHEST) + jnp.einsum(
        "...xk,jx->...jk", imag_y, sin_x, precision=HIGHEST
    )
    imag_part = jnp.einsum("...xk,jx->...jk", imag_y, cos_x, precision=HIGHEST) - jnp.einsum(
        "...xk,jx->...jk", real_y, sin_x, precision=HIGHEST
    )
    return (real_part, imag_part)


def plane_inverse(real_part, imag_part, cos_x, sin_x, cos_y, sin_y):
    real_x = jnp.einsum("...jk,jx->...xk", real_part, cos_x, precision=HIGHEST) - jnp.einsum(
        "...jk,jx->...xk", imag_part, sin_x, precision=HIGHEST
    )
    imag_x = jnp.einsum("...jk,jx->...xk", imag_part, cos_x, precision=HIGHEST) + jnp.einsum(
        "...jk,jx->...xk", real_part, sin_x, precision=HIGHEST
    )
    return jnp.einsum("...xk,ky->...xy", real_x, cos_y, precision=HIGHEST) - jnp.einsum(
        "...xk,ky->...xy", imag_x, sin_y, precision=HIGHEST
    )


def depth_forward(packed, cos_table, sin_table):
    width = packed.shape[-1] // 2
    real_in = packed[..., :width]
    imag_in = packed[..., width:]
    real_out = jnp.einsum("pszc,kz->pskc", real_in, cos_table, precision=HIGHEST) + jnp.einsum(
        "pszc,kz->pskc", imag_in, sin_table, precision=HIGHEST
    )
    imag_out = jnp.einsum("pszc,kz->pskc", imag_in, cos_table, precision=HIGHEST) - jnp.einsum(
        "pszc,kz->pskc", real_in, sin_table, precision=HIGHEST
    )
    return jnp.concatenate([real_out, imag_out], axis=-1)


def depth_inverse(real_modes, imag_modes, cos_table, sin_table):
    real_out = jnp.einsum("pskc,kz->pszc", real_modes, cos_table, precision=HIGHEST) - jnp.einsum(
        "pskc,kz->pszc", imag_modes, sin_table, precision=HIGHEST
    )
    imag_out = jnp.einsum("pskc,kz->pszc", imag_modes, cos_table, precision=HIGHEST) + jnp.einsum(
        "pskc,kz->pszc", real_modes, sin_table, precision=HIGHEST
    )
    return jnp.concatenate([real_out, imag_out], axis=-1)


def rim_planes(field):
    return extended(field, (("slab", 2),), 1)


def local_any(feats, grains, spec_weight, taps, point_weight, bias, cotangent):
    samples_here = feats.shape[0]
    channels = feats.shape[1]
    planes = feats.shape[2]
    cos_x, sin_x = tables(KX, NX, NX)
    cos_y, sin_y = tables(KY, NY, NY)
    cos_full, sin_full = tables(KZ, NZ, NZ)
    cell_scale = math.sqrt(NX * NY * NZ)
    mode_scale = math.sqrt(KX * KY * KZ)
    mode_rows = spec_weight.shape[0]
    weights = spec_weight.astype(jnp.float32).reshape(mode_rows, KZ, 2, channels, channels)
    w_real = weights[:, :, 0]
    w_imag = weights[:, :, 1]
    moving = mobility(grains)[:, None]

    def to_modes(field):
        real_plane, imag_plane = plane_forward(field, cos_x, sin_x, cos_y, sin_y)
        packed = jnp.stack([real_plane, imag_plane], axis=1)
        packed = packed.transpose(4, 5, 0, 3, 1, 2).reshape(
            KX * KY, samples_here, planes, 2 * channels
        )
        moved = lax.all_to_all(packed, "slab", split_axis=0, concat_axis=2, tiled=True)
        summed = depth_forward(moved, cos_full, sin_full)
        return (summed[..., :channels], summed[..., channels:])

    def from_modes(real_modes, imag_modes):
        planar = depth_inverse(real_modes, imag_modes, cos_full, sin_full)
        packed = lax.all_to_all(planar, "slab", split_axis=2, concat_axis=0, tiled=True)
        grouped = packed.reshape(KX, KY, samples_here, planes, 2, channels).transpose(
            2, 4, 5, 3, 0, 1
        )
        return plane_inverse(grouped[:, 0], grouped[:, 1], cos_x, sin_x, cos_y, sin_y)

    zero_rim = ((0, 0), (0, 0), (0, 0), (1, 1), (1, 1))
    padded = jnp.pad(rim_planes(feats), zero_rim)
    smooth = stencil(padded, taps, False).astype(jnp.bfloat16)
    local_part = moving * jnp.einsum(
        "sczxy,co->sozxy", smooth, point_weight, preferred_element_type=jnp.float32
    )
    spec_real, spec_imag = to_modes(feats.astype(jnp.float32))
    spec_real = spec_real / cell_scale
    spec_imag = spec_imag / cell_scale
    mixed_real = jnp.einsum("pskc,pkco->psko", spec_real, w_real, precision=HIGHEST) - jnp.einsum(
        "pskc,pkco->psko", spec_imag, w_imag, precision=HIGHEST
    )
    mixed_imag = jnp.einsum("pskc,pkco->psko", spec_real, w_imag, precision=HIGHEST) + jnp.einsum(
        "pskc,pkco->psko", spec_imag, w_real, precision=HIGHEST
    )
    spectral = from_modes(mixed_real, mixed_imag) / mode_scale
    pre = spectral + local_part + bias[None, :, None, None, None]
    gate = jax.nn.sigmoid(pre)
    delta = (cotangent.astype(jnp.float32) * gate * (1.0 + pre * (1.0 - gate))).astype(jnp.bfloat16)
    dual_real, dual_imag = to_modes(delta.astype(jnp.float32))
    dual_real = dual_real / mode_scale
    dual_imag = dual_imag / mode_scale
    batch_total = samples_here * lax.axis_size("dp")
    grad_real = jnp.einsum("pskc,psko->pkco", spec_real, dual_real, precision=HIGHEST) + jnp.einsum(
        "pskc,psko->pkco", spec_imag, dual_imag, precision=HIGHEST
    )
    grad_imag = jnp.einsum("pskc,psko->pkco", spec_real, dual_imag, precision=HIGHEST) - jnp.einsum(
        "pskc,psko->pkco", spec_imag, dual_real, precision=HIGHEST
    )
    grad_terms = (jnp.stack([grad_real, grad_imag], axis=2) / batch_total).reshape(
        mode_rows, KZ, 2 * channels * channels
    )
    grad_spec = lax.psum_scatter(
        grad_terms.astype(jnp.bfloat16), "dp", scatter_dimension=2, tiled=True
    ).astype(jnp.float32)
    back_real = jnp.einsum("psko,pkco->pskc", dual_real, w_real, precision=HIGHEST) + jnp.einsum(
        "psko,pkco->pskc", dual_imag, w_imag, precision=HIGHEST
    )
    back_imag = jnp.einsum("psko,pkco->pskc", dual_imag, w_real, precision=HIGHEST) - jnp.einsum(
        "psko,pkco->pskc", dual_real, w_imag, precision=HIGHEST
    )
    spectral_back = from_modes(back_real, back_imag) / cell_scale
    spread = (
        moving
        * jnp.einsum("sozxy,co->sczxy", delta, point_weight, preferred_element_type=jnp.float32)
    ).astype(jnp.bfloat16)
    spread_padded = jnp.pad(rim_planes(spread), zero_rim)
    local_back = stencil(spread_padded, taps, True)
    grad_feats = (spectral_back + local_back).astype(jnp.bfloat16)
    return (grad_feats, grad_spec)


def frequencies(count, length):
    index = np.arange(count)
    return np.where(index < count // 2, index, length - count + index)


def angles(count, length):
    phases = np.outer(frequencies(count, length), np.arange(length)) % length
    return phases * (2.0 * np.pi / length)


def constant(array):
    return jnp.asarray(np.asarray(array, np.float32).astype(ml_dtypes.bfloat16))


def forward_x_table(slabs, split):
    a = angles(KX, NX).reshape(slabs, KX // slabs, NX)
    trig = np.stack([np.cos(a), np.sin(a)])
    table = np.einsum("tsjx,cd->tscjdx", trig, np.eye(2)).reshape(-1, 2, NX // 8, 8)
    if split:
        table = table.transpose(0, 2, 1, 3)
    return table.reshape(4 * KX, 2 * NX)


def halved(table, planes):
    table = table.reshape(-1, planes * 2, 2, KY // 2).transpose(0, 2, 1, 3)
    return table.reshape(-1, planes * 2 * KY)


def forward_y_table(planes):
    a = angles(KY, NY)
    cos, sin = np.cos(a).T, np.sin(a).T
    block = np.stack([np.stack([cos, -sin], 1), np.stack([-sin, -cos], 1)])
    pick = np.eye(planes).reshape(planes // 2, 2, planes)
    table = np.einsum("pqz,tyrk->ptqyzrk", pick, block)
    return halved(table.reshape(planes * 2 * NY, planes * 2 * KY), planes)


def forward_z_table():
    a = angles(KZ, NZ)
    cos, sin = np.cos(a).T, np.sin(a).T
    block = np.stack([np.stack([cos, -sin], 1), np.stack([sin, cos], 1)], 1)
    table = np.einsum("zrqm,kl->zrkqlm", block, np.eye(KY // 2))
    return table.reshape(NZ * KY, KY * KZ)


def inverse_z_table():
    a = angles(KZ, NZ)
    cos, sin = np.cos(a), np.sin(a)
    block = np.stack([np.stack([cos, sin], 2), np.stack([-sin, cos], 2)])
    table = np.einsum("rmzq,kl->rkmzql", block, np.eye(KY // 2))
    return table.reshape(KY * KZ, NZ * KY)


def inverse_y_table(planes, group):
    a = angles(KY, NY)
    cos, sin = np.cos(a), np.sin(a)
    block = np.stack([np.stack([cos, -sin], 1), np.stack([-sin, -cos], 1)])
    pick = np.eye(planes).reshape(planes // group, group, planes)
    table = np.einsum("pqz,rkty->ptqyzrk", pick, block)
    table = halved(table.reshape(-1, planes * 2 * KY), planes)
    return table.reshape(planes // group, 2 * group * NY, planes * 2 * KY).transpose(0, 2, 1)


def inverse_x_table(slabs, group):
    a = angles(KX, NX).reshape(slabs, KX // slabs, NX)
    trig = np.stack([np.cos(a), np.sin(a)])
    table = np.einsum("tsjx,cd->cxstdj", trig, np.eye(group))
    return table.reshape(group * NX, 2 * KX * group)


def first_table(channels, depth):
    table = np.einsum("ac,j,b->ajcb", np.eye(channels), np.ones(depth), np.ones(channels))
    return table.reshape(channels * depth, channels * channels)


def second_table(channels, depth):
    table = np.einsum("ac,j,b->ajbc", np.eye(channels), np.ones(depth), np.ones(channels))
    return table.reshape(channels * depth, channels * channels)


LIGHT = pl.CostEstimate(flops=10**7, bytes_accessed=10**5, transcendentals=0)
HEAVY = pl.CostEstimate(flops=10**11, bytes_accessed=10**8, transcendentals=0)


def dot(a, b):
    return jnp.dot(a, b, preferred_element_type=jnp.float32)


def whole(shape):
    return pl.BlockSpec(shape, lambda *_: (0,) * len(shape))


def params(limit=63438848):
    return pltpu.CompilerParams(vmem_limit_bytes=limit)


ROOMY = 48 * 2**20


def store_rows(rows, pair, x_table, load):
    slabs, lines = rows.shape[2:4]
    for i in range(lines // 16):
        parts = [dot(x_table[...], load(2 * i + k)) for k in range(2)]
        for t in range(2):
            for s in range(slabs):
                here = slice(8 * (t * slabs + s), 8 * (t * slabs + s) + 8)
                both = jnp.concatenate([part[here] for part in parts], axis=0)
                rows[pair, t, s, 16 * i : 16 * i + 16, :] = both.astype(jnp.bfloat16)


def store_modes(rows, y_table, out):
    pairs, _, slabs, lines, _ = rows.shape
    left = [
        jnp.concatenate([rows[p, t, s] for p in range(pairs) for t in range(2)], axis=1)
        for s in range(slabs)
    ]
    modes = dot(jnp.concatenate(left, axis=0), y_table[...])
    for s in range(slabs):
        out[s] = modes[s * lines : (s + 1) * lines].astype(jnp.bfloat16)


def low_channels(channels):
    return 3 * channels // 8


def rims_kernel(field, *refs):
    rims, held, got, put = refs[:4], refs[4:8], refs[8], refs[9]
    last = field.shape[1] - 1
    loads, stores = [], []
    for k in range(4):
        count = rims[k].shape[0]
        source = field.at[pl.ds((k % 2) * rims[0].shape[0], count), pl.ds(last * (k // 2), 1)]
        loads.append(pltpu.make_async_copy(source, held[k], got.at[k]))
        stores.append(pltpu.make_async_copy(held[k], rims[k], put.at[k]))
    for load in loads:
        load.start()
    for load, store in zip(loads, stores):
        load.wait()
        store.start()
    for store in stores:
        store.wait()


def cut_rims(field):
    channels = field.shape[0]
    low = low_channels(channels)
    rims = [
        jax.ShapeDtypeStruct((count, 1, NX, NY), jnp.bfloat16) for count in (low, channels - low) * 2
    ]
    return pl.pallas_call(
        rims_kernel,
        in_specs=[pl.BlockSpec(memory_space=pl.ANY)],
        out_specs=[pl.BlockSpec(memory_space=pl.ANY)] * 4,
        out_shape=rims,
        scratch_shapes=[
            *(pltpu.VMEM(rim.shape, jnp.bfloat16) for rim in rims),
            pltpu.SemaphoreType.DMA((4,)),
            pltpu.SemaphoreType.DMA((4,)),
        ],
        compiler_params=params(),
        cost_estimate=LIGHT,
        name="rims",
    )(field)


def forward_kernel(field, x_table, y_table, out, rows):
    pair = pl.program_id(0)
    pairs = rows.shape[0]

    def load(i):
        halves = [field[2 * i : 2 * i + 2, q].reshape(2 * NX, NY) for q in range(2)]
        return jnp.concatenate(halves, axis=1)

    store_rows(rows, pair, x_table, load)

    @pl.when(pair == pairs - 1)
    def _():
        store_modes(rows, y_table, out)


def forward_modes(field, slabs):
    channels, planes = field.shape[:2]
    lines = channels * (KX // slabs)
    x_table = constant(forward_x_table(slabs, False))
    y_table = constant(forward_y_table(planes))
    shape = (slabs, lines, planes * 2 * KY)
    return pl.pallas_call(
        forward_kernel,
        grid=(planes // 2,),
        in_specs=[
            pl.BlockSpec((channels, 2, NX, NY), lambda p: (0, p, 0, 0)),
            whole(x_table.shape),
            whole(y_table.shape),
        ],
        out_specs=whole(shape),
        out_shape=jax.ShapeDtypeStruct(shape, jnp.bfloat16),
        scratch_shapes=[pltpu.VMEM((planes // 2, 2, slabs, lines, 2 * NY), jnp.bfloat16)],
        compiler_params=params(),
        cost_estimate=LIGHT,
        name="forward_modes",
    )(field, x_table, y_table)


def mixing_kernel(scale_in, scale_out, adjoint, planar, weight, z_in, z_out, spread_table,
                  sum_table, *rest):
    if adjoint:
        partner, out, send, spectrum, total, wide, product = rest
    else:
        spectrum, out, total, wide, product = rest
    step = pl.program_id(0)
    steps = pl.num_programs(0)
    slabs, lines, width = planar.shape
    half = width // 2
    quarter = spectrum.shape[0] // 4
    lanes = weight.shape[1] // 2
    depth = weight.shape[0] // (2 * quarter)

    @pl.when(step == 0)
    def _():
        left = [
            jnp.concatenate([planar[s, :, h : h + half] for s in range(slabs)], axis=1)
            for h in (0, half)
        ]
        modes = dot(jnp.concatenate(left, axis=0), z_in[...]) * scale_in
        for h in range(2):
            here = modes[h * lines : (h + 1) * lines].T.astype(jnp.bfloat16)
            spectrum[2 * h * quarter : 2 * (h + 1) * quarter] = here
            if adjoint:
                for d in range(send.shape[0]):
                    send[d, 2 * (h + 1) * quarter : 2 * (h + 2) * quarter] = here
        if adjoint:
            rows = [partner[2 * h * quarter : 2 * (h + 1) * quarter] for h in range(2)]
            rows = [row.astype(jnp.float32) for row in rows]
            left = lax.broadcasted_iota(jnp.int32, (1, lines), 1) < lines // 2
            turned = [pltpu.roll(row, lines // 2, axis=1) for row in rows]
            packed = [jnp.where(left, rows[0], turned[1]), jnp.where(left, turned[0], rows[1])]
            for d in range(send.shape[0]):
                send[d, : 2 * quarter] = packed[d % 2].astype(jnp.bfloat16)
        total[...] = jnp.zeros_like(total)

    lane = lax.broadcasted_iota(jnp.int32, (1, lines), 1) % (depth * steps)
    block = 32
    tile = wide.shape[1]
    for j in range(depth):
        mine = lane == depth * step + j
        wide[...] = dot(jnp.where(mine, spectrum[...], 0), spread_table[...])
        for at in range(0, 2 * quarter, block):
            row = 2 * j * quarter + at
            real_at = at + (at // quarter) * quarter
            imag_at = real_at + quarter
            sums = [0.0, 0.0]
            for column in range(0, lanes, 128):
                here = slice(column, column + 128) if tile == lanes else slice(None)
                real_wide = wide[real_at : real_at + block, here]
                imag_wide = wide[imag_at : imag_at + block, here]
                w_real = weight[row : row + block, column : column + 128]
                w_imag = weight[row : row + block, lanes + column : lanes + column + 128]
                w_real = w_real.astype(jnp.float32)
                w_imag = w_imag.astype(jnp.float32)
                if adjoint:
                    real = real_wide * w_real + imag_wide * w_imag
                    imag = imag_wide * w_real - real_wide * w_imag
                    there = slice(column, column + 128)
                    product[real_at : real_at + block, there] = real.astype(jnp.bfloat16)
                    product[imag_at : imag_at + block, there] = imag.astype(jnp.bfloat16)
                else:
                    sums[0] = sums[0] + (real_wide * w_real - imag_wide * w_imag)
                    sums[1] = sums[1] + (real_wide * w_imag + imag_wide * w_real)
            if not adjoint:
                product[real_at : real_at + block] = sums[0].astype(jnp.bfloat16)
                product[imag_at : imag_at + block] = sums[1].astype(jnp.bfloat16)
        total[...] += jnp.where(mine, dot(product[...], sum_table[...]), 0.0)

    @pl.when(step == steps - 1)
    def _():
        modes = total[...] * scale_out
        left = [modes[2 * h * quarter : 2 * (h + 1) * quarter].T for h in range(2)]
        modes = dot(jnp.concatenate(left, axis=0).astype(jnp.bfloat16), z_out[...])
        for s in range(slabs):
            for h in range(2):
                here = modes[h * lines : (h + 1) * lines, s * half : (s + 1) * half]
                out[s, :, h * half : (h + 1) * half] = here.astype(jnp.bfloat16)


def mix(planar, weight, scale_in, scale_out, partner=None, copies=0):
    slabs, lines, width = planar.shape
    adjoint = partner is not None
    depth = KX // slabs
    channels = lines // depth
    rows = KY * KZ
    steps = 2
    z_in = constant(forward_z_table())
    z_out = constant(inverse_z_table())
    first = first_table(channels, depth)
    second = second_table(channels, depth)
    spread_table = constant(second[:, :128] if adjoint else first)
    sum_table = constant(first.T if adjoint else second[:, :128].T)
    shape = (2 * rows, lines)
    in_specs = [
        whole(planar.shape),
        pl.BlockSpec((depth // steps * rows, weight.shape[1]), lambda j: (j, 0)),
        whole(z_in.shape),
        whole(z_out.shape),
        whole(spread_table.shape),
        whole(sum_table.shape),
    ]
    operands = [planar, weight, z_in, z_out, spread_table, sum_table]
    scratch = [
        pltpu.VMEM(shape, jnp.float32),
        pltpu.VMEM((2 * rows, spread_table.shape[1]), jnp.float32),
        pltpu.VMEM((2 * rows, sum_table.shape[0]), jnp.bfloat16),
    ]
    if adjoint:
        in_specs.append(whole(shape))
        operands.append(partner)
        scratch = [pltpu.VMEM(shape, jnp.bfloat16)] + scratch
        outs = [planar.shape, (copies, 3 * rows, lines)]
    else:
        outs = [shape, planar.shape]
    return pl.pallas_call(
        functools.partial(mixing_kernel, scale_in, scale_out, adjoint),
        grid=(steps,),
        in_specs=in_specs,
        out_specs=[whole(out) for out in outs],
        out_shape=[jax.ShapeDtypeStruct(out, jnp.bfloat16) for out in outs],
        scratch_shapes=scratch,
        compiler_params=params(ROOMY),
        cost_estimate=HEAVY,
        name="mix_back" if adjoint else "mix",
    )(*operands)


def plane_mobility(grains):
    same = [
        jnp.concatenate([grains[:1], grains[:-1]], axis=0),
        jnp.concatenate([grains[1:], grains[-1:]], axis=0),
        jnp.concatenate([grains[:, :1], grains[:, :-1]], axis=1),
        jnp.concatenate([grains[:, 1:], grains[:, -1:]], axis=1),
    ]
    total = jnp.full(grains.shape, 0.25, jnp.float32)
    for other in same:
        total = total + jnp.where(grains != other, 0.25, 0.0)
    return total


def layer_kernel(bias, planar, smooth, cotangent, grains, point_weight, repeat, ix_table, iy_table,
                 x_table, y_table, spread, out, first, last, *rest):
    pair = pl.program_id(0)
    waves, spectral, moving, delta, rows, bias_wide, mix_out, mix_in = rest
    pairs = rows.shape[0]
    channels = cotangent.shape[0]
    slabs = planar.shape[0]

    @pl.when(pair == 0)
    def _():
        for c in range(channels):
            bias_wide[c] = jnp.full(bias_wide.shape[1:], 0.5 * bias[c], jnp.float32)
        tall = dot(repeat[...], point_weight[...]).astype(jnp.bfloat16)
        square = lax.dot_general(
            tall, repeat[...], (((1,), (1,)), ((), ())), preferred_element_type=jnp.float32
        )
        row = lax.broadcasted_iota(jnp.int32, square.shape, 0) % 8
        column = lax.broadcasted_iota(jnp.int32, square.shape, 1) % 8
        square = jnp.where(row == column, square, 0.0)
        mix_in[...] = square.astype(jnp.bfloat16)
        mix_out[...] = square.T.astype(jnp.bfloat16)

    lines = planar.shape[1]
    step = jnp.concatenate([planar[s] for s in range(slabs)], axis=0)
    step = dot(step, iy_table[0]).astype(jnp.bfloat16)
    for s in range(slabs):
        for t in range(2):
            waves[s, t] = step[s * lines : (s + 1) * lines, 2 * NY * t : 2 * NY * (t + 1)]
    group = 8 * (KX // slabs)
    for g in range(channels // 8):
        here = slice(g * group, (g + 1) * group)
        wave = [waves[s, t, here, :] for s in range(slabs) for t in range(2)]
        step = dot(ix_table[...], jnp.concatenate(wave, axis=0))
        spectral[8 * g : 8 * g + 8] = step.reshape(8, NX, 2 * NY)
    for q in range(2):
        moving[:, q * NY : (q + 1) * NY] = 0.5 * plane_mobility(grains[q])

    def body(i, _):
        x = pl.multiple_of(16 * i, 16)
        halves = [cotangent[:, q, pl.ds(x, 16), :] for q in range(2)]
        cotangent_here = jnp.concatenate(halves, axis=2).astype(jnp.float32)
        spreads = []
        for h in range(2):
            at = pl.ds(pl.multiple_of(x + 8 * h, 8), 8)
            mobile = moving[at, :][None]
            local = dot(mix_out[...], smooth[0, 2 * i + h]).reshape(channels, 8, 2 * NY)
            half = spectral[:, at, :] + mobile * local + bias_wide[...]
            wave = jnp.tanh(half)
            slope = (1.0 + wave) * (1.0 + (half - half * wave))
            change = cotangent_here[:, 8 * h : 8 * h + 8, :] * slope
            right = change.reshape(8 * channels, 2 * NY).astype(jnp.bfloat16)
            delta[2 * i + h] = right
            back = dot(mix_in[...], right).reshape(channels, 8, 2 * NY)
            spreads.append(mobile * back)
        both = jnp.concatenate(spreads, axis=1).astype(jnp.bfloat16)
        for q in range(2):
            spread[:, q, pl.ds(x, 16), :] = both[:, :, q * NY : (q + 1) * NY]
        return 0

    lax.fori_loop(0, NX // 16, body, 0, unroll=8)


    @pl.when(pair == 0)
    def _():
        first[:, 0] = spread[:, 0]

    @pl.when(pair == pairs - 1)
    def _():
        last[:, 0] = spread[:, 1]

    def load(i):
        return delta[:, 16 * i : 16 * i + 16, :].reshape(2 * NX, 2 * NY)

    store_rows(rows, pair, x_table, load)

    @pl.when(pair == pairs - 1)
    def _():
        store_modes(rows, y_table, out)


def layer(planar, smooth, cotangent, grains, bias, point_weight):
    slabs, lines, width = planar.shape
    channels, planes = cotangent.shape[:2]
    pairs = planes // 2
    repeat = constant(np.repeat(np.eye(channels), 8, axis=0))
    ix_table = constant(inverse_x_table(slabs, 8))
    iy_table = constant(inverse_y_table(planes, 2))
    x_table = constant(forward_x_table(slabs, True))
    y_table = constant(forward_y_table(planes))
    field = pl.BlockSpec((channels, 2, NX, NY), lambda p: (0, p, 0, 0))
    outs = [cotangent.shape, planar.shape] + [(channels, 1, NX, NY)] * 2
    return pl.pallas_call(
        layer_kernel,
        grid=(pairs,),
        in_specs=[
            pl.BlockSpec(memory_space=pltpu.SMEM),
            whole(planar.shape),
            pl.BlockSpec((1,) + smooth.shape[1:], lambda p: (p, 0, 0, 0)),
            field,
            pl.BlockSpec((2, NX, NY), lambda p: (p, 0, 0)),
            whole(point_weight.shape),
            whole(repeat.shape),
            whole(ix_table.shape),
            pl.BlockSpec((1,) + iy_table.shape[1:], lambda p: (p, 0, 0)),
            whole(x_table.shape),
            whole(y_table.shape),
        ],
        out_specs=[field] + [whole(out) for out in outs[1:]],
        out_shape=[jax.ShapeDtypeStruct(out, jnp.bfloat16) for out in outs],
        scratch_shapes=[
            pltpu.VMEM((slabs, 2, lines, 2 * NY), jnp.bfloat16),
            pltpu.VMEM((channels, NX, 2 * NY), jnp.float32),
            pltpu.VMEM((NX, 2 * NY), jnp.float32),
            pltpu.VMEM((NX // 8, 8 * channels, 2 * NY), jnp.bfloat16),
            pltpu.VMEM((pairs, 2, slabs, lines, 2 * NY), jnp.bfloat16),
            pltpu.VMEM((channels, 8, 2 * NY), jnp.float32),
            pltpu.VMEM((8 * channels, 8 * channels), jnp.bfloat16),
            pltpu.VMEM((8 * channels, 8 * channels), jnp.bfloat16),
        ],
        compiler_params=params(),
        cost_estimate=LIGHT,
        name="layer",
    )(bias, planar, smooth, cotangent, grains, point_weight, repeat, ix_table, iy_table, x_table,
      y_table)


def build_tile(adjoint, taps, channel, dy, q, planes, span):
    row = lax.broadcasted_iota(jnp.int32, (8, 128), 0)
    lane = lax.broadcasted_iota(jnp.int32, (8, 128), 1)
    tile = jnp.zeros((8, 128), jnp.float32)
    for k, plane in enumerate(planes):
        dz = plane - q
        if not 0 <= dz <= 2:
            continue
        for dx in range(3):
            number = 9 * dz + 3 * dx + dy
            tap = taps[26 - number if adjoint else number, channel]
            tile = jnp.where(lane == (span * k + row + (dx - 1)) % 128, tap, tile)
    return tile


def build_band(adjoint, taps, channel, band, tail):
    row = lax.broadcasted_iota(jnp.int32, (8, 128), 0)
    lane = lax.broadcasted_iota(jnp.int32, (8, 128), 1)
    heads, middles, tails = [], [], []
    for dy in range(3):
        for q in range(2):
            sides = []
            for planes in ((0, 1), (2, 3)):
                tile = build_tile(adjoint, taps, channel, dy, q, planes, 64)
                tiles = [pltpu.roll(tile, 8 * k, axis=1) for k in range(1, 7)]
                first = jnp.where((row == 0) & (lane % 64 == 63), 0.0, tile)
                sides.append([first] + tiles)
            blocks = [jnp.concatenate(pair, axis=1) for pair in zip(*sides)]
            heads += blocks
            middles += blocks[1:]
            tile = build_tile(adjoint, taps, channel, dy, q, range(4), 32)
            tiles = [pltpu.roll(tile, 8 * k, axis=1) for k in range(1, 4)]
            tiles[2] = jnp.where((row == 7) & (lane % 32 == 0), 0.0, tiles[2])
            tails += tiles
    band[...] = jnp.concatenate(heads + middles, axis=0).astype(jnp.bfloat16)
    tail[...] = jnp.concatenate(tails, axis=0).astype(jnp.bfloat16)


def apply_band(quads, band):
    band, tail = band
    counts = (56, 48, 24)
    ends = (6 * counts[0], 6 * (counts[0] + counts[1]))
    lefts = (band[: ends[0], :], band[ends[0] : ends[1], :], tail[...])
    lane = lax.broadcasted_iota(jnp.int32, (NX, NY), 1)
    totals = []
    for group in range(0, len(quads), 2):
        products = []
        for left, x, span in zip(lefts, (0, 48, 96), (64, 64, 32)):
            right = [
                jnp.concatenate([sheet[x : x + span] for sheet in quads[group + p]], axis=0)
                for p in range(2)
            ]
            products.append(dot(left, jnp.concatenate(right, axis=1)))
        for p in range(2):
            wide = slice(NY * p, NY * (p + 1))
            pair = []
            for q in range(2):
                shifted = []
                for dy in range(3):
                    b = 2 * dy + q
                    pieces = [
                        product[count * b : count * (b + 1), wide]
                        for product, count in zip(products, counts)
                    ]
                    shifted.append(jnp.concatenate(pieces, axis=0))
                before = jnp.where(lane == 0, 0.0, pltpu.roll(shifted[0], 1, axis=1))
                after = jnp.where(lane == NY - 1, 0.0, pltpu.roll(shifted[2], NY - 1, axis=1))
                pair.append(shifted[1] + before + after)
            totals.append(jnp.concatenate(pair, axis=1))
    return totals


def banded(adjoint, taps, start, bands, channels):
    step = pl.program_id(0)
    final = start + channels * pl.num_programs(0) - 1

    @pl.when(step == 0)
    def _():
        build_band(adjoint, taps, start, *bands[0])

    def run(visit):
        for c in range(channels):
            following = jnp.minimum(start + channels * step + c + 1, final)
            build_band(adjoint, taps, following, *bands[(c + 1) % channels])
            visit(c, bands[c])

    return run


def band_scratch(channels):
    shapes = [(6 * (56 + 48), 256), (6 * 24, 128)]
    return [pltpu.VMEM(shape, jnp.bfloat16) for shape in shapes * channels]


def paired(refs):
    return list(zip(refs[0::2], refs[1::2]))


def smooth_kernel(start, taps, before, field, after, *rest):
    out, *bands = rest[-2 * field.shape[0] - 1 :]
    bands = paired(bands)
    planes = field.shape[1]
    totals = []

    def visit(c, band):
        sheets = [before[c, 0]] + [field[c, z] for z in range(planes)] + [after[c, 0]]
        totals.append(apply_band([sheets[z : z + 4] for z in range(0, planes, 2)], band))

        if c % 2 == 1:
            for p in range(planes // 2):
                both = [total[p].reshape(NX // 8, 8, 2 * NY) for total in totals[c - 1 : c + 1]]
                both = jnp.concatenate(both, axis=1).astype(jnp.bfloat16)
                out[p, :, 8 * (c - 1) : 8 * (c + 1), :] = both

    banded(False, taps, start, bands, field.shape[0])(visit)


def smooth_planes(field, rims, taps, done=None):
    channels, planes = field.shape[:2]
    pairs = planes // 2
    low = low_channels(channels)
    start = 0 if done is None else low
    count = low if done is None else channels - low
    step = 4
    skip = start // step
    rim = pl.BlockSpec((step, 1, NX, NY), lambda c: (c, 0, 0, 0))
    sheets = pl.BlockSpec((step, planes, NX, NY), lambda c: (c + skip, 0, 0, 0))
    in_specs = [pl.BlockSpec(memory_space=pltpu.SMEM), rim, sheets, rim]
    operands = [taps, rims[0], field, rims[1]]
    if done is not None:
        in_specs.append(pl.BlockSpec(memory_space=pl.ANY))
        operands.append(done)
    return pl.pallas_call(
        functools.partial(smooth_kernel, start),
        grid=(count // step,),
        in_specs=in_specs,
        out_specs=pl.BlockSpec((pairs, NX // 8, 8 * step, 2 * NY), lambda c: (0, 0, c + skip, 0)),
        out_shape=jax.ShapeDtypeStruct((pairs, NX // 8, 8 * channels, 2 * NY), jnp.bfloat16),
        input_output_aliases={} if done is None else {4: 0},
        scratch_shapes=band_scratch(step),
        compiler_params=params(ROOMY),
        cost_estimate=LIGHT,
        name="smooth_low" if done is None else "smooth_high",
    )(*operands)


def inner_kernel(taps, field, out, *bands):
    bands = paired(bands)
    planes = field.shape[1]

    def visit(c, band):
        quads = [[field[c, z + k] for k in range(4)] for z in range(1, planes - 3, 2)]
        for p, near in enumerate(apply_band(quads, band)):
            total = near.astype(jnp.bfloat16)
            out[c, 2 * p] = total[:, :NY]
            out[c, 2 * p + 1] = total[:, NY:]

    banded(True, taps, 0, bands, field.shape[0])(visit)


def near_inner(field, taps):
    channels, planes = field.shape[:2]
    step = 8
    shape = (channels, planes - 4, NX, NY)
    return pl.pallas_call(
        inner_kernel,
        grid=(channels // step,),
        in_specs=[
            pl.BlockSpec(memory_space=pltpu.SMEM),
            pl.BlockSpec((step, planes, NX, NY), lambda c: (c, 0, 0, 0)),
        ],
        out_specs=pl.BlockSpec((step,) + shape[1:], lambda c: (c, 0, 0, 0)),
        out_shape=jax.ShapeDtypeStruct(shape, jnp.bfloat16),
        scratch_shapes=band_scratch(step),
        compiler_params=params(),
        cost_estimate=LIGHT,
        name="near_inner",
    )(taps, field)


def finish_kernel(taps, before, field, after, inner, planar, ix_table, iy_table, out, waves,
                  *bands):
    bands = paired(bands)
    step = pl.program_id(0)
    slabs, lines = planar.shape[:2]
    planes = field.shape[1]
    span = planes * NY

    @pl.when(step == 0)
    def _():
        left = jnp.concatenate([planar[s] for s in range(slabs)], axis=0)
        for t in range(2):
            wave = dot(left, iy_table[0, :, t * span : (t + 1) * span]).astype(jnp.bfloat16)
            for s in range(slabs):
                waves[s, t] = wave[s * lines : (s + 1) * lines]

    rows = field.shape[0] * (KX // slabs)
    here = pl.ds(pl.multiple_of(rows * step, rows), rows)
    right = [waves[s, t, here, :] for s in range(slabs) for t in range(2)]
    right = jnp.concatenate(right, axis=0)
    far = [
        dot(ix_table[...], right[:, 2 * p * NY : 2 * (p + 1) * NY]) for p in range(planes // 2)
    ]

    def store(c, p, near):
        for q in range(2):
            total = near[q] + far[p][c * NX : (c + 1) * NX, q * NY : (q + 1) * NY]
            out[c, 2 * p + q] = total.astype(jnp.bfloat16)

    def visit(c, band):
        low = [before[c, 0]] + [field[c, z] for z in range(3)]
        high = [field[c, z] for z in range(planes - 3, planes)] + [after[c, 0]]
        for p, near in zip((0, planes // 2 - 1), apply_band([low, high], band)):
            store(c, p, [near[:, :NY], near[:, NY:]])
        for p in range(1, planes // 2 - 1):
            store(c, p, [inner[c, 2 * p - 2 + q].astype(jnp.float32) for q in range(2)])

    banded(True, taps, 0, bands, field.shape[0])(visit)


def finish(planar, spread, rims, inner, taps):
    slabs, lines, width = planar.shape
    channels, planes = spread.shape[:2]
    step = 8
    ix_table = constant(inverse_x_table(slabs, step))
    iy_table = constant(inverse_y_table(planes, planes))
    rim = pl.BlockSpec((step, 1, NX, NY), lambda c: (c, 0, 0, 0))
    sheets = pl.BlockSpec((step, planes, NX, NY), lambda c: (c, 0, 0, 0))
    return pl.pallas_call(
        finish_kernel,
        grid=(channels // step,),
        in_specs=[
            pl.BlockSpec(memory_space=pltpu.SMEM),
            rim,
            sheets,
            rim,
            pl.BlockSpec((step,) + inner.shape[1:], lambda c: (c, 0, 0, 0)),
            whole(planar.shape),
            whole(ix_table.shape),
            whole(iy_table.shape),
        ],
        out_specs=sheets,
        out_shape=jax.ShapeDtypeStruct(spread.shape, jnp.bfloat16),
        scratch_shapes=[
            pltpu.VMEM((slabs, 2, lines, planes * NY), jnp.bfloat16),
            *band_scratch(step),
        ],
        compiler_params=params(ROOMY),
        cost_estimate=HEAVY,
        name="finish",
    )(taps, rims[0], spread, rims[1], inner, planar, ix_table, iy_table)


def gradient_kernel(gathered, first, second, out):
    step = pl.program_id(0)
    samples, rows, lines = gathered.shape
    quarter = rows // 6
    depth = out.shape[0] // (2 * quarter)
    real_part = lax.axis_index("dp") < lax.axis_size("dp") // 2
    lane = lax.broadcasted_iota(jnp.int32, (1, lines), 1)
    duals = []
    for s in range(samples):
        for h in range(2):
            at = (2 * h + 2) * quarter
            real = gathered[s, at : at + quarter]
            imag = gathered[s, at + quarter : at + 2 * quarter]
            duals.append(jnp.where(real_part, real, imag))
            duals.append(jnp.where(real_part, imag, -real))
    duals = jnp.concatenate(duals, axis=0)
    for j in range(depth):
        mine = lane % (depth * pl.num_programs(0)) == depth * step + j
        spectra = []
        for s in range(samples):
            for h in range(2):
                here = mine & (lane // (lines // 2) == h)
                spectra.append(jnp.where(here, gathered[s, : 2 * quarter], 0))
        spectra = jnp.concatenate(spectra, axis=0)
        wide = dot(jnp.where(mine, duals, 0), second[...])
        for column in range(0, out.shape[1], 256):
            product = dot(spectra, first[:, column : column + 256])
            for at in range(0, 256, 128):
                for h in range(2):
                    total = 0.0
                    for s in range(samples):
                        for part in range(2):
                            row = (4 * s + 2 * h + part) * quarter
                            here = slice(row, row + quarter)
                            total = total + product[here, at : at + 128] * wide[here]
                    row = (2 * j + h) * quarter
                    there = slice(column + at, column + at + 128)
                    out[row : row + quarter, there] = total * (1.0 / samples)


def weight_gradient(gathered, depth, width):
    samples, rows, lines = gathered.shape
    channels = lines // depth
    first = np.repeat(np.eye(channels // 2), channels, axis=1)
    first = constant(np.tile(np.repeat(first, depth, axis=0), (2, 1)))
    second = constant(second_table(channels, depth)[:, :128])
    steps = 2
    half = rows // 3
    return pl.pallas_call(
        gradient_kernel,
        grid=(steps,),
        in_specs=[whole(gathered.shape), whole(first.shape), whole(second.shape)],
        out_specs=pl.BlockSpec((depth // steps * half, width), lambda j: (j, 0)),
        out_shape=jax.ShapeDtypeStruct((depth * half, width), jnp.float32),
        compiler_params=params(ROOMY),
        cost_estimate=LIGHT,
        name="weight_gradient",
    )(gathered, first, second)


def exchange(first, last):
    size = lax.axis_size("slab")
    up = [(i, i + 1) for i in range(size - 1)]
    down = [(j, i) for i, j in up]
    return lax.ppermute(last, "slab", up), lax.ppermute(first, "slab", down)


def swap(planar):
    return lax.all_to_all(planar, "slab", split_axis=0, concat_axis=0)


def local_fast(feats, grains, spec_weight, taps, point_weight, bias, cotangent):
    slabs = lax.axis_size("slab")
    copies = lax.axis_size("dp")
    barrier = lax.optimization_barrier
    field = feats[0]
    channels = field.shape[0]
    cell_scale = 1.0 / math.sqrt(NX * NY * NZ)
    mode_scale = 1.0 / math.sqrt(KX * KY * KZ)
    mode_rows = spec_weight.shape[0]
    weight = spec_weight.reshape(mode_rows * KZ, 2 * channels * channels)
    width = weight.shape[1] // copies

    first, first_high, last, last_high = cut_rims(field)
    rims = exchange(first, last)
    planar = swap(forward_modes(field, slabs))
    rims, first, last = barrier((rims, first_high, last_high))
    rims_high = exchange(first, last)
    planar, smooth = barrier((planar, smooth_planes(field, rims, taps)))
    spectrum, planar = mix(planar, weight, cell_scale, 0.5 * mode_scale)
    smooth, spectrum = barrier((smooth, spectrum))
    planar = swap(planar)
    smooth = smooth_planes(field, rims_high, taps, smooth)
    spread, planar, first, last = layer(planar, smooth, cotangent[0], grains[0], bias, point_weight)
    rims = exchange(first, last)
    planar, send = mix(swap(planar), weight, 0.5 * mode_scale, cell_scale, spectrum, copies)
    send, spread = barrier((send, spread))
    inner = near_inner(spread, taps)
    gathered = lax.all_to_all(send, "dp", split_axis=0, concat_axis=0)
    planar, gathered, inner, rims = barrier((planar, gathered, inner, rims))
    planar = swap(planar)
    grad_spec = weight_gradient(gathered, KX // slabs, width)
    planar, grad_spec = barrier((planar, grad_spec))
    grad_feats = finish(planar, spread, rims, inner, taps)[None]
    return (grad_feats, grad_spec.reshape(mode_rows, KZ, width))


def local(feats, grains, spec_weight, taps, point_weight, bias, cotangent):
    samples, channels, planes = feats.shape[:3]
    width = spec_weight.shape[2] // lax.axis_size("dp")
    fits = (
        lax.axis_size("slab") * 4 == KX
        and samples == 1
        and channels == 32
        and planes == 8
        and channels * channels == 2 * width
    )
    form = local_fast if fits else local_any
    return form(feats, grains, spec_weight, taps, point_weight, bias, cotangent)


def solution(mesh):
    in_specs = (
        P(("grp", "dp"), None, "slab", None, None),
        P(("grp", "dp"), "slab", None, None),
        P("slab", None, None),
        P(),
        P(),
        P(),
        P(("grp", "dp"), None, "slab", None, None),
    )
    out_specs = (P(("grp", "dp"), None, "slab", None, None), P("slab", "grp", "dp"))
    return jax.shard_map(local, mesh=mesh, in_specs=in_specs, out_specs=out_specs, check_vma=False)
```
